32 devices in a mesh: wide: 4 (over y, x), narrow: 8 (over z, core).
Axes of the slice: x: 2, y: 2, z: 4, core: 2. Of those that a mesh axis runs over, the one named last changes fastest.
Arguments:
- messages: bfloat16 [49152, 512], P(('wide', 'narrow')), may hold values from -6 to 6
- reverse_position: int32 [49152], P(('wide', 'narrow')), may hold values from 0 to 383, as said below
- route_slot: int32 [49152], P(('wide', 'narrow')), may hold values from 0 to 3071, as said below
- atom_slots: int32 [49152], P(('wide', 'narrow')), may hold values from 0 to 3071, as said below
- angles: bfloat16 [1536, 1024], P(('wide', 'narrow')), may hold values from -1 to 1
- weight_message: bfloat16 [2, 512, 512], replicated, may hold values from -0.25 to 0.25
- weight_reverse: bfloat16 [2, 512, 512], replicated, may hold values from -0.25 to 0.25
- weight_combine: bfloat16 [2, 512, 512], replicated, may hold values from -0.25 to 0.25
- weight_inner: bfloat16 [2, 512, 512], replicated, may hold values from -0.25 to 0.25
- weight_outer: bfloat16 [2, 512, 512], replicated, may hold values from -0.25 to 0.25
- weight_lift: bfloat16 [2, 512, 512], replicated, may hold values from -0.25 to 0.25
- weight_expand: bfloat16 [2, 512, 512], replicated, may hold values from -0.25 to 0.25
- weight_reduce: bfloat16 [2, 512, 512], replicated, may hold values from -0.25 to 0.25
Outputs:
- updated: bfloat16 [49152, 512], P(('wide', 'narrow'))
The draws below stay inside these ranges and needn't reach their ends.
Inputs may be any that keep to these rules, and one draw needn't show every extreme that they name: With e written as ((w * 8 + n) * 4 + s) * 384 + i, the reverse edge of e is ((s * 8 + n) * 4 + w) * 384 + reverse_position[e]; the reverse of the reverse is e, no edge is its own reverse, and the source atom of e is the target atom of its reverse. The target atom of an edge of device block w * 8 + n lies in atom block w * 8 + o (atom j in block j // 48), and route_slot = o * 384 + c with c distinct among the edges of one device block that have the same o. In every device block 384 edges have one o, none another o, and 192 each of the others; within each sub-block of the device block, 96 edges have that first o, none the second, and 48 each of the others. `atom_slots`: entry j * 32 + q, for atom j in block w * 8 + o, names the q-th incoming edge of j as n * 384 + c: the edge of device block w * 8 + n whose route_slot is o * 384 + c. Every atom has exactly 32 incoming edges, every edge is named once, and entries q from s * 8 to (s + 1) * 8 - 1 name edges of sub-block s.
All inputs are finite; a program needn't handle non-finite values.
Results may differ from the reference program's by a relative error of at most 0.015.
Values may be sent and summed in bfloat16 or wider, within the bound.
No kernel may reach another device: no remote copies, remote signals or barrier semaphores. Data moves between devices by JAX's collectives and lax.ppermute only.
A program may use at most 128 MiB of HBM per device.

```python
import jax
import jax.numpy as jnp
from jax import lax

D = 512
SLOTS = 32
ATOM_DEV = 48
BLOCKS = 2
EDGE_DEV = 1536
COPIES = 8
SUBBLOCK = 384
CAP = 384
ATOMS = 1536
EDGES = 49152
N_WIDE = 4
N_NARROW = 8


def shuffled(key, shape):
    length = shape[-1]
    limit = 2147483647 // length
    scores = jax.random.randint(key, shape, 0, limit, dtype=jnp.int32) * length
    scores = scores + lax.broadcasted_iota(jnp.int32, shape, len(shape) - 1)
    return jnp.argsort(scores, axis=-1).astype(jnp.int32)


def build_graph(key):
    wide_count = N_WIDE
    narrow_count = N_NARROW
    sub_rows = SUBBLOCK
    device_rows = EDGE_DEV
    capacity = CAP
    share = sub_rows // narrow_count
    keys = jax.random.split(jax.random.fold_in(key, 271), 5)
    first_owner = shuffled(keys[0], (wide_count, narrow_count))
    second_owner = jnp.roll(first_owner, 1, axis=1)
    owner_ids = jnp.arange(narrow_count, dtype=jnp.int32)
    heavy = (owner_ids[None, None, :] == first_owner[:, :, None]).astype(jnp.int32)
    empty_pair = (owner_ids[None, None, :] == second_owner[:, :, None]).astype(jnp.int32)
    counts = share * (1 + heavy - empty_pair)
    piece_start = jnp.cumsum(counts, axis=1) - counts
    row_end = jnp.cumsum(counts, axis=2)
    row_start = row_end - counts
    positions = jnp.arange(sub_rows, dtype=jnp.int32)
    owner_at = jnp.sum((row_end[:, :, None, :] <= positions[None, None, :, None]).astype(jnp.int32), axis=3)
    start_at = jnp.take_along_axis(row_start, owner_at, axis=2)
    offset_at = jnp.take_along_axis(piece_start, owner_at, axis=2)
    item_pos = offset_at + positions[None, None, :] - start_at
    orders = shuffled(keys[1], (wide_count, wide_count, narrow_count, sub_rows))
    wide_ids = jnp.arange(wide_count, dtype=jnp.int32)[:, None, None, None]
    side_ids = jnp.arange(wide_count, dtype=jnp.int32)[None, None, :, None]
    items = orders[wide_ids, side_ids, owner_at[:, :, None, :], item_pos[:, :, None, :]]
    placing = shuffled(keys[2], (wide_count, narrow_count, wide_count, sub_rows))
    items = jnp.take_along_axis(items, placing, axis=3)
    owners = jnp.take_along_axis(jnp.broadcast_to(owner_at[:, :, None, :], items.shape), placing, axis=3)
    local_atom = items // COPIES
    copy_index = items % COPIES
    base_perm = shuffled(keys[3], (wide_count, narrow_count, wide_count, sub_rows))
    inverse_perm = jnp.argsort(base_perm, axis=3).astype(jnp.int32)
    mirrored = jnp.transpose(inverse_perm, (2, 1, 0, 3))
    paired = jnp.take_along_axis(base_perm, jnp.bitwise_xor(inverse_perm, 1), axis=3)
    row_wide = jnp.arange(wide_count, dtype=jnp.int32)[:, None, None, None]
    reverse_position = jnp.where(row_wide < side_ids, base_perm, jnp.where(row_wide > side_ids, mirrored, paired))
    flat_owner = owners.reshape(wide_count, narrow_count, device_rows)
    random_rank = shuffled(keys[4], (wide_count, narrow_count, device_rows))
    order_rows = jnp.argsort(flat_owner * device_rows + random_rank, axis=2).astype(jnp.int32)
    ranking = jnp.argsort(order_rows, axis=2).astype(jnp.int32)
    totals = counts * wide_count
    device_start = jnp.cumsum(totals, axis=2) - totals
    slot_rows = ranking - jnp.take_along_axis(device_start, flat_owner, axis=2)
    route_slot = flat_owner * capacity + slot_rows
    wide_three = jnp.arange(wide_count, dtype=jnp.int32)[:, None, None]
    narrow_three = jnp.arange(narrow_count, dtype=jnp.int32)[None, :, None]
    atom_index = (wide_three * narrow_count + flat_owner) * ATOM_DEV + local_atom.reshape(wide_count, narrow_count, device_rows)
    side_index = (jnp.arange(device_rows, dtype=jnp.int32) // sub_rows)[None, None, :]
    list_index = side_index * COPIES + copy_index.reshape(wide_count, narrow_count, device_rows)
    target_entry = atom_index * SLOTS + list_index
    entry_value = narrow_three * capacity + slot_rows
    atom_slots = jnp.zeros((EDGES,), jnp.int32).at[target_entry.reshape(-1)].set(entry_value.reshape(-1))
    return (reverse_position.reshape(-1), route_slot.reshape(-1), atom_slots)


def draw_reverse_position(key, part):
    return build_graph(key)[0]


def draw_route_slot(key, part):
    return build_graph(key)[1]


def draw_atom_slots(key, part):
    return build_graph(key)[2]


def block_levels(rng, dims, pieces, low, top_value):
    loudness = 1.0
    for dim, shards_of in pieces:
        draws = jax.random.uniform(jax.random.fold_in(jax.random.fold_in(rng, 6), dim), (shards_of,), jnp.float32, low / len(pieces), top_value / len(pieces))
        loudness = loudness * jnp.repeat(jnp.exp(draws), dims[dim] // shards_of).reshape((-1,) + (1,) * (len(dims) - 1 - dim))
    return loudness


def bell_draw(rng, dims, spread, most, shards=(), held_as=jnp.bfloat16):
    entries = spread * jax.random.normal(rng, dims, jnp.float32)
    if shards:
        entries = entries * block_levels(rng, dims, shards, -0.22, 0.18)
    return jnp.clip(entries, -most, most).astype(held_as)


def setup_inputs(seed: int = 0) -> dict:
    key_list = jax.random.split(jax.random.key(seed), 14)
    messages = bell_draw(key_list[0], (EDGES, D), 1.0, 6.0, ((0, 32),))
    reverse_position = draw_reverse_position(jax.random.fold_in(key_list[13], 71), 0)
    route_slot = draw_route_slot(jax.random.fold_in(key_list[13], 71), 0)
    atom_slots = draw_atom_slots(jax.random.fold_in(key_list[13], 71), 0)
    angles = bell_draw(key_list[4], (ATOMS, SLOTS * SLOTS), SLOTS ** -0.5, 1.0, ((0, 32),))
    weight_message = bell_draw(key_list[5], (BLOCKS, D, D), D ** -0.5, 0.25)
    weight_reverse = bell_draw(key_list[6], (BLOCKS, D, D), D ** -0.5, 0.25)
    weight_combine = bell_draw(key_list[7], (BLOCKS, D, D), D ** -0.5, 0.25)
    weight_inner = bell_draw(key_list[8], (BLOCKS, D, D), D ** -0.5, 0.25)
    weight_outer = bell_draw(key_list[9], (BLOCKS, D, D), D ** -0.5, 0.25)
    weight_lift = bell_draw(key_list[10], (BLOCKS, D, D), D ** -0.5, 0.25)
    weight_expand = bell_draw(key_list[11], (BLOCKS, D, D), D ** -0.5, 0.25)
    weight_reduce = bell_draw(key_list[12], (BLOCKS, D, D), D ** -0.5, 0.25)
    return dict(messages=messages, reverse_position=reverse_position, route_slot=route_slot, atom_slots=atom_slots, angles=angles, weight_message=weight_message, weight_reverse=weight_reverse, weight_combine=weight_combine, weight_inner=weight_inner, weight_outer=weight_outer, weight_lift=weight_lift, weight_expand=weight_expand, weight_reduce=weight_reduce)


ROOT_HALF = 0.7071067811865476


def project(operand, weight):
    return jnp.dot(operand, weight, preferred_element_type=jnp.float32)


def residual(previous, branch):
    return ((previous.astype(jnp.float32) + branch) * ROOT_HALF).astype(jnp.bfloat16)


def reverse_index(reverse_position):
    edge_ids = jnp.arange(EDGES, dtype=jnp.int32)
    block_rows = edge_ids // SUBBLOCK
    side_index = block_rows % N_WIDE
    narrow_index = (block_rows // N_WIDE) % N_NARROW
    wide_index = block_rows // (N_WIDE * N_NARROW)
    return ((side_index * N_NARROW + narrow_index) * N_WIDE + wide_index) * SUBBLOCK + reverse_position


def edge_lists(route_slot, atom_slots):
    edge_ids = jnp.arange(EDGES, dtype=jnp.int32)
    device_index = edge_ids // EDGE_DEV
    narrow_index = device_index % N_NARROW
    owner_block = device_index - narrow_index + route_slot // CAP
    table_key = owner_block * (N_NARROW * CAP) + narrow_index * CAP + route_slot % CAP
    edge_table = jnp.zeros((N_WIDE * N_NARROW * N_NARROW * CAP,), jnp.int32).at[table_key].set(edge_ids)
    entry_ids = jnp.arange(ATOMS * SLOTS, dtype=jnp.int32)
    atom_block = entry_ids // (SLOTS * ATOM_DEV)
    listed = edge_table[atom_block * (N_NARROW * CAP) + atom_slots]
    entry_of = jnp.zeros((EDGES,), jnp.int32).at[listed].set(entry_ids)
    return listed, entry_of


def mix_block(operands):
    return jnp.einsum("apq,aqd->apd", operands[0], operands[1].astype(jnp.float32),
                      precision=lax.Precision.HIGHEST).astype(jnp.bfloat16)


def reference(messages, reverse_position, route_slot, atom_slots, angles, weight_message, weight_reverse,
              weight_combine, weight_inner, weight_outer, weight_lift, weight_expand, weight_reduce):
    partner = reverse_index(reverse_position)
    listed, entry_of = edge_lists(route_slot, atom_slots)
    turn_rows = entry_of[partner]
    mixing = angles.astype(jnp.float32).reshape(N_WIDE * N_NARROW, ATOM_DEV, SLOTS, SLOTS)
    current = messages
    for section_index in range(BLOCKS):
        reverse = current[partner]
        hidden = jax.nn.silu(project(current, weight_message[section_index])
                             + project(reverse, weight_reverse[section_index])).astype(jnp.bfloat16)
        first_res = residual(current, project(hidden, weight_combine[section_index]))
        inner_value = jax.nn.silu(project(first_res, weight_inner[section_index])).astype(jnp.bfloat16)
        second = residual(first_res, jax.nn.silu(project(inner_value, weight_outer[section_index])))
        gathered = second[listed].reshape(N_WIDE * N_NARROW, ATOM_DEV, SLOTS, D)
        mixed_rows = lax.map(mix_block, (mixing, gathered)).reshape(EDGES, D)
        turned = mixed_rows[turn_rows]
        third_res = residual(second, jax.nn.silu(project(turned, weight_lift[section_index])))
        expand = jax.nn.silu(project(third_res, weight_expand[section_index])).astype(jnp.bfloat16)
        current = residual(third_res, jax.nn.silu(project(expand, weight_reduce[section_index])))
    return current
```

```python
import functools

import jax
import jax.numpy as jnp
from jax import lax
from jax.experimental import pallas as pl
from jax.experimental.pallas import tpu as pltpu
from jax.sharding import PartitionSpec as P

SLOTS = 32
BLOCKS = 2
LANES = 128
HALF = LANES // 2
GROUP = 8


ROOT_HALF = 0.7071067811865476


def project(operand, weight):
    return jnp.dot(operand, weight, preferred_element_type=jnp.float32)


def residual(previous, branch):
    return ((previous.astype(jnp.float32) + branch) * ROOT_HALF).astype(jnp.bfloat16)


def reverse_edges(values, partner_rows):
    exchanged = lax.all_to_all(values, "wide", split_axis=0, concat_axis=0, tiled=True)
    return jnp.take(exchanged, partner_rows, axis=0)


def edge_front(current, reverse, weights, section_index):
    hidden = jax.nn.silu(
        project(current, weights[0][section_index]) + project(reverse, weights[1][section_index])
    ).astype(jnp.bfloat16)
    first_res = residual(current, project(hidden, weights[2][section_index]))
    inner_value = jax.nn.silu(project(first_res, weights[3][section_index])).astype(jnp.bfloat16)
    return residual(first_res, jax.nn.silu(project(inner_value, weights[4][section_index])))


def edge_back(second, turned, weights, section_index):
    third_res = residual(second, jax.nn.silu(project(turned, weights[5][section_index])))
    expand = jax.nn.silu(project(third_res, weights[6][section_index])).astype(jnp.bfloat16)
    return residual(third_res, jax.nn.silu(project(expand, weights[7][section_index])))


def owners_mix(second, route_slot, atom_slots, mixing):
    features = second.shape[1]
    buffer_rows = 2 * second.shape[0]
    outgoing = jnp.zeros((buffer_rows, features), jnp.bfloat16).at[route_slot].set(second)
    received = lax.all_to_all(outgoing, "narrow", split_axis=0, concat_axis=0, tiled=True)
    gathered = jnp.take(received, atom_slots, axis=0).reshape(mixing.shape[0], SLOTS, features)
    mixed_rows = jnp.einsum(
        "apq,aqd->apd", mixing, gathered, preferred_element_type=jnp.float32
    ).astype(jnp.bfloat16)
    return mixed_rows.reshape(-1, features)


def back_to_edges(mixed_flat, route_slot, atom_slots):
    features = mixed_flat.shape[1]
    buffer_rows = 2 * route_slot.shape[0]
    answer = jnp.zeros((buffer_rows, features), jnp.bfloat16).at[atom_slots].set(mixed_flat)
    incoming = lax.all_to_all(answer, "narrow", split_axis=0, concat_axis=0, tiled=True)
    return jnp.take(incoming, route_slot, axis=0)


def general_local(messages, reverse_position, route_slot, atom_slots, angles, weights):
    edge_rows = messages.shape[0]
    sub_rows = edge_rows // lax.axis_size("wide")
    partner_rows = jnp.arange(edge_rows, dtype=jnp.int32) // sub_rows * sub_rows + reverse_position
    mixing = angles.reshape(angles.shape[0], SLOTS, SLOTS)
    current = messages
    for section_index in range(BLOCKS):
        reverse = reverse_edges(current, partner_rows)
        second = edge_front(current, reverse, weights, section_index)
        mixed_flat = owners_mix(second, route_slot, atom_slots, mixing)
        returned = back_to_edges(mixed_flat, route_slot, atom_slots)
        turned = reverse_edges(returned, partner_rows)
        current = edge_back(second, turned, weights, section_index)
    return current


def silu(value):
    return 0.5 * value * (1.0 + jnp.tanh(0.5 * value))


def dot(left, right):
    return jnp.dot(left, right, preferred_element_type=jnp.float32)


def halve(previous, branch):
    return ((previous.astype(jnp.float32) + branch) * ROOT_HALF).astype(jnp.bfloat16)


def iotas(size):
    shape = (size, size)
    return lax.broadcasted_iota(jnp.int32, shape, 0), lax.broadcasted_iota(jnp.int32, shape, 1)


def as_column(row, rows_iota, lanes_iota):
    return jnp.sum(jnp.where(rows_iota == lanes_iota, row, 0), axis=1, keepdims=True)


def one_hot(mask):
    return jnp.where(mask, 1.0, 0.0).astype(jnp.bfloat16)


def front_kernel(cur_ref, recv_ref, back_ref, rank_ref, wm, wr, wc, wi, wo, second_ref, packed_ref):
    rows_iota, lanes_iota = iotas(cur_ref.shape[1])
    current = cur_ref[0]
    partner = as_column(back_ref[0], rows_iota, lanes_iota)
    reverse = dot(one_hot(partner == lanes_iota), recv_ref[0]).astype(jnp.bfloat16)
    hidden = silu(dot(current, wm[0]) + dot(reverse, wr[0])).astype(jnp.bfloat16)
    first_res = halve(current, dot(hidden, wc[0]))
    inner = silu(dot(first_res, wi[0])).astype(jnp.bfloat16)
    second = halve(first_res, silu(dot(inner, wo[0])))
    second_ref[0] = second
    ordered = dot(one_hot(rows_iota == rank_ref[0]), second)
    half = ordered.shape[0] // 2
    low = lax.broadcasted_iota(jnp.int32, (half, LANES), 1) < HALF
    for tile in range(ordered.shape[1] // LANES):
        top = ordered[:half, tile * LANES : (tile + 1) * LANES]
        bottom = ordered[half:, tile * LANES : (tile + 1) * LANES]
        packed_ref[2 * tile, 0] = jnp.where(low, top, pltpu.roll(bottom, HALF, 1)).astype(jnp.bfloat16)
        packed_ref[2 * tile + 1, 0] = jnp.where(low, pltpu.roll(top, HALF, 1), bottom).astype(jnp.bfloat16)


def back_kernel(second_ref, packed_ref, rank_ref, wl, we, wd, out_ref):
    rows_iota, lanes_iota = iotas(second_ref.shape[1])
    half = rows_iota.shape[0] // 2
    low = lax.broadcasted_iota(jnp.int32, (half, LANES), 1) < HALF
    tops, bottoms = [], []
    for tile in range(second_ref.shape[2] // LANES):
        even = packed_ref[0, 2 * tile].astype(jnp.float32)
        odd = packed_ref[0, 2 * tile + 1].astype(jnp.float32)
        tops.append(jnp.where(low, even, pltpu.roll(odd, HALF, 1)).astype(jnp.bfloat16))
        bottoms.append(jnp.where(low, pltpu.roll(even, HALF, 1), odd).astype(jnp.bfloat16))
    ordered = jnp.concatenate(
        [jnp.concatenate(tops, axis=1), jnp.concatenate(bottoms, axis=1)], axis=0
    )
    source = as_column(rank_ref[0], rows_iota, lanes_iota)
    turned = dot(one_hot(source == lanes_iota), ordered).astype(jnp.bfloat16)
    third_res = halve(second_ref[0], silu(dot(turned, wl[0])))
    expand = silu(dot(third_res, we[0])).astype(jnp.bfloat16)
    out_ref[0] = halve(third_res, silu(dot(expand, wd[0])))


def table_kernel(entry_ref, angles_ref, take_ref, give_ref, blocks_ref):
    size = entry_ref.shape[3]
    rows_iota, lanes_iota = iotas(size)
    for side in range(entry_ref.shape[1]):
        row = entry_ref[0, side]
        column = as_column(row, rows_iota, lanes_iota)
        rank_column = jnp.sum(jnp.where(row < column, 1, 0), axis=1, keepdims=True)
        rank_row = jnp.sum(jnp.where(column < row, 1, 0), axis=0, keepdims=True)
        take_ref[0, side] = one_hot(rank_column == lanes_iota)
        give_ref[0, side] = one_hot(rows_iota == rank_row)
    span = GROUP * SLOTS
    rows_iota, lanes_iota = iotas(span)
    own = rows_iota % GROUP == lanes_iota % GROUP
    spread_rows = lax.broadcasted_iota(jnp.int32, (SLOTS, span), 0)
    spread_lanes = lax.broadcasted_iota(jnp.int32, (SLOTS, span), 1)
    spread = one_hot(spread_lanes // GROUP == spread_rows)
    for group in range(angles_ref.shape[1] // GROUP):
        local = angles_ref[0, group * GROUP : (group + 1) * GROUP, :].astype(jnp.float32)
        stacked = jnp.concatenate(
            [local[:, p * SLOTS : (p + 1) * SLOTS] for p in range(SLOTS)], axis=0
        ).astype(jnp.bfloat16)
        blocks_ref[0, group] = jnp.where(own, dot(stacked, spread), 0.0).astype(jnp.bfloat16)


def mix_kernel(owner_ref, place_ref, recv_ref, take_ref, give_ref, blocks_ref, out_ref, ins, outs):
    step = pl.program_id(0)
    sides = take_ref.shape[1]
    devices = recv_ref.shape[0]
    unit = ins.shape[3]
    rows = devices * unit
    groups = blocks_ref.shape[1]
    strip = blocks_ref.shape[2] // sides
    pairs = devices // 2

    @pl.when(step == 0)
    def _():
        @pl.loop(0, devices)
        def _(source):
            for index in range(devices):
                owner = owner_ref[source, index]
                place = place_ref[source, index]
                at = (index % pairs) * unit
                for side in range(sides):
                    block = recv_ref[source, side, at : at + unit, :]
                    if index >= pairs:
                        block = pltpu.roll(block.astype(jnp.float32), HALF, 1).astype(jnp.bfloat16)
                    ins[side, owner, place] = block

    gathered = [
        dot(take_ref[0, side], ins[side, step].reshape(rows, LANES)).astype(jnp.bfloat16)
        for side in range(sides)
    ]
    mixed = []
    for group in range(groups):
        operand = jnp.concatenate(
            [part[group * strip : (group + 1) * strip] for part in gathered], axis=0
        )
        mixed.append(dot(blocks_ref[0, group], operand).astype(jnp.bfloat16))
    for side in range(sides):
        operand = jnp.concatenate(
            [part[side * strip : (side + 1) * strip] for part in mixed], axis=0
        )
        outs[side, step] = (
            dot(give_ref[0, side], operand).astype(jnp.bfloat16).reshape(devices, unit, LANES)
        )

    @pl.when(step == pl.num_programs(0) - 1)
    def _():
        low = lax.broadcasted_iota(jnp.int32, (unit, LANES), 1) < HALF

        @pl.loop(0, devices)
        def _(source):
            for index in range(pairs):
                owner = owner_ref[source, index]
                place = place_ref[source, index]
                owner_far = owner_ref[source, index + pairs]
                place_far = place_ref[source, index + pairs]
                for side in range(sides):
                    near = outs[side, owner, place].astype(jnp.float32)
                    far = outs[side, owner_far, place_far].astype(jnp.float32)
                    joined = jnp.where(low, near, pltpu.roll(far, HALF, 1)).astype(jnp.bfloat16)
                    out_ref[side, source, index * unit : (index + 1) * unit, :] = joined


VMEM_BYTES = 48 * 1024 * 1024


def params():
    return pltpu.CompilerParams(vmem_limit_bytes=VMEM_BYTES)


def weight_spec(section, features):
    return pl.BlockSpec((1, features, features), lambda i: (section, 0, 0))


def run_front(current, received, back_rows, rank_rows, weights, section, narrow):
    sides, rows, features = current.shape
    edge_spec = pl.BlockSpec((1, rows, features), lambda i: (i, 0, 0))
    row_spec = pl.BlockSpec((1, 1, rows), lambda i: (i, 0, 0))
    return pl.pallas_call(
        front_kernel,
        grid=(sides,),
        in_specs=[edge_spec, edge_spec, row_spec, row_spec] + [weight_spec(section, features)] * 5,
        out_specs=[
            edge_spec,
            pl.BlockSpec((narrow, 1, rows // 2, LANES), lambda i: (0, i, 0, 0)),
        ],
        out_shape=[
            jax.ShapeDtypeStruct(current.shape, jnp.bfloat16),
            jax.ShapeDtypeStruct((narrow, sides, rows // 2, LANES), jnp.bfloat16),
        ],
        compiler_params=params(),
        name="front",
    )(current, received, back_rows, rank_rows, *weights[:5])


def run_back(second, packed, rank_rows, weights, section):
    sides, rows, features = second.shape
    narrow = packed.shape[1]
    edge_spec = pl.BlockSpec((1, rows, features), lambda i: (i, 0, 0))
    return pl.pallas_call(
        back_kernel,
        grid=(sides,),
        in_specs=[
            edge_spec,
            pl.BlockSpec((1, narrow, rows // 2, LANES), lambda i: (i, 0, 0, 0)),
            pl.BlockSpec((1, 1, rows), lambda i: (i, 0, 0)),
        ]
        + [weight_spec(section, features)] * 3,
        out_specs=edge_spec,
        out_shape=jax.ShapeDtypeStruct(second.shape, jnp.bfloat16),
        compiler_params=params(),
        name="back",
    )(second, packed, rank_rows, *weights[5:])


def run_tables(entries, angles):
    owners, sides, _, rows = entries.shape
    atoms = angles.shape[1]
    groups = atoms // GROUP
    span = GROUP * SLOTS
    hot = jax.ShapeDtypeStruct((owners, sides, rows, rows), jnp.bfloat16)
    hot_spec = pl.BlockSpec((1, sides, rows, rows), lambda i: (i, 0, 0, 0))
    return pl.pallas_call(
        table_kernel,
        grid=(owners,),
        in_specs=[
            pl.BlockSpec((1, sides, 1, rows), lambda i: (i, 0, 0, 0)),
            pl.BlockSpec((1, atoms, angles.shape[2]), lambda i: (i, 0, 0)),
        ],
        out_specs=[hot_spec, hot_spec, pl.BlockSpec((1, groups, span, span), lambda i: (i, 0, 0, 0))],
        out_shape=[hot, hot, jax.ShapeDtypeStruct((owners, groups, span, span), jnp.bfloat16)],
        compiler_params=params(),
        name="tables",
    )(entries, angles)


def run_mix(owner_of, place_of, received, take, give, blocks):
    devices, sides, half, _ = received.shape
    rows = 2 * half
    unit = rows // devices
    smem = pl.BlockSpec(memory_space=pltpu.SMEM)
    hot_spec = pl.BlockSpec((1, sides, rows, rows), lambda i: (i, 0, 0, 0))
    return pl.pallas_call(
        mix_kernel,
        grid=(devices,),
        in_specs=[
            smem,
            smem,
            pl.BlockSpec(received.shape, lambda i: (0, 0, 0, 0)),
            hot_spec,
            hot_spec,
            pl.BlockSpec((1,) + blocks.shape[1:], lambda i: (i, 0, 0, 0)),
        ],
        out_specs=pl.BlockSpec((sides, devices, half, LANES), lambda i: (0, 0, 0, 0)),
        out_shape=jax.ShapeDtypeStruct((sides, devices, half, LANES), jnp.bfloat16),
        scratch_shapes=[
            pltpu.VMEM((sides, devices, devices, unit, LANES), jnp.bfloat16),
            pltpu.VMEM((sides, devices, devices, unit, LANES), jnp.bfloat16),
        ],
        compiler_params=params(),
        name="mix",
    )(owner_of, place_of, received, take, give, blocks)


def unit_tables(entries, capacity, unit):
    owners, sides, rows = entries.shape
    ids = jnp.arange(owners, dtype=jnp.int32)
    source = entries.reshape(owners, sides * rows) // capacity
    counts = jnp.sum((source[None] == ids[:, None, None]).astype(jnp.int32), axis=2) // (unit * sides)
    before = ids[:, None] < ids[None, :]
    starts = jnp.sum(jnp.where(before[None], counts[:, :, None], 0), axis=1)
    places = jnp.sum(jnp.where(before[:, :, None], counts[:, None, :], 0), axis=0)
    inside = (starts[:, :, None] <= ids) & (ids < (starts + counts)[:, :, None])
    owner_of = jnp.sum(jnp.where(inside, ids[None, :, None], 0), axis=1)
    place_of = jnp.sum(jnp.where(inside, (places - starts)[:, :, None] + ids, 0), axis=1)
    return owner_of, place_of


def ranks(values):
    return jnp.sum((values[:, :, None] < values[:, None, :]).astype(jnp.int32), axis=1)


def tiled_local(messages, reverse_position, route_slot, atom_slots, angles, weights):
    wide = lax.axis_size("wide")
    narrow = lax.axis_size("narrow")
    edge_rows, features = messages.shape
    rows = edge_rows // wide
    unit = rows // narrow
    capacity = 2 * edge_rows // narrow
    atoms = angles.shape[0]
    back_rows = reverse_position.reshape(wide, rows)
    current = messages.reshape(wide, rows, features)
    received = lax.all_to_all(current, "wide", 0, 0, tiled=True)
    rank = ranks(route_slot.reshape(wide, rows))
    partner_rank = lax.all_to_all(rank, "wide", 0, 0, tiled=True)
    hits = back_rows[:, :, None] == jnp.arange(rows, dtype=jnp.int32)
    turned_rank = jnp.sum(jnp.where(hits, partner_rank[:, None, :], 0), axis=2)
    listed = atom_slots.reshape(atoms // GROUP, GROUP, wide, SLOTS // wide)
    listed = jnp.transpose(listed, (2, 0, 3, 1)).reshape(wide, rows)
    entries = lax.all_gather(listed, "narrow", axis=0)
    all_angles = lax.all_gather(angles, "narrow", axis=0)
    owner_of, place_of = unit_tables(entries, capacity, unit)
    take, give, blocks = run_tables(entries[:, :, None, :], all_angles)
    back_rows = back_rows[:, None, :]
    rank = rank[:, None, :]
    turned_rank = turned_rank[:, None, :]
    for section in range(BLOCKS):
        if section:
            received = lax.all_to_all(current, "wide", 0, 0, tiled=True)
        second, packed = run_front(current, received, back_rows, rank, weights, section, narrow)
        spread = lax.all_to_all(packed, "narrow", 0, 0, tiled=True)
        mixed = run_mix(owner_of, place_of, spread, take, give, blocks)
        flat = mixed.reshape(wide * narrow, rows // 2, LANES)
        returned = lax.all_to_all(flat, ("wide", "narrow"), 0, 0, tiled=True)
        returned = returned.reshape(wide, narrow, rows // 2, LANES)
        current = run_back(second, returned, turned_rank, weights, section)
    return current.reshape(edge_rows, features)


def local(
    messages,
    reverse_position,
    route_slot,
    atom_slots,
    angles,
    weight_message,
    weight_reverse,
    weight_combine,
    weight_inner,
    weight_outer,
    weight_lift,
    weight_expand,
    weight_reduce,
):
    weights = (
        weight_message,
        weight_reverse,
        weight_combine,
        weight_inner,
        weight_outer,
        weight_lift,
        weight_expand,
        weight_reduce,
    )
    wide = lax.axis_size("wide")
    narrow = lax.axis_size("narrow")
    edge_rows, features = messages.shape
    unit = edge_rows // wide // narrow
    fits = (
        features == narrow * HALF
        and unit % 16 == 0
        and narrow % 2 == 0
        and angles.shape[0] % GROUP == 0
        and (SLOTS // wide * GROUP) % 16 == 0
    )
    run = tiled_local if fits else general_local
    return run(messages, reverse_position, route_slot, atom_slots, angles, weights)


def solution(mesh):
    in_specs = (
        P(("wide", "narrow"), None),
        P(("wide", "narrow")),
        P(("wide", "narrow")),
        P(("wide", "narrow")),
        P(("wide", "narrow"), None),
        P(),
        P(),
        P(),
        P(),
        P(),
        P(),
        P(),
        P(),
    )
    out_specs = P(("wide", "narrow"), None)
    return jax.shard_map(local, mesh=mesh, in_specs=in_specs, out_specs=out_specs, check_vma=False)
```

```python
import functools

import jax
import jax.numpy as jnp
from jax import lax
from jax.experimental import pallas as pl
from jax.experimental.pallas import tpu as pltpu
from jax.sharding import PartitionSpec as P

SLOTS = 32
BLOCKS = 2
LANES = 128
HALF = LANES // 2
GROUP = 8


ROOT_HALF = 0.7071067811865476


def project(operand, weight):
    return jnp.dot(operand, weight, preferred_element_type=jnp.float32)


def residual(previous, branch):
    return ((previous.astype(jnp.float32) + branch) * ROOT_HALF).astype(jnp.bfloat16)


def reverse_edges(values, partner_rows):
    exchanged = lax.all_to_all(values, "wide", split_axis=0, concat_axis=0, tiled=True)
    return jnp.take(exchanged, partner_rows, axis=0)


def edge_front(current, reverse, weights, section_index):
    hidden = jax.nn.silu(
        project(current, weights[0][section_index]) + project(reverse, weights[1][section_index])
    ).astype(jnp.bfloat16)
    first_res = residual(current, project(hidden, weights[2][section_index]))
    inner_value = jax.nn.silu(project(first_res, weights[3][section_index])).astype(jnp.bfloat16)
    return residual(first_res, jax.nn.silu(project(inner_value, weights[4][section_index])))


def edge_back(second, turned, weights, section_index):
    third_res = residual(second, jax.nn.silu(project(turned, weights[5][section_index])))
    expand = jax.nn.silu(project(third_res, weights[6][section_index])).astype(jnp.bfloat16)
    return residual(third_res, jax.nn.silu(project(expand, weights[7][section_index])))


def owners_mix(second, route_slot, atom_slots, mixing):
    features = second.shape[1]
    buffer_rows = 2 * second.shape[0]
    outgoing = jnp.zeros((buffer_rows, features), jnp.bfloat16).at[route_slot].set(second)
    received = lax.all_to_all(outgoing, "narrow", split_axis=0, concat_axis=0, tiled=True)
    gathered = jnp.take(received, atom_slots, axis=0).reshape(mixing.shape[0], SLOTS, features)
    mixed_rows = jnp.einsum(
        "apq,aqd->apd", mixing, gathered, preferred_element_type=jnp.float32
    ).astype(jnp.bfloat16)
    return mixed_rows.reshape(-1, features)


def back_to_edges(mixed_flat, route_slot, atom_slots):
    features = mixed_flat.shape[1]
    buffer_rows = 2 * route_slot.shape[0]
    answer = jnp.zeros((buffer_rows, features), jnp.bfloat16).at[atom_slots].set(mixed_flat)
    incoming = lax.all_to_all(answer, "narrow", split_axis=0, concat_axis=0, tiled=True)
    return jnp.take(incoming, route_slot, axis=0)


def general_local(messages, reverse_position, route_slot, atom_slots, angles, weights):
    edge_rows = messages.shape[0]
    sub_rows = edge_rows // lax.axis_size("wide")
    partner_rows = jnp.arange(edge_rows, dtype=jnp.int32) // sub_rows * sub_rows + reverse_position
    mixing = angles.reshape(angles.shape[0], SLOTS, SLOTS)
    current = messages
    for section_index in range(BLOCKS):
        reverse = reverse_edges(current, partner_rows)
        second = edge_front(current, reverse, weights, section_index)
        mixed_flat = owners_mix(second, route_slot, atom_slots, mixing)
        returned = back_to_edges(mixed_flat, route_slot, atom_slots)
        turned = reverse_edges(returned, partner_rows)
        current = edge_back(second, turned, weights, section_index)
    return current


def silu(value):
    return 0.5 * value * (1.0 + jnp.tanh(0.5 * value))


def dot(left, right):
    return jnp.dot(left, right, preferred_element_type=jnp.float32)


def halve(previous, branch):
    return ((previous.astype(jnp.float32) + branch) * ROOT_HALF).astype(jnp.bfloat16)


def iotas(size):
    shape = (size, size)
    return lax.broadcasted_iota(jnp.int32, shape, 0), lax.broadcasted_iota(jnp.int32, shape, 1)


def as_column(row, rows_iota, lanes_iota):
    return jnp.sum(jnp.where(rows_iota == lanes_iota, row, 0), axis=1, keepdims=True)


def one_hot(mask):
    return jnp.where(mask, 1.0, 0.0).astype(jnp.bfloat16)


def front_kernel(own, count, where_ref, cur_ref, back_ref, rank_ref, wm, wr, wc, wi, wo, *refs):
    recv_refs, (second_ref, packed_ref, reverse_ref) = refs[:-3], refs[-3:]
    rows_iota, lanes_iota = iotas(cur_ref.shape[1])
    partner = as_column(back_ref[0], rows_iota, lanes_iota)
    hot = one_hot(partner == lanes_iota)
    sources = ([cur_ref.at[0]] if own else []) + list(recv_refs)
    for index in range(count):

        @pl.when(pl.program_id(0) == index)
        def _():
            reverse_ref[...] = dot(hot, sources[index][...]).astype(jnp.bfloat16)

    current = cur_ref[0]
    hidden = silu(dot(current, wm[0]) + dot(reverse_ref[...], wr[0])).astype(jnp.bfloat16)
    first_res = halve(current, dot(hidden, wc[0]))
    inner = silu(dot(first_res, wi[0])).astype(jnp.bfloat16)
    second = halve(first_res, silu(dot(inner, wo[0])))
    second_ref[0] = second
    ordered = dot(one_hot(rows_iota == rank_ref[0]), second)
    half = ordered.shape[0] // 2
    low = lax.broadcasted_iota(jnp.int32, (half, LANES), 1) < HALF
    for tile in range(ordered.shape[1] // LANES):
        top = ordered[:half, tile * LANES : (tile + 1) * LANES]
        bottom = ordered[half:, tile * LANES : (tile + 1) * LANES]
        packed_ref[2 * tile, 0] = jnp.where(low, top, pltpu.roll(bottom, HALF, 1)).astype(jnp.bfloat16)
        packed_ref[2 * tile + 1, 0] = jnp.where(low, pltpu.roll(top, HALF, 1), bottom).astype(jnp.bfloat16)


def back_kernel(layout, where_ref, second_ref, rank_ref, wl, we, wd, *refs):
    out_ref, ordered_ref = refs[-2:]
    rows_iota, lanes_iota = iotas(second_ref.shape[1])
    half = rows_iota.shape[0] // 2
    low = lax.broadcasted_iota(jnp.int32, (half, LANES), 1) < HALF
    for index, (array, side) in enumerate(layout):

        @pl.when(pl.program_id(0) == index)
        def _():
            for tile in range(second_ref.shape[2] // LANES):
                lanes = slice(tile * LANES, (tile + 1) * LANES)
                even = refs[array][2 * tile, side].astype(jnp.float32)
                odd = refs[array][2 * tile + 1, side].astype(jnp.float32)
                top = jnp.where(low, even, pltpu.roll(odd, HALF, 1))
                bottom = jnp.where(low, pltpu.roll(even, HALF, 1), odd)
                ordered_ref[:half, lanes] = top.astype(jnp.bfloat16)
                ordered_ref[half:, lanes] = bottom.astype(jnp.bfloat16)

    source = as_column(rank_ref[0], rows_iota, lanes_iota)
    turned = dot(one_hot(source == lanes_iota), ordered_ref[...]).astype(jnp.bfloat16)
    third_res = halve(second_ref[0], silu(dot(turned, wl[0])))
    expand = silu(dot(third_res, we[0])).astype(jnp.bfloat16)
    out_ref[0] = halve(third_res, silu(dot(expand, wd[0])))


def table_kernel(chunks, wide_ref, entry_ref, angles_ref, take_ref, give_ref, blocks_ref):
    sides, _, size = entry_ref.shape[1:]
    count = sides // chunks
    group_id = wide_ref[0]
    rows_iota, lanes_iota = iotas(size)
    for side in range(sides):
        row = entry_ref[0, side]
        column = as_column(row, rows_iota, lanes_iota)
        rank_column = jnp.sum(jnp.where(row < column, 1, 0), axis=1, keepdims=True)
        rank_row = jnp.sum(jnp.where(column < row, 1, 0), axis=0, keepdims=True)
        take_ref[0, side] = one_hot(rank_column == lanes_iota)
        give_ref[0, side] = one_hot(rows_iota == rank_row)
    span = GROUP * SLOTS
    strip = span // sides
    rows_iota, lanes_iota = iotas(span)
    own = rows_iota % GROUP == lanes_iota % GROUP
    spread_rows = lax.broadcasted_iota(jnp.int32, (SLOTS, span), 0)
    spread_lanes = lax.broadcasted_iota(jnp.int32, (SLOTS, span), 1)
    place = spread_lanes // strip
    side_at = (place // count + place % count * chunks) ^ group_id
    spread = one_hot(side_at * (SLOTS // sides) + spread_lanes % strip // GROUP == spread_rows)
    for group in range(angles_ref.shape[1] // GROUP):
        local = angles_ref[0, group * GROUP : (group + 1) * GROUP, :].astype(jnp.float32)
        stacked = jnp.concatenate(
            [local[:, p * SLOTS : (p + 1) * SLOTS] for p in range(SLOTS)], axis=0
        ).astype(jnp.bfloat16)
        block = jnp.where(own, dot(stacked, spread), 0.0).astype(jnp.bfloat16)
        for side in range(sides):
            offset = group_id ^ side
            to = pl.multiple_of((offset % chunks * count + offset // chunks) * strip, strip)
            blocks_ref[0, group, pl.ds(to, strip), :] = block[side * strip : (side + 1) * strip]


def gather_kernel(owner_ref, place_ref, recv_ref, take_ref, out_ref, ins):
    step = pl.program_id(0)
    sides = take_ref.shape[1]
    devices = recv_ref.shape[0]
    unit = ins.shape[3]
    pairs = devices // 2

    @pl.when(step == 0)
    def _():
        @pl.loop(0, devices)
        def _(source):
            for index in range(devices):
                owner = owner_ref[source, index]
                place = place_ref[source, index]
                at = (index % pairs) * unit
                for side in range(sides):
                    block = recv_ref[source, side, at : at + unit, :]
                    if index >= pairs:
                        block = pltpu.roll(block.astype(jnp.float32), HALF, 1).astype(jnp.bfloat16)
                    ins[side, owner, place] = block

    for side in range(sides):
        operand = ins[side, step].reshape(devices * unit, LANES)
        out_ref[0, side] = dot(take_ref[0, side], operand).astype(jnp.bfloat16)


def mix_kernel(chunk, chunks, owner_ref, place_ref, give_ref, blocks_ref, *refs):
    gathered_refs, out_refs, outs = refs[:chunks], refs[chunks:-1], refs[-1]
    step = pl.program_id(0)
    count = give_ref.shape[1]
    devices = outs.shape[1]
    unit = outs.shape[3]
    groups = blocks_ref.shape[1]
    strip = blocks_ref.shape[2] // (chunks * count)
    pairs = devices // 2
    first = chunk * count * strip
    mixed = []
    for group in range(groups):
        operand = jnp.concatenate(
            [
                ref[0, index, group * strip : (group + 1) * strip, :]
                for ref in gathered_refs
                for index in range(count)
            ],
            axis=0,
        )
        mixing = blocks_ref[0, group, first : first + count * strip, :]
        mixed.append(dot(mixing, operand).astype(jnp.bfloat16))
    for side in range(count):
        operand = jnp.concatenate(
            [part[side * strip : (side + 1) * strip] for part in mixed], axis=0
        )
        outs[side, step] = (
            dot(give_ref[0, side], operand).astype(jnp.bfloat16).reshape(devices, unit, LANES)
        )

    @pl.when(step == pl.num_programs(0) - 1)
    def _():
        low = lax.broadcasted_iota(jnp.int32, (unit, LANES), 1) < HALF

        @pl.loop(0, devices)
        def _(source):
            for index in range(pairs):
                owner = owner_ref[source, index]
                place = place_ref[source, index]
                owner_far = owner_ref[source, index + pairs]
                place_far = place_ref[source, index + pairs]
                rows = slice(index * unit, (index + 1) * unit)
                for side in range(count):
                    near = outs[side, owner, place].astype(jnp.float32)
                    far = outs[side, owner_far, place_far].astype(jnp.float32)
                    joined = jnp.where(low, near, pltpu.roll(far, HALF, 1)).astype(jnp.bfloat16)
                    if len(out_refs) == 1:
                        out_refs[0][source, side, rows, :] = joined
                    else:
                        out_refs[side][source, 0, rows, :] = joined


VMEM_BYTES = 40 * 1024 * 1024


def params():
    return pltpu.CompilerParams(vmem_limit_bytes=VMEM_BYTES)


def cost(flops, moved, waves=0):
    return pl.CostEstimate(flops=flops, bytes_accessed=moved, transcendentals=waves)


def whole_spec(array):
    zeros = (0,) * array.ndim
    return pl.BlockSpec(array.shape, lambda i, *_: zeros)


def weight_spec(section, features):
    return pl.BlockSpec((1, features, features), lambda i, *_: (section, 0, 0))


def run_front(current, where, received, own, chunk, back_rows, rank_rows, weights, section, narrow):
    _, rows, features = current.shape
    count = where.shape[0]
    edge_spec = pl.BlockSpec((1, rows, features), lambda i, where: (i, 0, 0))
    row_spec = pl.BlockSpec((1, 1, rows), lambda i, where: (chunk * count + i, 0, 0))
    return pl.pallas_call(
        functools.partial(front_kernel, own, count),
        grid_spec=pltpu.PrefetchScalarGridSpec(
            num_scalar_prefetch=1,
            grid=(count,),
            in_specs=[
                pl.BlockSpec((1, rows, features), lambda i, where: (where[i], 0, 0)),
                row_spec,
                row_spec,
            ]
            + [weight_spec(section, features)] * 5
            + [whole_spec(array) for array in received],
            out_specs=[
                edge_spec,
                pl.BlockSpec((narrow, 1, rows // 2, LANES), lambda i, where: (0, i, 0, 0)),
            ],
            scratch_shapes=[pltpu.VMEM((rows, features), jnp.bfloat16)],
        ),
        out_shape=[
            jax.ShapeDtypeStruct((count, rows, features), jnp.bfloat16),
            jax.ShapeDtypeStruct((narrow, count, rows // 2, LANES), jnp.bfloat16),
        ],
        compiler_params=params(),
        cost_estimate=cost(12 * count * rows * features**2, 8 * count * rows * features),
        name="front",
    )(where, current, back_rows, rank_rows, *weights[:5], *received)


def run_back(second, packed, layout, chunk, rank_rows, weights, section, where, total, target):
    count, rows, features = second.shape
    edge_spec = pl.BlockSpec((1, rows, features), lambda i, where: (i, 0, 0))
    extra = [] if target is None else [target]
    return pl.pallas_call(
        functools.partial(back_kernel, layout),
        grid_spec=pltpu.PrefetchScalarGridSpec(
            num_scalar_prefetch=1,
            grid=(count,),
            in_specs=[
                edge_spec,
                pl.BlockSpec((1, 1, rows), lambda i, where: (chunk * count + i, 0, 0)),
            ]
            + [weight_spec(section, features)] * 3
            + [whole_spec(array) for array in packed]
            + [pl.BlockSpec(memory_space=pl.ANY)] * len(extra),
            out_specs=pl.BlockSpec((1, rows, features), lambda i, where: (where[i], 0, 0)),
            scratch_shapes=[pltpu.VMEM((rows, features), jnp.bfloat16)],
        ),
        out_shape=jax.ShapeDtypeStruct((total, rows, features), jnp.bfloat16),
        input_output_aliases={6 + len(packed): 0} if extra else {},
        compiler_params=params(),
        cost_estimate=cost(8 * count * rows * features**2, 6 * count * rows * features),
        name="back",
    )(where, second, rank_rows, *weights[5:], *packed, *extra)


def run_tables(group_id, entries, angles, chunks):
    owners, sides, _, rows = entries.shape
    atoms = angles.shape[1]
    groups = atoms // GROUP
    span = GROUP * SLOTS
    hot = jax.ShapeDtypeStruct((owners, sides, rows, rows), jnp.bfloat16)
    hot_spec = pl.BlockSpec((1, sides, rows, rows), lambda i: (i, 0, 0, 0))
    return pl.pallas_call(
        functools.partial(table_kernel, chunks),
        grid=(owners,),
        in_specs=[
            pl.BlockSpec(memory_space=pltpu.SMEM),
            pl.BlockSpec((1, sides, 1, rows), lambda i: (i, 0, 0, 0)),
            pl.BlockSpec((1, atoms, angles.shape[2]), lambda i: (i, 0, 0)),
        ],
        out_specs=[hot_spec, hot_spec, pl.BlockSpec((1, groups, span, span), lambda i: (i, 0, 0, 0))],
        out_shape=[hot, hot, jax.ShapeDtypeStruct((owners, groups, span, span), jnp.bfloat16)],
        compiler_params=params(),
        cost_estimate=cost(0, 4 * owners * (sides * rows**2 + groups * span**2)),
        name="tables",
    )(group_id, entries, angles)


def run_gather(owner_of, place_of, received, take, chunk):
    devices, count, half, _ = received.shape
    rows = 2 * half
    smem = pl.BlockSpec(memory_space=pltpu.SMEM)
    return pl.pallas_call(
        gather_kernel,
        grid=(devices,),
        in_specs=[
            smem,
            smem,
            whole_spec(received),
            pl.BlockSpec((1, count, rows, rows), lambda i: (i, chunk, 0, 0)),
        ],
        out_specs=pl.BlockSpec((1, count, rows, LANES), lambda i: (i, 0, 0, 0)),
        out_shape=jax.ShapeDtypeStruct((devices, count, rows, LANES), jnp.bfloat16),
        scratch_shapes=[
            pltpu.VMEM((count, devices, devices, rows // devices, LANES), jnp.bfloat16)
        ],
        compiler_params=params(),
        cost_estimate=cost(4 * devices * count * rows**2 * LANES, 4 * devices * count * rows**2),
        name="gather",
    )(owner_of, place_of, received, take)


def run_mix(owner_of, place_of, gathered, give, blocks, chunk, apart):
    chunks = len(gathered)
    devices, count, rows, _ = gathered[0].shape
    half = rows // 2
    smem = pl.BlockSpec(memory_space=pltpu.SMEM)
    shapes = [(devices, 1, half, LANES)] * count if apart else [(devices, count, half, LANES)]
    shapes = [jax.ShapeDtypeStruct(shape, jnp.bfloat16) for shape in shapes]
    part_spec = pl.BlockSpec((1, count, rows, LANES), lambda i: (i, 0, 0, 0))
    return pl.pallas_call(
        functools.partial(mix_kernel, chunk, chunks),
        grid=(devices,),
        in_specs=[
            smem,
            smem,
            pl.BlockSpec((1, count, rows, rows), lambda i: (i, chunk, 0, 0)),
            pl.BlockSpec((1,) + blocks.shape[1:], lambda i: (i, 0, 0, 0)),
        ]
        + [part_spec] * chunks,
        out_specs=[whole_spec(shape) for shape in shapes],
        out_shape=shapes,
        scratch_shapes=[
            pltpu.VMEM((count, devices, devices, rows // devices, LANES), jnp.bfloat16)
        ],
        compiler_params=params(),
        cost_estimate=cost(6 * devices * count * rows**2 * LANES, 6 * devices * count * rows**2),
        name="mix",
    )(owner_of, place_of, give, blocks, *gathered)


def unit_tables(entries, capacity, unit):
    owners, sides, rows = entries.shape
    ids = jnp.arange(owners, dtype=jnp.int32)
    source = entries.reshape(owners, sides * rows) // capacity
    counts = jnp.sum((source[None] == ids[:, None, None]).astype(jnp.int32), axis=2) // (unit * sides)
    before = ids[:, None] < ids[None, :]
    starts = jnp.sum(jnp.where(before[None], counts[:, :, None], 0), axis=1)
    places = jnp.sum(jnp.where(before[:, :, None], counts[:, None, :], 0), axis=0)
    inside = (starts[:, :, None] <= ids) & (ids < (starts + counts)[:, :, None])
    owner_of = jnp.sum(jnp.where(inside, ids[None, :, None], 0), axis=1)
    place_of = jnp.sum(jnp.where(inside, (places - starts)[:, :, None] + ids, 0), axis=1)
    return owner_of, place_of


def ranks(values):
    return jnp.sum((values[:, :, None] < values[:, None, :]).astype(jnp.int32), axis=1)


CHUNKS = 2


def reorder(values, order):
    hits = order[:, None] == jnp.arange(values.shape[0], dtype=jnp.int32)
    return jnp.sum(jnp.where(hits[:, :, None], values[None], 0), axis=1)


def shift(values, offset, wide):
    if offset == 0:
        return values
    return lax.ppermute(values, "wide", [(i, i ^ offset) for i in range(wide)])


def swap(values):
    return lax.all_to_all(values, "narrow", 0, 0, tiled=True)


BASE = 64


def share_lists(listed, angles):
    narrow = lax.axis_size("narrow")
    atoms, width = angles.shape
    digits = jnp.stack([listed // BASE, listed % BASE]).reshape(atoms, -1).astype(jnp.bfloat16)
    joined = jnp.concatenate([angles, digits], axis=1)
    shared = swap(jnp.broadcast_to(joined[None], (narrow,) + joined.shape).reshape(narrow * atoms, -1))
    shared = shared.reshape(narrow, atoms, -1)
    digits = shared[:, :, width:].reshape((narrow, 2) + listed.shape).astype(jnp.int32)
    return digits[:, 0] * BASE + digits[:, 1], shared[:, :, :width]


def tiled_local(messages, reverse_position, route_slot, atom_slots, angles, weights):
    wide = lax.axis_size("wide")
    narrow = lax.axis_size("narrow")
    edge_rows, features = messages.shape
    rows = edge_rows // wide
    unit = rows // narrow
    capacity = 2 * edge_rows // narrow
    atoms = angles.shape[0]
    count = wide // CHUNKS
    offsets = [[chunk + index * CHUNKS for index in range(count)] for chunk in range(CHUNKS)]
    group_id = lax.axis_index("wide").astype(jnp.int32)
    order = group_id ^ jnp.array(sum(offsets, []), jnp.int32)
    places = [order[chunk * count : (chunk + 1) * count] for chunk in range(CHUNKS)]
    plain = jnp.arange(count, dtype=jnp.int32)

    blocks_of = messages.reshape(wide, rows, features)
    received = [
        [
            shift(lax.dynamic_index_in_dim(blocks_of, group_id ^ offset, 0, False), offset, wide)
            for offset in offsets[chunk]
            if offset
        ]
        for chunk in range(CHUNKS)
    ]
    listed = atom_slots.reshape(atoms // GROUP, GROUP, wide, SLOTS // wide)
    listed = reorder(jnp.transpose(listed, (2, 0, 3, 1)).reshape(wide, rows), order)
    entries, all_angles = share_lists(listed, angles)
    rank = ranks(route_slot.reshape(wide, rows))
    partner_rank = lax.all_to_all(rank, "wide", 0, 0, tiled=True)
    back_rows = reverse_position.reshape(wide, rows)
    hits = back_rows[:, :, None] == jnp.arange(rows, dtype=jnp.int32)
    turned_rank = jnp.sum(jnp.where(hits, partner_rank[:, None, :], 0), axis=2)
    back_rows = reorder(back_rows, order)[:, None, :]
    rank = reorder(rank, order)[:, None, :]
    turned_rank = reorder(turned_rank, order)[:, None, :]

    current = [blocks_of] * CHUNKS
    where = places
    chunk_order = list(range(CHUNKS))
    target = None
    tables = None
    for section in range(BLOCKS):
        last = section == BLOCKS - 1
        seconds, spreads = {}, {}
        for chunk in chunk_order:
            seconds[chunk], packed = run_front(
                current[chunk], where[chunk], received[chunk], offsets[chunk][0] == 0, chunk,
                back_rows, rank, weights, section, narrow,
            )
            spreads[chunk] = packed
        if tables is None:
            held = [spreads[chunk] for chunk in chunk_order]
            entries, all_angles, held[-1] = lax.optimization_barrier((entries, all_angles, held[-1]))
            spreads = dict(zip(chunk_order, held))
            owner_of, place_of = unit_tables(entries, capacity, unit)
            tables = run_tables(group_id[None], entries[:, :, None, :], all_angles, CHUNKS)
        take, give, blocks = tables
        gathered = [None] * CHUNKS
        for chunk in chunk_order:
            gathered[chunk] = run_gather(owner_of, place_of, swap(spreads[chunk]), take, chunk)
        chunk_order = list(range(CHUNKS))[::-1]
        returned = {}
        for chunk in chunk_order:
            early = chunk == 0
            mixed = run_mix(owner_of, place_of, gathered, give, blocks, chunk, early)
            if early:
                mixed = [shift(part, offset, wide) for part, offset in zip(mixed, offsets[chunk])]
                parts = [swap(jnp.concatenate(mixed, axis=1))]
                layout = [(0, index) for index in range(count)]
            else:
                whole = swap(mixed[0])
                parts = [
                    shift(whole[:, index : index + 1], offset, wide)
                    for index, offset in enumerate(offsets[chunk])
                ]
                layout = [(index, 0) for index in range(count)]
            returned[chunk] = (parts, layout)
        current = [None] * CHUNKS
        received = [None] * CHUNKS
        for chunk in chunk_order:
            parts, layout = returned[chunk]
            result = run_back(
                seconds[chunk], parts, layout, chunk, turned_rank, weights, section,
                places[chunk] if last else plain, wide if last else count, target,
            )
            if last:
                target = result
            else:
                current[chunk] = result
                received[chunk] = [
                    shift(result[index], offset, wide)
                    for index, offset in enumerate(offsets[chunk])
                    if offset
                ]
        where = [plain] * CHUNKS
    return target.reshape(edge_rows, features)


def local(
    messages,
    reverse_position,
    route_slot,
    atom_slots,
    angles,
    weight_message,
    weight_reverse,
    weight_combine,
    weight_inner,
    weight_outer,
    weight_lift,
    weight_expand,
    weight_reduce,
):
    weights = (
        weight_message,
        weight_reverse,
        weight_combine,
        weight_inner,
        weight_outer,
        weight_lift,
        weight_expand,
        weight_reduce,
    )
    wide = lax.axis_size("wide")
    narrow = lax.axis_size("narrow")
    edge_rows, features = messages.shape
    unit = edge_rows // wide // narrow
    fits = (
        features == narrow * HALF
        and unit % 16 == 0
        and narrow % 2 == 0
        and wide % CHUNKS == 0
        and wide & (wide - 1) == 0
        and angles.shape[0] % GROUP == 0
        and (SLOTS // wide * GROUP) % 16 == 0
    )
    run = tiled_local if fits else general_local
    return run(messages, reverse_position, route_slot, atom_slots, angles, weights)


def solution(mesh):
    in_specs = (
        P(("wide", "narrow"), None),
        P(("wide", "narrow")),
        P(("wide", "narrow")),
        P(("wide", "narrow")),
        P(("wide", "narrow"), None),
        P(),
        P(),
        P(),
        P(),
        P(),
        P(),
        P(),
        P(),
    )
    out_specs = P(("wide", "narrow"), None)
    return jax.shard_map(local, mesh=mesh, in_specs=in_specs, out_specs=out_specs, check_vma=False)
```

```python
import functools

import jax
import jax.numpy as jnp
from jax import lax
from jax.experimental import pallas as pl
from jax.experimental.pallas import tpu as pltpu
from jax.sharding import PartitionSpec as P

SLOTS = 32
BLOCKS = 2
LANES = 128
HALF = LANES // 2
GROUP = 8


ROOT_HALF = 0.7071067811865476


def project(operand, weight):
    return jnp.dot(operand, weight, preferred_element_type=jnp.float32)


def residual(previous, branch):
    return ((previous.astype(jnp.float32) + branch) * ROOT_HALF).astype(jnp.bfloat16)


def reverse_edges(values, partner_rows):
    exchanged = lax.all_to_all(values, "wide", split_axis=0, concat_axis=0, tiled=True)
    return jnp.take(exchanged, partner_rows, axis=0)


def edge_front(current, reverse, weights, section_index):
    hidden = jax.nn.silu(
        project(current, weights[0][section_index]) + project(reverse, weights[1][section_index])
    ).astype(jnp.bfloat16)
    first_res = residual(current, project(hidden, weights[2][section_index]))
    inner_value = jax.nn.silu(project(first_res, weights[3][section_index])).astype(jnp.bfloat16)
    return residual(first_res, jax.nn.silu(project(inner_value, weights[4][section_index])))


def edge_back(second, turned, weights, section_index):
    third_res = residual(second, jax.nn.silu(project(turned, weights[5][section_index])))
    expand = jax.nn.silu(project(third_res, weights[6][section_index])).astype(jnp.bfloat16)
    return residual(third_res, jax.nn.silu(project(expand, weights[7][section_index])))


def owners_mix(second, route_slot, atom_slots, mixing):
    features = second.shape[1]
    buffer_rows = 2 * second.shape[0]
    outgoing = jnp.zeros((buffer_rows, features), jnp.bfloat16).at[route_slot].set(second)
    received = lax.all_to_all(outgoing, "narrow", split_axis=0, concat_axis=0, tiled=True)
    gathered = jnp.take(received, atom_slots, axis=0).reshape(mixing.shape[0], SLOTS, features)
    mixed_rows = jnp.einsum(
        "apq,aqd->apd", mixing, gathered, preferred_element_type=jnp.float32
    ).astype(jnp.bfloat16)
    return mixed_rows.reshape(-1, features)


def back_to_edges(mixed_flat, route_slot, atom_slots):
    features = mixed_flat.shape[1]
    buffer_rows = 2 * route_slot.shape[0]
    answer = jnp.zeros((buffer_rows, features), jnp.bfloat16).at[atom_slots].set(mixed_flat)
    incoming = lax.all_to_all(answer, "narrow", split_axis=0, concat_axis=0, tiled=True)
    return jnp.take(incoming, route_slot, axis=0)


def general_local(messages, reverse_position, route_slot, atom_slots, angles, weights):
    edge_rows = messages.shape[0]
    sub_rows = edge_rows // lax.axis_size("wide")
    partner_rows = jnp.arange(edge_rows, dtype=jnp.int32) // sub_rows * sub_rows + reverse_position
    mixing = angles.reshape(angles.shape[0], SLOTS, SLOTS)
    current = messages
    for section_index in range(BLOCKS):
        reverse = reverse_edges(current, partner_rows)
        second = edge_front(current, reverse, weights, section_index)
        mixed_flat = owners_mix(second, route_slot, atom_slots, mixing)
        returned = back_to_edges(mixed_flat, route_slot, atom_slots)
        turned = reverse_edges(returned, partner_rows)
        current = edge_back(second, turned, weights, section_index)
    return current


def silu(value):
    return 0.5 * value * (1.0 + jnp.tanh(0.5 * value))


def dot(left, right):
    return jnp.dot(left, right, preferred_element_type=jnp.float32)


def halve(previous, branch):
    return ((previous.astype(jnp.float32) + branch) * ROOT_HALF).astype(jnp.bfloat16)


def iotas(size):
    shape = (size, size)
    return lax.broadcasted_iota(jnp.int32, shape, 0), lax.broadcasted_iota(jnp.int32, shape, 1)


def as_column(row, rows_iota, lanes_iota):
    return jnp.sum(jnp.where(rows_iota == lanes_iota, row, 0), axis=1, keepdims=True)


def one_hot(mask):
    return jnp.where(mask, 1.0, 0.0).astype(jnp.bfloat16)


def front_kernel(own, count, where_ref, cur_ref, back_ref, rank_ref, wm, wr, wc, wi, wo, *refs):
    recv_refs, (second_ref, packed_ref, reverse_ref) = refs[:-3], refs[-3:]
    rows_iota, lanes_iota = iotas(cur_ref.shape[1])
    partner = as_column(back_ref[0], rows_iota, lanes_iota)
    hot = one_hot(partner == lanes_iota)
    sources = ([cur_ref.at[0]] if own else []) + list(recv_refs)
    for index in range(count):

        @pl.when(pl.program_id(0) == index)
        def _():
            reverse_ref[...] = dot(hot, sources[index][...]).astype(jnp.bfloat16)

    current = cur_ref[0]
    hidden = silu(dot(current, wm[0]) + dot(reverse_ref[...], wr[0])).astype(jnp.bfloat16)
    first_res = halve(current, dot(hidden, wc[0]))
    inner = silu(dot(first_res, wi[0])).astype(jnp.bfloat16)
    second = halve(first_res, silu(dot(inner, wo[0])))
    second_ref[0] = second
    ordered = dot(one_hot(rows_iota == rank_ref[0]), second)
    half = ordered.shape[0] // 2
    low = lax.broadcasted_iota(jnp.int32, (half, LANES), 1) < HALF
    for tile in range(ordered.shape[1] // LANES):
        top = ordered[:half, tile * LANES : (tile + 1) * LANES]
        bottom = ordered[half:, tile * LANES : (tile + 1) * LANES]
        packed_ref[2 * tile, 0] = jnp.where(low, top, pltpu.roll(bottom, HALF, 1)).astype(jnp.bfloat16)
        packed_ref[2 * tile + 1, 0] = jnp.where(low, pltpu.roll(top, HALF, 1), bottom).astype(jnp.bfloat16)


def back_kernel(layout, where_ref, second_ref, rank_ref, wl, we, wd, *refs):
    out_ref, ordered_ref = refs[-2:]
    rows_iota, lanes_iota = iotas(second_ref.shape[1])
    half = rows_iota.shape[0] // 2
    low = lax.broadcasted_iota(jnp.int32, (half, LANES), 1) < HALF
    for index, (array, side) in enumerate(layout):

        @pl.when(pl.program_id(0) == index)
        def _():
            for tile in range(second_ref.shape[2] // LANES):
                lanes = slice(tile * LANES, (tile + 1) * LANES)
                even = refs[array][2 * tile, side].astype(jnp.float32)
                odd = refs[array][2 * tile + 1, side].astype(jnp.float32)
                top = jnp.where(low, even, pltpu.roll(odd, HALF, 1))
                bottom = jnp.where(low, pltpu.roll(even, HALF, 1), odd)
                ordered_ref[:half, lanes] = top.astype(jnp.bfloat16)
                ordered_ref[half:, lanes] = bottom.astype(jnp.bfloat16)

    source = as_column(rank_ref[0], rows_iota, lanes_iota)
    turned = dot(one_hot(source == lanes_iota), ordered_ref[...]).astype(jnp.bfloat16)
    third_res = halve(second_ref[0], silu(dot(turned, wl[0])))
    expand = silu(dot(third_res, we[0])).astype(jnp.bfloat16)
    out_ref[0] = halve(third_res, silu(dot(expand, wd[0])))


def table_kernel(chunks, places_ref, wide_ref, entry_ref, angles_ref, take_ref, give_ref, blocks_ref):
    sides, _, size = entry_ref.shape[1:]
    count = sides // chunks
    group_id = wide_ref[0]
    rows_iota, lanes_iota = iotas(size)
    for side in range(sides):
        row = entry_ref[0, side]
        column = as_column(row, rows_iota, lanes_iota)
        rank_column = jnp.sum(jnp.where(row < column, 1, 0), axis=1, keepdims=True)
        rank_row = jnp.sum(jnp.where(column < row, 1, 0), axis=0, keepdims=True)
        take_ref[0, side] = one_hot(rank_column == lanes_iota)
        give_ref[0, side] = one_hot(rows_iota == rank_row)
    span = GROUP * SLOTS
    strip = span // sides
    rows_iota, lanes_iota = iotas(span)
    own = rows_iota % GROUP == lanes_iota % GROUP
    spread_rows = lax.broadcasted_iota(jnp.int32, (SLOTS, span), 0)
    spread_lanes = lax.broadcasted_iota(jnp.int32, (SLOTS, span), 1)
    place = spread_lanes // strip
    side_at = (place // count + place % count * chunks) ^ group_id
    spread = one_hot(side_at * (SLOTS // sides) + spread_lanes % strip // GROUP == spread_rows)
    for group in range(angles_ref.shape[1] // GROUP):
        local = angles_ref[0, group * GROUP : (group + 1) * GROUP, :].astype(jnp.float32)
        stacked = jnp.concatenate(
            [local[:, p * SLOTS : (p + 1) * SLOTS] for p in range(SLOTS)], axis=0
        ).astype(jnp.bfloat16)
        block = jnp.where(own, dot(stacked, spread), 0.0).astype(jnp.bfloat16)
        for side in range(sides):
            offset = group_id ^ side
            to = pl.multiple_of((offset % chunks * count + offset // chunks) * strip, strip)
            blocks_ref[0, group, pl.ds(to, strip), :] = block[side * strip : (side + 1) * strip]


def gather_kernel(owner_ref, place_ref, recv_ref, take_ref, out_ref, ins):
    step = pl.program_id(0)
    sides = take_ref.shape[1]
    devices = recv_ref.shape[0]
    unit = ins.shape[3]
    pairs = devices // 2

    @pl.when(step == 0)
    def _():
        @pl.loop(0, devices)
        def _(source):
            for index in range(devices):
                owner = owner_ref[source, index]
                place = place_ref[source, index]
                at = (index % pairs) * unit
                for side in range(sides):
                    block = recv_ref[source, side, at : at + unit, :]
                    if index >= pairs:
                        block = pltpu.roll(block.astype(jnp.float32), HALF, 1).astype(jnp.bfloat16)
                    ins[side, owner, place] = block

    for side in range(sides):
        operand = ins[side, step].reshape(devices * unit, LANES)
        out_ref[0, side] = dot(take_ref[0, side], operand).astype(jnp.bfloat16)


def mix_kernel(chunk, chunks, owner_ref, place_ref, give_ref, blocks_ref, *refs):
    gathered_refs, out_refs, outs = refs[:chunks], refs[chunks:-1], refs[-1]
    step = pl.program_id(0)
    count = give_ref.shape[1]
    devices = outs.shape[1]
    unit = outs.shape[3]
    groups = blocks_ref.shape[1]
    strip = blocks_ref.shape[2] // (chunks * count)
    pairs = devices // 2
    first = chunk * count * strip
    mixed = []
    for group in range(groups):
        operand = jnp.concatenate(
            [
                ref[0, index, group * strip : (group + 1) * strip, :]
                for ref in gathered_refs
                for index in range(count)
            ],
            axis=0,
        )
        mixing = blocks_ref[0, group, first : first + count * strip, :]
        mixed.append(dot(mixing, operand).astype(jnp.bfloat16))
    for side in range(count):
        operand = jnp.concatenate(
            [part[side * strip : (side + 1) * strip] for part in mixed], axis=0
        )
        outs[side, step] = (
            dot(give_ref[0, side], operand).astype(jnp.bfloat16).reshape(devices, unit, LANES)
        )

    @pl.when(step == pl.num_programs(0) - 1)
    def _():
        low = lax.broadcasted_iota(jnp.int32, (unit, LANES), 1) < HALF

        @pl.loop(0, devices)
        def _(source):
            for index in range(pairs):
                owner = owner_ref[source, index]
                place = place_ref[source, index]
                owner_far = owner_ref[source, index + pairs]
                place_far = place_ref[source, index + pairs]
                rows = slice(index * unit, (index + 1) * unit)
                for side in range(count):
                    near = outs[side, owner, place].astype(jnp.float32)
                    far = outs[side, owner_far, place_far].astype(jnp.float32)
                    joined = jnp.where(low, near, pltpu.roll(far, HALF, 1)).astype(jnp.bfloat16)
                    if len(out_refs) == 1:
                        out_refs[0][source, side, rows, :] = joined
                    else:
                        out_refs[side][source, 0, rows, :] = joined


VMEM_BYTES = 60 * 1024 * 1024


def params():
    return pltpu.CompilerParams(vmem_limit_bytes=VMEM_BYTES)


def cost(flops, moved, waves=0):
    return pl.CostEstimate(flops=flops, bytes_accessed=moved, transcendentals=waves)


def whole_spec(array):
    zeros = (0,) * array.ndim
    return pl.BlockSpec(array.shape, lambda i, *_: zeros)


def weight_spec(section, features):
    return pl.BlockSpec((1, features, features), lambda i, *_: (section, 0, 0))


def run_front(current, where, received, own, chunk, back_rows, rank_rows, weights, section, narrow):
    _, rows, features = current.shape
    count = where.shape[0]
    edge_spec = pl.BlockSpec((1, rows, features), lambda i, where: (i, 0, 0))
    row_spec = pl.BlockSpec((1, 1, rows), lambda i, where: (chunk * count + i, 0, 0))
    return pl.pallas_call(
        functools.partial(front_kernel, own, count),
        grid_spec=pltpu.PrefetchScalarGridSpec(
            num_scalar_prefetch=1,
            grid=(count,),
            in_specs=[
                pl.BlockSpec((1, rows, features), lambda i, where: (where[i], 0, 0)),
                row_spec,
                row_spec,
            ]
            + [weight_spec(section, features)] * 5
            + [whole_spec(array) for array in received],
            out_specs=[
                edge_spec,
                pl.BlockSpec((narrow, 1, rows // 2, LANES), lambda i, where: (0, i, 0, 0)),
            ],
            scratch_shapes=[pltpu.VMEM((rows, features), jnp.bfloat16)],
        ),
        out_shape=[
            jax.ShapeDtypeStruct((count, rows, features), jnp.bfloat16),
            jax.ShapeDtypeStruct((narrow, count, rows // 2, LANES), jnp.bfloat16),
        ],
        compiler_params=params(),
        cost_estimate=cost(12 * count * rows * features**2, 8 * count * rows * features),
        name="front",
    )(where, current, back_rows, rank_rows, *weights[:5], *received)


def run_back(second, packed, layout, chunk, rank_rows, weights, section, where, total, target):
    count, rows, features = second.shape
    edge_spec = pl.BlockSpec((1, rows, features), lambda i, where: (i, 0, 0))
    extra = [] if target is None else [target]
    return pl.pallas_call(
        functools.partial(back_kernel, layout),
        grid_spec=pltpu.PrefetchScalarGridSpec(
            num_scalar_prefetch=1,
            grid=(count,),
            in_specs=[
                edge_spec,
                pl.BlockSpec((1, 1, rows), lambda i, where: (chunk * count + i, 0, 0)),
            ]
            + [weight_spec(section, features)] * 3
            + [whole_spec(array) for array in packed]
            + [pl.BlockSpec(memory_space=pl.ANY)] * len(extra),
            out_specs=pl.BlockSpec((1, rows, features), lambda i, where: (where[i], 0, 0)),
            scratch_shapes=[pltpu.VMEM((rows, features), jnp.bfloat16)],
        ),
        out_shape=jax.ShapeDtypeStruct((total, rows, features), jnp.bfloat16),
        input_output_aliases={6 + len(packed): 0} if extra else {},
        compiler_params=params(),
        cost_estimate=cost(8 * count * rows * features**2, 6 * count * rows * features),
        name="back",
    )(where, second, rank_rows, *weights[5:], *packed, *extra)


def run_tables(places, group_id, entries, angles, chunks):
    owners, sides, _, rows = entries.shape
    atoms = angles.shape[1]
    groups = atoms // GROUP
    span = GROUP * SLOTS
    hot = jax.ShapeDtypeStruct((owners, sides, rows, rows), jnp.bfloat16)
    hot_spec = pl.BlockSpec((1, sides, rows, rows), lambda i, *_: (i, 0, 0, 0))
    return pl.pallas_call(
        functools.partial(table_kernel, chunks),
        grid_spec=pltpu.PrefetchScalarGridSpec(
            num_scalar_prefetch=2,
            grid=(owners,),
            in_specs=[
                pl.BlockSpec((1, sides, 1, rows), lambda i, *_: (i, 0, 0, 0)),
                pl.BlockSpec((1, atoms, angles.shape[2]), lambda i, places, _: (places[i], 0, 0)),
            ],
            out_specs=[
                hot_spec,
                hot_spec,
                pl.BlockSpec((1, groups, span, span), lambda i, *_: (i, 0, 0, 0)),
            ],
        ),
        out_shape=[hot, hot, jax.ShapeDtypeStruct((owners, groups, span, span), jnp.bfloat16)],
        compiler_params=params(),
        cost_estimate=cost(0, 4 * owners * (sides * rows**2 + groups * span**2)),
        name="tables",
    )(places, group_id, entries, angles)


def run_gather(owner_of, place_of, received, take, chunk):
    devices, count, half, _ = received.shape
    rows = 2 * half
    smem = pl.BlockSpec(memory_space=pltpu.SMEM)
    return pl.pallas_call(
        gather_kernel,
        grid=(devices,),
        in_specs=[
            smem,
            smem,
            whole_spec(received),
            pl.BlockSpec((1, count, rows, rows), lambda i: (i, chunk, 0, 0)),
        ],
        out_specs=pl.BlockSpec((1, count, rows, LANES), lambda i: (i, 0, 0, 0)),
        out_shape=jax.ShapeDtypeStruct((devices, count, rows, LANES), jnp.bfloat16),
        scratch_shapes=[
            pltpu.VMEM((count, devices, devices, rows // devices, LANES), jnp.bfloat16)
        ],
        compiler_params=params(),
        cost_estimate=cost(4 * devices * count * rows**2 * LANES, 4 * devices * count * rows**2),
        name="gather",
    )(owner_of, place_of, received, take)


def run_mix(owner_of, place_of, gathered, give, blocks, chunk, apart):
    chunks = len(gathered)
    devices, count, rows, _ = gathered[0].shape
    half = rows // 2
    smem = pl.BlockSpec(memory_space=pltpu.SMEM)
    shapes = [(devices, 1, half, LANES)] * count if apart else [(devices, count, half, LANES)]
    shapes = [jax.ShapeDtypeStruct(shape, jnp.bfloat16) for shape in shapes]
    part_spec = pl.BlockSpec((1, count, rows, LANES), lambda i: (i, 0, 0, 0))
    return pl.pallas_call(
        functools.partial(mix_kernel, chunk, chunks),
        grid=(devices,),
        in_specs=[
            smem,
            smem,
            pl.BlockSpec((1, count, rows, rows), lambda i: (i, chunk, 0, 0)),
            pl.BlockSpec((1,) + blocks.shape[1:], lambda i: (i, 0, 0, 0)),
        ]
        + [part_spec] * chunks,
        out_specs=[whole_spec(shape) for shape in shapes],
        out_shape=shapes,
        scratch_shapes=[
            pltpu.VMEM((count, devices, devices, rows // devices, LANES), jnp.bfloat16)
        ],
        compiler_params=params(),
        cost_estimate=cost(6 * devices * count * rows**2 * LANES, 6 * devices * count * rows**2),
        name="mix",
    )(owner_of, place_of, give, blocks, *gathered)


def unit_tables(entries, capacity, unit):
    owners, sides, rows = entries.shape
    ids = jnp.arange(owners, dtype=jnp.int32)
    source = entries.reshape(owners, sides * rows) // capacity
    counts = jnp.sum((source[None] == ids[:, None, None]).astype(jnp.int32), axis=2) // (unit * sides)
    before = ids[:, None] < ids[None, :]
    starts = jnp.sum(jnp.where(before[None], counts[:, :, None], 0), axis=1)
    places = jnp.sum(jnp.where(before[:, :, None], counts[:, None, :], 0), axis=0)
    inside = (starts[:, :, None] <= ids) & (ids < (starts + counts)[:, :, None])
    owner_of = jnp.sum(jnp.where(inside, ids[None, :, None], 0), axis=1)
    place_of = jnp.sum(jnp.where(inside, (places - starts)[:, :, None] + ids, 0), axis=1)
    return owner_of, place_of


def ranks(values):
    return jnp.sum((values[:, :, None] < values[:, None, :]).astype(jnp.int32), axis=1)


CHUNKS = 2


def reorder(values, order):
    hits = order[:, None] == jnp.arange(values.shape[0], dtype=jnp.int32)
    return jnp.sum(jnp.where(hits[:, :, None], values[None], 0), axis=1)


def shift(values, offset, wide):
    if offset == 0:
        return values
    return lax.ppermute(values, "wide", [(i, i ^ offset) for i in range(wide)])


def swap(values):
    return lax.all_to_all(values, "narrow", 0, 0, tiled=True)


BASE = 64


def share_lists(listed, angles):
    narrow = lax.axis_size("narrow")
    atoms, width = angles.shape
    digits = jnp.stack([listed // BASE, listed % BASE]).reshape(atoms, -1).astype(jnp.bfloat16)
    shared = jnp.concatenate([angles, digits], axis=1)[None]
    held = [0]
    hop = narrow // 2
    while hop:
        other = lax.ppermute(shared, "narrow", [(i, i ^ hop) for i in range(narrow)])
        shared = jnp.concatenate([shared, other], axis=0)
        held += [offset ^ hop for offset in held]
        hop //= 2
    inverse = jnp.array([held.index(offset) for offset in range(narrow)], jnp.int32)
    mine = lax.axis_index("narrow").astype(jnp.int32)
    owners = jnp.arange(narrow, dtype=jnp.int32) ^ mine
    places = jnp.sum(jnp.where(owners[:, None] == jnp.arange(narrow), inverse, 0), axis=1)
    digits = shared[:, :, width:].reshape((narrow, 2) + listed.shape).astype(jnp.int32)
    entries = digits[:, 0] * BASE + digits[:, 1]
    entries = reorder(entries.reshape(narrow, -1), places).reshape(entries.shape)
    return entries, shared, places


def tiled_local(messages, reverse_position, route_slot, atom_slots, angles, weights):
    wide = lax.axis_size("wide")
    narrow = lax.axis_size("narrow")
    edge_rows, features = messages.shape
    rows = edge_rows // wide
    unit = rows // narrow
    capacity = 2 * edge_rows // narrow
    atoms = angles.shape[0]
    count = wide // CHUNKS
    offsets = [[chunk + index * CHUNKS for index in range(count)] for chunk in range(CHUNKS)]
    group_id = lax.axis_index("wide").astype(jnp.int32)
    order = group_id ^ jnp.array(sum(offsets, []), jnp.int32)
    places = [order[chunk * count : (chunk + 1) * count] for chunk in range(CHUNKS)]
    plain = jnp.arange(count, dtype=jnp.int32)

    blocks_of = messages.reshape(wide, rows, features)
    received = [
        [
            shift(lax.dynamic_index_in_dim(blocks_of, group_id ^ offset, 0, False), offset, wide)
            for offset in offsets[chunk]
            if offset
        ]
        for chunk in range(CHUNKS)
    ]
    listed = atom_slots.reshape(atoms // GROUP, GROUP, wide, SLOTS // wide)
    listed = reorder(jnp.transpose(listed, (2, 0, 3, 1)).reshape(wide, rows), order)
    entries, all_angles, owner_places = share_lists(listed, angles)
    rank = ranks(route_slot.reshape(wide, rows))
    back_rows = reverse_position.reshape(wide, rows)
    back_rows = reorder(back_rows, order)
    rank = reorder(rank, order)
    partner_rank = jnp.stack(
        [shift(rank[place], offset, wide) for place, offset in enumerate(sum(offsets, []))]
    )
    hits = back_rows[:, :, None] == jnp.arange(rows, dtype=jnp.int32)
    turned_rank = jnp.sum(jnp.where(hits, partner_rank[:, None, :], 0), axis=2)[:, None, :]
    back_rows = back_rows[:, None, :]
    rank = rank[:, None, :]

    current = [blocks_of] * CHUNKS
    where = places
    chunk_order = list(range(CHUNKS))
    target = None
    tables = None
    for section in range(BLOCKS):
        last = section == BLOCKS - 1
        seconds, spreads = {}, {}
        for chunk in chunk_order:
            seconds[chunk], packed = run_front(
                current[chunk], where[chunk], received[chunk], offsets[chunk][0] == 0, chunk,
                back_rows, rank, weights, section, narrow,
            )
            spreads[chunk] = packed
        if tables is None:
            held = [spreads[chunk] for chunk in chunk_order]
            entries, all_angles, held[-1] = lax.optimization_barrier((entries, all_angles, held[-1]))
            spreads = dict(zip(chunk_order, held))
            owner_of, place_of = unit_tables(entries, capacity, unit)
            tables = run_tables(owner_places, group_id[None], entries[:, :, None, :], all_angles, CHUNKS)
        take, give, blocks = tables
        gathered = [None] * CHUNKS
        for chunk in chunk_order:
            gathered[chunk] = run_gather(owner_of, place_of, swap(spreads[chunk]), take, chunk)
        chunk_order = list(range(CHUNKS))[::-1]
        returned = {}
        for chunk in chunk_order:
            early = chunk == 0
            mixed = list(run_mix(owner_of, place_of, gathered, give, blocks, chunk, early))
            if chunk != chunk_order[-1]:
                mixed[0], gathered[0] = lax.optimization_barrier((mixed[0], gathered[0]))
            if early:
                mixed = [shift(part, offset, wide) for part, offset in zip(mixed, offsets[chunk])]
                parts = [swap(jnp.concatenate(mixed, axis=1))]
                layout = [(0, index) for index in range(count)]
            else:
                whole = swap(mixed[0])
                parts = [
                    shift(whole[:, index : index + 1], offset, wide)
                    for index, offset in enumerate(offsets[chunk])
                ]
                layout = [(index, 0) for index in range(count)]
            returned[chunk] = (parts, layout)
        current = [None] * CHUNKS
        received = [None] * CHUNKS
        for chunk in chunk_order:
            parts, layout = returned[chunk]
            result = run_back(
                seconds[chunk], parts, layout, chunk, turned_rank, weights, section,
                places[chunk] if last else plain, wide if last else count, target,
            )
            if last:
                target = result
            else:
                current[chunk] = result
                received[chunk] = [
                    shift(result[index], offset, wide)
                    for index, offset in enumerate(offsets[chunk])
                    if offset
                ]
        where = [plain] * CHUNKS
    return target.reshape(edge_rows, features)


def local(
    messages,
    reverse_position,
    route_slot,
    atom_slots,
    angles,
    weight_message,
    weight_reverse,
    weight_combine,
    weight_inner,
    weight_outer,
    weight_lift,
    weight_expand,
    weight_reduce,
):
    weights = (
        weight_message,
        weight_reverse,
        weight_combine,
        weight_inner,
        weight_outer,
        weight_lift,
        weight_expand,
        weight_reduce,
    )
    wide = lax.axis_size("wide")
    narrow = lax.axis_size("narrow")
    edge_rows, features = messages.shape
    unit = edge_rows // wide // narrow
    fits = (
        features == narrow * HALF
        and unit % 16 == 0
        and narrow % 2 == 0
        and wide % CHUNKS == 0
        and wide & (wide - 1) == 0
        and narrow & (narrow - 1) == 0
        and angles.shape[0] % GROUP == 0
        and (SLOTS // wide * GROUP) % 16 == 0
    )
    run = tiled_local if fits else general_local
    return run(messages, reverse_position, route_slot, atom_slots, angles, weights)


def solution(mesh):
    in_specs = (
        P(("wide", "narrow"), None),
        P(("wide", "narrow")),
        P(("wide", "narrow")),
        P(("wide", "narrow")),
        P(("wide", "narrow"), None),
        P(),
        P(),
        P(),
        P(),
        P(),
        P(),
        P(),
        P(),
    )
    out_specs = P(("wide", "narrow"), None)
    return jax.shard_map(local, mesh=mesh, in_specs=in_specs, out_specs=out_specs, check_vma=False)
```

```python
import functools

import jax
import jax.numpy as jnp
from jax import lax
from jax.experimental import pallas as pl
from jax.experimental.pallas import tpu as pltpu
from jax.sharding import PartitionSpec as P

SLOTS = 32
BLOCKS = 2
LANES = 128
HALF = LANES // 2
GROUP = 8


ROOT_HALF = 0.7071067811865476


def project(operand, weight):
    return jnp.dot(operand, weight, preferred_element_type=jnp.float32)


def residual(previous, branch):
    return ((previous.astype(jnp.float32) + branch) * ROOT_HALF).astype(jnp.bfloat16)


def reverse_edges(values, partner_rows):
    exchanged = lax.all_to_all(values, "wide", split_axis=0, concat_axis=0, tiled=True)
    return jnp.take(exchanged, partner_rows, axis=0)


def edge_front(current, reverse, weights, section_index):
    hidden = jax.nn.silu(
        project(current, weights[0][section_index]) + project(reverse, weights[1][section_index])
    ).astype(jnp.bfloat16)
    first_res = residual(current, project(hidden, weights[2][section_index]))
    inner_value = jax.nn.silu(project(first_res, weights[3][section_index])).astype(jnp.bfloat16)
    return residual(first_res, jax.nn.silu(project(inner_value, weights[4][section_index])))


def edge_back(second, turned, weights, section_index):
    third_res = residual(second, jax.nn.silu(project(turned, weights[5][section_index])))
    expand = jax.nn.silu(project(third_res, weights[6][section_index])).astype(jnp.bfloat16)
    return residual(third_res, jax.nn.silu(project(expand, weights[7][section_index])))


def owners_mix(second, route_slot, atom_slots, mixing):
    features = second.shape[1]
    buffer_rows = 2 * second.shape[0]
    outgoing = jnp.zeros((buffer_rows, features), jnp.bfloat16).at[route_slot].set(second)
    received = lax.all_to_all(outgoing, "narrow", split_axis=0, concat_axis=0, tiled=True)
    gathered = jnp.take(received, atom_slots, axis=0).reshape(mixing.shape[0], SLOTS, features)
    mixed_rows = jnp.einsum(
        "apq,aqd->apd", mixing, gathered, preferred_element_type=jnp.float32
    ).astype(jnp.bfloat16)
    return mixed_rows.reshape(-1, features)


def back_to_edges(mixed_flat, route_slot, atom_slots):
    features = mixed_flat.shape[1]
    buffer_rows = 2 * route_slot.shape[0]
    answer = jnp.zeros((buffer_rows, features), jnp.bfloat16).at[atom_slots].set(mixed_flat)
    incoming = lax.all_to_all(answer, "narrow", split_axis=0, concat_axis=0, tiled=True)
    return jnp.take(incoming, route_slot, axis=0)


def general_local(messages, reverse_position, route_slot, atom_slots, angles, weights):
    edge_rows = messages.shape[0]
    sub_rows = edge_rows // lax.axis_size("wide")
    partner_rows = jnp.arange(edge_rows, dtype=jnp.int32) // sub_rows * sub_rows + reverse_position
    mixing = angles.reshape(angles.shape[0], SLOTS, SLOTS)
    current = messages
    for section_index in range(BLOCKS):
        reverse = reverse_edges(current, partner_rows)
        second = edge_front(current, reverse, weights, section_index)
        mixed_flat = owners_mix(second, route_slot, atom_slots, mixing)
        returned = back_to_edges(mixed_flat, route_slot, atom_slots)
        turned = reverse_edges(returned, partner_rows)
        current = edge_back(second, turned, weights, section_index)
    return current


def silu(value):
    return 0.5 * value * (1.0 + jnp.tanh(0.5 * value))


def dot(left, right):
    return jnp.dot(left, right, preferred_element_type=jnp.float32)


def halve(previous, branch):
    return ((previous.astype(jnp.float32) + branch) * ROOT_HALF).astype(jnp.bfloat16)


def iotas(size):
    shape = (size, size)
    return lax.broadcasted_iota(jnp.int32, shape, 0), lax.broadcasted_iota(jnp.int32, shape, 1)


def as_column(row, rows_iota, lanes_iota):
    return jnp.sum(jnp.where(rows_iota == lanes_iota, row, 0), axis=1, keepdims=True)


def one_hot(mask):
    return jnp.where(mask, 1.0, 0.0).astype(jnp.bfloat16)


def front_kernel(own, count, where_ref, cur_ref, back_ref, rank_ref, wm, wr, wc, wi, wo, *refs):
    recv_refs, (second_ref, packed_ref, reverse_ref) = refs[:-3], refs[-3:]
    rows_iota, lanes_iota = iotas(cur_ref.shape[1])
    partner = as_column(back_ref[0], rows_iota, lanes_iota)
    hot = one_hot(partner == lanes_iota)
    sources = ([cur_ref.at[0]] if own else []) + list(recv_refs)
    for index in range(count):

        @pl.when(pl.program_id(0) == index)
        def _():
            reverse_ref[...] = dot(hot, sources[index][...]).astype(jnp.bfloat16)

    current = cur_ref[0]
    hidden = silu(dot(current, wm[0]) + dot(reverse_ref[...], wr[0])).astype(jnp.bfloat16)
    first_res = halve(current, dot(hidden, wc[0]))
    inner = silu(dot(first_res, wi[0])).astype(jnp.bfloat16)
    second = halve(first_res, silu(dot(inner, wo[0])))
    second_ref[0] = second
    ordered = dot(one_hot(rows_iota == rank_ref[0]), second)
    half = ordered.shape[0] // 2
    low = lax.broadcasted_iota(jnp.int32, (half, LANES), 1) < HALF
    for tile in range(ordered.shape[1] // LANES):
        top = ordered[:half, tile * LANES : (tile + 1) * LANES]
        bottom = ordered[half:, tile * LANES : (tile + 1) * LANES]
        packed_ref[2 * tile, 0] = jnp.where(low, top, pltpu.roll(bottom, HALF, 1)).astype(jnp.bfloat16)
        packed_ref[2 * tile + 1, 0] = jnp.where(low, pltpu.roll(top, HALF, 1), bottom).astype(jnp.bfloat16)


def back_kernel(layout, where_ref, second_ref, rank_ref, wl, we, wd, *refs):
    out_ref, ordered_ref = refs[-2:]
    rows_iota, lanes_iota = iotas(second_ref.shape[1])
    half = rows_iota.shape[0] // 2
    low = lax.broadcasted_iota(jnp.int32, (half, LANES), 1) < HALF
    for index, (array, side) in enumerate(layout):

        @pl.when(pl.program_id(0) == index)
        def _():
            for tile in range(second_ref.shape[2] // LANES):
                lanes = slice(tile * LANES, (tile + 1) * LANES)
                even = refs[array][2 * tile, side].astype(jnp.float32)
                odd = refs[array][2 * tile + 1, side].astype(jnp.float32)
                top = jnp.where(low, even, pltpu.roll(odd, HALF, 1))
                bottom = jnp.where(low, pltpu.roll(even, HALF, 1), odd)
                ordered_ref[:half, lanes] = top.astype(jnp.bfloat16)
                ordered_ref[half:, lanes] = bottom.astype(jnp.bfloat16)

    source = as_column(rank_ref[0], rows_iota, lanes_iota)
    turned = dot(one_hot(source == lanes_iota), ordered_ref[...]).astype(jnp.bfloat16)
    third_res = halve(second_ref[0], silu(dot(turned, wl[0])))
    expand = silu(dot(third_res, we[0])).astype(jnp.bfloat16)
    out_ref[0] = halve(third_res, silu(dot(expand, wd[0])))


def table_kernel(places_ref, order_ref, position_ref, entry_ref, angles_ref, rank_ref, blocks_ref):
    sides, _, size = entry_ref.shape[1:]
    rows_iota, lanes_iota = iotas(size)
    for side in range(sides):
        row = entry_ref[0, side]
        column = as_column(row, rows_iota, lanes_iota)
        rank_ref[0, side] = jnp.sum(jnp.where(column < row, 1, 0), axis=0, keepdims=True)
    span = GROUP * SLOTS
    strip = span // sides
    rows_iota, lanes_iota = iotas(span)
    own = rows_iota % GROUP == lanes_iota % GROUP
    spread_rows = lax.broadcasted_iota(jnp.int32, (SLOTS, span), 0)
    spread_lanes = lax.broadcasted_iota(jnp.int32, (SLOTS, span), 1)
    side_at = jnp.zeros((SLOTS, span), jnp.int32)
    for place in range(sides):
        side_at = jnp.where(spread_lanes // strip == place, order_ref[place], side_at)
    spread = one_hot(side_at * (SLOTS // sides) + spread_lanes % strip // GROUP == spread_rows)
    for group in range(angles_ref.shape[1] // GROUP):
        local = angles_ref[0, group * GROUP : (group + 1) * GROUP, :].astype(jnp.float32)
        stacked = jnp.concatenate(
            [local[:, p * SLOTS : (p + 1) * SLOTS] for p in range(SLOTS)], axis=0
        ).astype(jnp.bfloat16)
        block = jnp.where(own, dot(stacked, spread), 0.0).astype(jnp.bfloat16)
        for side in range(sides):
            to = pl.multiple_of(position_ref[side] * strip, strip)
            blocks_ref[0, group, pl.ds(to, strip), :] = block[side * strip : (side + 1) * strip]


def gather_kernel(chunk, owner_ref, place_ref, recv_ref, rank_ref, out_ref, ins):
    step = pl.program_id(0)
    sides = recv_ref.shape[1]
    devices = recv_ref.shape[0]
    unit = ins.shape[3]
    pairs = devices // 2

    @pl.when(step == 0)
    def _():
        @pl.loop(0, devices)
        def _(source):
            for index in range(devices):
                owner = owner_ref[source, index]
                place = place_ref[source, index]
                at = (index % pairs) * unit
                for side in range(sides):
                    block = recv_ref[source, side, at : at + unit, :]
                    if index >= pairs:
                        block = pltpu.roll(block.astype(jnp.float32), HALF, 1).astype(jnp.bfloat16)
                    ins[side, owner, place] = block

    rows_iota, lanes_iota = iotas(devices * unit)
    for side in range(sides):
        operand = ins[side, step].reshape(devices * unit, LANES)
        source = as_column(rank_ref[0, chunk * sides + side], rows_iota, lanes_iota)
        out_ref[0, side] = dot(one_hot(source == lanes_iota), operand).astype(jnp.bfloat16)


def mix_kernel(chunk, chunks, owner_ref, place_ref, rank_ref, blocks_ref, *refs):
    gathered_refs, out_refs, outs = refs[:chunks], refs[chunks:-1], refs[-1]
    step = pl.program_id(0)
    count = outs.shape[0]
    devices = outs.shape[1]
    unit = outs.shape[3]
    groups = blocks_ref.shape[1]
    strip = blocks_ref.shape[2] // count
    pairs = devices // 2
    rows_iota = iotas(devices * unit)[0]
    mixed = []
    for group in range(groups):
        operand = jnp.concatenate(
            [
                ref[0, index, group * strip : (group + 1) * strip, :]
                for ref in gathered_refs
                for index in range(count)
            ],
            axis=0,
        )
        mixed.append(dot(blocks_ref[0, group], operand).astype(jnp.bfloat16))
    for side in range(count):
        operand = jnp.concatenate(
            [part[side * strip : (side + 1) * strip] for part in mixed], axis=0
        )
        outs[side, step] = (
            dot(one_hot(rows_iota == rank_ref[0, chunk * count + side]), operand)
            .astype(jnp.bfloat16)
            .reshape(devices, unit, LANES)
        )

    @pl.when(step == pl.num_programs(0) - 1)
    def _():
        low = lax.broadcasted_iota(jnp.int32, (unit, LANES), 1) < HALF

        @pl.loop(0, devices)
        def _(source):
            for index in range(pairs):
                owner = owner_ref[source, index]
                place = place_ref[source, index]
                owner_far = owner_ref[source, index + pairs]
                place_far = place_ref[source, index + pairs]
                rows = slice(index * unit, (index + 1) * unit)
                for side in range(count):
                    near = outs[side, owner, place].astype(jnp.float32)
                    far = outs[side, owner_far, place_far].astype(jnp.float32)
                    joined = jnp.where(low, near, pltpu.roll(far, HALF, 1)).astype(jnp.bfloat16)
                    if len(out_refs) == 1:
                        out_refs[0][source, side, rows, :] = joined
                    else:
                        out_refs[side][source, 0, rows, :] = joined


VMEM_BYTES = 24 * 1024 * 1024


def params():
    return pltpu.CompilerParams(vmem_limit_bytes=VMEM_BYTES)


def cost(flops, moved, waves=0):
    return pl.CostEstimate(flops=flops, bytes_accessed=moved, transcendentals=waves)


def whole_spec(array):
    zeros = (0,) * array.ndim
    return pl.BlockSpec(array.shape, lambda i, *_: zeros)


def weight_spec(section, features):
    return pl.BlockSpec((1, features, features), lambda i, *_: (section, 0, 0))


def run_front(current, where, received, own, chunk, back_rows, rank_rows, weights, section, narrow):
    _, rows, features = current.shape
    count = where.shape[0]
    edge_spec = pl.BlockSpec((1, rows, features), lambda i, where: (i, 0, 0))
    row_spec = pl.BlockSpec((1, 1, rows), lambda i, where: (chunk * count + i, 0, 0))
    return pl.pallas_call(
        functools.partial(front_kernel, own, count),
        grid_spec=pltpu.PrefetchScalarGridSpec(
            num_scalar_prefetch=1,
            grid=(count,),
            in_specs=[
                pl.BlockSpec((1, rows, features), lambda i, where: (where[i], 0, 0)),
                row_spec,
                row_spec,
            ]
            + [weight_spec(section, features)] * 5
            + [whole_spec(array) for array in received],
            out_specs=[
                edge_spec,
                pl.BlockSpec((narrow, 1, rows // 2, LANES), lambda i, where: (0, i, 0, 0)),
            ],
            scratch_shapes=[pltpu.VMEM((rows, features), jnp.bfloat16)],
        ),
        out_shape=[
            jax.ShapeDtypeStruct((count, rows, features), jnp.bfloat16),
            jax.ShapeDtypeStruct((narrow, count, rows // 2, LANES), jnp.bfloat16),
        ],
        compiler_params=params(),
        cost_estimate=cost(12 * count * rows * features**2, 8 * count * rows * features),
        name="front",
    )(where, current, back_rows, rank_rows, *weights[:5], *received)


def run_back(second, packed, layout, chunk, rank_rows, weights, section, where, total, target):
    count, rows, features = second.shape
    edge_spec = pl.BlockSpec((1, rows, features), lambda i, where: (i, 0, 0))
    extra = [] if target is None else [target]
    return pl.pallas_call(
        functools.partial(back_kernel, layout),
        grid_spec=pltpu.PrefetchScalarGridSpec(
            num_scalar_prefetch=1,
            grid=(count,),
            in_specs=[
                edge_spec,
                pl.BlockSpec((1, 1, rows), lambda i, where: (chunk * count + i, 0, 0)),
            ]
            + [weight_spec(section, features)] * 3
            + [whole_spec(array) for array in packed]
            + [pl.BlockSpec(memory_space=pl.ANY)] * len(extra),
            out_specs=pl.BlockSpec((1, rows, features), lambda i, where: (where[i], 0, 0)),
            scratch_shapes=[pltpu.VMEM((rows, features), jnp.bfloat16)],
        ),
        out_shape=jax.ShapeDtypeStruct((total, rows, features), jnp.bfloat16),
        input_output_aliases={6 + len(packed): 0} if extra else {},
        compiler_params=params(),
        cost_estimate=cost(8 * count * rows * features**2, 6 * count * rows * features),
        name="back",
    )(where, second, rank_rows, *weights[5:], *packed, *extra)


def rank_spec(entries):
    return pl.BlockSpec((1,) + entries.shape[1:], lambda i, *_: (i, 0, 0, 0))


def run_tables(places, order, position, entries, angles):
    owners = entries.shape[0]
    atoms = angles.shape[1]
    groups = atoms // GROUP
    span = GROUP * SLOTS
    return pl.pallas_call(
        table_kernel,
        grid_spec=pltpu.PrefetchScalarGridSpec(
            num_scalar_prefetch=3,
            grid=(owners,),
            in_specs=[
                rank_spec(entries),
                pl.BlockSpec((1, atoms, angles.shape[2]), lambda i, places, *_: (places[i], 0, 0)),
            ],
            out_specs=[
                rank_spec(entries),
                pl.BlockSpec((1, groups, span, span), lambda i, *_: (i, 0, 0, 0)),
            ],
        ),
        out_shape=[
            jax.ShapeDtypeStruct(entries.shape, jnp.int32),
            jax.ShapeDtypeStruct((owners, groups, span, span), jnp.bfloat16),
        ],
        compiler_params=params(),
        cost_estimate=cost(0, 8 * owners * groups * span**2),
        name="tables",
    )(places, order, position, entries, angles)


def run_gather(owner_of, place_of, received, rank, chunk):
    devices, count, half, _ = received.shape
    rows = 2 * half
    smem = pl.BlockSpec(memory_space=pltpu.SMEM)
    return pl.pallas_call(
        functools.partial(gather_kernel, chunk),
        grid=(devices,),
        in_specs=[
            smem,
            smem,
            whole_spec(received),
            rank_spec(rank),
        ],
        out_specs=pl.BlockSpec((1, count, rows, LANES), lambda i: (i, 0, 0, 0)),
        out_shape=jax.ShapeDtypeStruct((devices, count, rows, LANES), jnp.bfloat16),
        scratch_shapes=[
            pltpu.VMEM((count, devices, devices, rows // devices, LANES), jnp.bfloat16)
        ],
        compiler_params=params(),
        cost_estimate=cost(4 * devices * count * rows**2 * LANES, 4 * devices * count * rows**2),
        name="gather",
    )(owner_of, place_of, received, rank)


def run_mix(owner_of, place_of, gathered, rank, blocks, chunk, apart):
    chunks = len(gathered)
    devices, count, rows, _ = gathered[0].shape
    half = rows // 2
    groups, span = blocks.shape[1:3]
    smem = pl.BlockSpec(memory_space=pltpu.SMEM)
    shapes = [(devices, 1, half, LANES)] * count if apart else [(devices, count, half, LANES)]
    shapes = [jax.ShapeDtypeStruct(shape, jnp.bfloat16) for shape in shapes]
    part_spec = pl.BlockSpec((1, count, rows, LANES), lambda i: (i, 0, 0, 0))
    return pl.pallas_call(
        functools.partial(mix_kernel, chunk, chunks),
        grid=(devices,),
        in_specs=[
            smem,
            smem,
            rank_spec(rank),
            pl.BlockSpec((1, groups, span // chunks, span), lambda i: (i, 0, chunk, 0)),
        ]
        + [part_spec] * chunks,
        out_specs=[whole_spec(shape) for shape in shapes],
        out_shape=shapes,
        scratch_shapes=[
            pltpu.VMEM((count, devices, devices, rows // devices, LANES), jnp.bfloat16)
        ],
        compiler_params=params(),
        cost_estimate=cost(6 * devices * count * rows**2 * LANES, 6 * devices * count * rows**2),
        name="mix",
    )(owner_of, place_of, rank, blocks, *gathered)


def unit_tables(entries, capacity, unit):
    owners, sides, rows = entries.shape
    ids = jnp.arange(owners, dtype=jnp.int32)
    source = entries.reshape(owners, sides * rows) // capacity
    counts = jnp.sum((source[None] == ids[:, None, None]).astype(jnp.int32), axis=2) // (unit * sides)
    before = ids[:, None] < ids[None, :]
    starts = jnp.sum(jnp.where(before[None], counts[:, :, None], 0), axis=1)
    places = jnp.sum(jnp.where(before[:, :, None], counts[:, None, :], 0), axis=0)
    inside = (starts[:, :, None] <= ids) & (ids < (starts + counts)[:, :, None])
    owner_of = jnp.sum(jnp.where(inside, ids[None, :, None], 0), axis=1)
    place_of = jnp.sum(jnp.where(inside, (places - starts)[:, :, None] + ids, 0), axis=1)
    return owner_of, place_of


def ranks(values):
    return jnp.sum((values[:, :, None] < values[:, None, :]).astype(jnp.int32), axis=1)


CHUNKS = 2


def reorder(values, order):
    hits = order[:, None] == jnp.arange(values.shape[0], dtype=jnp.int32)
    return jnp.sum(jnp.where(hits[:, :, None], values[None], 0), axis=1)


def shift(values, offset, wide):
    if offset == 0:
        return values
    return lax.ppermute(values, "wide", [(i, i ^ offset) for i in range(wide)])


def swap(values):
    return lax.all_to_all(values, "narrow", 0, 0, tiled=True)


BASE = 64


def share_lists(listed, angles):
    narrow = lax.axis_size("narrow")
    atoms, width = angles.shape
    digits = jnp.stack([listed // BASE, listed % BASE]).reshape(atoms, -1).astype(jnp.bfloat16)
    shared = jnp.concatenate([angles, digits], axis=1)[None]
    held = [0]
    hop = narrow // 2
    while hop:
        other = lax.ppermute(shared, "narrow", [(i, i ^ hop) for i in range(narrow)])
        shared = jnp.concatenate([shared, other], axis=0)
        held += [offset ^ hop for offset in held]
        hop //= 2
    inverse = jnp.array([held.index(offset) for offset in range(narrow)], jnp.int32)
    mine = lax.axis_index("narrow").astype(jnp.int32)
    owners = jnp.arange(narrow, dtype=jnp.int32) ^ mine
    places = jnp.sum(jnp.where(owners[:, None] == jnp.arange(narrow), inverse, 0), axis=1)
    digits = shared[:, :, width:].reshape((narrow, 2) + listed.shape).astype(jnp.int32)
    entries = digits[:, 0] * BASE + digits[:, 1]
    entries = reorder(entries.reshape(narrow, -1), places).reshape(entries.shape)
    return entries, shared, places


def tiled_local(messages, reverse_position, route_slot, atom_slots, angles, weights):
    wide = lax.axis_size("wide")
    narrow = lax.axis_size("narrow")
    edge_rows, features = messages.shape
    rows = edge_rows // wide
    unit = rows // narrow
    capacity = 2 * edge_rows // narrow
    atoms = angles.shape[0]
    count = wide // CHUNKS
    spread_out = [offset for index in range(wide // 2) for offset in (index, wide - 1 - index)]
    offsets = [spread_out[chunk * count : (chunk + 1) * count] for chunk in range(CHUNKS)]
    group_id = lax.axis_index("wide").astype(jnp.int32)
    order = group_id ^ jnp.array(sum(offsets, []), jnp.int32)
    inverse = jnp.array([spread_out.index(offset) for offset in range(wide)], jnp.int32)
    owners_wide = (jnp.arange(wide, dtype=jnp.int32) ^ group_id)[:, None]
    position = jnp.sum(jnp.where(owners_wide == jnp.arange(wide), inverse, 0), axis=1)
    places = [order[chunk * count : (chunk + 1) * count] for chunk in range(CHUNKS)]
    plain = jnp.arange(count, dtype=jnp.int32)

    blocks_of = messages.reshape(wide, rows, features)
    received = [
        [
            shift(lax.dynamic_index_in_dim(blocks_of, group_id ^ offset, 0, False), offset, wide)
            for offset in offsets[chunk]
            if offset
        ]
        for chunk in range(CHUNKS)
    ]
    listed = atom_slots.reshape(atoms // GROUP, GROUP, wide, SLOTS // wide)
    listed = reorder(jnp.transpose(listed, (2, 0, 3, 1)).reshape(wide, rows), order)
    entries, all_angles, owner_places = share_lists(listed, angles)
    rank = ranks(route_slot.reshape(wide, rows))
    back_rows = reverse_position.reshape(wide, rows)
    back_rows = reorder(back_rows, order)
    rank = reorder(rank, order)
    partner_rank = jnp.stack(
        [shift(rank[place], offset, wide) for place, offset in enumerate(sum(offsets, []))]
    )
    hits = back_rows[:, :, None] == jnp.arange(rows, dtype=jnp.int32)
    turned_rank = jnp.sum(jnp.where(hits, partner_rank[:, None, :], 0), axis=2)[:, None, :]
    back_rows = back_rows[:, None, :]
    rank = rank[:, None, :]

    current = [blocks_of] * CHUNKS
    where = places
    chunk_order = list(range(CHUNKS))
    target = None
    tables = None
    for section in range(BLOCKS):
        last = section == BLOCKS - 1
        seconds, spreads = {}, {}
        for chunk in chunk_order:
            seconds[chunk], packed = run_front(
                current[chunk], where[chunk], received[chunk], offsets[chunk][0] == 0, chunk,
                back_rows, rank, weights, section, narrow,
            )
            spreads[chunk] = packed
        if tables is None:
            held = [spreads[chunk] for chunk in chunk_order]
            entries, all_angles, held[-1] = lax.optimization_barrier((entries, all_angles, held[-1]))
            spreads = dict(zip(chunk_order, held))
            owner_of, place_of = unit_tables(entries, capacity, unit)
            tables = run_tables(owner_places, order, position, entries[:, :, None, :], all_angles)
        listed_rank, blocks = tables
        gathered = [None] * CHUNKS
        for chunk in chunk_order:
            gathered[chunk] = run_gather(owner_of, place_of, swap(spreads[chunk]), listed_rank, chunk)
        chunk_order = list(range(CHUNKS))[::-1]
        returned = {}
        sent = None
        for chunk in chunk_order:
            early = chunk == 0
            mixed = list(run_mix(owner_of, place_of, gathered, listed_rank, blocks, chunk, early))
            if chunk != chunk_order[-1]:
                mixed[0], gathered[0] = lax.optimization_barrier((mixed[0], gathered[0]))
            if early:
                mixed = [shift(part, offset, wide) for part, offset in zip(mixed, offsets[chunk])]
                if sent is not None:
                    sent, mixed[0] = lax.optimization_barrier((sent, mixed[0]))
                    returned[chunk_order[0]] = (sent, returned[chunk_order[0]][1])
                parts = [swap(jnp.concatenate(mixed, axis=1))]
                layout = [(0, index) for index in range(count)]
            else:
                sent = swap(mixed[0])
                parts = sent
                layout = [(index, 0) for index in range(count)]
            returned[chunk] = (parts, layout)
        current = [None] * CHUNKS
        received = [None] * CHUNKS
        for chunk in chunk_order:
            parts, layout = returned[chunk]
            if chunk:
                parts = [
                    shift(parts[:, index : index + 1], offset, wide)
                    for index, offset in enumerate(offsets[chunk])
                ]
            result = run_back(
                seconds[chunk], parts, layout, chunk, turned_rank, weights, section,
                places[chunk] if last else plain, wide if last else count, target,
            )
            if last:
                target = result
            else:
                current[chunk] = result
                received[chunk] = [
                    shift(result[index], offset, wide)
                    for index, offset in enumerate(offsets[chunk])
                    if offset
                ]
        where = [plain] * CHUNKS
    return target.reshape(edge_rows, features)


def local(
    messages,
    reverse_position,
    route_slot,
    atom_slots,
    angles,
    weight_message,
    weight_reverse,
    weight_combine,
    weight_inner,
    weight_outer,
    weight_lift,
    weight_expand,
    weight_reduce,
):
    weights = (
        weight_message,
        weight_reverse,
        weight_combine,
        weight_inner,
        weight_outer,
        weight_lift,
        weight_expand,
        weight_reduce,
    )
    wide = lax.axis_size("wide")
    narrow = lax.axis_size("narrow")
    edge_rows, features = messages.shape
    unit = edge_rows // wide // narrow
    fits = (
        features == narrow * HALF
        and unit % 16 == 0
        and narrow % 2 == 0
        and wide % CHUNKS == 0
        and wide & (wide - 1) == 0
        and narrow & (narrow - 1) == 0
        and angles.shape[0] % GROUP == 0
        and (SLOTS // wide * GROUP) % 16 == 0
    )
    run = tiled_local if fits else general_local
    return run(messages, reverse_position, route_slot, atom_slots, angles, weights)


def solution(mesh):
    in_specs = (
        P(("wide", "narrow"), None),
        P(("wide", "narrow")),
        P(("wide", "narrow")),
        P(("wide", "narrow")),
        P(("wide", "narrow"), None),
        P(),
        P(),
        P(),
        P(),
        P(),
        P(),
        P(),
        P(),
    )
    out_specs = P(("wide", "narrow"), None)
    return jax.shard_map(local, mesh=mesh, in_specs=in_specs, out_specs=out_specs, check_vma=False)
```

```python
import functools

import jax
import jax.numpy as jnp
from jax import lax
from jax.experimental import pallas as pl
from jax.experimental.pallas import tpu as pltpu
from jax.sharding import PartitionSpec as P

SLOTS = 32
BLOCKS = 2
LANES = 128
HALF = LANES // 2
GROUP = 8


ROOT_HALF = 0.7071067811865476


def project(operand, weight):
    return jnp.dot(operand, weight, preferred_element_type=jnp.float32)


def residual(previous, branch):
    return ((previous.astype(jnp.float32) + branch) * ROOT_HALF).astype(jnp.bfloat16)


def reverse_edges(values, partner_rows):
    exchanged = lax.all_to_all(values, "wide", split_axis=0, concat_axis=0, tiled=True)
    return jnp.take(exchanged, partner_rows, axis=0)


def edge_front(current, reverse, weights, section_index):
    hidden = jax.nn.silu(
        project(current, weights[0][section_index]) + project(reverse, weights[1][section_index])
    ).astype(jnp.bfloat16)
    first_res = residual(current, project(hidden, weights[2][section_index]))
    inner_value = jax.nn.silu(project(first_res, weights[3][section_index])).astype(jnp.bfloat16)
    return residual(first_res, jax.nn.silu(project(inner_value, weights[4][section_index])))


def edge_back(second, turned, weights, section_index):
    third_res = residual(second, jax.nn.silu(project(turned, weights[5][section_index])))
    expand = jax.nn.silu(project(third_res, weights[6][section_index])).astype(jnp.bfloat16)
    return residual(third_res, jax.nn.silu(project(expand, weights[7][section_index])))


def owners_mix(second, route_slot, atom_slots, mixing):
    features = second.shape[1]
    buffer_rows = 2 * second.shape[0]
    outgoing = jnp.zeros((buffer_rows, features), jnp.bfloat16).at[route_slot].set(second)
    received = lax.all_to_all(outgoing, "narrow", split_axis=0, concat_axis=0, tiled=True)
    gathered = jnp.take(received, atom_slots, axis=0).reshape(mixing.shape[0], SLOTS, features)
    mixed_rows = jnp.einsum(
        "apq,aqd->apd", mixing, gathered, preferred_element_type=jnp.float32
    ).astype(jnp.bfloat16)
    return mixed_rows.reshape(-1, features)


def back_to_edges(mixed_flat, route_slot, atom_slots):
    features = mixed_flat.shape[1]
    buffer_rows = 2 * route_slot.shape[0]
    answer = jnp.zeros((buffer_rows, features), jnp.bfloat16).at[atom_slots].set(mixed_flat)
    incoming = lax.all_to_all(answer, "narrow", split_axis=0, concat_axis=0, tiled=True)
    return jnp.take(incoming, route_slot, axis=0)


def general_local(messages, reverse_position, route_slot, atom_slots, angles, weights):
    edge_rows = messages.shape[0]
    sub_rows = edge_rows // lax.axis_size("wide")
    partner_rows = jnp.arange(edge_rows, dtype=jnp.int32) // sub_rows * sub_rows + reverse_position
    mixing = angles.reshape(angles.shape[0], SLOTS, SLOTS)
    current = messages
    for section_index in range(BLOCKS):
        reverse = reverse_edges(current, partner_rows)
        second = edge_front(current, reverse, weights, section_index)
        mixed_flat = owners_mix(second, route_slot, atom_slots, mixing)
        returned = back_to_edges(mixed_flat, route_slot, atom_slots)
        turned = reverse_edges(returned, partner_rows)
        current = edge_back(second, turned, weights, section_index)
    return current


def silu(value):
    return 0.5 * value * (1.0 + jnp.tanh(0.5 * value))


def dot(left, right):
    return jnp.dot(left, right, preferred_element_type=jnp.float32)


def halve(previous, branch):
    return ((previous.astype(jnp.float32) + branch) * ROOT_HALF).astype(jnp.bfloat16)


def iotas(size):
    shape = (size, size)
    return lax.broadcasted_iota(jnp.int32, shape, 0), lax.broadcasted_iota(jnp.int32, shape, 1)


def as_column(row, rows_iota, lanes_iota):
    return jnp.sum(jnp.where(rows_iota == lanes_iota, row, 0), axis=1, keepdims=True)


def one_hot(mask):
    return jnp.where(mask, 1.0, 0.0).astype(jnp.bfloat16)


def fetcher(weight_refs, section, held, sems):
    first = pl.program_id(0) == 0
    copies = [
        pltpu.make_async_copy(ref.at[section], held.at[index], sems.at[index])
        for index, ref in enumerate(weight_refs)
    ]

    @pl.when(first)
    def _():
        for copy in copies:
            copy.start()

    def weight(index):
        @pl.when(first)
        def _():
            copies[index].wait()

        return held[index]

    return weight


def front_kernel(own, count, section, where_ref, cur_ref, back_ref, rank_ref, *refs):
    weight_refs, refs = refs[:5], refs[5:]
    recv_refs, (second_ref, packed_ref, reverse_ref, held, sems) = refs[:-5], refs[-5:]
    weight = fetcher(weight_refs, section, held, sems)
    rows_iota, lanes_iota = iotas(cur_ref.shape[1])
    partner = as_column(back_ref[0], rows_iota, lanes_iota)
    hot = one_hot(partner == lanes_iota)
    sources = ([cur_ref.at[0]] if own else []) + list(recv_refs)
    for index in range(count):

        @pl.when(pl.program_id(0) == index)
        def _():
            reverse_ref[...] = dot(hot, sources[index][...]).astype(jnp.bfloat16)

    current = cur_ref[0]
    own_part = dot(current, weight(0))
    hidden = silu(own_part + dot(reverse_ref[...], weight(1))).astype(jnp.bfloat16)
    first_res = halve(current, dot(hidden, weight(2)))
    inner = silu(dot(first_res, weight(3))).astype(jnp.bfloat16)
    second = halve(first_res, silu(dot(inner, weight(4))))
    second_ref[0] = second
    ordered = dot(one_hot(rows_iota == rank_ref[0]), second)
    half = ordered.shape[0] // 2
    low = lax.broadcasted_iota(jnp.int32, (half, LANES), 1) < HALF
    for tile in range(ordered.shape[1] // LANES):
        top = ordered[:half, tile * LANES : (tile + 1) * LANES]
        bottom = ordered[half:, tile * LANES : (tile + 1) * LANES]
        packed_ref[2 * tile, 0] = jnp.where(low, top, pltpu.roll(bottom, HALF, 1)).astype(jnp.bfloat16)
        packed_ref[2 * tile + 1, 0] = jnp.where(low, pltpu.roll(top, HALF, 1), bottom).astype(jnp.bfloat16)


def back_kernel(layout, section, where_ref, second_ref, rank_ref, *refs):
    weight_refs, refs = refs[:3], refs[3:]
    out_ref, ordered_ref, held, sems = refs[-4:]
    weight = fetcher(weight_refs, section, held, sems)
    rows_iota, lanes_iota = iotas(second_ref.shape[1])
    half = rows_iota.shape[0] // 2
    low = lax.broadcasted_iota(jnp.int32, (half, LANES), 1) < HALF
    for index, (array, side) in enumerate(layout):

        @pl.when(pl.program_id(0) == index)
        def _():
            for tile in range(second_ref.shape[2] // LANES):
                lanes = slice(tile * LANES, (tile + 1) * LANES)
                even = refs[array][2 * tile, side].astype(jnp.float32)
                odd = refs[array][2 * tile + 1, side].astype(jnp.float32)
                top = jnp.where(low, even, pltpu.roll(odd, HALF, 1))
                bottom = jnp.where(low, pltpu.roll(even, HALF, 1), odd)
                ordered_ref[:half, lanes] = top.astype(jnp.bfloat16)
                ordered_ref[half:, lanes] = bottom.astype(jnp.bfloat16)

    source = as_column(rank_ref[0], rows_iota, lanes_iota)
    turned = dot(one_hot(source == lanes_iota), ordered_ref[...]).astype(jnp.bfloat16)
    third_res = halve(second_ref[0], silu(dot(turned, weight(0))))
    expand = silu(dot(third_res, weight(1))).astype(jnp.bfloat16)
    out_ref[0] = halve(third_res, silu(dot(expand, weight(2))))


def table_kernel(places_ref, order_ref, position_ref, entry_ref, angles_ref, rank_ref, blocks_ref):
    sides, _, size = entry_ref.shape[1:]
    rows_iota, lanes_iota = iotas(size)
    for side in range(sides):
        row = entry_ref[0, side]
        column = as_column(row, rows_iota, lanes_iota)
        rank_ref[0, side] = jnp.sum(jnp.where(column < row, 1, 0), axis=0, keepdims=True)
    span = GROUP * SLOTS
    strip = span // sides
    rows_iota, lanes_iota = iotas(span)
    own = rows_iota % GROUP == lanes_iota % GROUP
    spread_rows = lax.broadcasted_iota(jnp.int32, (SLOTS, span), 0)
    spread_lanes = lax.broadcasted_iota(jnp.int32, (SLOTS, span), 1)
    side_at = jnp.zeros((SLOTS, span), jnp.int32)
    for place in range(sides):
        side_at = jnp.where(spread_lanes // strip == place, order_ref[place], side_at)
    spread = one_hot(side_at * (SLOTS // sides) + spread_lanes % strip // GROUP == spread_rows)
    for group in range(angles_ref.shape[1] // GROUP):
        local = angles_ref[0, group * GROUP : (group + 1) * GROUP, :].astype(jnp.float32)
        stacked = jnp.concatenate(
            [local[:, p * SLOTS : (p + 1) * SLOTS] for p in range(SLOTS)], axis=0
        ).astype(jnp.bfloat16)
        block = jnp.where(own, dot(stacked, spread), 0.0).astype(jnp.bfloat16)
        for side in range(sides):
            to = pl.multiple_of(position_ref[side] * strip, strip)
            blocks_ref[0, group, pl.ds(to, strip), :] = block[side * strip : (side + 1) * strip]


def gather_kernel(chunk, owner_ref, place_ref, recv_ref, rank_ref, out_ref, ins):
    step = pl.program_id(0)
    sides = recv_ref.shape[1]
    devices = recv_ref.shape[0]
    unit = ins.shape[3]
    pairs = devices // 2

    @pl.when(step == 0)
    def _():
        @pl.loop(0, devices)
        def _(source):
            for index in range(devices):
                owner = owner_ref[source, index]
                place = place_ref[source, index]
                at = (index % pairs) * unit
                for side in range(sides):
                    block = recv_ref[source, side, at : at + unit, :]
                    if index >= pairs:
                        block = pltpu.roll(block.astype(jnp.float32), HALF, 1).astype(jnp.bfloat16)
                    ins[side, owner, place] = block

    rows_iota, lanes_iota = iotas(devices * unit)
    for side in range(sides):
        operand = ins[side, step].reshape(devices * unit, LANES)
        source = as_column(rank_ref[0, chunk * sides + side], rows_iota, lanes_iota)
        out_ref[0, side] = dot(one_hot(source == lanes_iota), operand).astype(jnp.bfloat16)


def mix_kernel(chunk, chunks, owner_ref, place_ref, rank_ref, blocks_ref, *refs):
    gathered_refs, out_refs, (outs, held, sems) = refs[:chunks], refs[chunks:-3], refs[-3:]
    step = pl.program_id(0)
    part = held.shape[2]

    def fetch(owner):
        rows = pl.ds(chunk * part, part)
        return pltpu.make_async_copy(blocks_ref.at[owner, :, rows, :], held.at[owner], sems.at[owner])

    @pl.when(step == 0)
    def _():
        for owner in range(held.shape[0]):
            fetch(owner).start()

    fetch(step).wait()
    count = outs.shape[0]
    devices = outs.shape[1]
    unit = outs.shape[3]
    groups = blocks_ref.shape[1]
    strip = part // count
    pairs = devices // 2
    rows_iota = iotas(devices * unit)[0]
    mixed = []
    for group in range(groups):
        operand = jnp.concatenate(
            [
                ref[0, index, group * strip : (group + 1) * strip, :]
                for ref in gathered_refs
                for index in range(count)
            ],
            axis=0,
        )
        mixed.append(dot(held[step, group], operand).astype(jnp.bfloat16))
    for side in range(count):
        operand = jnp.concatenate(
            [rows[side * strip : (side + 1) * strip] for rows in mixed], axis=0
        )
        outs[side, step] = (
            dot(one_hot(rows_iota == rank_ref[0, chunk * count + side]), operand)
            .astype(jnp.bfloat16)
            .reshape(devices, unit, LANES)
        )

    @pl.when(step == pl.num_programs(0) - 1)
    def _():
        low = lax.broadcasted_iota(jnp.int32, (unit, LANES), 1) < HALF

        @pl.loop(0, devices)
        def _(source):
            for index in range(pairs):
                owner = owner_ref[source, index]
                place = place_ref[source, index]
                owner_far = owner_ref[source, index + pairs]
                place_far = place_ref[source, index + pairs]
                rows = slice(index * unit, (index + 1) * unit)
                for side in range(count):
                    near = outs[side, owner, place].astype(jnp.float32)
                    far = outs[side, owner_far, place_far].astype(jnp.float32)
                    joined = jnp.where(low, near, pltpu.roll(far, HALF, 1)).astype(jnp.bfloat16)
                    if len(out_refs) == 1:
                        out_refs[0][source, side, rows, :] = joined
                    else:
                        out_refs[side][source, 0, rows, :] = joined


VMEM_BYTES = 60 * 1024 * 1024


def params():
    return pltpu.CompilerParams(vmem_limit_bytes=VMEM_BYTES)


def cost(flops, moved, waves=0):
    return pl.CostEstimate(flops=flops, bytes_accessed=moved, transcendentals=waves)


def whole_spec(array):
    zeros = (0,) * array.ndim
    return pl.BlockSpec(array.shape, lambda i, *_: zeros)


HBM_SPEC = pl.BlockSpec(memory_space=pltpu.HBM)


def weight_scratch(number, features):
    return [
        pltpu.VMEM((number, features, features), jnp.bfloat16),
        pltpu.SemaphoreType.DMA((number,)),
    ]


def run_front(current, where, received, own, chunk, back_rows, rank_rows, weights, section, narrow):
    _, rows, features = current.shape
    count = where.shape[0]
    edge_spec = pl.BlockSpec((1, rows, features), lambda i, where: (i, 0, 0))
    row_spec = pl.BlockSpec((1, 1, rows), lambda i, where: (chunk * count + i, 0, 0))
    return pl.pallas_call(
        functools.partial(front_kernel, own, count, section),
        grid_spec=pltpu.PrefetchScalarGridSpec(
            num_scalar_prefetch=1,
            grid=(count,),
            in_specs=[
                pl.BlockSpec((1, rows, features), lambda i, where: (where[i], 0, 0)),
                row_spec,
                row_spec,
            ]
            + [HBM_SPEC] * 5
            + [whole_spec(array) for array in received],
            out_specs=[
                edge_spec,
                pl.BlockSpec((narrow, 1, rows // 2, LANES), lambda i, where: (0, i, 0, 0)),
            ],
            scratch_shapes=[pltpu.VMEM((rows, features), jnp.bfloat16)] + weight_scratch(5, features),
        ),
        out_shape=[
            jax.ShapeDtypeStruct((count, rows, features), jnp.bfloat16),
            jax.ShapeDtypeStruct((narrow, count, rows // 2, LANES), jnp.bfloat16),
        ],
        compiler_params=params(),
        cost_estimate=cost(12 * count * rows * features**2, 8 * count * rows * features),
        name="front",
    )(where, current, back_rows, rank_rows, *weights[:5], *received)


def run_back(second, packed, layout, chunk, rank_rows, weights, section, where, total, target):
    count, rows, features = second.shape
    edge_spec = pl.BlockSpec((1, rows, features), lambda i, where: (i, 0, 0))
    extra = [] if target is None else [target]
    return pl.pallas_call(
        functools.partial(back_kernel, layout, section),
        grid_spec=pltpu.PrefetchScalarGridSpec(
            num_scalar_prefetch=1,
            grid=(count,),
            in_specs=[
                edge_spec,
                pl.BlockSpec((1, 1, rows), lambda i, where: (chunk * count + i, 0, 0)),
            ]
            + [HBM_SPEC] * 3
            + [whole_spec(array) for array in packed]
            + [HBM_SPEC] * len(extra),
            out_specs=pl.BlockSpec((1, rows, features), lambda i, where: (where[i], 0, 0)),
            scratch_shapes=[pltpu.VMEM((rows, features), jnp.bfloat16)] + weight_scratch(3, features),
        ),
        out_shape=jax.ShapeDtypeStruct((total, rows, features), jnp.bfloat16),
        input_output_aliases={6 + len(packed): 0} if extra else {},
        compiler_params=params(),
        cost_estimate=cost(8 * count * rows * features**2, 6 * count * rows * features),
        name="back",
    )(where, second, rank_rows, *weights[5:], *packed, *extra)


def rank_spec(entries):
    return pl.BlockSpec((1,) + entries.shape[1:], lambda i, *_: (i, 0, 0, 0))


def run_tables(places, order, position, entries, angles):
    owners = entries.shape[0]
    atoms = angles.shape[1]
    groups = atoms // GROUP
    span = GROUP * SLOTS
    return pl.pallas_call(
        table_kernel,
        grid_spec=pltpu.PrefetchScalarGridSpec(
            num_scalar_prefetch=3,
            grid=(owners,),
            in_specs=[
                rank_spec(entries),
                pl.BlockSpec((1, atoms, angles.shape[2]), lambda i, places, *_: (places[i], 0, 0)),
            ],
            out_specs=[
                rank_spec(entries),
                pl.BlockSpec((1, groups, span, span), lambda i, *_: (i, 0, 0, 0)),
            ],
        ),
        out_shape=[
            jax.ShapeDtypeStruct(entries.shape, jnp.int32),
            jax.ShapeDtypeStruct((owners, groups, span, span), jnp.bfloat16),
        ],
        compiler_params=params(),
        cost_estimate=cost(0, 8 * owners * groups * span**2),
        name="tables",
    )(places, order, position, entries, angles)


def run_gather(owner_of, place_of, received, rank, chunk):
    devices, count, half, _ = received.shape
    rows = 2 * half
    smem = pl.BlockSpec(memory_space=pltpu.SMEM)
    return pl.pallas_call(
        functools.partial(gather_kernel, chunk),
        grid=(devices,),
        in_specs=[
            smem,
            smem,
            whole_spec(received),
            rank_spec(rank),
        ],
        out_specs=pl.BlockSpec((1, count, rows, LANES), lambda i: (i, 0, 0, 0)),
        out_shape=jax.ShapeDtypeStruct((devices, count, rows, LANES), jnp.bfloat16),
        scratch_shapes=[
            pltpu.VMEM((count, devices, devices, rows // devices, LANES), jnp.bfloat16)
        ],
        compiler_params=params(),
        cost_estimate=cost(4 * devices * count * rows**2 * LANES, 4 * devices * count * rows**2),
        name="gather",
    )(owner_of, place_of, received, rank)


def run_mix(owner_of, place_of, gathered, rank, blocks, chunk, apart):
    chunks = len(gathered)
    devices, count, rows, _ = gathered[0].shape
    half = rows // 2
    groups, span = blocks.shape[1:3]
    smem = pl.BlockSpec(memory_space=pltpu.SMEM)
    shapes = [(devices, 1, half, LANES)] * count if apart else [(devices, count, half, LANES)]
    shapes = [jax.ShapeDtypeStruct(shape, jnp.bfloat16) for shape in shapes]
    part_spec = pl.BlockSpec((1, count, rows, LANES), lambda i: (i, 0, 0, 0))
    return pl.pallas_call(
        functools.partial(mix_kernel, chunk, chunks),
        grid=(devices,),
        in_specs=[
            smem,
            smem,
            rank_spec(rank),
            HBM_SPEC,
        ]
        + [part_spec] * chunks,
        out_specs=[whole_spec(shape) for shape in shapes],
        out_shape=shapes,
        scratch_shapes=[
            pltpu.VMEM((count, devices, devices, rows // devices, LANES), jnp.bfloat16),
            pltpu.VMEM((devices, groups, span // chunks, span), jnp.bfloat16),
            pltpu.SemaphoreType.DMA((devices,)),
        ],
        compiler_params=params(),
        cost_estimate=cost(6 * devices * count * rows**2 * LANES, 6 * devices * count * rows**2),
        name="mix",
    )(owner_of, place_of, rank, blocks, *gathered)


def unit_tables(entries, capacity, unit):
    owners, sides, rows = entries.shape
    ids = jnp.arange(owners, dtype=jnp.int32)
    source = entries.reshape(owners, sides * rows) // capacity
    counts = jnp.sum((source[None] == ids[:, None, None]).astype(jnp.int32), axis=2) // (unit * sides)
    before = ids[:, None] < ids[None, :]
    starts = jnp.sum(jnp.where(before[None], counts[:, :, None], 0), axis=1)
    places = jnp.sum(jnp.where(before[:, :, None], counts[:, None, :], 0), axis=0)
    inside = (starts[:, :, None] <= ids) & (ids < (starts + counts)[:, :, None])
    owner_of = jnp.sum(jnp.where(inside, ids[None, :, None], 0), axis=1)
    place_of = jnp.sum(jnp.where(inside, (places - starts)[:, :, None] + ids, 0), axis=1)
    return owner_of, place_of


def ranks(values):
    return jnp.sum((values[:, :, None] < values[:, None, :]).astype(jnp.int32), axis=1)


CHUNKS = 2


def reorder(values, order):
    hits = order[:, None] == jnp.arange(values.shape[0], dtype=jnp.int32)
    return jnp.sum(jnp.where(hits[:, :, None], values[None], 0), axis=1)


def shift(values, offset, wide):
    if offset == 0:
        return values
    return lax.ppermute(values, "wide", [(i, i ^ offset) for i in range(wide)])


def swap(values):
    return lax.all_to_all(values, "narrow", 0, 0, tiled=True)


BASE = 64


def share_lists(listed, angles):
    narrow = lax.axis_size("narrow")
    atoms, width = angles.shape
    digits = jnp.stack([listed // BASE, listed % BASE]).reshape(atoms, -1).astype(jnp.bfloat16)
    shared = jnp.concatenate([angles, digits], axis=1)[None]
    held = [0]
    hop = narrow // 2
    while hop:
        other = lax.ppermute(shared, "narrow", [(i, i ^ hop) for i in range(narrow)])
        shared = jnp.concatenate([shared, other], axis=0)
        held += [offset ^ hop for offset in held]
        hop //= 2
    inverse = jnp.array([held.index(offset) for offset in range(narrow)], jnp.int32)
    mine = lax.axis_index("narrow").astype(jnp.int32)
    owners = jnp.arange(narrow, dtype=jnp.int32) ^ mine
    places = jnp.sum(jnp.where(owners[:, None] == jnp.arange(narrow), inverse, 0), axis=1)
    digits = shared[:, :, width:].reshape((narrow, 2) + listed.shape).astype(jnp.int32)
    entries = digits[:, 0] * BASE + digits[:, 1]
    entries = reorder(entries.reshape(narrow, -1), places).reshape(entries.shape)
    return entries, shared, places


def tiled_local(messages, reverse_position, route_slot, atom_slots, angles, weights):
    wide = lax.axis_size("wide")
    narrow = lax.axis_size("narrow")
    edge_rows, features = messages.shape
    rows = edge_rows // wide
    unit = rows // narrow
    capacity = 2 * edge_rows // narrow
    atoms = angles.shape[0]
    count = wide // CHUNKS
    spread_out = [offset for index in range(wide // 2) for offset in (index, wide - 1 - index)]
    offsets = [spread_out[chunk * count : (chunk + 1) * count] for chunk in range(CHUNKS)]
    group_id = lax.axis_index("wide").astype(jnp.int32)
    order = group_id ^ jnp.array(sum(offsets, []), jnp.int32)
    inverse = jnp.array([spread_out.index(offset) for offset in range(wide)], jnp.int32)
    owners_wide = (jnp.arange(wide, dtype=jnp.int32) ^ group_id)[:, None]
    position = jnp.sum(jnp.where(owners_wide == jnp.arange(wide), inverse, 0), axis=1)
    places = [order[chunk * count : (chunk + 1) * count] for chunk in range(CHUNKS)]
    plain = jnp.arange(count, dtype=jnp.int32)

    blocks_of = messages.reshape(wide, rows, features)
    received = [
        [
            shift(lax.dynamic_index_in_dim(blocks_of, group_id ^ offset, 0, False), offset, wide)
            for offset in offsets[chunk]
            if offset
        ]
        for chunk in range(CHUNKS)
    ]
    listed = atom_slots.reshape(atoms // GROUP, GROUP, wide, SLOTS // wide)
    listed = reorder(jnp.transpose(listed, (2, 0, 3, 1)).reshape(wide, rows), order)
    rank = ranks(route_slot.reshape(wide, rows))
    back_rows = reverse_position.reshape(wide, rows)
    back_rows = reorder(back_rows, order)
    rank = reorder(rank, order)
    partner_rank = jnp.stack(
        [shift(rank[place], offset, wide) for place, offset in enumerate(sum(offsets, []))]
    )
    hits = back_rows[:, :, None] == jnp.arange(rows, dtype=jnp.int32)
    turned_rank = jnp.sum(jnp.where(hits, partner_rank[:, None, :], 0), axis=2)[:, None, :]
    back_rows = back_rows[:, None, :]
    rank = rank[:, None, :]

    current = [blocks_of] * CHUNKS
    where = places
    chunk_order = list(range(CHUNKS))
    target = None
    tables = None
    for section in range(BLOCKS):
        last = section == BLOCKS - 1
        seconds, spreads = {}, {}
        for chunk in chunk_order:
            seconds[chunk], packed = run_front(
                current[chunk], where[chunk], received[chunk], offsets[chunk][0] == 0, chunk,
                back_rows, rank, weights, section, narrow,
            )
            if tables is None and chunk == chunk_order[0]:
                listed, packed = lax.optimization_barrier((listed, packed))
                entries, all_angles, owner_places = share_lists(listed, angles)
            spreads[chunk] = packed
        if tables is None:
            held = [spreads[chunk] for chunk in chunk_order]
            entries, all_angles, held[-1] = lax.optimization_barrier((entries, all_angles, held[-1]))
            spreads = dict(zip(chunk_order, held))
            owner_of, place_of = unit_tables(entries, capacity, unit)
            tables = run_tables(owner_places, order, position, entries[:, :, None, :], all_angles)
        listed_rank, blocks = tables
        gathered = [None] * CHUNKS
        for chunk in chunk_order:
            gathered[chunk] = run_gather(owner_of, place_of, swap(spreads[chunk]), listed_rank, chunk)
        chunk_order = list(range(CHUNKS))[::-1]
        returned = {}
        sent = None
        for chunk in chunk_order:
            early = chunk == 0
            mixed = list(run_mix(owner_of, place_of, gathered, listed_rank, blocks, chunk, early))
            if chunk != chunk_order[-1]:
                mixed[0], gathered[0] = lax.optimization_barrier((mixed[0], gathered[0]))
            if early:
                mixed = [shift(part, offset, wide) for part, offset in zip(mixed, offsets[chunk])]
                if sent is not None:
                    *sent, mixed[0] = lax.optimization_barrier((*sent, mixed[0]))
                    returned[chunk_order[0]] = (sent, returned[chunk_order[0]][1])
                parts = [swap(jnp.concatenate(mixed, axis=1))]
                layout = [(0, index) for index in range(count)]
            else:
                whole = swap(mixed[0])
                sent = [whole[:, index : index + 1] for index in range(count)]
                parts = sent
                layout = [(index, 0) for index in range(count)]
            returned[chunk] = (parts, layout)
        current = [None] * CHUNKS
        received = [None] * CHUNKS
        for chunk in chunk_order:
            parts, layout = returned[chunk]
            if chunk:
                parts = [shift(part, offset, wide) for part, offset in zip(parts, offsets[chunk])]
            result = run_back(
                seconds[chunk], parts, layout, chunk, turned_rank, weights, section,
                places[chunk] if last else plain, wide if last else count, target,
            )
            if last:
                target = result
            else:
                current[chunk] = result
                received[chunk] = [
                    shift(result[index], offset, wide)
                    for index, offset in enumerate(offsets[chunk])
                    if offset
                ]
        where = [plain] * CHUNKS
    return target.reshape(edge_rows, features)


def local(
    messages,
    reverse_position,
    route_slot,
    atom_slots,
    angles,
    weight_message,
    weight_reverse,
    weight_combine,
    weight_inner,
    weight_outer,
    weight_lift,
    weight_expand,
    weight_reduce,
):
    weights = (
        weight_message,
        weight_reverse,
        weight_combine,
        weight_inner,
        weight_outer,
        weight_lift,
        weight_expand,
        weight_reduce,
    )
    wide = lax.axis_size("wide")
    narrow = lax.axis_size("narrow")
    edge_rows, features = messages.shape
    unit = edge_rows // wide // narrow
    fits = (
        features == narrow * HALF
        and unit % 16 == 0
        and narrow % 2 == 0
        and wide % CHUNKS == 0
        and wide & (wide - 1) == 0
        and narrow & (narrow - 1) == 0
        and angles.shape[0] % GROUP == 0
        and (SLOTS // wide * GROUP) % 16 == 0
    )
    run = tiled_local if fits else general_local
    return run(messages, reverse_position, route_slot, atom_slots, angles, weights)


def solution(mesh):
    in_specs = (
        P(("wide", "narrow"), None),
        P(("wide", "narrow")),
        P(("wide", "narrow")),
        P(("wide", "narrow")),
        P(("wide", "narrow"), None),
        P(),
        P(),
        P(),
        P(),
        P(),
        P(),
        P(),
        P(),
    )
    out_specs = P(("wide", "narrow"), None)
    return jax.shard_map(local, mesh=mesh, in_specs=in_specs, out_specs=out_specs, check_vma=False)
```

```python
import functools

import jax
import jax.numpy as jnp
from jax import lax
from jax.experimental import pallas as pl
from jax.experimental.pallas import tpu as pltpu
from jax.sharding import PartitionSpec as P

SLOTS = 32
BLOCKS = 2
CHUNKS = 2
LANES = 128
HALF = LANES // 2
GROUP = 8


ROOT_HALF = 0.7071067811865476


def project(operand, weight):
    return jnp.dot(operand, weight, preferred_element_type=jnp.float32)


def residual(previous, branch):
    return ((previous.astype(jnp.float32) + branch) * ROOT_HALF).astype(jnp.bfloat16)


def reverse_edges(values, partner_rows):
    exchanged = lax.all_to_all(values, "wide", split_axis=0, concat_axis=0, tiled=True)
    return jnp.take(exchanged, partner_rows, axis=0)


def edge_front(current, reverse, weights, section_index):
    hidden = jax.nn.silu(
        project(current, weights[0][section_index]) + project(reverse, weights[1][section_index])
    ).astype(jnp.bfloat16)
    first_res = residual(current, project(hidden, weights[2][section_index]))
    inner_value = jax.nn.silu(project(first_res, weights[3][section_index])).astype(jnp.bfloat16)
    return residual(first_res, jax.nn.silu(project(inner_value, weights[4][section_index])))


def edge_back(second, turned, weights, section_index):
    third_res = residual(second, jax.nn.silu(project(turned, weights[5][section_index])))
    expand = jax.nn.silu(project(third_res, weights[6][section_index])).astype(jnp.bfloat16)
    return residual(third_res, jax.nn.silu(project(expand, weights[7][section_index])))


def owners_mix(second, route_slot, atom_slots, mixing):
    features = second.shape[1]
    buffer_rows = 2 * second.shape[0]
    outgoing = jnp.zeros((buffer_rows, features), jnp.bfloat16).at[route_slot].set(second)
    received = lax.all_to_all(outgoing, "narrow", split_axis=0, concat_axis=0, tiled=True)
    gathered = jnp.take(received, atom_slots, axis=0).reshape(mixing.shape[0], SLOTS, features)
    mixed_rows = jnp.einsum(
        "apq,aqd->apd", mixing, gathered, preferred_element_type=jnp.float32
    ).astype(jnp.bfloat16)
    return mixed_rows.reshape(-1, features)


def back_to_edges(mixed_flat, route_slot, atom_slots):
    features = mixed_flat.shape[1]
    buffer_rows = 2 * route_slot.shape[0]
    answer = jnp.zeros((buffer_rows, features), jnp.bfloat16).at[atom_slots].set(mixed_flat)
    incoming = lax.all_to_all(answer, "narrow", split_axis=0, concat_axis=0, tiled=True)
    return jnp.take(incoming, route_slot, axis=0)


def general_local(messages, reverse_position, route_slot, atom_slots, angles, weights):
    edge_rows = messages.shape[0]
    sub_rows = edge_rows // lax.axis_size("wide")
    partner_rows = jnp.arange(edge_rows, dtype=jnp.int32) // sub_rows * sub_rows + reverse_position
    mixing = angles.reshape(angles.shape[0], SLOTS, SLOTS)
    current = messages
    for section_index in range(BLOCKS):
        reverse = reverse_edges(current, partner_rows)
        second = edge_front(current, reverse, weights, section_index)
        mixed_flat = owners_mix(second, route_slot, atom_slots, mixing)
        returned = back_to_edges(mixed_flat, route_slot, atom_slots)
        turned = reverse_edges(returned, partner_rows)
        current = edge_back(second, turned, weights, section_index)
    return current


def silu(value):
    return 0.5 * value * (1.0 + jnp.tanh(0.5 * value))


def dot(left, right):
    return jnp.dot(left, right, preferred_element_type=jnp.float32)


def halve(previous, branch):
    return ((previous.astype(jnp.float32) + branch) * ROOT_HALF).astype(jnp.bfloat16)


def iotas(size):
    shape = (size, size)
    return lax.broadcasted_iota(jnp.int32, shape, 0), lax.broadcasted_iota(jnp.int32, shape, 1)


def as_column(row, rows_iota, lanes_iota):
    return jnp.sum(jnp.where(rows_iota == lanes_iota, row, 0), axis=1, keepdims=True)


def one_hot(mask):
    return jnp.where(mask, 1.0, 0.0).astype(jnp.bfloat16)


def fetcher(weight_refs, section, held, sems):
    first = pl.program_id(0) == 0
    copies = [
        pltpu.make_async_copy(ref.at[section], held.at[index], sems.at[index])
        for index, ref in enumerate(weight_refs)
    ]

    @pl.when(first)
    def _():
        for copy in copies:
            copy.start()

    def weight(index):
        @pl.when(first)
        def _():
            copies[index].wait()

        return held[index]

    return weight


def front_kernel(own, count, section, where_ref, cur_ref, back_ref, rank_ref, *refs):
    weight_refs, refs = refs[:5], refs[5:]
    if section is None:
        recv_refs, (second_ref, packed_ref, reverse_ref) = refs[:-3], refs[-3:]

        def weight(index):
            return weight_refs[index][0]

    else:
        recv_refs, (second_ref, packed_ref, reverse_ref, held, sems) = refs[:-5], refs[-5:]
        weight = fetcher(weight_refs, section, held, sems)
    rows_iota, lanes_iota = iotas(cur_ref.shape[1])
    partner = as_column(back_ref[0], rows_iota, lanes_iota)
    hot = one_hot(partner == lanes_iota)
    sources = ([cur_ref.at[0]] if own else []) + list(recv_refs)
    for index in range(count):

        @pl.when(pl.program_id(0) == index)
        def _():
            reverse_ref[...] = dot(hot, sources[index][...]).astype(jnp.bfloat16)

    current = cur_ref[0]
    own_part = dot(current, weight(0))
    hidden = silu(own_part + dot(reverse_ref[...], weight(1))).astype(jnp.bfloat16)
    first_res = halve(current, dot(hidden, weight(2)))
    inner = silu(dot(first_res, weight(3))).astype(jnp.bfloat16)
    second = halve(first_res, silu(dot(inner, weight(4))))
    second_ref[0] = second
    ordered = dot(one_hot(rows_iota == rank_ref[0]), second)
    half = ordered.shape[0] // 2
    low = lax.broadcasted_iota(jnp.int32, (half, LANES), 1) < HALF
    for tile in range(ordered.shape[1] // LANES):
        top = ordered[:half, tile * LANES : (tile + 1) * LANES]
        bottom = ordered[half:, tile * LANES : (tile + 1) * LANES]
        packed_ref[2 * tile, 0] = jnp.where(low, top, pltpu.roll(bottom, HALF, 1)).astype(jnp.bfloat16)
        packed_ref[2 * tile + 1, 0] = jnp.where(low, pltpu.roll(top, HALF, 1), bottom).astype(jnp.bfloat16)


def back_kernel(layout, where_ref, second_ref, rank_ref, wl, we, wd, *refs):
    out_ref, ordered_ref = refs[-2:]
    rows_iota, lanes_iota = iotas(second_ref.shape[1])
    half = rows_iota.shape[0] // 2
    low = lax.broadcasted_iota(jnp.int32, (half, LANES), 1) < HALF
    for index, (array, side) in enumerate(layout):

        @pl.when(pl.program_id(0) == index)
        def _():
            for tile in range(second_ref.shape[2] // LANES):
                lanes = slice(tile * LANES, (tile + 1) * LANES)
                even = refs[array][2 * tile, side].astype(jnp.float32)
                odd = refs[array][2 * tile + 1, side].astype(jnp.float32)
                top = jnp.where(low, even, pltpu.roll(odd, HALF, 1))
                bottom = jnp.where(low, pltpu.roll(even, HALF, 1), odd)
                ordered_ref[:half, lanes] = top.astype(jnp.bfloat16)
                ordered_ref[half:, lanes] = bottom.astype(jnp.bfloat16)

    source = as_column(rank_ref[0], rows_iota, lanes_iota)
    turned = dot(one_hot(source == lanes_iota), ordered_ref[...]).astype(jnp.bfloat16)
    third_res = halve(second_ref[0], silu(dot(turned, wl[0])))
    expand = silu(dot(third_res, we[0])).astype(jnp.bfloat16)
    out_ref[0] = halve(third_res, silu(dot(expand, wd[0])))


def table_kernel(places_ref, order_ref, position_ref, entry_ref, angles_ref, rank_ref, *refs):
    block_refs, whole_ref = refs[:-1], refs[-1]
    sides, _, size = entry_ref.shape[1:]
    rows_iota, lanes_iota = iotas(size)
    for side in range(sides):
        row = entry_ref[0, side]
        column = as_column(row, rows_iota, lanes_iota)
        rank_ref[0, side] = jnp.sum(jnp.where(column < row, 1, 0), axis=0, keepdims=True)
    span = GROUP * SLOTS
    strip = span // sides
    rows_iota, lanes_iota = iotas(span)
    own = rows_iota % GROUP == lanes_iota % GROUP
    spread_rows = lax.broadcasted_iota(jnp.int32, (SLOTS, span), 0)
    spread_lanes = lax.broadcasted_iota(jnp.int32, (SLOTS, span), 1)
    side_at = jnp.zeros((SLOTS, span), jnp.int32)
    for place in range(sides):
        side_at = jnp.where(spread_lanes // strip == place, order_ref[place], side_at)
    spread = one_hot(side_at * (SLOTS // sides) + spread_lanes % strip // GROUP == spread_rows)
    for group in range(angles_ref.shape[1] // GROUP):
        local = angles_ref[0, group * GROUP : (group + 1) * GROUP, :].astype(jnp.float32)
        stacked = jnp.concatenate(
            [local[:, p * SLOTS : (p + 1) * SLOTS] for p in range(SLOTS)], axis=0
        ).astype(jnp.bfloat16)
        block = jnp.where(own, dot(stacked, spread), 0.0).astype(jnp.bfloat16)
        for side in range(sides):
            to = pl.multiple_of(position_ref[side] * strip, strip)
            whole_ref[pl.ds(to, strip), :] = block[side * strip : (side + 1) * strip]
        part = span // len(block_refs)
        for chunk, block_ref in enumerate(block_refs):
            block_ref[0, group] = whole_ref[chunk * part : (chunk + 1) * part, :]


def gather_kernel(chunk, owner_ref, place_ref, recv_ref, rank_ref, out_ref, ins):
    step = pl.program_id(0)
    sides = recv_ref.shape[1]
    devices = recv_ref.shape[0]
    unit = ins.shape[3]
    pairs = devices // 2

    @pl.when(step == 0)
    def _():
        @pl.loop(0, devices)
        def _(source):
            for index in range(devices):
                owner = owner_ref[source, index]
                place = place_ref[source, index]
                at = (index % pairs) * unit
                for side in range(sides):
                    block = recv_ref[source, side, at : at + unit, :]
                    if index >= pairs:
                        block = pltpu.roll(block.astype(jnp.float32), HALF, 1).astype(jnp.bfloat16)
                    ins[side, owner, place] = block

    rows_iota, lanes_iota = iotas(devices * unit)
    for side in range(sides):
        operand = ins[side, step].reshape(devices * unit, LANES)
        source = as_column(rank_ref[0, chunk * sides + side], rows_iota, lanes_iota)
        out_ref[0, side] = dot(one_hot(source == lanes_iota), operand).astype(jnp.bfloat16)


def mix_kernel(chunk, chunks, owner_ref, place_ref, rank_ref, blocks_ref, *refs):
    gathered_refs, out_refs, outs = refs[:chunks], refs[chunks:-1], refs[-1]
    step = pl.program_id(0)
    count = outs.shape[0]
    devices = outs.shape[1]
    unit = outs.shape[3]
    groups = blocks_ref.shape[1]
    strip = blocks_ref.shape[2] // count
    pairs = devices // 2
    rows_iota = iotas(devices * unit)[0]
    mixed = []
    for group in range(groups):
        operand = jnp.concatenate(
            [
                ref[0, index, group * strip : (group + 1) * strip, :]
                for ref in gathered_refs
                for index in range(count)
            ],
            axis=0,
        )
        mixed.append(dot(blocks_ref[0, group], operand).astype(jnp.bfloat16))
    for side in range(count):
        operand = jnp.concatenate(
            [rows[side * strip : (side + 1) * strip] for rows in mixed], axis=0
        )
        outs[side, step] = (
            dot(one_hot(rows_iota == rank_ref[0, chunk * count + side]), operand)
            .astype(jnp.bfloat16)
            .reshape(devices, unit, LANES)
        )

    @pl.when(step == pl.num_programs(0) - 1)
    def _():
        low = lax.broadcasted_iota(jnp.int32, (unit, LANES), 1) < HALF

        @pl.loop(0, devices)
        def _(source):
            for index in range(pairs):
                owner = owner_ref[source, index]
                place = place_ref[source, index]
                owner_far = owner_ref[source, index + pairs]
                place_far = place_ref[source, index + pairs]
                rows = slice(index * unit, (index + 1) * unit)
                for side in range(count):
                    near = outs[side, owner, place].astype(jnp.float32)
                    far = outs[side, owner_far, place_far].astype(jnp.float32)
                    joined = jnp.where(low, near, pltpu.roll(far, HALF, 1)).astype(jnp.bfloat16)
                    if len(out_refs) == 1:
                        out_refs[0][source, side, rows, :] = joined
                    else:
                        out_refs[side][source, 0, rows, :] = joined


VMEM_BYTES = 20 * 1024 * 1024


def params():
    return pltpu.CompilerParams(vmem_limit_bytes=VMEM_BYTES)


def whole_spec(array):
    zeros = (0,) * array.ndim
    return pl.BlockSpec(array.shape, lambda i, *_: zeros)


HBM_SPEC = pl.BlockSpec(memory_space=pltpu.HBM)


def weight_spec(section, features):
    return pl.BlockSpec((1, features, features), lambda i, *_: (section, 0, 0))


def weight_scratch(number, features):
    return [
        pltpu.VMEM((number, features, features), jnp.bfloat16),
        pltpu.SemaphoreType.DMA((number,)),
    ]


def run_front(current, where, received, own, chunk, back_rows, rank_rows, weights, section, narrow):
    _, rows, features = current.shape
    count = where.shape[0]
    edge_spec = pl.BlockSpec((1, rows, features), lambda i, where: (i, 0, 0))
    row_spec = pl.BlockSpec((1, 1, rows), lambda i, where: (chunk * count + i, 0, 0))
    return pl.pallas_call(
        functools.partial(front_kernel, own, count, None if section else section),
        grid_spec=pltpu.PrefetchScalarGridSpec(
            num_scalar_prefetch=1,
            grid=(count,),
            in_specs=[
                pl.BlockSpec((1, rows, features), lambda i, where: (where[i], 0, 0)),
                row_spec,
                row_spec,
            ]
            + ([weight_spec(section, features)] if section else [HBM_SPEC]) * 5
            + [whole_spec(array) for array in received],
            out_specs=[
                edge_spec,
                pl.BlockSpec((narrow, 1, rows // 2, LANES), lambda i, where: (0, i, 0, 0)),
            ],
            scratch_shapes=[pltpu.VMEM((rows, features), jnp.bfloat16)]
            + ([] if section else weight_scratch(5, features)),
        ),
        out_shape=[
            jax.ShapeDtypeStruct((count, rows, features), jnp.bfloat16),
            jax.ShapeDtypeStruct((narrow, count, rows // 2, LANES), jnp.bfloat16),
        ],
        compiler_params=params(),
        cost_estimate=pl.CostEstimate(flops=1, bytes_accessed=1, transcendentals=0),
        name="front",
    )(where, current, back_rows, rank_rows, *weights[:5], *received)


def run_back(second, packed, layout, chunk, rank_rows, weights, section, where, total, target):
    count, rows, features = second.shape
    edge_spec = pl.BlockSpec((1, rows, features), lambda i, where: (i, 0, 0))
    extra = [] if target is None else [target]
    return pl.pallas_call(
        functools.partial(back_kernel, layout),
        grid_spec=pltpu.PrefetchScalarGridSpec(
            num_scalar_prefetch=1,
            grid=(count,),
            in_specs=[
                edge_spec,
                pl.BlockSpec((1, 1, rows), lambda i, where: (chunk * count + i, 0, 0)),
            ]
            + [weight_spec(section, features)] * 3
            + [whole_spec(array) for array in packed]
            + [HBM_SPEC] * len(extra),
            out_specs=pl.BlockSpec((1, rows, features), lambda i, where: (where[i], 0, 0)),
            scratch_shapes=[pltpu.VMEM((rows, features), jnp.bfloat16)],
        ),
        out_shape=jax.ShapeDtypeStruct((total, rows, features), jnp.bfloat16),
        input_output_aliases={6 + len(packed): 0} if extra else {},
        compiler_params=params(),
        cost_estimate=pl.CostEstimate(flops=1, bytes_accessed=1, transcendentals=0),
        name="back",
    )(where, second, rank_rows, *weights[5:], *packed, *extra)


def rank_spec(entries):
    return pl.BlockSpec((1,) + entries.shape[1:], lambda i, *_: (i, 0, 0, 0))


def run_tables(places, order, position, entries, angles):
    owners = entries.shape[0]
    atoms = angles.shape[1]
    groups = atoms // GROUP
    span = GROUP * SLOTS
    return pl.pallas_call(
        table_kernel,
        grid_spec=pltpu.PrefetchScalarGridSpec(
            num_scalar_prefetch=3,
            grid=(owners,),
            in_specs=[
                rank_spec(entries),
                pl.BlockSpec((1, atoms, angles.shape[2]), lambda i, places, *_: (places[i], 0, 0)),
            ],
            out_specs=[
                rank_spec(entries),
            ]
            + [pl.BlockSpec((1, groups, span // CHUNKS, span), lambda i, *_: (i, 0, 0, 0))] * CHUNKS,
            scratch_shapes=[pltpu.VMEM((span, span), jnp.bfloat16)],
        ),
        out_shape=[
            jax.ShapeDtypeStruct(entries.shape, jnp.int32),
        ]
        + [jax.ShapeDtypeStruct((owners, groups, span // CHUNKS, span), jnp.bfloat16)] * CHUNKS,
        compiler_params=params(),
        cost_estimate=pl.CostEstimate(flops=1, bytes_accessed=1, transcendentals=0),
        name="tables",
    )(places, order, position, entries, angles)


def run_gather(owner_of, place_of, received, rank, chunk):
    devices, count, half, _ = received.shape
    rows = 2 * half
    smem = pl.BlockSpec(memory_space=pltpu.SMEM)
    return pl.pallas_call(
        functools.partial(gather_kernel, chunk),
        grid=(devices,),
        in_specs=[
            smem,
            smem,
            whole_spec(received),
            rank_spec(rank),
        ],
        out_specs=pl.BlockSpec((1, count, rows, LANES), lambda i: (i, 0, 0, 0)),
        out_shape=jax.ShapeDtypeStruct((devices, count, rows, LANES), jnp.bfloat16),
        scratch_shapes=[
            pltpu.VMEM((count, devices, devices, rows // devices, LANES), jnp.bfloat16)
        ],
        compiler_params=params(),
        cost_estimate=pl.CostEstimate(flops=1, bytes_accessed=1, transcendentals=0),
        name="gather",
    )(owner_of, place_of, received, rank)


def run_mix(owner_of, place_of, gathered, rank, blocks, chunk, apart):
    chunks = len(gathered)
    devices, count, rows, _ = gathered[0].shape
    half = rows // 2
    groups, part, span = blocks.shape[1:]
    smem = pl.BlockSpec(memory_space=pltpu.SMEM)
    shapes = [(devices, 1, half, LANES)] * count if apart else [(devices, count, half, LANES)]
    shapes = [jax.ShapeDtypeStruct(shape, jnp.bfloat16) for shape in shapes]
    part_spec = pl.BlockSpec((1, count, rows, LANES), lambda i: (i, 0, 0, 0))
    return pl.pallas_call(
        functools.partial(mix_kernel, chunk, chunks),
        grid=(devices,),
        in_specs=[
            smem,
            smem,
            rank_spec(rank),
            pl.BlockSpec((1, groups, part, span), lambda i: (i, 0, 0, 0)),
        ]
        + [part_spec] * chunks,
        out_specs=[whole_spec(shape) for shape in shapes],
        out_shape=shapes,
        scratch_shapes=[
            pltpu.VMEM((count, devices, devices, rows // devices, LANES), jnp.bfloat16),
        ],
        compiler_params=params(),
        cost_estimate=pl.CostEstimate(flops=1, bytes_accessed=1, transcendentals=0),
        name="mix",
    )(owner_of, place_of, rank, blocks, *gathered)


def unit_tables(entries, capacity, unit):
    owners, sides, rows = entries.shape
    ids = jnp.arange(owners, dtype=jnp.int32)
    source = entries.reshape(owners, sides * rows) // capacity
    counts = jnp.sum((source[None] == ids[:, None, None]).astype(jnp.int32), axis=2) // (unit * sides)
    before = ids[:, None] < ids[None, :]
    starts = jnp.sum(jnp.where(before[None], counts[:, :, None], 0), axis=1)
    places = jnp.sum(jnp.where(before[:, :, None], counts[:, None, :], 0), axis=0)
    inside = (starts[:, :, None] <= ids) & (ids < (starts + counts)[:, :, None])
    owner_of = jnp.sum(jnp.where(inside, ids[None, :, None], 0), axis=1)
    place_of = jnp.sum(jnp.where(inside, (places - starts)[:, :, None] + ids, 0), axis=1)
    return owner_of, place_of


def ranks(values):
    return jnp.sum((values[:, :, None] < values[:, None, :]).astype(jnp.int32), axis=1)


def reorder(values, order):
    hits = order[:, None] == jnp.arange(values.shape[0], dtype=jnp.int32)
    return jnp.sum(jnp.where(hits[:, :, None], values[None], 0), axis=1)


def shift(values, offset, wide):
    if offset == 0:
        return values
    return lax.ppermute(values, "wide", [(i, i ^ offset) for i in range(wide)])


def swap(values):
    return lax.all_to_all(values, "narrow", 0, 0, tiled=True)


BASE = 64


def share_lists(listed, angles):
    narrow = lax.axis_size("narrow")
    atoms, width = angles.shape
    digits = jnp.stack([listed // BASE, listed % BASE]).reshape(atoms, -1).astype(jnp.bfloat16)
    shared = jnp.concatenate([angles, digits], axis=1)[None]
    held = [0]
    hop = narrow // 2
    while hop:
        other = lax.ppermute(shared, "narrow", [(i, i ^ hop) for i in range(narrow)])
        shared = jnp.concatenate([shared, other], axis=0)
        held += [offset ^ hop for offset in held]
        hop //= 2
    inverse = jnp.array([held.index(offset) for offset in range(narrow)], jnp.int32)
    mine = lax.axis_index("narrow").astype(jnp.int32)
    owners = jnp.arange(narrow, dtype=jnp.int32) ^ mine
    places = jnp.sum(jnp.where(owners[:, None] == jnp.arange(narrow), inverse, 0), axis=1)
    digits = shared[:, :, width:].reshape((narrow, 2) + listed.shape).astype(jnp.int32)
    entries = digits[:, 0] * BASE + digits[:, 1]
    entries = reorder(entries.reshape(narrow, -1), places).reshape(entries.shape)
    return entries, shared, places


def tiled_local(messages, reverse_position, route_slot, atom_slots, angles, weights):
    wide = lax.axis_size("wide")
    narrow = lax.axis_size("narrow")
    edge_rows, features = messages.shape
    rows = edge_rows // wide
    unit = rows // narrow
    capacity = 2 * edge_rows // narrow
    atoms = angles.shape[0]
    count = wide // CHUNKS
    spread_out = [offset for index in range(wide // 2) for offset in (index, wide - 1 - index)]
    offsets = [spread_out[chunk * count : (chunk + 1) * count] for chunk in range(CHUNKS)]
    group_id = lax.axis_index("wide").astype(jnp.int32)
    order = group_id ^ jnp.array(sum(offsets, []), jnp.int32)
    inverse = jnp.array([spread_out.index(offset) for offset in range(wide)], jnp.int32)
    owners_wide = (jnp.arange(wide, dtype=jnp.int32) ^ group_id)[:, None]
    position = jnp.sum(jnp.where(owners_wide == jnp.arange(wide), inverse, 0), axis=1)
    places = [order[chunk * count : (chunk + 1) * count] for chunk in range(CHUNKS)]
    plain = jnp.arange(count, dtype=jnp.int32)

    blocks_of = messages.reshape(wide, rows, features)
    received = [
        [
            shift(lax.dynamic_index_in_dim(blocks_of, group_id ^ offset, 0, False), offset, wide)
            for offset in offsets[chunk]
            if offset
        ]
        for chunk in range(CHUNKS)
    ]
    listed = atom_slots.reshape(atoms // GROUP, GROUP, wide, SLOTS // wide)
    listed = reorder(jnp.transpose(listed, (2, 0, 3, 1)).reshape(wide, rows), order)
    rank = ranks(route_slot.reshape(wide, rows))
    back_rows = reverse_position.reshape(wide, rows)
    back_rows = reorder(back_rows, order)
    rank = reorder(rank, order)
    partner_rank = jnp.stack(
        [shift(rank[place], offset, wide) for place, offset in enumerate(sum(offsets, []))]
    )
    hits = back_rows[:, :, None] == jnp.arange(rows, dtype=jnp.int32)
    turned_rank = jnp.sum(jnp.where(hits, partner_rank[:, None, :], 0), axis=2)[:, None, :]
    back_rows = back_rows[:, None, :]
    rank = rank[:, None, :]

    current = [blocks_of] * CHUNKS
    where = places
    chunk_order = list(range(CHUNKS))
    target = None
    tables = None
    for section in range(BLOCKS):
        last = section == BLOCKS - 1
        seconds, spreads = {}, {}
        for chunk in chunk_order:
            seconds[chunk], packed = run_front(
                current[chunk], where[chunk], received[chunk], offsets[chunk][0] == 0, chunk,
                back_rows, rank, weights, section, narrow,
            )
            if tables is None and chunk == chunk_order[0]:
                listed, packed = lax.optimization_barrier((listed, packed))
                entries, all_angles, owner_places = share_lists(listed, angles)
            spreads[chunk] = packed
        if tables is None:
            held = [spreads[chunk] for chunk in chunk_order]
            entries, all_angles, held[-1] = lax.optimization_barrier((entries, all_angles, held[-1]))
            spreads = dict(zip(chunk_order, held))
            owner_of, place_of = unit_tables(entries, capacity, unit)
            tables = run_tables(owner_places, order, position, entries[:, :, None, :], all_angles)
        listed_rank, *blocks = tables
        gathered = [None] * CHUNKS
        for chunk in chunk_order:
            gathered[chunk] = run_gather(owner_of, place_of, swap(spreads[chunk]), listed_rank, chunk)
        chunk_order = list(range(CHUNKS))[::-1]
        returned = {}
        sent = None
        for chunk in chunk_order:
            early = last and chunk == 0
            mixed = list(run_mix(owner_of, place_of, gathered, listed_rank, blocks[chunk], chunk, early))
            if chunk != chunk_order[-1]:
                mixed[0], gathered[0] = lax.optimization_barrier((mixed[0], gathered[0]))
            if early:
                mixed = [shift(part, offset, wide) for part, offset in zip(mixed, offsets[chunk])]
                if sent is not None:
                    *sent, mixed[0] = lax.optimization_barrier((*sent, mixed[0]))
                    returned[chunk_order[0]] = (sent, returned[chunk_order[0]][1])
                parts = [swap(jnp.concatenate(mixed, axis=1))]
                layout = [(0, index) for index in range(count)]
            else:
                if sent is not None:
                    *sent, mixed[0] = lax.optimization_barrier((*sent, mixed[0]))
                    returned[chunk_order[0]] = (sent, returned[chunk_order[0]][1])
                whole = swap(mixed[0])
                sent = [whole[:, index : index + 1] for index in range(count)]
                parts = sent
                layout = [(index, 0) for index in range(count)]
            returned[chunk] = (parts, layout)
        current = [None] * CHUNKS
        received = [None] * CHUNKS
        for chunk in chunk_order:
            parts, layout = returned[chunk]
            if chunk or not last:
                parts = [shift(part, offset, wide) for part, offset in zip(parts, offsets[chunk])]
            result = run_back(
                seconds[chunk], parts, layout, chunk, turned_rank, weights, section,
                places[chunk] if last else plain, wide if last else count, target,
            )
            if last:
                target = result
            else:
                current[chunk] = result
                received[chunk] = [
                    shift(result[index], offset, wide)
                    for index, offset in enumerate(offsets[chunk])
                    if offset
                ]
        if not last:
            head, tail = chunk_order[0], chunk_order[-1]
            received[head][0], current[tail] = lax.optimization_barrier((received[head][0], current[tail]))
        where = [plain] * CHUNKS
    return target.reshape(edge_rows, features)


def local(
    messages,
    reverse_position,
    route_slot,
    atom_slots,
    angles,
    weight_message,
    weight_reverse,
    weight_combine,
    weight_inner,
    weight_outer,
    weight_lift,
    weight_expand,
    weight_reduce,
):
    weights = (
        weight_message,
        weight_reverse,
        weight_combine,
        weight_inner,
        weight_outer,
        weight_lift,
        weight_expand,
        weight_reduce,
    )
    wide = lax.axis_size("wide")
    narrow = lax.axis_size("narrow")
    edge_rows, features = messages.shape
    unit = edge_rows // wide // narrow
    fits = (
        features == narrow * HALF
        and unit % 16 == 0
        and narrow % 2 == 0
        and wide % CHUNKS == 0
        and wide & (wide - 1) == 0
        and narrow & (narrow - 1) == 0
        and angles.shape[0] % GROUP == 0
        and (SLOTS // wide * GROUP) % 16 == 0
    )
    run = tiled_local if fits else general_local
    return run(messages, reverse_position, route_slot, atom_slots, angles, weights)


def solution(mesh):
    in_specs = (
        P(("wide", "narrow"), None),
        P(("wide", "narrow")),
        P(("wide", "narrow")),
        P(("wide", "narrow")),
        P(("wide", "narrow"), None),
        P(),
        P(),
        P(),
        P(),
        P(),
        P(),
        P(),
        P(),
    )
    out_specs = P(("wide", "narrow"), None)
    return jax.shard_map(local, mesh=mesh, in_specs=in_specs, out_specs=out_specs, check_vma=False)
```

```python
import functools

import jax
import jax.numpy as jnp
from jax import lax
from jax.experimental import pallas as pl
from jax.experimental.pallas import tpu as pltpu
from jax.sharding import PartitionSpec as P

SLOTS = 32
BLOCKS = 2
CHUNKS = 2
LANES = 128
HALF = LANES // 2
GROUP = 8


ROOT_HALF = 0.7071067811865476


def project(operand, weight):
    return jnp.dot(operand, weight, preferred_element_type=jnp.float32)


def residual(previous, branch):
    return ((previous.astype(jnp.float32) + branch) * ROOT_HALF).astype(jnp.bfloat16)


def reverse_edges(values, partner_rows):
    exchanged = lax.all_to_all(values, "wide", split_axis=0, concat_axis=0, tiled=True)
    return jnp.take(exchanged, partner_rows, axis=0)


def edge_front(current, reverse, weights, section_index):
    hidden = jax.nn.silu(
        project(current, weights[0][section_index]) + project(reverse, weights[1][section_index])
    ).astype(jnp.bfloat16)
    first_res = residual(current, project(hidden, weights[2][section_index]))
    inner_value = jax.nn.silu(project(first_res, weights[3][section_index])).astype(jnp.bfloat16)
    return residual(first_res, jax.nn.silu(project(inner_value, weights[4][section_index])))


def edge_back(second, turned, weights, section_index):
    third_res = residual(second, jax.nn.silu(project(turned, weights[5][section_index])))
    expand = jax.nn.silu(project(third_res, weights[6][section_index])).astype(jnp.bfloat16)
    return residual(third_res, jax.nn.silu(project(expand, weights[7][section_index])))


def owners_mix(second, route_slot, atom_slots, mixing):
    features = second.shape[1]
    buffer_rows = 2 * second.shape[0]
    outgoing = jnp.zeros((buffer_rows, features), jnp.bfloat16).at[route_slot].set(second)
    received = lax.all_to_all(outgoing, "narrow", split_axis=0, concat_axis=0, tiled=True)
    gathered = jnp.take(received, atom_slots, axis=0).reshape(mixing.shape[0], SLOTS, features)
    mixed_rows = jnp.einsum(
        "apq,aqd->apd", mixing, gathered, preferred_element_type=jnp.float32
    ).astype(jnp.bfloat16)
    return mixed_rows.reshape(-1, features)


def back_to_edges(mixed_flat, route_slot, atom_slots):
    features = mixed_flat.shape[1]
    buffer_rows = 2 * route_slot.shape[0]
    answer = jnp.zeros((buffer_rows, features), jnp.bfloat16).at[atom_slots].set(mixed_flat)
    incoming = lax.all_to_all(answer, "narrow", split_axis=0, concat_axis=0, tiled=True)
    return jnp.take(incoming, route_slot, axis=0)


def general_local(messages, reverse_position, route_slot, atom_slots, angles, weights):
    edge_rows = messages.shape[0]
    sub_rows = edge_rows // lax.axis_size("wide")
    partner_rows = jnp.arange(edge_rows, dtype=jnp.int32) // sub_rows * sub_rows + reverse_position
    mixing = angles.reshape(angles.shape[0], SLOTS, SLOTS)
    current = messages
    for section_index in range(BLOCKS):
        reverse = reverse_edges(current, partner_rows)
        second = edge_front(current, reverse, weights, section_index)
        mixed_flat = owners_mix(second, route_slot, atom_slots, mixing)
        returned = back_to_edges(mixed_flat, route_slot, atom_slots)
        turned = reverse_edges(returned, partner_rows)
        current = edge_back(second, turned, weights, section_index)
    return current


def silu(value):
    return 0.5 * value * (1.0 + jnp.tanh(0.5 * value))


def dot(left, right):
    return jnp.dot(left, right, preferred_element_type=jnp.float32)


def halve(previous, branch):
    return ((previous.astype(jnp.float32) + branch) * ROOT_HALF).astype(jnp.bfloat16)


def iotas(size):
    shape = (size, size)
    return lax.broadcasted_iota(jnp.int32, shape, 0), lax.broadcasted_iota(jnp.int32, shape, 1)


def as_column(row, rows_iota, lanes_iota):
    return jnp.sum(jnp.where(rows_iota == lanes_iota, row, 0), axis=1, keepdims=True)


def one_hot(mask):
    return jnp.where(mask, 1.0, 0.0).astype(jnp.bfloat16)


def fetcher(weight_refs, section, held, sems):
    first = pl.program_id(0) == 0
    copies = [
        pltpu.make_async_copy(ref.at[section], held.at[index], sems.at[index])
        for index, ref in enumerate(weight_refs)
    ]

    @pl.when(first)
    def _():
        for copy in copies:
            copy.start()

    def weight(index):
        @pl.when(first)
        def _():
            copies[index].wait()

        return held[index]

    return weight


def front_kernel(own, count, section, where_ref, cur_ref, back_ref, rank_ref, *refs):
    weight_refs, refs = refs[:5], refs[5:]
    recv_refs, (second_ref, packed_ref, reverse_ref, held, sems) = refs[:-5], refs[-5:]
    weight = fetcher(weight_refs, section, held, sems)
    rows_iota, lanes_iota = iotas(cur_ref.shape[1])
    partner = as_column(back_ref[0], rows_iota, lanes_iota)
    hot = one_hot(partner == lanes_iota)
    sources = ([cur_ref.at[0]] if own else []) + list(recv_refs)
    for index in range(count):

        @pl.when(pl.program_id(0) == index)
        def _():
            reverse_ref[...] = dot(hot, sources[index][...]).astype(jnp.bfloat16)

    current = cur_ref[0]
    own_part = dot(current, weight(0))
    hidden = silu(own_part + dot(reverse_ref[...], weight(1))).astype(jnp.bfloat16)
    first_res = halve(current, dot(hidden, weight(2)))
    inner = silu(dot(first_res, weight(3))).astype(jnp.bfloat16)
    second = halve(first_res, silu(dot(inner, weight(4))))
    second_ref[0] = second
    ordered = dot(one_hot(rows_iota == rank_ref[0]), second)
    half = ordered.shape[0] // 2
    low = lax.broadcasted_iota(jnp.int32, (half, LANES), 1) < HALF
    for tile in range(ordered.shape[1] // LANES):
        top = ordered[:half, tile * LANES : (tile + 1) * LANES]
        bottom = ordered[half:, tile * LANES : (tile + 1) * LANES]
        packed_ref[2 * tile, 0] = jnp.where(low, top, pltpu.roll(bottom, HALF, 1)).astype(jnp.bfloat16)
        packed_ref[2 * tile + 1, 0] = jnp.where(low, pltpu.roll(top, HALF, 1), bottom).astype(jnp.bfloat16)


def back_kernel(layout, section, where_ref, second_ref, rank_ref, *refs):
    weight_refs, refs = refs[:3], refs[3:]
    out_ref, ordered_ref, held, sems = refs[-4:]
    weight = fetcher(weight_refs, section, held, sems)
    rows_iota, lanes_iota = iotas(second_ref.shape[1])
    half = rows_iota.shape[0] // 2
    low = lax.broadcasted_iota(jnp.int32, (half, LANES), 1) < HALF
    for index, (array, side) in enumerate(layout):

        @pl.when(pl.program_id(0) == index)
        def _():
            for tile in range(second_ref.shape[2] // LANES):
                lanes = slice(tile * LANES, (tile + 1) * LANES)
                even = refs[array][2 * tile, side].astype(jnp.float32)
                odd = refs[array][2 * tile + 1, side].astype(jnp.float32)
                top = jnp.where(low, even, pltpu.roll(odd, HALF, 1))
                bottom = jnp.where(low, pltpu.roll(even, HALF, 1), odd)
                ordered_ref[:half, lanes] = top.astype(jnp.bfloat16)
                ordered_ref[half:, lanes] = bottom.astype(jnp.bfloat16)

    source = as_column(rank_ref[0], rows_iota, lanes_iota)
    turned = dot(one_hot(source == lanes_iota), ordered_ref[...]).astype(jnp.bfloat16)
    third_res = halve(second_ref[0], silu(dot(turned, weight(0))))
    expand = silu(dot(third_res, weight(1))).astype(jnp.bfloat16)
    out_ref[0] = halve(third_res, silu(dot(expand, weight(2))))


def table_kernel(places_ref, order_ref, position_ref, entry_ref, angles_ref, rank_ref, *refs):
    block_refs, whole_ref = refs[:-1], refs[-1]
    sides, _, size = entry_ref.shape[1:]
    rows_iota, lanes_iota = iotas(size)
    for side in range(sides):
        row = entry_ref[0, side]
        column = as_column(row, rows_iota, lanes_iota)
        rank_ref[0, side] = jnp.sum(jnp.where(column < row, 1, 0), axis=0, keepdims=True)
    span = GROUP * SLOTS
    strip = span // sides
    rows_iota, lanes_iota = iotas(span)
    own = rows_iota % GROUP == lanes_iota % GROUP
    spread_rows = lax.broadcasted_iota(jnp.int32, (SLOTS, span), 0)
    spread_lanes = lax.broadcasted_iota(jnp.int32, (SLOTS, span), 1)
    side_at = jnp.zeros((SLOTS, span), jnp.int32)
    for place in range(sides):
        side_at = jnp.where(spread_lanes // strip == place, order_ref[place], side_at)
    spread = one_hot(side_at * (SLOTS // sides) + spread_lanes % strip // GROUP == spread_rows)
    for group in range(angles_ref.shape[1] // GROUP):
        local = angles_ref[0, group * GROUP : (group + 1) * GROUP, :].astype(jnp.float32)
        stacked = jnp.concatenate(
            [local[:, p * SLOTS : (p + 1) * SLOTS] for p in range(SLOTS)], axis=0
        ).astype(jnp.bfloat16)
        block = jnp.where(own, dot(stacked, spread), 0.0).astype(jnp.bfloat16)
        for side in range(sides):
            to = pl.multiple_of(position_ref[side] * strip, strip)
            whole_ref[pl.ds(to, strip), :] = block[side * strip : (side + 1) * strip]
        part = span // len(block_refs)
        for chunk, block_ref in enumerate(block_refs):
            block_ref[0, group] = whole_ref[chunk * part : (chunk + 1) * part, :]


def gather_kernel(chunk, owner_ref, place_ref, recv_ref, rank_ref, out_ref, ins):
    step = pl.program_id(0)
    sides = recv_ref.shape[1]
    devices = recv_ref.shape[0]
    unit = ins.shape[3]
    pairs = devices // 2

    @pl.when(step == 0)
    def _():
        @pl.loop(0, devices)
        def _(source):
            for index in range(devices):
                owner = owner_ref[source, index]
                place = place_ref[source, index]
                at = (index % pairs) * unit
                for side in range(sides):
                    block = recv_ref[source, side, at : at + unit, :]
                    if index >= pairs:
                        block = pltpu.roll(block.astype(jnp.float32), HALF, 1).astype(jnp.bfloat16)
                    ins[side, owner, place] = block

    rows_iota, lanes_iota = iotas(devices * unit)
    for side in range(sides):
        operand = ins[side, step].reshape(devices * unit, LANES)
        source = as_column(rank_ref[0, chunk * sides + side], rows_iota, lanes_iota)
        out_ref[0, side] = dot(one_hot(source == lanes_iota), operand).astype(jnp.bfloat16)


def mix_kernel(chunk, chunks, owner_ref, place_ref, rank_ref, blocks_ref, *refs):
    gathered_refs, out_refs, outs = refs[:chunks], refs[chunks:-1], refs[-1]
    step = pl.program_id(0)
    count = outs.shape[0]
    devices = outs.shape[1]
    unit = outs.shape[3]
    groups = blocks_ref.shape[1]
    strip = blocks_ref.shape[2] // count
    pairs = devices // 2
    rows_iota = iotas(devices * unit)[0]
    mixed = []
    for group in range(groups):
        operand = jnp.concatenate(
            [
                ref[0, index, group * strip : (group + 1) * strip, :]
                for ref in gathered_refs
                for index in range(count)
            ],
            axis=0,
        )
        mixed.append(dot(blocks_ref[0, group], operand).astype(jnp.bfloat16))
    for side in range(count):
        operand = jnp.concatenate(
            [rows[side * strip : (side + 1) * strip] for rows in mixed], axis=0
        )
        outs[side, step] = (
            dot(one_hot(rows_iota == rank_ref[0, chunk * count + side]), operand)
            .astype(jnp.bfloat16)
            .reshape(devices, unit, LANES)
        )

    @pl.when(step == pl.num_programs(0) - 1)
    def _():
        low = lax.broadcasted_iota(jnp.int32, (unit, LANES), 1) < HALF

        @pl.loop(0, devices)
        def _(source):
            for index in range(pairs):
                owner = owner_ref[source, index]
                place = place_ref[source, index]
                owner_far = owner_ref[source, index + pairs]
                place_far = place_ref[source, index + pairs]
                rows = slice(index * unit, (index + 1) * unit)
                for side in range(count):
                    near = outs[side, owner, place].astype(jnp.float32)
                    far = outs[side, owner_far, place_far].astype(jnp.float32)
                    joined = jnp.where(low, near, pltpu.roll(far, HALF, 1)).astype(jnp.bfloat16)
                    if len(out_refs) == 1:
                        out_refs[0][source, side, rows, :] = joined
                    else:
                        out_refs[side][source, 0, rows, :] = joined


VMEM_BYTES = 24 * 1024 * 1024


def params():
    return pltpu.CompilerParams(vmem_limit_bytes=VMEM_BYTES)


def cost(flops, moved):
    return pl.CostEstimate(flops=flops, bytes_accessed=moved, transcendentals=0)


def whole_spec(array):
    zeros = (0,) * array.ndim
    return pl.BlockSpec(array.shape, lambda i, *_: zeros)


HBM_SPEC = pl.BlockSpec(memory_space=pltpu.HBM)


def weight_scratch(number, features):
    return [
        pltpu.VMEM((number, features, features), jnp.bfloat16),
        pltpu.SemaphoreType.DMA((number,)),
    ]


def run_front(current, where, received, own, chunk, back_rows, rank_rows, weights, section, narrow):
    _, rows, features = current.shape
    count = where.shape[0]
    edge_spec = pl.BlockSpec((1, rows, features), lambda i, where: (i, 0, 0))
    row_spec = pl.BlockSpec((1, 1, rows), lambda i, where: (chunk * count + i, 0, 0))
    return pl.pallas_call(
        functools.partial(front_kernel, own, count, section),
        grid_spec=pltpu.PrefetchScalarGridSpec(
            num_scalar_prefetch=1,
            grid=(count,),
            in_specs=[
                pl.BlockSpec((1, rows, features), lambda i, where: (where[i], 0, 0)),
                row_spec,
                row_spec,
            ]
            + [HBM_SPEC] * 5
            + [whole_spec(array) for array in received],
            out_specs=[
                edge_spec,
                pl.BlockSpec((narrow, 1, rows // 2, LANES), lambda i, where: (0, i, 0, 0)),
            ],
            scratch_shapes=[pltpu.VMEM((rows, features), jnp.bfloat16)]
            + weight_scratch(5, features),
        ),
        out_shape=[
            jax.ShapeDtypeStruct((count, rows, features), jnp.bfloat16),
            jax.ShapeDtypeStruct((narrow, count, rows // 2, LANES), jnp.bfloat16),
        ],
        compiler_params=params(),
        cost_estimate=cost(12 * count * rows * features**2, 8 * count * rows * features),
        name="front",
    )(where, current, back_rows, rank_rows, *weights[:5], *received)


def run_back(second, packed, layout, chunk, rank_rows, weights, section, where, total, target):
    count, rows, features = second.shape
    edge_spec = pl.BlockSpec((1, rows, features), lambda i, where: (i, 0, 0))
    extra = [] if target is None else [target]
    return pl.pallas_call(
        functools.partial(back_kernel, layout, section),
        grid_spec=pltpu.PrefetchScalarGridSpec(
            num_scalar_prefetch=1,
            grid=(count,),
            in_specs=[
                edge_spec,
                pl.BlockSpec((1, 1, rows), lambda i, where: (chunk * count + i, 0, 0)),
            ]
            + [HBM_SPEC] * 3
            + [whole_spec(array) for array in packed]
            + [HBM_SPEC] * len(extra),
            out_specs=pl.BlockSpec((1, rows, features), lambda i, where: (where[i], 0, 0)),
            scratch_shapes=[pltpu.VMEM((rows, features), jnp.bfloat16)]
            + weight_scratch(3, features),
        ),
        out_shape=jax.ShapeDtypeStruct((total, rows, features), jnp.bfloat16),
        input_output_aliases={6 + len(packed): 0} if extra else {},
        compiler_params=params(),
        cost_estimate=cost(8 * count * rows * features**2, 6 * count * rows * features),
        name="back",
    )(where, second, rank_rows, *weights[5:], *packed, *extra)


def rank_spec(entries):
    return pl.BlockSpec((1,) + entries.shape[1:], lambda i, *_: (i, 0, 0, 0))


def run_tables(places, order, position, entries, angles):
    owners = entries.shape[0]
    atoms = angles.shape[1]
    groups = atoms // GROUP
    span = GROUP * SLOTS
    return pl.pallas_call(
        table_kernel,
        grid_spec=pltpu.PrefetchScalarGridSpec(
            num_scalar_prefetch=3,
            grid=(owners,),
            in_specs=[
                rank_spec(entries),
                pl.BlockSpec((1, atoms, angles.shape[2]), lambda i, places, *_: (places[i], 0, 0)),
            ],
            out_specs=[
                rank_spec(entries),
            ]
            + [pl.BlockSpec((1, groups, span // CHUNKS, span), lambda i, *_: (i, 0, 0, 0))] * CHUNKS,
            scratch_shapes=[pltpu.VMEM((span, span), jnp.bfloat16)],
        ),
        out_shape=[
            jax.ShapeDtypeStruct(entries.shape, jnp.int32),
        ]
        + [jax.ShapeDtypeStruct((owners, groups, span // CHUNKS, span), jnp.bfloat16)] * CHUNKS,
        compiler_params=params(),
        cost_estimate=cost(0, 8 * owners * groups * span**2),
        name="tables",
    )(places, order, position, entries, angles)


def run_gather(owner_of, place_of, received, rank, chunk):
    devices, count, half, _ = received.shape
    rows = 2 * half
    smem = pl.BlockSpec(memory_space=pltpu.SMEM)
    return pl.pallas_call(
        functools.partial(gather_kernel, chunk),
        grid=(devices,),
        in_specs=[
            smem,
            smem,
            whole_spec(received),
            rank_spec(rank),
        ],
        out_specs=pl.BlockSpec((1, count, rows, LANES), lambda i: (i, 0, 0, 0)),
        out_shape=jax.ShapeDtypeStruct((devices, count, rows, LANES), jnp.bfloat16),
        scratch_shapes=[
            pltpu.VMEM((count, devices, devices, rows // devices, LANES), jnp.bfloat16)
        ],
        compiler_params=params(),
        cost_estimate=cost(4 * devices * count * rows**2 * LANES, 4 * devices * count * rows**2),
        name="gather",
    )(owner_of, place_of, received, rank)


def run_mix(owner_of, place_of, gathered, rank, blocks, chunk, apart):
    chunks = len(gathered)
    devices, count, rows, _ = gathered[0].shape
    half = rows // 2
    groups, part, span = blocks.shape[1:]
    smem = pl.BlockSpec(memory_space=pltpu.SMEM)
    shapes = [(devices, 1, half, LANES)] * count if apart else [(devices, count, half, LANES)]
    shapes = [jax.ShapeDtypeStruct(shape, jnp.bfloat16) for shape in shapes]
    part_spec = pl.BlockSpec((1, count, rows, LANES), lambda i: (i, 0, 0, 0))
    return pl.pallas_call(
        functools.partial(mix_kernel, chunk, chunks),
        grid=(devices,),
        in_specs=[
            smem,
            smem,
            rank_spec(rank),
            pl.BlockSpec((1, groups, part, span), lambda i: (i, 0, 0, 0)),
        ]
        + [part_spec] * chunks,
        out_specs=[whole_spec(shape) for shape in shapes],
        out_shape=shapes,
        scratch_shapes=[
            pltpu.VMEM((count, devices, devices, rows // devices, LANES), jnp.bfloat16),
        ],
        compiler_params=params(),
        cost_estimate=cost(6 * devices * count * rows**2 * LANES, 6 * devices * count * rows**2),
        name="mix",
    )(owner_of, place_of, rank, blocks, *gathered)


def unit_tables(entries, capacity, unit):
    owners, sides, rows = entries.shape
    ids = jnp.arange(owners, dtype=jnp.int32)
    source = entries.reshape(owners, sides * rows) // capacity
    counts = jnp.sum((source[None] == ids[:, None, None]).astype(jnp.int32), axis=2) // (unit * sides)
    before = ids[:, None] < ids[None, :]
    starts = jnp.sum(jnp.where(before[None], counts[:, :, None], 0), axis=1)
    places = jnp.sum(jnp.where(before[:, :, None], counts[:, None, :], 0), axis=0)
    inside = (starts[:, :, None] <= ids) & (ids < (starts + counts)[:, :, None])
    owner_of = jnp.sum(jnp.where(inside, ids[None, :, None], 0), axis=1)
    place_of = jnp.sum(jnp.where(inside, (places - starts)[:, :, None] + ids, 0), axis=1)
    return owner_of, place_of


def ranks(values):
    return jnp.sum((values[:, :, None] < values[:, None, :]).astype(jnp.int32), axis=1)


def reorder(values, order):
    hits = order[:, None] == jnp.arange(values.shape[0], dtype=jnp.int32)
    return jnp.sum(jnp.where(hits[:, :, None], values[None], 0), axis=1)


def shift(values, offset, wide):
    if offset == 0:
        return values
    return lax.ppermute(values, "wide", [(i, i ^ offset) for i in range(wide)])


def swap(values):
    return lax.all_to_all(values, "narrow", 0, 0, tiled=True)


BASE = 64


def share_lists(listed, angles, after):
    narrow = lax.axis_size("narrow")
    atoms, width = angles.shape
    digits = jnp.stack([listed // BASE, listed % BASE]).reshape(atoms, -1).astype(jnp.bfloat16)
    shared = jnp.concatenate([angles, digits], axis=1)[None]
    held = [0]
    hop = narrow // 2
    while hop:
        if hop == narrow // 4:
            shared, after = lax.optimization_barrier((shared, after))
        other = lax.ppermute(shared, "narrow", [(i, i ^ hop) for i in range(narrow)])
        shared = jnp.concatenate([shared, other], axis=0)
        held += [offset ^ hop for offset in held]
        hop //= 2
    inverse = jnp.array([held.index(offset) for offset in range(narrow)], jnp.int32)
    mine = lax.axis_index("narrow").astype(jnp.int32)
    owners = jnp.arange(narrow, dtype=jnp.int32) ^ mine
    places = jnp.sum(jnp.where(owners[:, None] == jnp.arange(narrow), inverse, 0), axis=1)
    digits = shared[:, :, width:].reshape((narrow, 2) + listed.shape).astype(jnp.int32)
    entries = digits[:, 0] * BASE + digits[:, 1]
    entries = reorder(entries.reshape(narrow, -1), places).reshape(entries.shape)
    return entries, shared, places, after


def tiled_local(messages, reverse_position, route_slot, atom_slots, angles, weights):
    wide = lax.axis_size("wide")
    narrow = lax.axis_size("narrow")
    edge_rows, features = messages.shape
    rows = edge_rows // wide
    unit = rows // narrow
    capacity = 2 * edge_rows // narrow
    atoms = angles.shape[0]
    count = wide // CHUNKS
    spread_out = [offset for index in range(wide // 2) for offset in (index, wide - 1 - index)]
    offsets = [spread_out[chunk * count : (chunk + 1) * count] for chunk in range(CHUNKS)]
    group_id = lax.axis_index("wide").astype(jnp.int32)
    order = group_id ^ jnp.array(sum(offsets, []), jnp.int32)
    inverse = jnp.array([spread_out.index(offset) for offset in range(wide)], jnp.int32)
    owners_wide = (jnp.arange(wide, dtype=jnp.int32) ^ group_id)[:, None]
    position = jnp.sum(jnp.where(owners_wide == jnp.arange(wide), inverse, 0), axis=1)
    places = [order[chunk * count : (chunk + 1) * count] for chunk in range(CHUNKS)]
    plain = jnp.arange(count, dtype=jnp.int32)

    blocks_of = messages.reshape(wide, rows, features)
    received = [
        [
            shift(lax.dynamic_index_in_dim(blocks_of, group_id ^ offset, 0, False), offset, wide)
            for offset in offsets[chunk]
            if offset
        ]
        for chunk in range(CHUNKS)
    ]
    listed = atom_slots.reshape(atoms // GROUP, GROUP, wide, SLOTS // wide)
    listed = reorder(jnp.transpose(listed, (2, 0, 3, 1)).reshape(wide, rows), order)
    rank = ranks(route_slot.reshape(wide, rows))
    back_rows = reverse_position.reshape(wide, rows)
    back_rows = reorder(back_rows, order)
    rank = reorder(rank, order)
    partner_rank = jnp.stack(
        [shift(rank[place], offset, wide) for place, offset in enumerate(sum(offsets, []))]
    )
    hits = back_rows[:, :, None] == jnp.arange(rows, dtype=jnp.int32)
    turned_rank = jnp.sum(jnp.where(hits, partner_rank[:, None, :], 0), axis=2)[:, None, :]
    back_rows = back_rows[:, None, :]
    rank = rank[:, None, :]

    current = [blocks_of] * CHUNKS
    where = places
    chunk_order = list(range(CHUNKS))
    target = None
    tables = None
    for section in range(BLOCKS):
        last = section == BLOCKS - 1
        seconds, spreads = {}, {}
        for chunk in chunk_order:
            seconds[chunk], packed = run_front(
                current[chunk], where[chunk], received[chunk], offsets[chunk][0] == 0, chunk,
                back_rows, rank, weights, section, narrow,
            )
            if tables is None and chunk == chunk_order[-1]:
                entries, all_angles, owner_places, packed = share_lists(listed, angles, packed)
            spreads[chunk] = packed
        if tables is None:
            held = [spreads[chunk] for chunk in chunk_order]
            entries, all_angles, held[-1] = lax.optimization_barrier((entries, all_angles, held[-1]))
            spreads = dict(zip(chunk_order, held))
            owner_of, place_of = unit_tables(entries, capacity, unit)
            tables = run_tables(owner_places, order, position, entries[:, :, None, :], all_angles)
        listed_rank, *blocks = tables
        gathered = [None] * CHUNKS
        for chunk in chunk_order:
            gathered[chunk] = run_gather(owner_of, place_of, swap(spreads[chunk]), listed_rank, chunk)
        chunk_order = list(range(CHUNKS))[::-1]
        returned = {}
        sent = None
        for chunk in chunk_order:
            early = last and chunk == 0
            mixed = list(run_mix(owner_of, place_of, gathered, listed_rank, blocks[chunk], chunk, early))
            if chunk != chunk_order[-1]:
                mixed[0], gathered[0] = lax.optimization_barrier((mixed[0], gathered[0]))
            if early:
                mixed = [shift(part, offset, wide) for part, offset in zip(mixed, offsets[chunk])]
                if sent is not None:
                    *sent, mixed[0] = lax.optimization_barrier((*sent, mixed[0]))
                    returned[chunk_order[0]] = (sent, returned[chunk_order[0]][1])
                parts = [swap(jnp.concatenate(mixed, axis=1))]
                layout = [(0, index) for index in range(count)]
            else:
                if sent is not None:
                    *sent, mixed[0] = lax.optimization_barrier((*sent, mixed[0]))
                    returned[chunk_order[0]] = (sent, returned[chunk_order[0]][1])
                whole = swap(mixed[0])
                sent = [whole[:, index : index + 1] for index in range(count)]
                parts = sent
                layout = [(index, 0) for index in range(count)]
            returned[chunk] = (parts, layout)
        current = [None] * CHUNKS
        received = [None] * CHUNKS
        for chunk in chunk_order:
            parts, layout = returned[chunk]
            if chunk or not last:
                parts = [shift(part, offset, wide) for part, offset in zip(parts, offsets[chunk])]
            result = run_back(
                seconds[chunk], parts, layout, chunk, turned_rank, weights, section,
                places[chunk] if last else plain, wide if last else count, target,
            )
            if last:
                target = result
            else:
                current[chunk] = result
                received[chunk] = [
                    shift(result[index], offset, wide)
                    for index, offset in enumerate(offsets[chunk])
                    if offset
                ]
        if not last:
            head, tail = chunk_order[0], chunk_order[-1]
            received[head][0], current[tail] = lax.optimization_barrier((received[head][0], current[tail]))
        where = [plain] * CHUNKS
    return target.reshape(edge_rows, features)


def local(
    messages,
    reverse_position,
    route_slot,
    atom_slots,
    angles,
    weight_message,
    weight_reverse,
    weight_combine,
    weight_inner,
    weight_outer,
    weight_lift,
    weight_expand,
    weight_reduce,
):
    weights = (
        weight_message,
        weight_reverse,
        weight_combine,
        weight_inner,
        weight_outer,
        weight_lift,
        weight_expand,
        weight_reduce,
    )
    wide = lax.axis_size("wide")
    narrow = lax.axis_size("narrow")
    edge_rows, features = messages.shape
    unit = edge_rows // wide // narrow
    fits = (
        features == narrow * HALF
        and unit % 16 == 0
        and narrow % 2 == 0
        and wide % CHUNKS == 0
        and wide & (wide - 1) == 0
        and narrow & (narrow - 1) == 0
        and angles.shape[0] % GROUP == 0
        and (SLOTS // wide * GROUP) % 16 == 0
    )
    run = tiled_local if fits else general_local
    return run(messages, reverse_position, route_slot, atom_slots, angles, weights)


def solution(mesh):
    in_specs = (
        P(("wide", "narrow"), None),
        P(("wide", "narrow")),
        P(("wide", "narrow")),
        P(("wide", "narrow")),
        P(("wide", "narrow"), None),
        P(),
        P(),
        P(),
        P(),
        P(),
        P(),
        P(),
        P(),
    )
    out_specs = P(("wide", "narrow"), None)
    return jax.shard_map(local, mesh=mesh, in_specs=in_specs, out_specs=out_specs, check_vma=False)
```

```python
import functools

import jax
import jax.numpy as jnp
from jax import lax
from jax.experimental import pallas as pl
from jax.experimental.pallas import tpu as pltpu
from jax.sharding import PartitionSpec as P

SLOTS = 32
BLOCKS = 2
LANES = 128
HALF = LANES // 2
GROUP = 8


ROOT_HALF = 0.7071067811865476


def project(operand, weight):
    return jnp.dot(operand, weight, preferred_element_type=jnp.float32)


def residual(previous, branch):
    return ((previous.astype(jnp.float32) + branch) * ROOT_HALF).astype(jnp.bfloat16)


def reverse_edges(values, partner_rows):
    exchanged = lax.all_to_all(values, "wide", split_axis=0, concat_axis=0, tiled=True)
    return jnp.take(exchanged, partner_rows, axis=0)


def edge_front(current, reverse, weights, section_index):
    hidden = jax.nn.silu(
        project(current, weights[0][section_index]) + project(reverse, weights[1][section_index])
    ).astype(jnp.bfloat16)
    first_res = residual(current, project(hidden, weights[2][section_index]))
    inner_value = jax.nn.silu(project(first_res, weights[3][section_index])).astype(jnp.bfloat16)
    return residual(first_res, jax.nn.silu(project(inner_value, weights[4][section_index])))


def edge_back(second, turned, weights, section_index):
    third_res = residual(second, jax.nn.silu(project(turned, weights[5][section_index])))
    expand = jax.nn.silu(project(third_res, weights[6][section_index])).astype(jnp.bfloat16)
    return residual(third_res, jax.nn.silu(project(expand, weights[7][section_index])))


def owners_mix(second, route_slot, atom_slots, mixing):
    features = second.shape[1]
    buffer_rows = 2 * second.shape[0]
    outgoing = jnp.zeros((buffer_rows, features), jnp.bfloat16).at[route_slot].set(second)
    received = lax.all_to_all(outgoing, "narrow", split_axis=0, concat_axis=0, tiled=True)
    gathered = jnp.take(received, atom_slots, axis=0).reshape(mixing.shape[0], SLOTS, features)
    mixed_rows = jnp.einsum(
        "apq,aqd->apd", mixing, gathered, preferred_element_type=jnp.float32
    ).astype(jnp.bfloat16)
    return mixed_rows.reshape(-1, features)


def back_to_edges(mixed_flat, route_slot, atom_slots):
    features = mixed_flat.shape[1]
    buffer_rows = 2 * route_slot.shape[0]
    answer = jnp.zeros((buffer_rows, features), jnp.bfloat16).at[atom_slots].set(mixed_flat)
    incoming = lax.all_to_all(answer, "narrow", split_axis=0, concat_axis=0, tiled=True)
    return jnp.take(incoming, route_slot, axis=0)


def general_local(messages, reverse_position, route_slot, atom_slots, angles, weights):
    edge_rows = messages.shape[0]
    sub_rows = edge_rows // lax.axis_size("wide")
    partner_rows = jnp.arange(edge_rows, dtype=jnp.int32) // sub_rows * sub_rows + reverse_position
    mixing = angles.reshape(angles.shape[0], SLOTS, SLOTS)
    current = messages
    for section_index in range(BLOCKS):
        reverse = reverse_edges(current, partner_rows)
        second = edge_front(current, reverse, weights, section_index)
        mixed_flat = owners_mix(second, route_slot, atom_slots, mixing)
        returned = back_to_edges(mixed_flat, route_slot, atom_slots)
        turned = reverse_edges(returned, partner_rows)
        current = edge_back(second, turned, weights, section_index)
    return current


def silu(value):
    return 0.5 * value * (1.0 + jnp.tanh(0.5 * value))


def dot(left, right):
    return jnp.dot(left, right, preferred_element_type=jnp.float32)


def halve(previous, branch):
    return ((previous.astype(jnp.float32) + branch) * ROOT_HALF).astype(jnp.bfloat16)


def iotas(size):
    shape = (size, size)
    return lax.broadcasted_iota(jnp.int32, shape, 0), lax.broadcasted_iota(jnp.int32, shape, 1)


def as_column(row, rows_iota, lanes_iota):
    return jnp.sum(jnp.where(rows_iota == lanes_iota, row, 0), axis=1, keepdims=True)


def one_hot(mask):
    return jnp.where(mask, 1.0, 0.0).astype(jnp.bfloat16)


def front_kernel(own, count, where_ref, cur_ref, back_ref, rank_ref, wm, wr, wc, wi, wo, *refs):
    recv_refs, (second_ref, packed_ref, reverse_ref) = refs[: count - own], refs[-3:]
    rows_iota, lanes_iota = iotas(cur_ref.shape[1])
    partner = as_column(back_ref[0], rows_iota, lanes_iota)
    hot = one_hot(partner == lanes_iota)
    sources = ([cur_ref.at[0]] if own else []) + list(recv_refs)
    for index in range(count):

        @pl.when(pl.program_id(0) == index)
        def _():
            reverse_ref[...] = dot(hot, sources[index][...]).astype(jnp.bfloat16)

    current = cur_ref[0]
    hidden = silu(dot(current, wm[0]) + dot(reverse_ref[...], wr[0])).astype(jnp.bfloat16)
    first_res = halve(current, dot(hidden, wc[0]))
    inner = silu(dot(first_res, wi[0])).astype(jnp.bfloat16)
    second = halve(first_res, silu(dot(inner, wo[0])))
    second_ref[0] = second
    ordered = dot(one_hot(rows_iota == rank_ref[0]), second)
    half = ordered.shape[0] // 2
    low = lax.broadcasted_iota(jnp.int32, (half, LANES), 1) < HALF
    for tile in range(ordered.shape[1] // LANES):
        top = ordered[:half, tile * LANES : (tile + 1) * LANES]
        bottom = ordered[half:, tile * LANES : (tile + 1) * LANES]
        packed_ref[2 * tile, 0] = jnp.where(low, top, pltpu.roll(bottom, HALF, 1)).astype(jnp.bfloat16)
        packed_ref[2 * tile + 1, 0] = jnp.where(low, pltpu.roll(top, HALF, 1), bottom).astype(jnp.bfloat16)


def back_kernel(from_ref, to_ref, second_ref, packed_ref, rank_ref, wl, we, wd, out_ref):
    rows_iota, lanes_iota = iotas(second_ref.shape[1])
    half = rows_iota.shape[0] // 2
    low = lax.broadcasted_iota(jnp.int32, (half, LANES), 1) < HALF
    tops, bottoms = [], []
    for tile in range(second_ref.shape[2] // LANES):
        even = packed_ref[0, 2 * tile].astype(jnp.float32)
        odd = packed_ref[0, 2 * tile + 1].astype(jnp.float32)
        tops.append(jnp.where(low, even, pltpu.roll(odd, HALF, 1)).astype(jnp.bfloat16))
        bottoms.append(jnp.where(low, pltpu.roll(even, HALF, 1), odd).astype(jnp.bfloat16))
    ordered = jnp.concatenate(
        [jnp.concatenate(tops, axis=1), jnp.concatenate(bottoms, axis=1)], axis=0
    )
    source = as_column(rank_ref[0], rows_iota, lanes_iota)
    turned = dot(one_hot(source == lanes_iota), ordered).astype(jnp.bfloat16)
    third_res = halve(second_ref[0], silu(dot(turned, wl[0])))
    expand = silu(dot(third_res, we[0])).astype(jnp.bfloat16)
    out_ref[0] = halve(third_res, silu(dot(expand, wd[0])))


def table_kernel(places_ref, order_ref, position_ref, entry_ref, angles_ref, rank_ref, blocks_ref):
    sides, _, size = entry_ref.shape[1:]
    rows_iota, lanes_iota = iotas(size)
    for side in range(sides):
        row = entry_ref[0, side]
        column = as_column(row, rows_iota, lanes_iota)
        rank_ref[0, side] = jnp.sum(jnp.where(column < row, 1, 0), axis=0, keepdims=True)
    span = GROUP * SLOTS
    strip = span // sides
    rows_iota, lanes_iota = iotas(span)
    own = rows_iota % GROUP == lanes_iota % GROUP
    spread_rows = lax.broadcasted_iota(jnp.int32, (SLOTS, span), 0)
    spread_lanes = lax.broadcasted_iota(jnp.int32, (SLOTS, span), 1)
    side_at = jnp.zeros((SLOTS, span), jnp.int32)
    for place in range(sides):
        side_at = jnp.where(spread_lanes // strip == place, order_ref[place], side_at)
    spread = one_hot(side_at * (SLOTS // sides) + spread_lanes % strip // GROUP == spread_rows)
    for group in range(angles_ref.shape[1] // GROUP):
        local = angles_ref[0, group * GROUP : (group + 1) * GROUP, :].astype(jnp.float32)
        stacked = jnp.concatenate(
            [local[:, p * SLOTS : (p + 1) * SLOTS] for p in range(SLOTS)], axis=0
        ).astype(jnp.bfloat16)
        block = jnp.where(own, dot(stacked, spread), 0.0).astype(jnp.bfloat16)
        for side in range(sides):
            to = pl.multiple_of(position_ref[side] * strip, strip)
            blocks_ref[0, group, pl.ds(to, strip), :] = block[side * strip : (side + 1) * strip]


def mix_kernel(owner_ref, place_ref, order_ref, recv_ref, rank_ref, blocks_ref, out_ref, ins, outs):
    step = pl.program_id(0)
    devices, sides = recv_ref.shape[:2]
    unit = ins.shape[3]
    rows = devices * unit
    groups = blocks_ref.shape[1]
    strip = blocks_ref.shape[2] // sides
    pairs = devices // 2

    @pl.when(step == 0)
    def _():
        @pl.loop(0, devices)
        def _(source):
            for index in range(devices):
                owner = owner_ref[source, index]
                place = place_ref[source, index]
                at = (index % pairs) * unit
                for side in range(sides):
                    block = recv_ref[source, side, at : at + unit, :]
                    if index >= pairs:
                        block = pltpu.roll(block.astype(jnp.float32), HALF, 1).astype(jnp.bfloat16)
                    ins[side, owner, place] = block

    rows_iota, lanes_iota = iotas(rows)
    gathered = []
    for side in range(sides):
        source = as_column(rank_ref[0, side], rows_iota, lanes_iota)
        operand = ins[side, step].reshape(rows, LANES)
        gathered.append(dot(one_hot(source == lanes_iota), operand).astype(jnp.bfloat16))
    mixed = []
    for group in range(groups):
        operand = jnp.concatenate(
            [part[group * strip : (group + 1) * strip] for part in gathered], axis=0
        )
        mixed.append(dot(blocks_ref[0, group], operand).astype(jnp.bfloat16))
    for side in range(sides):
        operand = jnp.concatenate(
            [part[side * strip : (side + 1) * strip] for part in mixed], axis=0
        )
        outs[side, step] = (
            dot(one_hot(rows_iota == rank_ref[0, side]), operand)
            .astype(jnp.bfloat16)
            .reshape(devices, unit, LANES)
        )

    @pl.when(step == pl.num_programs(0) - 1)
    def _():
        low = lax.broadcasted_iota(jnp.int32, (unit, LANES), 1) < HALF

        @pl.loop(0, devices)
        def _(source):
            for index in range(pairs):
                owner = owner_ref[source, index]
                place = place_ref[source, index]
                owner_far = owner_ref[source, index + pairs]
                place_far = place_ref[source, index + pairs]
                for side in range(sides):
                    near = outs[side, owner, place].astype(jnp.float32)
                    far = outs[side, owner_far, place_far].astype(jnp.float32)
                    joined = jnp.where(low, near, pltpu.roll(far, HALF, 1)).astype(jnp.bfloat16)
                    out_ref[order_ref[side], source, index * unit : (index + 1) * unit, :] = joined


VMEM_BYTES = 24 * 1024 * 1024


def params():
    return pltpu.CompilerParams(vmem_limit_bytes=VMEM_BYTES)


def cost(flops, moved, waves=0):
    return pl.CostEstimate(flops=flops, bytes_accessed=moved, transcendentals=waves)


def whole_spec(array):
    zeros = (0,) * array.ndim
    return pl.BlockSpec(array.shape, lambda i, *_: zeros)


def weight_spec(section, features):
    return pl.BlockSpec((1, features, features), lambda i, *_: (section, 0, 0))


def run_front(current, where, received, own, start, sides, back_rows, rank_rows, weights, section, targets):
    _, rows, features = current.shape
    count = where.shape[0]
    narrow = features // HALF
    row_spec = pl.BlockSpec((1, 1, rows), lambda i, where: (start + i, 0, 0))
    first_target = 9 + len(received)
    return pl.pallas_call(
        functools.partial(front_kernel, own, count),
        grid_spec=pltpu.PrefetchScalarGridSpec(
            num_scalar_prefetch=1,
            grid=(count,),
            in_specs=[
                pl.BlockSpec((1, rows, features), lambda i, where: (where[i], 0, 0)),
                row_spec,
                row_spec,
            ]
            + [weight_spec(section, features)] * 5
            + [whole_spec(array) for array in received]
            + [pl.BlockSpec(memory_space=pl.ANY)] * len(targets),
            out_specs=[
                pl.BlockSpec((1, rows, features), lambda i, where: (start + i, 0, 0)),
                pl.BlockSpec((narrow, 1, rows // 2, LANES), lambda i, where: (0, start + i, 0, 0)),
            ],
            scratch_shapes=[pltpu.VMEM((rows, features), jnp.bfloat16)],
        ),
        out_shape=[
            jax.ShapeDtypeStruct((sides, rows, features), jnp.bfloat16),
            jax.ShapeDtypeStruct((narrow, sides, rows // 2, LANES), jnp.bfloat16),
        ],
        input_output_aliases={first_target + index: index for index in range(len(targets))},
        compiler_params=params(),
        cost_estimate=cost(12 * count * rows * features**2, 8 * count * rows * features),
        name="front",
    )(where, current, back_rows, rank_rows, *weights[:5], *received, *targets)


def run_back(second, packed, where, to, start, rank_rows, weights, section, total):
    _, rows, features = second.shape
    count = where.shape[0]
    narrow = packed.shape[1]
    return pl.pallas_call(
        back_kernel,
        grid_spec=pltpu.PrefetchScalarGridSpec(
            num_scalar_prefetch=2,
            grid=(count,),
            in_specs=[
                pl.BlockSpec((1, rows, features), lambda i, *_: (start + i, 0, 0)),
                pl.BlockSpec((1, narrow, rows // 2, LANES), lambda i, where, to: (where[i], 0, 0, 0)),
                pl.BlockSpec((1, 1, rows), lambda i, *_: (start + i, 0, 0)),
            ]
            + [weight_spec(section, features)] * 3,
            out_specs=pl.BlockSpec((1, rows, features), lambda i, where, to: (to[i], 0, 0)),
        ),
        out_shape=jax.ShapeDtypeStruct((total, rows, features), jnp.bfloat16),
        compiler_params=params(),
        cost_estimate=cost(8 * count * rows * features**2, 6 * count * rows * features),
        name="back",
    )(where, to, second, packed, rank_rows, *weights[5:])


def rank_spec(entries):
    return pl.BlockSpec((1,) + entries.shape[1:], lambda i, *_: (i, 0, 0, 0))


def run_tables(places, order, position, entries, angles):
    owners = entries.shape[0]
    atoms = angles.shape[1]
    groups = atoms // GROUP
    span = GROUP * SLOTS
    return pl.pallas_call(
        table_kernel,
        grid_spec=pltpu.PrefetchScalarGridSpec(
            num_scalar_prefetch=3,
            grid=(owners,),
            in_specs=[
                rank_spec(entries),
                pl.BlockSpec((1, atoms, angles.shape[2]), lambda i, places, *_: (places[i], 0, 0)),
            ],
            out_specs=[
                rank_spec(entries),
                pl.BlockSpec((1, groups, span, span), lambda i, *_: (i, 0, 0, 0)),
            ],
        ),
        out_shape=[
            jax.ShapeDtypeStruct(entries.shape, jnp.int32),
            jax.ShapeDtypeStruct((owners, groups, span, span), jnp.bfloat16),
        ],
        compiler_params=params(),
        cost_estimate=cost(0, 8 * owners * groups * span**2),
        name="tables",
    )(places, order, position, entries, angles)


def run_mix(owner_of, place_of, order, received, rank, blocks):
    devices, sides, half, _ = received.shape
    unit = 2 * half // devices
    smem = pl.BlockSpec(memory_space=pltpu.SMEM)
    shape = (sides, devices, half, LANES)
    scratch = pltpu.VMEM((sides, devices, devices, unit, LANES), jnp.bfloat16)
    return pl.pallas_call(
        mix_kernel,
        grid=(devices,),
        in_specs=[
            smem,
            smem,
            smem,
            whole_spec(received),
            rank_spec(rank),
            pl.BlockSpec((1,) + blocks.shape[1:], lambda i: (i, 0, 0, 0)),
        ],
        out_specs=pl.BlockSpec(shape, lambda i: (0, 0, 0, 0)),
        out_shape=jax.ShapeDtypeStruct(shape, jnp.bfloat16),
        scratch_shapes=[scratch, scratch],
        compiler_params=params(),
        cost_estimate=cost(10 * devices * sides * half**2 * LANES, 16 * devices * sides * half**2),
        name="mix",
    )(owner_of, place_of, order, received, rank, blocks)


def unit_tables(entries, capacity, unit):
    owners, sides, rows = entries.shape
    ids = jnp.arange(owners, dtype=jnp.int32)
    source = entries.reshape(owners, sides * rows) // capacity
    counts = jnp.sum((source[None] == ids[:, None, None]).astype(jnp.int32), axis=2) // (unit * sides)
    before = ids[:, None] < ids[None, :]
    starts = jnp.sum(jnp.where(before[None], counts[:, :, None], 0), axis=1)
    places = jnp.sum(jnp.where(before[:, :, None], counts[:, None, :], 0), axis=0)
    inside = (starts[:, :, None] <= ids) & (ids < (starts + counts)[:, :, None])
    owner_of = jnp.sum(jnp.where(inside, ids[None, :, None], 0), axis=1)
    place_of = jnp.sum(jnp.where(inside, (places - starts)[:, :, None] + ids, 0), axis=1)
    return owner_of, place_of


def ranks(values):
    return jnp.sum((values[:, :, None] < values[:, None, :]).astype(jnp.int32), axis=1)


CHUNKS = 2


def reorder(values, order):
    hits = order[:, None] == jnp.arange(values.shape[0], dtype=jnp.int32)
    return jnp.sum(jnp.where(hits[:, :, None], values[None], 0), axis=1)


def shift(values, offset, wide):
    if offset == 0:
        return values
    return lax.ppermute(values, "wide", [(i, i ^ offset) for i in range(wide)])


def swap(values):
    return lax.all_to_all(values, "narrow", 0, 0, tiled=True)


BASE = 64


def share_lists(listed, angles):
    narrow = lax.axis_size("narrow")
    atoms, width = angles.shape
    digits = jnp.stack([listed // BASE, listed % BASE]).reshape(atoms, -1).astype(jnp.bfloat16)
    shared = jnp.concatenate([angles, digits], axis=1)[None]
    held = [0]
    hop = narrow // 2
    while hop:
        other = lax.ppermute(shared, "narrow", [(i, i ^ hop) for i in range(narrow)])
        shared = jnp.concatenate([shared, other], axis=0)
        held += [offset ^ hop for offset in held]
        hop //= 2
    inverse = jnp.array([held.index(offset) for offset in range(narrow)], jnp.int32)
    mine = lax.axis_index("narrow").astype(jnp.int32)
    owners = jnp.arange(narrow, dtype=jnp.int32) ^ mine
    places = jnp.sum(jnp.where(owners[:, None] == jnp.arange(narrow), inverse, 0), axis=1)
    digits = shared[:, :, width:].reshape((narrow, 2) + listed.shape).astype(jnp.int32)
    entries = digits[:, 0] * BASE + digits[:, 1]
    entries = reorder(entries.reshape(narrow, -1), places).reshape(entries.shape)
    return entries, shared, places


def tiled_local(messages, reverse_position, route_slot, atom_slots, angles, weights):
    wide = lax.axis_size("wide")
    narrow = lax.axis_size("narrow")
    edge_rows, features = messages.shape
    rows = edge_rows // wide
    unit = rows // narrow
    capacity = 2 * edge_rows // narrow
    atoms = angles.shape[0]
    group_id = lax.axis_index("wide").astype(jnp.int32)
    offsets = [offset for index in range(wide // 2) for offset in (index, wide - 1 - index)]
    order = group_id ^ jnp.array(offsets, jnp.int32)
    inverse = jnp.array([offsets.index(offset) for offset in range(wide)], jnp.int32)
    owners_wide = (jnp.arange(wide, dtype=jnp.int32) ^ group_id)[:, None]
    position = jnp.sum(jnp.where(owners_wide == jnp.arange(wide), inverse, 0), axis=1)
    half = wide // 2
    pieces = [(0, 1), (1, half - 1), (half, wide - half)]
    halves = [(0, half), (half, wide - half)]

    blocks_of = messages.reshape(wide, rows, features)
    received = {
        offset: shift(lax.dynamic_index_in_dim(blocks_of, group_id ^ offset, 0, False), offset, wide)
        for offset in offsets[1:]
    }
    listed = atom_slots.reshape(atoms // GROUP, GROUP, wide, SLOTS // wide)
    listed = reorder(jnp.transpose(listed, (2, 0, 3, 1)).reshape(wide, rows), order)
    rank = reorder(ranks(route_slot.reshape(wide, rows)), order)
    back_rows = reorder(reverse_position.reshape(wide, rows), order)

    current = {start: (blocks_of, order[start : start + count]) for start, count in pieces}
    tables = None
    for section in range(BLOCKS):
        last = section == BLOCKS - 1
        targets = []
        for start, count in halves if section else pieces:
            array, where = current[start]
            needed = [received[offset] for offset in offsets[start : start + count] if offset]
            targets = run_front(
                array, where, needed, start == 0, start, wide,
                back_rows[:, None, :], rank[:, None, :], weights, section, targets,
            )
        second, packed = targets
        if tables is None:
            packed, listed, late_rank = lax.optimization_barrier((packed, listed, rank))
            entries, all_angles, owner_places = share_lists(listed, angles)
            owner_of, place_of = unit_tables(entries, capacity, unit)
            tables = run_tables(owner_places, order, position, entries[:, :, None, :], all_angles)
            partner_rank = jnp.stack(
                [shift(late_rank[place], offset, wide) for place, offset in enumerate(offsets)]
            )
            hits = back_rows[:, :, None] == jnp.arange(rows, dtype=jnp.int32)
            turned_rank = jnp.sum(jnp.where(hits, partner_rank[:, None, :], 0), axis=2)[:, None, :]
        mixed = run_mix(owner_of, place_of, order, swap(packed), *tables)
        mixed = mixed.reshape(wide * narrow, rows // 2, LANES)
        returned = lax.all_to_all(mixed, ("wide", "narrow"), 0, 0, tiled=True)
        returned = returned.reshape(wide, narrow, rows // 2, LANES)
        if last:
            current = run_back(second, returned, order, order, 0, turned_rank, weights, section, wide)
            return current.reshape(edge_rows, features)
        for start, count in halves:
            plain = jnp.arange(count, dtype=jnp.int32)
            where = order[start : start + count]
            result = run_back(second, returned, where, plain, start, turned_rank, weights, section, count)
            current[start] = (result, plain)
            for index, offset in enumerate(offsets[start : start + count]):
                if offset:
                    received[offset] = shift(result[index], offset, wide)


def local(
    messages,
    reverse_position,
    route_slot,
    atom_slots,
    angles,
    weight_message,
    weight_reverse,
    weight_combine,
    weight_inner,
    weight_outer,
    weight_lift,
    weight_expand,
    weight_reduce,
):
    weights = (
        weight_message,
        weight_reverse,
        weight_combine,
        weight_inner,
        weight_outer,
        weight_lift,
        weight_expand,
        weight_reduce,
    )
    wide = lax.axis_size("wide")
    narrow = lax.axis_size("narrow")
    edge_rows, features = messages.shape
    unit = edge_rows // wide // narrow
    fits = (
        features == narrow * HALF
        and unit % 16 == 0
        and narrow % 2 == 0
        and wide >= 4
        and wide & (wide - 1) == 0
        and narrow & (narrow - 1) == 0
        and angles.shape[0] % GROUP == 0
        and (SLOTS // wide * GROUP) % 16 == 0
    )
    run = tiled_local if fits else general_local
    return run(messages, reverse_position, route_slot, atom_slots, angles, weights)


def solution(mesh):
    in_specs = (
        P(("wide", "narrow"), None),
        P(("wide", "narrow")),
        P(("wide", "narrow")),
        P(("wide", "narrow")),
        P(("wide", "narrow"), None),
        P(),
        P(),
        P(),
        P(),
        P(),
        P(),
        P(),
        P(),
    )
    out_specs = P(("wide", "narrow"), None)
    return jax.shard_map(local, mesh=mesh, in_specs=in_specs, out_specs=out_specs, check_vma=False)
```

```python
import functools

import jax
import jax.numpy as jnp
from jax import lax
from jax.experimental import pallas as pl
from jax.experimental.pallas import tpu as pltpu
from jax.sharding import PartitionSpec as P

SLOTS = 32
BLOCKS = 2
LANES = 128
HALF = LANES // 2
GROUP = 8


ROOT_HALF = 0.7071067811865476


def project(operand, weight):
    return jnp.dot(operand, weight, preferred_element_type=jnp.float32)


def residual(previous, branch):
    return ((previous.astype(jnp.float32) + branch) * ROOT_HALF).astype(jnp.bfloat16)


def reverse_edges(values, partner_rows):
    exchanged = lax.all_to_all(values, "wide", split_axis=0, concat_axis=0, tiled=True)
    return jnp.take(exchanged, partner_rows, axis=0)


def edge_front(current, reverse, weights, section_index):
    hidden = jax.nn.silu(
        project(current, weights[0][section_index]) + project(reverse, weights[1][section_index])
    ).astype(jnp.bfloat16)
    first_res = residual(current, project(hidden, weights[2][section_index]))
    inner_value = jax.nn.silu(project(first_res, weights[3][section_index])).astype(jnp.bfloat16)
    return residual(first_res, jax.nn.silu(project(inner_value, weights[4][section_index])))


def edge_back(second, turned, weights, section_index):
    third_res = residual(second, jax.nn.silu(project(turned, weights[5][section_index])))
    expand = jax.nn.silu(project(third_res, weights[6][section_index])).astype(jnp.bfloat16)
    return residual(third_res, jax.nn.silu(project(expand, weights[7][section_index])))


def owners_mix(second, route_slot, atom_slots, mixing):
    features = second.shape[1]
    buffer_rows = 2 * second.shape[0]
    outgoing = jnp.zeros((buffer_rows, features), jnp.bfloat16).at[route_slot].set(second)
    received = lax.all_to_all(outgoing, "narrow", split_axis=0, concat_axis=0, tiled=True)
    gathered = jnp.take(received, atom_slots, axis=0).reshape(mixing.shape[0], SLOTS, features)
    mixed_rows = jnp.einsum(
        "apq,aqd->apd", mixing, gathered, preferred_element_type=jnp.float32
    ).astype(jnp.bfloat16)
    return mixed_rows.reshape(-1, features)


def back_to_edges(mixed_flat, route_slot, atom_slots):
    features = mixed_flat.shape[1]
    buffer_rows = 2 * route_slot.shape[0]
    answer = jnp.zeros((buffer_rows, features), jnp.bfloat16).at[atom_slots].set(mixed_flat)
    incoming = lax.all_to_all(answer, "narrow", split_axis=0, concat_axis=0, tiled=True)
    return jnp.take(incoming, route_slot, axis=0)


def general_local(messages, reverse_position, route_slot, atom_slots, angles, weights):
    edge_rows = messages.shape[0]
    sub_rows = edge_rows // lax.axis_size("wide")
    partner_rows = jnp.arange(edge_rows, dtype=jnp.int32) // sub_rows * sub_rows + reverse_position
    mixing = angles.reshape(angles.shape[0], SLOTS, SLOTS)
    current = messages
    for section_index in range(BLOCKS):
        reverse = reverse_edges(current, partner_rows)
        second = edge_front(current, reverse, weights, section_index)
        mixed_flat = owners_mix(second, route_slot, atom_slots, mixing)
        returned = back_to_edges(mixed_flat, route_slot, atom_slots)
        turned = reverse_edges(returned, partner_rows)
        current = edge_back(second, turned, weights, section_index)
    return current


def silu(value):
    return 0.5 * value * (1.0 + jnp.tanh(0.5 * value))


def dot(left, right):
    return jnp.dot(left, right, preferred_element_type=jnp.float32)


def halve(previous, branch):
    return ((previous.astype(jnp.float32) + branch) * ROOT_HALF).astype(jnp.bfloat16)


def iotas(size):
    shape = (size, size)
    return lax.broadcasted_iota(jnp.int32, shape, 0), lax.broadcasted_iota(jnp.int32, shape, 1)


def as_column(row, rows_iota, lanes_iota):
    return jnp.sum(jnp.where(rows_iota == lanes_iota, row, 0), axis=1, keepdims=True)


def one_hot(mask):
    return jnp.where(mask, 1.0, 0.0).astype(jnp.bfloat16)


def front_kernel(own, count, where_ref, cur_ref, back_ref, rank_ref, wm, wr, wc, wi, wo, *refs):
    recv_refs, (second_ref, packed_ref, reverse_ref) = refs[: count - own], refs[-3:]
    rows_iota, lanes_iota = iotas(cur_ref.shape[1])
    partner = as_column(back_ref[0], rows_iota, lanes_iota)
    hot = one_hot(partner == lanes_iota)
    sources = ([cur_ref.at[0]] if own else []) + list(recv_refs)
    for index in range(count):

        @pl.when(pl.program_id(0) == index)
        def _():
            reverse_ref[...] = dot(hot, sources[index][...]).astype(jnp.bfloat16)

    current = cur_ref[0]
    hidden = silu(dot(current, wm[0]) + dot(reverse_ref[...], wr[0])).astype(jnp.bfloat16)
    first_res = halve(current, dot(hidden, wc[0]))
    inner = silu(dot(first_res, wi[0])).astype(jnp.bfloat16)
    second = halve(first_res, silu(dot(inner, wo[0])))
    second_ref[0] = second
    ordered = dot(one_hot(rows_iota == rank_ref[0]), second)
    half = ordered.shape[0] // 2
    low = lax.broadcasted_iota(jnp.int32, (half, LANES), 1) < HALF
    for tile in range(ordered.shape[1] // LANES):
        top = ordered[:half, tile * LANES : (tile + 1) * LANES]
        bottom = ordered[half:, tile * LANES : (tile + 1) * LANES]
        packed_ref[2 * tile, 0] = jnp.where(low, top, pltpu.roll(bottom, HALF, 1)).astype(jnp.bfloat16)
        packed_ref[2 * tile + 1, 0] = jnp.where(low, pltpu.roll(top, HALF, 1), bottom).astype(jnp.bfloat16)


def back_kernel(from_ref, to_ref, second_ref, packed_ref, rank_ref, wl, we, wd, out_ref):
    rows_iota, lanes_iota = iotas(second_ref.shape[1])
    half = rows_iota.shape[0] // 2
    low = lax.broadcasted_iota(jnp.int32, (half, LANES), 1) < HALF
    tops, bottoms = [], []
    for tile in range(second_ref.shape[2] // LANES):
        even = packed_ref[0, 2 * tile].astype(jnp.float32)
        odd = packed_ref[0, 2 * tile + 1].astype(jnp.float32)
        tops.append(jnp.where(low, even, pltpu.roll(odd, HALF, 1)).astype(jnp.bfloat16))
        bottoms.append(jnp.where(low, pltpu.roll(even, HALF, 1), odd).astype(jnp.bfloat16))
    ordered = jnp.concatenate(
        [jnp.concatenate(tops, axis=1), jnp.concatenate(bottoms, axis=1)], axis=0
    )
    source = as_column(rank_ref[0], rows_iota, lanes_iota)
    turned = dot(one_hot(source == lanes_iota), ordered).astype(jnp.bfloat16)
    third_res = halve(second_ref[0], silu(dot(turned, wl[0])))
    expand = silu(dot(third_res, we[0])).astype(jnp.bfloat16)
    out_ref[0] = halve(third_res, silu(dot(expand, wd[0])))


def table_kernel(places_ref, order_ref, position_ref, entry_ref, angles_ref, rank_ref, blocks_ref):
    sides, _, size = entry_ref.shape[1:]
    rows_iota, lanes_iota = iotas(size)
    for side in range(sides):
        row = entry_ref[0, side]
        column = as_column(row, rows_iota, lanes_iota)
        rank_ref[0, side] = jnp.sum(jnp.where(column < row, 1, 0), axis=0, keepdims=True)
    span = GROUP * SLOTS
    strip = span // sides
    rows_iota, lanes_iota = iotas(span)
    own = rows_iota % GROUP == lanes_iota % GROUP
    spread_rows = lax.broadcasted_iota(jnp.int32, (SLOTS, span), 0)
    spread_lanes = lax.broadcasted_iota(jnp.int32, (SLOTS, span), 1)
    side_at = jnp.zeros((SLOTS, span), jnp.int32)
    for place in range(sides):
        side_at = jnp.where(spread_lanes // strip == place, order_ref[place], side_at)
    spread = one_hot(side_at * (SLOTS // sides) + spread_lanes % strip // GROUP == spread_rows)
    for group in range(angles_ref.shape[1] // GROUP):
        local = angles_ref[0, group * GROUP : (group + 1) * GROUP, :].astype(jnp.float32)
        stacked = jnp.concatenate(
            [local[:, p * SLOTS : (p + 1) * SLOTS] for p in range(SLOTS)], axis=0
        ).astype(jnp.bfloat16)
        block = jnp.where(own, dot(stacked, spread), 0.0).astype(jnp.bfloat16)
        for side in range(sides):
            to = pl.multiple_of(position_ref[side] * strip, strip)
            blocks_ref[0, group, pl.ds(to, strip), :] = block[side * strip : (side + 1) * strip]


def mix_kernel(owner_ref, place_ref, order_ref, recv_ref, rank_ref, blocks_ref, out_ref, ins, outs):
    step = pl.program_id(0)
    devices, sides = recv_ref.shape[:2]
    unit = ins.shape[3]
    rows = devices * unit
    groups = blocks_ref.shape[1]
    strip = blocks_ref.shape[2] // sides
    pairs = devices // 2

    @pl.when(step == 0)
    def _():
        @pl.loop(0, devices)
        def _(source):
            for index in range(devices):
                owner = owner_ref[source, index]
                place = place_ref[source, index]
                at = (index % pairs) * unit
                for side in range(sides):
                    block = recv_ref[source, side, at : at + unit, :]
                    if index >= pairs:
                        block = pltpu.roll(block.astype(jnp.float32), HALF, 1).astype(jnp.bfloat16)
                    ins[side, owner, place] = block

    rows_iota, lanes_iota = iotas(rows)
    gathered = []
    for side in range(sides):
        source = as_column(rank_ref[0, side], rows_iota, lanes_iota)
        operand = ins[side, step].reshape(rows, LANES)
        gathered.append(dot(one_hot(source == lanes_iota), operand).astype(jnp.bfloat16))
    mixed = []
    for group in range(groups):
        operand = jnp.concatenate(
            [part[group * strip : (group + 1) * strip] for part in gathered], axis=0
        )
        mixed.append(dot(blocks_ref[0, group], operand).astype(jnp.bfloat16))
    for side in range(sides):
        operand = jnp.concatenate(
            [part[side * strip : (side + 1) * strip] for part in mixed], axis=0
        )
        outs[side, step] = (
            dot(one_hot(rows_iota == rank_ref[0, side]), operand)
            .astype(jnp.bfloat16)
            .reshape(devices, unit, LANES)
        )

    @pl.when(step == pl.num_programs(0) - 1)
    def _():
        low = lax.broadcasted_iota(jnp.int32, (unit, LANES), 1) < HALF

        @pl.loop(0, devices)
        def _(source):
            for index in range(pairs):
                owner = owner_ref[source, index]
                place = place_ref[source, index]
                owner_far = owner_ref[source, index + pairs]
                place_far = place_ref[source, index + pairs]
                for side in range(sides):
                    near = outs[side, owner, place].astype(jnp.float32)
                    far = outs[side, owner_far, place_far].astype(jnp.float32)
                    joined = jnp.where(low, near, pltpu.roll(far, HALF, 1)).astype(jnp.bfloat16)
                    out_ref[order_ref[side], source, index * unit : (index + 1) * unit, :] = joined


VMEM_BYTES = 24 * 1024 * 1024
VMEM_MOST = 60 * 1024 * 1024


def params(limit=VMEM_BYTES):
    return pltpu.CompilerParams(vmem_limit_bytes=limit)


def cost(flops, moved, waves=0):
    return pl.CostEstimate(flops=flops, bytes_accessed=moved, transcendentals=waves)


def whole_spec(array):
    zeros = (0,) * array.ndim
    return pl.BlockSpec(array.shape, lambda i, *_: zeros)


def weight_spec(section, features):
    return pl.BlockSpec((1, features, features), lambda i, *_: (section, 0, 0))


def run_front(current, where, received, own, start, sides, back_rows, rank_rows, weights, section, targets):
    _, rows, features = current.shape
    count = where.shape[0]
    narrow = features // HALF
    row_spec = pl.BlockSpec((1, 1, rows), lambda i, where: (start + i, 0, 0))
    first_target = 9 + len(received)
    return pl.pallas_call(
        functools.partial(front_kernel, own, count),
        grid_spec=pltpu.PrefetchScalarGridSpec(
            num_scalar_prefetch=1,
            grid=(count,),
            in_specs=[
                pl.BlockSpec((1, rows, features), lambda i, where: (where[i], 0, 0)),
                row_spec,
                row_spec,
            ]
            + [weight_spec(section, features)] * 5
            + [whole_spec(array) for array in received]
            + [pl.BlockSpec(memory_space=pl.ANY)] * len(targets),
            out_specs=[
                pl.BlockSpec((1, rows, features), lambda i, where: (start + i, 0, 0)),
                pl.BlockSpec((narrow, 1, rows // 2, LANES), lambda i, where: (0, start + i, 0, 0)),
            ],
            scratch_shapes=[pltpu.VMEM((rows, features), jnp.bfloat16)],
        ),
        out_shape=[
            jax.ShapeDtypeStruct((sides, rows, features), jnp.bfloat16),
            jax.ShapeDtypeStruct((narrow, sides, rows // 2, LANES), jnp.bfloat16),
        ],
        input_output_aliases={first_target + index: index for index in range(len(targets))},
        compiler_params=params(VMEM_BYTES if section else VMEM_MOST),
        cost_estimate=cost(12 * count * rows * features**2, 8 * count * rows * features),
        name="front",
    )(where, current, back_rows, rank_rows, *weights[:5], *received, *targets)


def run_back(second, packed, where, to, start, rank_rows, weights, section, total):
    _, rows, features = second.shape
    count = where.shape[0]
    narrow = packed.shape[1]
    return pl.pallas_call(
        back_kernel,
        grid_spec=pltpu.PrefetchScalarGridSpec(
            num_scalar_prefetch=2,
            grid=(count,),
            in_specs=[
                pl.BlockSpec((1, rows, features), lambda i, *_: (start + i, 0, 0)),
                pl.BlockSpec((1, narrow, rows // 2, LANES), lambda i, where, to: (where[i], 0, 0, 0)),
                pl.BlockSpec((1, 1, rows), lambda i, *_: (start + i, 0, 0)),
            ]
            + [weight_spec(section, features)] * 3,
            out_specs=pl.BlockSpec((1, rows, features), lambda i, where, to: (to[i], 0, 0)),
        ),
        out_shape=jax.ShapeDtypeStruct((total, rows, features), jnp.bfloat16),
        compiler_params=params(),
        cost_estimate=cost(8 * count * rows * features**2, 6 * count * rows * features),
        name="back",
    )(where, to, second, packed, rank_rows, *weights[5:])


def rank_spec(entries):
    return pl.BlockSpec((1,) + entries.shape[1:], lambda i, *_: (i, 0, 0, 0))


def run_tables(places, order, position, entries, angles):
    owners = entries.shape[0]
    atoms = angles.shape[1]
    groups = atoms // GROUP
    span = GROUP * SLOTS
    return pl.pallas_call(
        table_kernel,
        grid_spec=pltpu.PrefetchScalarGridSpec(
            num_scalar_prefetch=3,
            grid=(owners,),
            in_specs=[
                rank_spec(entries),
                pl.BlockSpec((1, atoms, angles.shape[2]), lambda i, places, *_: (places[i], 0, 0)),
            ],
            out_specs=[
                rank_spec(entries),
                pl.BlockSpec((1, groups, span, span), lambda i, *_: (i, 0, 0, 0)),
            ],
        ),
        out_shape=[
            jax.ShapeDtypeStruct(entries.shape, jnp.int32),
            jax.ShapeDtypeStruct((owners, groups, span, span), jnp.bfloat16),
        ],
        compiler_params=params(),
        cost_estimate=cost(0, 8 * owners * groups * span**2),
        name="tables",
    )(places, order, position, entries, angles)


def run_mix(owner_of, place_of, order, received, rank, blocks):
    devices, sides, half, _ = received.shape
    unit = 2 * half // devices
    smem = pl.BlockSpec(memory_space=pltpu.SMEM)
    shape = (sides, devices, half, LANES)
    scratch = pltpu.VMEM((sides, devices, devices, unit, LANES), jnp.bfloat16)
    return pl.pallas_call(
        mix_kernel,
        grid=(devices,),
        in_specs=[
            smem,
            smem,
            smem,
            whole_spec(received),
            rank_spec(rank),
            pl.BlockSpec((1,) + blocks.shape[1:], lambda i: (i, 0, 0, 0)),
        ],
        out_specs=pl.BlockSpec(shape, lambda i: (0, 0, 0, 0)),
        out_shape=jax.ShapeDtypeStruct(shape, jnp.bfloat16),
        scratch_shapes=[scratch, scratch],
        compiler_params=params(),
        cost_estimate=cost(10 * devices * sides * half**2 * LANES, 16 * devices * sides * half**2),
        name="mix",
    )(owner_of, place_of, order, received, rank, blocks)


def unit_tables(entries, capacity, unit):
    owners, sides, rows = entries.shape
    ids = jnp.arange(owners, dtype=jnp.int32)
    source = entries.reshape(owners, sides * rows) // capacity
    counts = jnp.sum((source[None] == ids[:, None, None]).astype(jnp.int32), axis=2) // (unit * sides)
    before = ids[:, None] < ids[None, :]
    starts = jnp.sum(jnp.where(before[None], counts[:, :, None], 0), axis=1)
    places = jnp.sum(jnp.where(before[:, :, None], counts[:, None, :], 0), axis=0)
    inside = (starts[:, :, None] <= ids) & (ids < (starts + counts)[:, :, None])
    owner_of = jnp.sum(jnp.where(inside, ids[None, :, None], 0), axis=1)
    place_of = jnp.sum(jnp.where(inside, (places - starts)[:, :, None] + ids, 0), axis=1)
    return owner_of, place_of


def ranks(values):
    return jnp.sum((values[:, :, None] < values[:, None, :]).astype(jnp.int32), axis=1)


CHUNKS = 2


def reorder(values, order):
    hits = order[:, None] == jnp.arange(values.shape[0], dtype=jnp.int32)
    return jnp.sum(jnp.where(hits[:, :, None], values[None], 0), axis=1)


def shift(values, offset, wide):
    if offset == 0:
        return values
    return lax.ppermute(values, "wide", [(i, i ^ offset) for i in range(wide)])


def swap(values):
    return lax.all_to_all(values, "narrow", 0, 0, tiled=True)


BASE = 64


def share_lists(listed, angles, after):
    narrow = lax.axis_size("narrow")
    atoms, width = angles.shape
    digits = jnp.stack([listed // BASE, listed % BASE]).reshape(atoms, -1).astype(jnp.bfloat16)
    shared = jnp.concatenate([angles, digits], axis=1)[None]
    held = [0]
    hop = narrow // 2
    while hop:
        if hop == 1:
            shared, after = lax.optimization_barrier((shared, after))
        other = lax.ppermute(shared, "narrow", [(i, i ^ hop) for i in range(narrow)])
        shared = jnp.concatenate([shared, other], axis=0)
        held += [offset ^ hop for offset in held]
        hop //= 2
    inverse = jnp.array([held.index(offset) for offset in range(narrow)], jnp.int32)
    mine = lax.axis_index("narrow").astype(jnp.int32)
    owners = jnp.arange(narrow, dtype=jnp.int32) ^ mine
    places = jnp.sum(jnp.where(owners[:, None] == jnp.arange(narrow), inverse, 0), axis=1)
    digits = shared[:, :, width:].reshape((narrow, 2) + listed.shape).astype(jnp.int32)
    entries = digits[:, 0] * BASE + digits[:, 1]
    entries = reorder(entries.reshape(narrow, -1), places).reshape(entries.shape)
    return entries, shared, places, after


def tiled_local(messages, reverse_position, route_slot, atom_slots, angles, weights):
    wide = lax.axis_size("wide")
    narrow = lax.axis_size("narrow")
    edge_rows, features = messages.shape
    rows = edge_rows // wide
    unit = rows // narrow
    capacity = 2 * edge_rows // narrow
    atoms = angles.shape[0]
    group_id = lax.axis_index("wide").astype(jnp.int32)
    offsets = [offset for index in range(wide // 2) for offset in (index, wide - 1 - index)]
    order = group_id ^ jnp.array(offsets, jnp.int32)
    inverse = jnp.array([offsets.index(offset) for offset in range(wide)], jnp.int32)
    owners_wide = (jnp.arange(wide, dtype=jnp.int32) ^ group_id)[:, None]
    position = jnp.sum(jnp.where(owners_wide == jnp.arange(wide), inverse, 0), axis=1)
    half = wide // 2
    pieces = [(0, 1), (1, wide - 1)]
    halves = [(0, half), (half, wide - half)]

    blocks_of = messages.reshape(wide, rows, features)
    received = {
        offset: shift(lax.dynamic_index_in_dim(blocks_of, group_id ^ offset, 0, False), offset, wide)
        for offset in offsets[1:]
    }
    listed = atom_slots.reshape(atoms // GROUP, GROUP, wide, SLOTS // wide)
    listed = reorder(jnp.transpose(listed, (2, 0, 3, 1)).reshape(wide, rows), order)
    rank = reorder(ranks(route_slot.reshape(wide, rows)), order)
    back_rows = reorder(reverse_position.reshape(wide, rows), order)

    current = {start: (blocks_of, order[start : start + count]) for start, count in pieces}
    tables = None
    for section in range(BLOCKS):
        last = section == BLOCKS - 1
        targets = []
        for start, count in halves if section else pieces:
            array, where = current[start]
            needed = [received[offset] for offset in offsets[start : start + count] if offset]
            targets = run_front(
                array, where, needed, start == 0, start, wide,
                back_rows[:, None, :], rank[:, None, :], weights, section, targets,
            )
        second, packed = targets
        if tables is None:
            entries, all_angles, owner_places, packed = share_lists(listed, angles, packed)
            packed, late_rank = lax.optimization_barrier((packed, rank))
            owner_of, place_of = unit_tables(entries, capacity, unit)
            tables = run_tables(owner_places, order, position, entries[:, :, None, :], all_angles)
            partner_rank = jnp.stack(
                [shift(late_rank[place], offset, wide) for place, offset in enumerate(offsets)]
            )
            hits = back_rows[:, :, None] == jnp.arange(rows, dtype=jnp.int32)
            turned_rank = jnp.sum(jnp.where(hits, partner_rank[:, None, :], 0), axis=2)[:, None, :]
        mixed = run_mix(owner_of, place_of, order, swap(packed), *tables)
        mixed = mixed.reshape(wide * narrow, rows // 2, LANES)
        returned = lax.all_to_all(mixed, ("wide", "narrow"), 0, 0, tiled=True)
        returned = returned.reshape(wide, narrow, rows // 2, LANES)
        if last:
            current = run_back(second, returned, order, order, 0, turned_rank, weights, section, wide)
            return current.reshape(edge_rows, features)
        for start, count in halves:
            plain = jnp.arange(count, dtype=jnp.int32)
            where = order[start : start + count]
            result = run_back(second, returned, where, plain, start, turned_rank, weights, section, count)
            current[start] = (result, plain)
            for index, offset in enumerate(offsets[start : start + count]):
                if offset:
                    received[offset] = shift(result[index], offset, wide)


def local(
    messages,
    reverse_position,
    route_slot,
    atom_slots,
    angles,
    weight_message,
    weight_reverse,
    weight_combine,
    weight_inner,
    weight_outer,
    weight_lift,
    weight_expand,
    weight_reduce,
):
    weights = (
        weight_message,
        weight_reverse,
        weight_combine,
        weight_inner,
        weight_outer,
        weight_lift,
        weight_expand,
        weight_reduce,
    )
    wide = lax.axis_size("wide")
    narrow = lax.axis_size("narrow")
    edge_rows, features = messages.shape
    unit = edge_rows // wide // narrow
    fits = (
        features == narrow * HALF
        and unit % 16 == 0
        and narrow % 2 == 0
        and wide >= 4
        and wide & (wide - 1) == 0
        and narrow & (narrow - 1) == 0
        and angles.shape[0] % GROUP == 0
        and (SLOTS // wide * GROUP) % 16 == 0
    )
    run = tiled_local if fits else general_local
    return run(messages, reverse_position, route_slot, atom_slots, angles, weights)


def solution(mesh):
    in_specs = (
        P(("wide", "narrow"), None),
        P(("wide", "narrow")),
        P(("wide", "narrow")),
        P(("wide", "narrow")),
        P(("wide", "narrow"), None),
        P(),
        P(),
        P(),
        P(),
        P(),
        P(),
        P(),
        P(),
    )
    out_specs = P(("wide", "narrow"), None)
    return jax.shard_map(local, mesh=mesh, in_specs=in_specs, out_specs=out_specs, check_vma=False)
```

```python
import functools

import jax
import jax.numpy as jnp
from jax import lax
from jax.experimental import pallas as pl
from jax.experimental.pallas import tpu as pltpu
from jax.sharding import PartitionSpec as P

SLOTS = 32
BLOCKS = 2
LANES = 128
HALF = LANES // 2
GROUP = 8


ROOT_HALF = 0.7071067811865476


def project(operand, weight):
    return jnp.dot(operand, weight, preferred_element_type=jnp.float32)


def residual(previous, branch):
    return ((previous.astype(jnp.float32) + branch) * ROOT_HALF).astype(jnp.bfloat16)


def reverse_edges(values, partner_rows):
    exchanged = lax.all_to_all(values, "wide", split_axis=0, concat_axis=0, tiled=True)
    return jnp.take(exchanged, partner_rows, axis=0)


def edge_front(current, reverse, weights, section_index):
    hidden = jax.nn.silu(
        project(current, weights[0][section_index]) + project(reverse, weights[1][section_index])
    ).astype(jnp.bfloat16)
    first_res = residual(current, project(hidden, weights[2][section_index]))
    inner_value = jax.nn.silu(project(first_res, weights[3][section_index])).astype(jnp.bfloat16)
    return residual(first_res, jax.nn.silu(project(inner_value, weights[4][section_index])))


def edge_back(second, turned, weights, section_index):
    third_res = residual(second, jax.nn.silu(project(turned, weights[5][section_index])))
    expand = jax.nn.silu(project(third_res, weights[6][section_index])).astype(jnp.bfloat16)
    return residual(third_res, jax.nn.silu(project(expand, weights[7][section_index])))


def owners_mix(second, route_slot, atom_slots, mixing):
    features = second.shape[1]
    buffer_rows = 2 * second.shape[0]
    outgoing = jnp.zeros((buffer_rows, features), jnp.bfloat16).at[route_slot].set(second)
    received = lax.all_to_all(outgoing, "narrow", split_axis=0, concat_axis=0, tiled=True)
    gathered = jnp.take(received, atom_slots, axis=0).reshape(mixing.shape[0], SLOTS, features)
    mixed_rows = jnp.einsum(
        "apq,aqd->apd", mixing, gathered, preferred_element_type=jnp.float32
    ).astype(jnp.bfloat16)
    return mixed_rows.reshape(-1, features)


def back_to_edges(mixed_flat, route_slot, atom_slots):
    features = mixed_flat.shape[1]
    buffer_rows = 2 * route_slot.shape[0]
    answer = jnp.zeros((buffer_rows, features), jnp.bfloat16).at[atom_slots].set(mixed_flat)
    incoming = lax.all_to_all(answer, "narrow", split_axis=0, concat_axis=0, tiled=True)
    return jnp.take(incoming, route_slot, axis=0)


def general_local(messages, reverse_position, route_slot, atom_slots, angles, weights):
    edge_rows = messages.shape[0]
    sub_rows = edge_rows // lax.axis_size("wide")
    partner_rows = jnp.arange(edge_rows, dtype=jnp.int32) // sub_rows * sub_rows + reverse_position
    mixing = angles.reshape(angles.shape[0], SLOTS, SLOTS)
    current = messages
    for section_index in range(BLOCKS):
        reverse = reverse_edges(current, partner_rows)
        second = edge_front(current, reverse, weights, section_index)
        mixed_flat = owners_mix(second, route_slot, atom_slots, mixing)
        returned = back_to_edges(mixed_flat, route_slot, atom_slots)
        turned = reverse_edges(returned, partner_rows)
        current = edge_back(second, turned, weights, section_index)
    return current


def silu(value):
    return 0.5 * value * (1.0 + jnp.tanh(0.5 * value))


def dot(left, right):
    return jnp.dot(left, right, preferred_element_type=jnp.float32)


def halve(previous, branch):
    return ((previous.astype(jnp.float32) + branch) * ROOT_HALF).astype(jnp.bfloat16)


def iotas(size):
    shape = (size, size)
    return lax.broadcasted_iota(jnp.int32, shape, 0), lax.broadcasted_iota(jnp.int32, shape, 1)


def as_column(row, rows_iota, lanes_iota):
    return jnp.sum(jnp.where(rows_iota == lanes_iota, row, 0), axis=1, keepdims=True)


def one_hot(mask):
    return jnp.where(mask, 1.0, 0.0).astype(jnp.bfloat16)


def front_kernel(own, count, where_ref, cur_ref, back_ref, rank_ref, wm, wr, wc, wi, wo, *refs):
    recv_refs, (second_ref, packed_ref, reverse_ref) = refs[: count - own], refs[-3:]
    rows_iota, lanes_iota = iotas(cur_ref.shape[1])
    partner = as_column(back_ref[0], rows_iota, lanes_iota)
    hot = one_hot(partner == lanes_iota)
    sources = ([cur_ref.at[0]] if own else []) + list(recv_refs)
    for index in range(count):

        @pl.when(pl.program_id(0) == index)
        def _():
            reverse_ref[...] = dot(hot, sources[index][...]).astype(jnp.bfloat16)

    current = cur_ref[0]
    hidden = silu(dot(current, wm[0]) + dot(reverse_ref[...], wr[0])).astype(jnp.bfloat16)
    first_res = halve(current, dot(hidden, wc[0]))
    inner = silu(dot(first_res, wi[0])).astype(jnp.bfloat16)
    second = halve(first_res, silu(dot(inner, wo[0])))
    second_ref[0] = second
    ordered = dot(one_hot(rows_iota == rank_ref[0]), second)
    half = ordered.shape[0] // 2
    low = lax.broadcasted_iota(jnp.int32, (half, LANES), 1) < HALF
    for tile in range(ordered.shape[1] // LANES):
        top = ordered[:half, tile * LANES : (tile + 1) * LANES]
        bottom = ordered[half:, tile * LANES : (tile + 1) * LANES]
        packed_ref[2 * tile, 0] = jnp.where(low, top, pltpu.roll(bottom, HALF, 1)).astype(jnp.bfloat16)
        packed_ref[2 * tile + 1, 0] = jnp.where(low, pltpu.roll(top, HALF, 1), bottom).astype(jnp.bfloat16)


def back_kernel(from_ref, to_ref, second_ref, packed_ref, rank_ref, weights_ref, out_ref):
    rows_iota, lanes_iota = iotas(second_ref.shape[1])
    half = rows_iota.shape[0] // 2
    low = lax.broadcasted_iota(jnp.int32, (half, LANES), 1) < HALF
    tops, bottoms = [], []
    for tile in range(second_ref.shape[2] // LANES):
        even = packed_ref[0, 2 * tile].astype(jnp.float32)
        odd = packed_ref[0, 2 * tile + 1].astype(jnp.float32)
        tops.append(jnp.where(low, even, pltpu.roll(odd, HALF, 1)).astype(jnp.bfloat16))
        bottoms.append(jnp.where(low, pltpu.roll(even, HALF, 1), odd).astype(jnp.bfloat16))
    ordered = jnp.concatenate(
        [jnp.concatenate(tops, axis=1), jnp.concatenate(bottoms, axis=1)], axis=0
    )
    source = as_column(rank_ref[0], rows_iota, lanes_iota)
    turned = dot(one_hot(source == lanes_iota), ordered).astype(jnp.bfloat16)
    third_res = halve(second_ref[0], silu(dot(turned, weights_ref[0])))
    expand = silu(dot(third_res, weights_ref[1])).astype(jnp.bfloat16)
    out_ref[0] = halve(third_res, silu(dot(expand, weights_ref[2])))


def table_kernel(places_ref, order_ref, position_ref, entry_ref, angles_ref, rank_ref, blocks_ref):
    sides, _, size = entry_ref.shape[1:]
    rows_iota, lanes_iota = iotas(size)
    for side in range(sides):
        row = entry_ref[0, side]
        column = as_column(row, rows_iota, lanes_iota)
        rank_ref[0, side] = jnp.sum(jnp.where(column < row, 1, 0), axis=0, keepdims=True)
    span = GROUP * SLOTS
    strip = span // sides
    rows_iota, lanes_iota = iotas(span)
    own = rows_iota % GROUP == lanes_iota % GROUP
    spread_rows = lax.broadcasted_iota(jnp.int32, (SLOTS, span), 0)
    spread_lanes = lax.broadcasted_iota(jnp.int32, (SLOTS, span), 1)
    side_at = jnp.zeros((SLOTS, span), jnp.int32)
    for place in range(sides):
        side_at = jnp.where(spread_lanes // strip == place, order_ref[place], side_at)
    spread = one_hot(side_at * (SLOTS // sides) + spread_lanes % strip // GROUP == spread_rows)
    for group in range(angles_ref.shape[1] // GROUP):
        local = angles_ref[0, group * GROUP : (group + 1) * GROUP, :].astype(jnp.float32)
        stacked = jnp.concatenate(
            [local[:, p * SLOTS : (p + 1) * SLOTS] for p in range(SLOTS)], axis=0
        ).astype(jnp.bfloat16)
        block = jnp.where(own, dot(stacked, spread), 0.0).astype(jnp.bfloat16)
        for side in range(sides):
            to = pl.multiple_of(position_ref[side] * strip, strip)
            blocks_ref[0, group, pl.ds(to, strip), :] = block[side * strip : (side + 1) * strip]


def mix_kernel(owner_ref, place_ref, order_ref, recv_ref, rank_ref, blocks_ref, out_ref, ins, outs):
    step = pl.program_id(0)
    devices, sides = recv_ref.shape[:2]
    unit = ins.shape[3]
    rows = devices * unit
    groups = blocks_ref.shape[1]
    strip = blocks_ref.shape[2] // sides
    pairs = devices // 2

    @pl.when(step == 0)
    def _():
        @pl.loop(0, devices)
        def _(source):
            for index in range(devices):
                owner = owner_ref[source, index]
                place = place_ref[source, index]
                at = (index % pairs) * unit
                for side in range(sides):
                    block = recv_ref[source, side, at : at + unit, :]
                    if index >= pairs:
                        block = pltpu.roll(block.astype(jnp.float32), HALF, 1).astype(jnp.bfloat16)
                    ins[side, owner, place] = block

    rows_iota, lanes_iota = iotas(rows)
    gathered = []
    for side in range(sides):
        source = as_column(rank_ref[0, side], rows_iota, lanes_iota)
        operand = ins[side, step].reshape(rows, LANES)
        gathered.append(dot(one_hot(source == lanes_iota), operand).astype(jnp.bfloat16))
    mixed = []
    for group in range(groups):
        operand = jnp.concatenate(
            [part[group * strip : (group + 1) * strip] for part in gathered], axis=0
        )
        mixed.append(dot(blocks_ref[0, group], operand).astype(jnp.bfloat16))
    for side in range(sides):
        operand = jnp.concatenate(
            [part[side * strip : (side + 1) * strip] for part in mixed], axis=0
        )
        outs[side, step] = (
            dot(one_hot(rows_iota == rank_ref[0, side]), operand)
            .astype(jnp.bfloat16)
            .reshape(devices, unit, LANES)
        )

    @pl.when(step == pl.num_programs(0) - 1)
    def _():
        low = lax.broadcasted_iota(jnp.int32, (unit, LANES), 1) < HALF

        @pl.loop(0, devices)
        def _(source):
            for index in range(pairs):
                owner = owner_ref[source, index]
                place = place_ref[source, index]
                owner_far = owner_ref[source, index + pairs]
                place_far = place_ref[source, index + pairs]
                for side in range(sides):
                    near = outs[side, owner, place].astype(jnp.float32)
                    far = outs[side, owner_far, place_far].astype(jnp.float32)
                    joined = jnp.where(low, near, pltpu.roll(far, HALF, 1)).astype(jnp.bfloat16)
                    out_ref[order_ref[side], source, index * unit : (index + 1) * unit, :] = joined


VMEM_BYTES = 24 * 1024 * 1024
VMEM_MOST = 60 * 1024 * 1024


def params(limit=VMEM_BYTES):
    return pltpu.CompilerParams(vmem_limit_bytes=limit)


def cost(flops, moved, waves=0):
    return pl.CostEstimate(flops=flops, bytes_accessed=moved, transcendentals=waves)


def whole_spec(array):
    zeros = (0,) * array.ndim
    return pl.BlockSpec(array.shape, lambda i, *_: zeros)


def weight_spec(section, features):
    return pl.BlockSpec((1, features, features), lambda i, *_: (section, 0, 0))


def run_front(current, where, received, own, start, sides, back_rows, rank_rows, weights, section, targets):
    _, rows, features = current.shape
    count = where.shape[0]
    narrow = features // HALF
    row_spec = pl.BlockSpec((1, 1, rows), lambda i, where: (start + i, 0, 0))
    first_target = 9 + len(received)
    return pl.pallas_call(
        functools.partial(front_kernel, own, count),
        grid_spec=pltpu.PrefetchScalarGridSpec(
            num_scalar_prefetch=1,
            grid=(count,),
            in_specs=[
                pl.BlockSpec((1, rows, features), lambda i, where: (where[i], 0, 0)),
                row_spec,
                row_spec,
            ]
            + [weight_spec(section, features)] * 5
            + [whole_spec(array) for array in received]
            + [pl.BlockSpec(memory_space=pl.ANY)] * len(targets),
            out_specs=[
                pl.BlockSpec((1, rows, features), lambda i, where: (start + i, 0, 0)),
                pl.BlockSpec((narrow, 1, rows // 2, LANES), lambda i, where: (0, start + i, 0, 0)),
            ],
            scratch_shapes=[pltpu.VMEM((rows, features), jnp.bfloat16)],
        ),
        out_shape=[
            jax.ShapeDtypeStruct((sides, rows, features), jnp.bfloat16),
            jax.ShapeDtypeStruct((narrow, sides, rows // 2, LANES), jnp.bfloat16),
        ],
        input_output_aliases={first_target + index: index for index in range(len(targets))},
        compiler_params=params(VMEM_BYTES if section else VMEM_MOST),
        cost_estimate=cost(12 * count * rows * features**2, 8 * count * rows * features),
        name="front",
    )(where, current, back_rows, rank_rows, *weights[:5], *received, *targets)


def run_back(second, packed, where, to, start, rank_rows, stacked, total):
    _, rows, features = second.shape
    count = where.shape[0]
    narrow = packed.shape[1]
    return pl.pallas_call(
        back_kernel,
        grid_spec=pltpu.PrefetchScalarGridSpec(
            num_scalar_prefetch=2,
            grid=(count,),
            in_specs=[
                pl.BlockSpec((1, rows, features), lambda i, *_: (start + i, 0, 0)),
                pl.BlockSpec((1, narrow, rows // 2, LANES), lambda i, where, to: (where[i], 0, 0, 0)),
                pl.BlockSpec((1, 1, rows), lambda i, *_: (start + i, 0, 0)),
                whole_spec(stacked),
            ],
            out_specs=pl.BlockSpec((1, rows, features), lambda i, where, to: (to[i], 0, 0)),
        ),
        out_shape=jax.ShapeDtypeStruct((total, rows, features), jnp.bfloat16),
        compiler_params=params(),
        cost_estimate=cost(8 * count * rows * features**2, 6 * count * rows * features),
        name="back",
    )(where, to, second, packed, rank_rows, stacked)


def rank_spec(entries):
    return pl.BlockSpec((1,) + entries.shape[1:], lambda i, *_: (i, 0, 0, 0))


def run_tables(places, order, position, entries, angles):
    owners = entries.shape[0]
    atoms = angles.shape[1]
    groups = atoms // GROUP
    span = GROUP * SLOTS
    return pl.pallas_call(
        table_kernel,
        grid_spec=pltpu.PrefetchScalarGridSpec(
            num_scalar_prefetch=3,
            grid=(owners,),
            in_specs=[
                rank_spec(entries),
                pl.BlockSpec((1, atoms, angles.shape[2]), lambda i, places, *_: (places[i], 0, 0)),
            ],
            out_specs=[
                rank_spec(entries),
                pl.BlockSpec((1, groups, span, span), lambda i, *_: (i, 0, 0, 0)),
            ],
        ),
        out_shape=[
            jax.ShapeDtypeStruct(entries.shape, jnp.int32),
            jax.ShapeDtypeStruct((owners, groups, span, span), jnp.bfloat16),
        ],
        compiler_params=params(),
        cost_estimate=cost(0, 8 * owners * groups * span**2),
        name="tables",
    )(places, order, position, entries, angles)


def run_mix(owner_of, place_of, order, received, rank, blocks):
    devices, sides, half, _ = received.shape
    unit = 2 * half // devices
    smem = pl.BlockSpec(memory_space=pltpu.SMEM)
    shape = (sides, devices, half, LANES)
    scratch = pltpu.VMEM((sides, devices, devices, unit, LANES), jnp.bfloat16)
    return pl.pallas_call(
        mix_kernel,
        grid=(devices,),
        in_specs=[
            smem,
            smem,
            smem,
            whole_spec(received),
            rank_spec(rank),
            pl.BlockSpec((1,) + blocks.shape[1:], lambda i: (i, 0, 0, 0)),
        ],
        out_specs=pl.BlockSpec(shape, lambda i: (0, 0, 0, 0)),
        out_shape=jax.ShapeDtypeStruct(shape, jnp.bfloat16),
        scratch_shapes=[scratch, scratch],
        compiler_params=params(),
        cost_estimate=cost(10 * devices * sides * half**2 * LANES, 16 * devices * sides * half**2),
        name="mix",
    )(owner_of, place_of, order, received, rank, blocks)


def unit_tables(entries, capacity, unit):
    owners, sides, rows = entries.shape
    ids = jnp.arange(owners, dtype=jnp.int32)
    source = entries.reshape(owners, sides * rows) // capacity
    counts = jnp.sum((source[None] == ids[:, None, None]).astype(jnp.int32), axis=2) // (unit * sides)
    before = ids[:, None] < ids[None, :]
    starts = jnp.sum(jnp.where(before[None], counts[:, :, None], 0), axis=1)
    places = jnp.sum(jnp.where(before[:, :, None], counts[:, None, :], 0), axis=0)
    inside = (starts[:, :, None] <= ids) & (ids < (starts + counts)[:, :, None])
    owner_of = jnp.sum(jnp.where(inside, ids[None, :, None], 0), axis=1)
    place_of = jnp.sum(jnp.where(inside, (places - starts)[:, :, None] + ids, 0), axis=1)
    return owner_of, place_of


def ranks(values):
    return jnp.sum((values[:, :, None] < values[:, None, :]).astype(jnp.int32), axis=1)


CHUNKS = 2


def reorder(values, order):
    hits = order[:, None] == jnp.arange(values.shape[0], dtype=jnp.int32)
    return jnp.sum(jnp.where(hits[:, :, None], values[None], 0), axis=1)


def shift(values, offset, wide):
    if offset == 0:
        return values
    return lax.ppermute(values, "wide", [(i, i ^ offset) for i in range(wide)])


def swap(values):
    return lax.all_to_all(values, "narrow", 0, 0, tiled=True)


BASE = 64


def share_lists(listed, angles, after):
    narrow = lax.axis_size("narrow")
    atoms, width = angles.shape
    digits = jnp.stack([listed // BASE, listed % BASE]).reshape(atoms, -1).astype(jnp.bfloat16)
    shared = jnp.concatenate([angles, digits], axis=1)[None]
    held = [0]
    hop = narrow // 2
    while hop:
        if hop == 1:
            shared, after = lax.optimization_barrier((shared, after))
        other = lax.ppermute(shared, "narrow", [(i, i ^ hop) for i in range(narrow)])
        shared = jnp.concatenate([shared, other], axis=0)
        held += [offset ^ hop for offset in held]
        hop //= 2
    inverse = jnp.array([held.index(offset) for offset in range(narrow)], jnp.int32)
    mine = lax.axis_index("narrow").astype(jnp.int32)
    owners = jnp.arange(narrow, dtype=jnp.int32) ^ mine
    places = jnp.sum(jnp.where(owners[:, None] == jnp.arange(narrow), inverse, 0), axis=1)
    digits = shared[:, :, width:].reshape((narrow, 2) + listed.shape).astype(jnp.int32)
    entries = digits[:, 0] * BASE + digits[:, 1]
    entries = reorder(entries.reshape(narrow, -1), places).reshape(entries.shape)
    return entries, shared, places, after


def tiled_local(messages, reverse_position, route_slot, atom_slots, angles, weights):
    wide = lax.axis_size("wide")
    narrow = lax.axis_size("narrow")
    edge_rows, features = messages.shape
    rows = edge_rows // wide
    unit = rows // narrow
    capacity = 2 * edge_rows // narrow
    atoms = angles.shape[0]
    group_id = lax.axis_index("wide").astype(jnp.int32)
    offsets = [offset for index in range(wide // 2) for offset in (index, wide - 1 - index)]
    order = group_id ^ jnp.array(offsets, jnp.int32)
    inverse = jnp.array([offsets.index(offset) for offset in range(wide)], jnp.int32)
    owners_wide = (jnp.arange(wide, dtype=jnp.int32) ^ group_id)[:, None]
    position = jnp.sum(jnp.where(owners_wide == jnp.arange(wide), inverse, 0), axis=1)
    half = wide // 2
    pieces = [(0, 1), (1, wide - 1)]
    halves = [(0, half), (half, wide - half)]

    blocks_of = messages.reshape(wide, rows, features)
    received = {
        offset: shift(lax.dynamic_index_in_dim(blocks_of, group_id ^ offset, 0, False), offset, wide)
        for offset in offsets[1:]
    }
    rank = reorder(ranks(route_slot.reshape(wide, rows)), order)
    back_rows = reorder(reverse_position.reshape(wide, rows), order)

    current = {start: (blocks_of, order[start : start + count]) for start, count in pieces}
    tables = None
    for section in range(BLOCKS):
        last = section == BLOCKS - 1
        targets = []
        for start, count in halves if section else pieces:
            array, where = current[start]
            needed = [received[offset] for offset in offsets[start : start + count] if offset]
            targets = list(run_front(
                array, where, needed, start == 0, start, wide,
                back_rows[:, None, :], rank[:, None, :], weights, section, targets,
            ))
            if tables is None and start == 0:
                listed, targets[0] = lax.optimization_barrier((atom_slots, targets[0]))
                listed = listed.reshape(atoms // GROUP, GROUP, wide, SLOTS // wide)
                listed = reorder(jnp.transpose(listed, (2, 0, 3, 1)).reshape(wide, rows), order)
        second, packed = targets
        if tables is None:
            entries, all_angles, owner_places, packed = share_lists(listed, angles, packed)
            packed, late_rank = lax.optimization_barrier((packed, rank))
            owner_of, place_of = unit_tables(entries, capacity, unit)
            tables = run_tables(owner_places, order, position, entries[:, :, None, :], all_angles)
            partner_rank = jnp.stack(
                [shift(late_rank[place], offset, wide) for place, offset in enumerate(offsets)]
            )
            hits = back_rows[:, :, None] == jnp.arange(rows, dtype=jnp.int32)
            turned_rank = jnp.sum(jnp.where(hits, partner_rank[:, None, :], 0), axis=2)[:, None, :]
        mixed = run_mix(owner_of, place_of, order, swap(packed), *tables)
        mixed, *late = lax.optimization_barrier((mixed, *weights[5:]))
        stacked = jnp.stack([weight[section] for weight in late])
        mixed = mixed.reshape(wide * narrow, rows // 2, LANES)
        returned = lax.all_to_all(mixed, ("wide", "narrow"), 0, 0, tiled=True)
        returned = returned.reshape(wide, narrow, rows // 2, LANES)
        if last:
            current = run_back(second, returned, order, order, 0, turned_rank, stacked, wide)
            return current.reshape(edge_rows, features)
        for start, count in halves:
            plain = jnp.arange(count, dtype=jnp.int32)
            where = order[start : start + count]
            result = run_back(second, returned, where, plain, start, turned_rank, stacked, count)
            current[start] = (result, plain)
            for index, offset in enumerate(offsets[start : start + count]):
                if offset:
                    received[offset] = shift(result[index], offset, wide)


def local(
    messages,
    reverse_position,
    route_slot,
    atom_slots,
    angles,
    weight_message,
    weight_reverse,
    weight_combine,
    weight_inner,
    weight_outer,
    weight_lift,
    weight_expand,
    weight_reduce,
):
    weights = (
        weight_message,
        weight_reverse,
        weight_combine,
        weight_inner,
        weight_outer,
        weight_lift,
        weight_expand,
        weight_reduce,
    )
    wide = lax.axis_size("wide")
    narrow = lax.axis_size("narrow")
    edge_rows, features = messages.shape
    unit = edge_rows // wide // narrow
    fits = (
        features == narrow * HALF
        and unit % 16 == 0
        and narrow % 2 == 0
        and wide >= 4
        and wide & (wide - 1) == 0
        and narrow & (narrow - 1) == 0
        and angles.shape[0] % GROUP == 0
        and (SLOTS // wide * GROUP) % 16 == 0
    )
    run = tiled_local if fits else general_local
    return run(messages, reverse_position, route_slot, atom_slots, angles, weights)


def solution(mesh):
    in_specs = (
        P(("wide", "narrow"), None),
        P(("wide", "narrow")),
        P(("wide", "narrow")),
        P(("wide", "narrow")),
        P(("wide", "narrow"), None),
        P(),
        P(),
        P(),
        P(),
        P(),
        P(),
        P(),
        P(),
    )
    out_specs = P(("wide", "narrow"), None)
    return jax.shard_map(local, mesh=mesh, in_specs=in_specs, out_specs=out_specs, check_vma=False)
```

```python
import functools

import jax
import jax.numpy as jnp
from jax import lax
from jax.experimental import pallas as pl
from jax.experimental.pallas import tpu as pltpu
from jax.sharding import PartitionSpec as P

SLOTS = 32
BLOCKS = 2
LANES = 128
HALF = LANES // 2
GROUP = 8


ROOT_HALF = 0.7071067811865476


def project(operand, weight):
    return jnp.dot(operand, weight, preferred_element_type=jnp.float32)


def residual(previous, branch):
    return ((previous.astype(jnp.float32) + branch) * ROOT_HALF).astype(jnp.bfloat16)


def reverse_edges(values, partner_rows):
    exchanged = lax.all_to_all(values, "wide", split_axis=0, concat_axis=0, tiled=True)
    return jnp.take(exchanged, partner_rows, axis=0)


def edge_front(current, reverse, weights, section_index):
    hidden = jax.nn.silu(
        project(current, weights[0][section_index]) + project(reverse, weights[1][section_index])
    ).astype(jnp.bfloat16)
    first_res = residual(current, project(hidden, weights[2][section_index]))
    inner_value = jax.nn.silu(project(first_res, weights[3][section_index])).astype(jnp.bfloat16)
    return residual(first_res, jax.nn.silu(project(inner_value, weights[4][section_index])))


def edge_back(second, turned, weights, section_index):
    third_res = residual(second, jax.nn.silu(project(turned, weights[5][section_index])))
    expand = jax.nn.silu(project(third_res, weights[6][section_index])).astype(jnp.bfloat16)
    return residual(third_res, jax.nn.silu(project(expand, weights[7][section_index])))


def owners_mix(second, route_slot, atom_slots, mixing):
    features = second.shape[1]
    buffer_rows = 2 * second.shape[0]
    outgoing = jnp.zeros((buffer_rows, features), jnp.bfloat16).at[route_slot].set(second)
    received = lax.all_to_all(outgoing, "narrow", split_axis=0, concat_axis=0, tiled=True)
    gathered = jnp.take(received, atom_slots, axis=0).reshape(mixing.shape[0], SLOTS, features)
    mixed_rows = jnp.einsum(
        "apq,aqd->apd", mixing, gathered, preferred_element_type=jnp.float32
    ).astype(jnp.bfloat16)
    return mixed_rows.reshape(-1, features)


def back_to_edges(mixed_flat, route_slot, atom_slots):
    features = mixed_flat.shape[1]
    buffer_rows = 2 * route_slot.shape[0]
    answer = jnp.zeros((buffer_rows, features), jnp.bfloat16).at[atom_slots].set(mixed_flat)
    incoming = lax.all_to_all(answer, "narrow", split_axis=0, concat_axis=0, tiled=True)
    return jnp.take(incoming, route_slot, axis=0)


def general_local(messages, reverse_position, route_slot, atom_slots, angles, weights):
    edge_rows = messages.shape[0]
    sub_rows = edge_rows // lax.axis_size("wide")
    partner_rows = jnp.arange(edge_rows, dtype=jnp.int32) // sub_rows * sub_rows + reverse_position
    mixing = angles.reshape(angles.shape[0], SLOTS, SLOTS)
    current = messages
    for section_index in range(BLOCKS):
        reverse = reverse_edges(current, partner_rows)
        second = edge_front(current, reverse, weights, section_index)
        mixed_flat = owners_mix(second, route_slot, atom_slots, mixing)
        returned = back_to_edges(mixed_flat, route_slot, atom_slots)
        turned = reverse_edges(returned, partner_rows)
        current = edge_back(second, turned, weights, section_index)
    return current


def silu(value):
    return 0.5 * value * (1.0 + jnp.tanh(0.5 * value))


def dot(left, right):
    return jnp.dot(left, right, preferred_element_type=jnp.float32)


def halve(previous, branch):
    return ((previous.astype(jnp.float32) + branch) * ROOT_HALF).astype(jnp.bfloat16)


def iotas(size):
    shape = (size, size)
    return lax.broadcasted_iota(jnp.int32, shape, 0), lax.broadcasted_iota(jnp.int32, shape, 1)


def as_column(row, rows_iota, lanes_iota):
    return jnp.sum(jnp.where(rows_iota == lanes_iota, row, 0), axis=1, keepdims=True)


def one_hot(mask):
    return jnp.where(mask, 1.0, 0.0).astype(jnp.bfloat16)


def front_kernel(own, count, where_ref, cur_ref, back_ref, rank_ref, wm, wr, wc, wi, wo, *refs):
    recv_refs, (second_ref, packed_ref, reverse_ref) = refs[: count - own], refs[-3:]
    rows_iota, lanes_iota = iotas(cur_ref.shape[1])
    partner = as_column(back_ref[0], rows_iota, lanes_iota)
    hot = one_hot(partner == lanes_iota)
    sources = ([cur_ref.at[0]] if own else []) + list(recv_refs)
    for index in range(count):

        @pl.when(pl.program_id(0) == index)
        def _():
            reverse_ref[...] = dot(hot, sources[index][...]).astype(jnp.bfloat16)

    current = cur_ref[0]
    hidden = silu(dot(current, wm[0]) + dot(reverse_ref[...], wr[0])).astype(jnp.bfloat16)
    first_res = halve(current, dot(hidden, wc[0]))
    inner = silu(dot(first_res, wi[0])).astype(jnp.bfloat16)
    second = halve(first_res, silu(dot(inner, wo[0])))
    second_ref[0] = second
    ordered = dot(one_hot(rows_iota == rank_ref[0]), second)
    half = ordered.shape[0] // 2
    low = lax.broadcasted_iota(jnp.int32, (half, LANES), 1) < HALF
    for tile in range(ordered.shape[1] // LANES):
        top = ordered[:half, tile * LANES : (tile + 1) * LANES]
        bottom = ordered[half:, tile * LANES : (tile + 1) * LANES]
        packed_ref[2 * tile, 0] = jnp.where(low, top, pltpu.roll(bottom, HALF, 1)).astype(jnp.bfloat16)
        packed_ref[2 * tile + 1, 0] = jnp.where(low, pltpu.roll(top, HALF, 1), bottom).astype(jnp.bfloat16)


def back_kernel(from_ref, to_ref, second_ref, packed_ref, rank_ref, wl, we, wd, out_ref):
    rows_iota, lanes_iota = iotas(second_ref.shape[1])
    half = rows_iota.shape[0] // 2
    low = lax.broadcasted_iota(jnp.int32, (half, LANES), 1) < HALF
    tops, bottoms = [], []
    for tile in range(second_ref.shape[2] // LANES):
        even = packed_ref[0, 2 * tile].astype(jnp.float32)
        odd = packed_ref[0, 2 * tile + 1].astype(jnp.float32)
        tops.append(jnp.where(low, even, pltpu.roll(odd, HALF, 1)).astype(jnp.bfloat16))
        bottoms.append(jnp.where(low, pltpu.roll(even, HALF, 1), odd).astype(jnp.bfloat16))
    ordered = jnp.concatenate(
        [jnp.concatenate(tops, axis=1), jnp.concatenate(bottoms, axis=1)], axis=0
    )
    source = as_column(rank_ref[0], rows_iota, lanes_iota)
    turned = dot(one_hot(source == lanes_iota), ordered).astype(jnp.bfloat16)
    third_res = halve(second_ref[0], silu(dot(turned, wl[0])))
    expand = silu(dot(third_res, we[0])).astype(jnp.bfloat16)
    out_ref[0] = halve(third_res, silu(dot(expand, wd[0])))


def table_kernel(places_ref, order_ref, position_ref, entry_ref, angles_ref, rank_ref, blocks_ref):
    sides, _, size = entry_ref.shape[1:]
    rows_iota, lanes_iota = iotas(size)
    for side in range(sides):
        row = entry_ref[0, side]
        column = as_column(row, rows_iota, lanes_iota)
        rank_ref[0, side] = jnp.sum(jnp.where(column < row, 1, 0), axis=0, keepdims=True)
    span = GROUP * SLOTS
    strip = span // sides
    rows_iota, lanes_iota = iotas(span)
    own = rows_iota % GROUP == lanes_iota % GROUP
    spread_rows = lax.broadcasted_iota(jnp.int32, (SLOTS, span), 0)
    spread_lanes = lax.broadcasted_iota(jnp.int32, (SLOTS, span), 1)
    side_at = jnp.zeros((SLOTS, span), jnp.int32)
    for place in range(sides):
        side_at = jnp.where(spread_lanes // strip == place, order_ref[place], side_at)
    spread = one_hot(side_at * (SLOTS // sides) + spread_lanes % strip // GROUP == spread_rows)
    for group in range(angles_ref.shape[1] // GROUP):
        local = angles_ref[0, group * GROUP : (group + 1) * GROUP, :].astype(jnp.float32)
        stacked = jnp.concatenate(
            [local[:, p * SLOTS : (p + 1) * SLOTS] for p in range(SLOTS)], axis=0
        ).astype(jnp.bfloat16)
        block = jnp.where(own, dot(stacked, spread), 0.0).astype(jnp.bfloat16)
        for side in range(sides):
            to = pl.multiple_of(position_ref[side] * strip, strip)
            blocks_ref[0, group, pl.ds(to, strip), :] = block[side * strip : (side + 1) * strip]


def mix_kernel(owner_ref, place_ref, order_ref, recv_ref, rank_ref, blocks_ref, out_ref, ins, outs):
    step = pl.program_id(0)
    devices, sides = recv_ref.shape[:2]
    unit = ins.shape[3]
    rows = devices * unit
    groups = blocks_ref.shape[1]
    strip = blocks_ref.shape[2] // sides
    pairs = devices // 2

    @pl.when(step == 0)
    def _():
        @pl.loop(0, devices)
        def _(source):
            for index in range(devices):
                owner = owner_ref[source, index]
                place = place_ref[source, index]
                at = (index % pairs) * unit
                for side in range(sides):
                    block = recv_ref[source, side, at : at + unit, :]
                    if index >= pairs:
                        block = pltpu.roll(block.astype(jnp.float32), HALF, 1).astype(jnp.bfloat16)
                    ins[side, owner, place] = block

    rows_iota, lanes_iota = iotas(rows)
    gathered = []
    for side in range(sides):
        source = as_column(rank_ref[0, side], rows_iota, lanes_iota)
        operand = ins[side, step].reshape(rows, LANES)
        gathered.append(dot(one_hot(source == lanes_iota), operand).astype(jnp.bfloat16))
    mixed = []
    for group in range(groups):
        operand = jnp.concatenate(
            [part[group * strip : (group + 1) * strip] for part in gathered], axis=0
        )
        mixed.append(dot(blocks_ref[0, group], operand).astype(jnp.bfloat16))
    for side in range(sides):
        operand = jnp.concatenate(
            [part[side * strip : (side + 1) * strip] for part in mixed], axis=0
        )
        outs[side, step] = (
            dot(one_hot(rows_iota == rank_ref[0, side]), operand)
            .astype(jnp.bfloat16)
            .reshape(devices, unit, LANES)
        )

    @pl.when(step == pl.num_programs(0) - 1)
    def _():
        low = lax.broadcasted_iota(jnp.int32, (unit, LANES), 1) < HALF

        @pl.loop(0, devices)
        def _(source):
            for index in range(pairs):
                owner = owner_ref[source, index]
                place = place_ref[source, index]
                owner_far = owner_ref[source, index + pairs]
                place_far = place_ref[source, index + pairs]
                for side in range(sides):
                    near = outs[side, owner, place].astype(jnp.float32)
                    far = outs[side, owner_far, place_far].astype(jnp.float32)
                    joined = jnp.where(low, near, pltpu.roll(far, HALF, 1)).astype(jnp.bfloat16)
                    out_ref[order_ref[side], source, index * unit : (index + 1) * unit, :] = joined


VMEM_BYTES = 24 * 1024 * 1024
VMEM_MOST = 60 * 1024 * 1024


def params(limit=VMEM_BYTES):
    return pltpu.CompilerParams(vmem_limit_bytes=limit)


def cost(flops, moved, waves=0):
    return pl.CostEstimate(flops=flops, bytes_accessed=moved, transcendentals=waves)


def whole_spec(array):
    zeros = (0,) * array.ndim
    return pl.BlockSpec(array.shape, lambda i, *_: zeros)


def weight_spec(section, features):
    return pl.BlockSpec((1, features, features), lambda i, *_: (section, 0, 0))


def run_front(current, where, received, own, start, sides, back_rows, rank_rows, weights, section, targets):
    _, rows, features = current.shape
    count = where.shape[0]
    narrow = features // HALF
    row_spec = pl.BlockSpec((1, 1, rows), lambda i, where: (start + i, 0, 0))
    first_target = 9 + len(received)
    return pl.pallas_call(
        functools.partial(front_kernel, own, count),
        grid_spec=pltpu.PrefetchScalarGridSpec(
            num_scalar_prefetch=1,
            grid=(count,),
            in_specs=[
                pl.BlockSpec((1, rows, features), lambda i, where: (where[i], 0, 0)),
                row_spec,
                row_spec,
            ]
            + [weight_spec(section, features)] * 5
            + [whole_spec(array) for array in received]
            + [pl.BlockSpec(memory_space=pl.ANY)] * len(targets),
            out_specs=[
                pl.BlockSpec((1, rows, features), lambda i, where: (start + i, 0, 0)),
                pl.BlockSpec((narrow, 1, rows // 2, LANES), lambda i, where: (0, start + i, 0, 0)),
            ],
            scratch_shapes=[pltpu.VMEM((rows, features), jnp.bfloat16)],
        ),
        out_shape=[
            jax.ShapeDtypeStruct((sides, rows, features), jnp.bfloat16),
            jax.ShapeDtypeStruct((narrow, sides, rows // 2, LANES), jnp.bfloat16),
        ],
        input_output_aliases={first_target + index: index for index in range(len(targets))},
        compiler_params=params(VMEM_BYTES if section else VMEM_MOST),
        cost_estimate=cost(12 * count * rows * features**2, 8 * count * rows * features),
        name="front",
    )(where, current, back_rows, rank_rows, *weights[:5], *received, *targets)


def run_back(second, packed, where, to, start, rank_rows, weights, at, total):
    _, rows, features = second.shape
    count = where.shape[0]
    narrow = packed.shape[1]
    return pl.pallas_call(
        back_kernel,
        grid_spec=pltpu.PrefetchScalarGridSpec(
            num_scalar_prefetch=2,
            grid=(count,),
            in_specs=[
                pl.BlockSpec((1, rows, features), lambda i, *_: (start + i, 0, 0)),
                pl.BlockSpec((1, narrow, rows // 2, LANES), lambda i, where, to: (where[i], 0, 0, 0)),
                pl.BlockSpec((1, 1, rows), lambda i, *_: (start + i, 0, 0)),
            ]
            + [weight_spec(index, features) for index in at],
            out_specs=pl.BlockSpec((1, rows, features), lambda i, where, to: (to[i], 0, 0)),
        ),
        out_shape=jax.ShapeDtypeStruct((total, rows, features), jnp.bfloat16),
        compiler_params=params(),
        cost_estimate=cost(8 * count * rows * features**2, 6 * count * rows * features),
        name="back",
    )(where, to, second, packed, rank_rows, *weights)


def rank_spec(entries):
    return pl.BlockSpec((1,) + entries.shape[1:], lambda i, *_: (i, 0, 0, 0))


def run_tables(places, order, position, entries, angles):
    owners = entries.shape[0]
    atoms = angles.shape[1]
    groups = atoms // GROUP
    span = GROUP * SLOTS
    return pl.pallas_call(
        table_kernel,
        grid_spec=pltpu.PrefetchScalarGridSpec(
            num_scalar_prefetch=3,
            grid=(owners,),
            in_specs=[
                rank_spec(entries),
                pl.BlockSpec((1, atoms, angles.shape[2]), lambda i, places, *_: (places[i], 0, 0)),
            ],
            out_specs=[
                rank_spec(entries),
                pl.BlockSpec((1, groups, span, span), lambda i, *_: (i, 0, 0, 0)),
            ],
        ),
        out_shape=[
            jax.ShapeDtypeStruct(entries.shape, jnp.int32),
            jax.ShapeDtypeStruct((owners, groups, span, span), jnp.bfloat16),
        ],
        compiler_params=params(),
        cost_estimate=cost(0, 8 * owners * groups * span**2),
        name="tables",
    )(places, order, position, entries, angles)


def run_mix(owner_of, place_of, order, received, rank, blocks):
    devices, sides, half, _ = received.shape
    unit = 2 * half // devices
    smem = pl.BlockSpec(memory_space=pltpu.SMEM)
    shape = (sides, devices, half, LANES)
    scratch = pltpu.VMEM((sides, devices, devices, unit, LANES), jnp.bfloat16)
    return pl.pallas_call(
        mix_kernel,
        grid=(devices,),
        in_specs=[
            smem,
            smem,
            smem,
            whole_spec(received),
            rank_spec(rank),
            pl.BlockSpec((1,) + blocks.shape[1:], lambda i: (i, 0, 0, 0)),
        ],
        out_specs=pl.BlockSpec(shape, lambda i: (0, 0, 0, 0)),
        out_shape=jax.ShapeDtypeStruct(shape, jnp.bfloat16),
        scratch_shapes=[scratch, scratch],
        compiler_params=params(),
        cost_estimate=cost(10 * devices * sides * half**2 * LANES, 16 * devices * sides * half**2),
        name="mix",
    )(owner_of, place_of, order, received, rank, blocks)


def unit_tables(entries, capacity, unit):
    owners, sides, rows = entries.shape
    ids = jnp.arange(owners, dtype=jnp.int32)
    source = entries.reshape(owners, sides * rows) // capacity
    counts = jnp.sum((source[None] == ids[:, None, None]).astype(jnp.int32), axis=2) // (unit * sides)
    before = ids[:, None] < ids[None, :]
    starts = jnp.sum(jnp.where(before[None], counts[:, :, None], 0), axis=1)
    places = jnp.sum(jnp.where(before[:, :, None], counts[:, None, :], 0), axis=0)
    inside = (starts[:, :, None] <= ids) & (ids < (starts + counts)[:, :, None])
    owner_of = jnp.sum(jnp.where(inside, ids[None, :, None], 0), axis=1)
    place_of = jnp.sum(jnp.where(inside, (places - starts)[:, :, None] + ids, 0), axis=1)
    return owner_of, place_of


def ranks(values):
    return jnp.sum((values[:, :, None] < values[:, None, :]).astype(jnp.int32), axis=1)


CHUNKS = 2


def reorder(values, order):
    hits = order[:, None] == jnp.arange(values.shape[0], dtype=jnp.int32)
    return jnp.sum(jnp.where(hits[:, :, None], values[None], 0), axis=1)


def shift(values, offset, wide):
    if offset == 0:
        return values
    return lax.ppermute(values, "wide", [(i, i ^ offset) for i in range(wide)])


def swap(values):
    return lax.all_to_all(values, "narrow", 0, 0, tiled=True)


BASE = 64


def share_lists(listed, angles, after):
    narrow = lax.axis_size("narrow")
    atoms, width = angles.shape
    digits = jnp.stack([listed // BASE, listed % BASE]).reshape(atoms, -1).astype(jnp.bfloat16)
    shared = jnp.concatenate([angles, digits], axis=1)[None]
    held = [0]
    hop = narrow // 2
    while hop:
        if hop == 1:
            shared, after = lax.optimization_barrier((shared, after))
        other = lax.ppermute(shared, "narrow", [(i, i ^ hop) for i in range(narrow)])
        shared = jnp.concatenate([shared, other], axis=0)
        held += [offset ^ hop for offset in held]
        hop //= 2
    inverse = jnp.array([held.index(offset) for offset in range(narrow)], jnp.int32)
    mine = lax.axis_index("narrow").astype(jnp.int32)
    owners = jnp.arange(narrow, dtype=jnp.int32) ^ mine
    places = jnp.sum(jnp.where(owners[:, None] == jnp.arange(narrow), inverse, 0), axis=1)
    digits = shared[:, :, width:].reshape((narrow, 2) + listed.shape).astype(jnp.int32)
    entries = digits[:, 0] * BASE + digits[:, 1]
    entries = reorder(entries.reshape(narrow, -1), places).reshape(entries.shape)
    return entries, shared, places, after


def tiled_local(messages, reverse_position, route_slot, atom_slots, angles, weights):
    wide = lax.axis_size("wide")
    narrow = lax.axis_size("narrow")
    edge_rows, features = messages.shape
    rows = edge_rows // wide
    unit = rows // narrow
    capacity = 2 * edge_rows // narrow
    atoms = angles.shape[0]
    group_id = lax.axis_index("wide").astype(jnp.int32)
    offsets = [offset for index in range(wide // 2) for offset in (index, wide - 1 - index)]
    order = group_id ^ jnp.array(offsets, jnp.int32)
    inverse = jnp.array([offsets.index(offset) for offset in range(wide)], jnp.int32)
    owners_wide = (jnp.arange(wide, dtype=jnp.int32) ^ group_id)[:, None]
    position = jnp.sum(jnp.where(owners_wide == jnp.arange(wide), inverse, 0), axis=1)
    half = wide // 2
    pieces = [(0, 1), (1, wide - 1)]
    halves = [(0, half), (half, wide - half)]

    blocks_of = messages.reshape(wide, rows, features)
    sent = [
        lax.dynamic_index_in_dim(blocks_of, group_id ^ offset, 0, False) for offset in offsets[1:]
    ]
    *sent, atom_slots = lax.optimization_barrier((*sent, atom_slots))
    received = {offset: shift(part, offset, wide) for offset, part in zip(offsets[1:], sent)}
    listed = atom_slots.reshape(atoms // GROUP, GROUP, wide, SLOTS // wide)
    listed = reorder(jnp.transpose(listed, (2, 0, 3, 1)).reshape(wide, rows), order)
    rank = reorder(ranks(route_slot.reshape(wide, rows)), order)
    back_rows = reorder(reverse_position.reshape(wide, rows), order)

    current = {start: (blocks_of, order[start : start + count]) for start, count in pieces}
    tables = None
    for section in range(BLOCKS):
        last = section == BLOCKS - 1
        targets = []
        for start, count in halves if section else pieces:
            array, where = current[start]
            needed = [received[offset] for offset in offsets[start : start + count] if offset]
            targets = list(run_front(
                array, where, needed, start == 0, start, wide,
                back_rows[:, None, :], rank[:, None, :], weights, section, targets,
            ))
        second, packed = targets
        if tables is None:
            entries, all_angles, owner_places, packed = share_lists(listed, angles, packed)
            packed, late_rank = lax.optimization_barrier((packed, rank))
            owner_of, place_of = unit_tables(entries, capacity, unit)
            tables = run_tables(owner_places, order, position, entries[:, :, None, :], all_angles)
            partner_rank = jnp.stack(
                [shift(late_rank[place], offset, wide) for place, offset in enumerate(offsets)]
            )
            hits = back_rows[:, :, None] == jnp.arange(rows, dtype=jnp.int32)
            turned_rank = jnp.sum(jnp.where(hits, partner_rank[:, None, :], 0), axis=2)[:, None, :]
        mixed = run_mix(owner_of, place_of, order, swap(packed), *tables)
        late, at = weights[5:], [section] * 3
        if not last:
            mixed, *late = lax.optimization_barrier((mixed, *late))
            late, at = [jnp.stack([weight[section] for weight in late])] * 3, range(3)
        mixed = mixed.reshape(wide * narrow, rows // 2, LANES)
        returned = lax.all_to_all(mixed, ("wide", "narrow"), 0, 0, tiled=True)
        returned = returned.reshape(wide, narrow, rows // 2, LANES)
        if last:
            current = run_back(second, returned, order, order, 0, turned_rank, late, at, wide)
            return current.reshape(edge_rows, features)
        for start, count in halves:
            plain = jnp.arange(count, dtype=jnp.int32)
            where = order[start : start + count]
            result = run_back(second, returned, where, plain, start, turned_rank, late, at, count)
            current[start] = (result, plain)
            for index, offset in enumerate(offsets[start : start + count]):
                if offset:
                    received[offset] = shift(result[index], offset, wide)


def local(
    messages,
    reverse_position,
    route_slot,
    atom_slots,
    angles,
    weight_message,
    weight_reverse,
    weight_combine,
    weight_inner,
    weight_outer,
    weight_lift,
    weight_expand,
    weight_reduce,
):
    weights = (
        weight_message,
        weight_reverse,
        weight_combine,
        weight_inner,
        weight_outer,
        weight_lift,
        weight_expand,
        weight_reduce,
    )
    wide = lax.axis_size("wide")
    narrow = lax.axis_size("narrow")
    edge_rows, features = messages.shape
    unit = edge_rows // wide // narrow
    fits = (
        features == narrow * HALF
        and unit % 16 == 0
        and narrow % 2 == 0
        and wide >= 4
        and wide & (wide - 1) == 0
        and narrow & (narrow - 1) == 0
        and angles.shape[0] % GROUP == 0
        and (SLOTS // wide * GROUP) % 16 == 0
    )
    run = tiled_local if fits else general_local
    return run(messages, reverse_position, route_slot, atom_slots, angles, weights)


def solution(mesh):
    in_specs = (
        P(("wide", "narrow"), None),
        P(("wide", "narrow")),
        P(("wide", "narrow")),
        P(("wide", "narrow")),
        P(("wide", "narrow"), None),
        P(),
        P(),
        P(),
        P(),
        P(),
        P(),
        P(),
        P(),
    )
    out_specs = P(("wide", "narrow"), None)
    return jax.shard_map(local, mesh=mesh, in_specs=in_specs, out_specs=out_specs, check_vma=False)
```

```python
import functools

import jax
import jax.numpy as jnp
from jax import lax
from jax.experimental import pallas as pl
from jax.experimental.pallas import tpu as pltpu
from jax.sharding import PartitionSpec as P

SLOTS = 32
BLOCKS = 2
LANES = 128
HALF = LANES // 2
GROUP = 8


ROOT_HALF = 0.7071067811865476


def project(operand, weight):
    return jnp.dot(operand, weight, preferred_element_type=jnp.float32)


def residual(previous, branch):
    return ((previous.astype(jnp.float32) + branch) * ROOT_HALF).astype(jnp.bfloat16)


def reverse_edges(values, partner_rows):
    exchanged = lax.all_to_all(values, "wide", split_axis=0, concat_axis=0, tiled=True)
    return jnp.take(exchanged, partner_rows, axis=0)


def edge_front(current, reverse, weights, section_index):
    hidden = jax.nn.silu(
        project(current, weights[0][section_index]) + project(reverse, weights[1][section_index])
    ).astype(jnp.bfloat16)
    first_res = residual(current, project(hidden, weights[2][section_index]))
    inner_value = jax.nn.silu(project(first_res, weights[3][section_index])).astype(jnp.bfloat16)
    return residual(first_res, jax.nn.silu(project(inner_value, weights[4][section_index])))


def edge_back(second, turned, weights, section_index):
    third_res = residual(second, jax.nn.silu(project(turned, weights[5][section_index])))
    expand = jax.nn.silu(project(third_res, weights[6][section_index])).astype(jnp.bfloat16)
    return residual(third_res, jax.nn.silu(project(expand, weights[7][section_index])))


def owners_mix(second, route_slot, atom_slots, mixing):
    features = second.shape[1]
    buffer_rows = 2 * second.shape[0]
    outgoing = jnp.zeros((buffer_rows, features), jnp.bfloat16).at[route_slot].set(second)
    received = lax.all_to_all(outgoing, "narrow", split_axis=0, concat_axis=0, tiled=True)
    gathered = jnp.take(received, atom_slots, axis=0).reshape(mixing.shape[0], SLOTS, features)
    mixed_rows = jnp.einsum(
        "apq,aqd->apd", mixing, gathered, preferred_element_type=jnp.float32
    ).astype(jnp.bfloat16)
    return mixed_rows.reshape(-1, features)


def back_to_edges(mixed_flat, route_slot, atom_slots):
    features = mixed_flat.shape[1]
    buffer_rows = 2 * route_slot.shape[0]
    answer = jnp.zeros((buffer_rows, features), jnp.bfloat16).at[atom_slots].set(mixed_flat)
    incoming = lax.all_to_all(answer, "narrow", split_axis=0, concat_axis=0, tiled=True)
    return jnp.take(incoming, route_slot, axis=0)


def general_local(messages, reverse_position, route_slot, atom_slots, angles, weights):
    edge_rows = messages.shape[0]
    sub_rows = edge_rows // lax.axis_size("wide")
    partner_rows = jnp.arange(edge_rows, dtype=jnp.int32) // sub_rows * sub_rows + reverse_position
    mixing = angles.reshape(angles.shape[0], SLOTS, SLOTS)
    current = messages
    for section_index in range(BLOCKS):
        reverse = reverse_edges(current, partner_rows)
        second = edge_front(current, reverse, weights, section_index)
        mixed_flat = owners_mix(second, route_slot, atom_slots, mixing)
        returned = back_to_edges(mixed_flat, route_slot, atom_slots)
        turned = reverse_edges(returned, partner_rows)
        current = edge_back(second, turned, weights, section_index)
    return current


def silu(value):
    return 0.5 * value * (1.0 + jnp.tanh(0.5 * value))


def dot(left, right):
    return jnp.dot(left, right, preferred_element_type=jnp.float32)


def halve(previous, branch):
    return ((previous.astype(jnp.float32) + branch) * ROOT_HALF).astype(jnp.bfloat16)


def iotas(size):
    shape = (size, size)
    return lax.broadcasted_iota(jnp.int32, shape, 0), lax.broadcasted_iota(jnp.int32, shape, 1)


def as_column(row, rows_iota, lanes_iota):
    return jnp.sum(jnp.where(rows_iota == lanes_iota, row, 0), axis=1, keepdims=True)


def one_hot(mask):
    return jnp.where(mask, 1.0, 0.0).astype(jnp.bfloat16)


def row_parts(rows):
    half = rows // 2
    return [slice(0, half), slice(half, rows)]


def front_kernel(own, count, where_ref, cur_ref, back_ref, rank_ref, wm, wr, wc, wi, wo, *refs):
    recv_refs, (second_ref, packed_ref, reverse_ref) = refs[: count - own], refs[-3:]
    rows_iota, lanes_iota = iotas(cur_ref.shape[1])
    partner = as_column(back_ref[0], rows_iota, lanes_iota)
    hot = one_hot(partner == lanes_iota)
    sources = ([cur_ref.at[0]] if own else []) + list(recv_refs)
    for index in range(count):

        @pl.when(pl.program_id(0) == index)
        def _():
            reverse_ref[...] = dot(hot, sources[index][...]).astype(jnp.bfloat16)

    parts = row_parts(cur_ref.shape[1])
    current = [cur_ref[0, part, :] for part in parts]
    sums = [dot(rows, wm[0]) + dot(reverse_ref[part, :], wr[0]) for rows, part in zip(current, parts)]
    hidden = [silu(rows).astype(jnp.bfloat16) for rows in sums]
    first_res = [halve(rows, dot(left, wc[0])) for rows, left in zip(current, hidden)]
    inner = [silu(dot(rows, wi[0])).astype(jnp.bfloat16) for rows in first_res]
    for rows, left, part in zip(first_res, inner, parts):
        second_ref[0, part, :] = halve(rows, silu(dot(left, wo[0])))
    second = second_ref[0]
    ordered = dot(one_hot(rows_iota == rank_ref[0]), second)
    half = ordered.shape[0] // 2
    low = lax.broadcasted_iota(jnp.int32, (half, LANES), 1) < HALF
    for tile in range(ordered.shape[1] // LANES):
        top = ordered[:half, tile * LANES : (tile + 1) * LANES]
        bottom = ordered[half:, tile * LANES : (tile + 1) * LANES]
        packed_ref[2 * tile, 0] = jnp.where(low, top, pltpu.roll(bottom, HALF, 1)).astype(jnp.bfloat16)
        packed_ref[2 * tile + 1, 0] = jnp.where(low, pltpu.roll(top, HALF, 1), bottom).astype(jnp.bfloat16)


def back_kernel(from_ref, to_ref, second_ref, packed_ref, rank_ref, wl, we, wd, out_ref):
    rows_iota, lanes_iota = iotas(second_ref.shape[1])
    half = rows_iota.shape[0] // 2
    low = lax.broadcasted_iota(jnp.int32, (half, LANES), 1) < HALF
    tops, bottoms = [], []
    for tile in range(second_ref.shape[2] // LANES):
        even = packed_ref[0, 2 * tile].astype(jnp.float32)
        odd = packed_ref[0, 2 * tile + 1].astype(jnp.float32)
        tops.append(jnp.where(low, even, pltpu.roll(odd, HALF, 1)).astype(jnp.bfloat16))
        bottoms.append(jnp.where(low, pltpu.roll(even, HALF, 1), odd).astype(jnp.bfloat16))
    ordered = jnp.concatenate(
        [jnp.concatenate(tops, axis=1), jnp.concatenate(bottoms, axis=1)], axis=0
    )
    source = as_column(rank_ref[0], rows_iota, lanes_iota)
    hot = one_hot(source == lanes_iota)
    parts = row_parts(hot.shape[0])
    turned = [dot(hot[part, :], ordered).astype(jnp.bfloat16) for part in parts]
    third_res = [
        halve(second_ref[0, part, :], silu(dot(rows, wl[0]))) for rows, part in zip(turned, parts)
    ]
    expand = [silu(dot(rows, we[0])).astype(jnp.bfloat16) for rows in third_res]
    for rows, left, part in zip(third_res, expand, parts):
        out_ref[0, part, :] = halve(rows, silu(dot(left, wd[0])))


def table_kernel(places_ref, order_ref, position_ref, entry_ref, angles_ref, rank_ref, blocks_ref):
    sides, _, size = entry_ref.shape[1:]
    rows_iota, lanes_iota = iotas(size)
    for side in range(sides):
        row = entry_ref[0, side]
        column = as_column(row, rows_iota, lanes_iota)
        rank_ref[0, side] = jnp.sum(jnp.where(column < row, 1, 0), axis=0, keepdims=True)
    span = GROUP * SLOTS
    strip = span // sides
    rows_iota, lanes_iota = iotas(span)
    own = rows_iota % GROUP == lanes_iota % GROUP
    spread_rows = lax.broadcasted_iota(jnp.int32, (SLOTS, span), 0)
    spread_lanes = lax.broadcasted_iota(jnp.int32, (SLOTS, span), 1)
    side_at = jnp.zeros((SLOTS, span), jnp.int32)
    for place in range(sides):
        side_at = jnp.where(spread_lanes // strip == place, order_ref[place], side_at)
    spread = one_hot(side_at * (SLOTS // sides) + spread_lanes % strip // GROUP == spread_rows)
    for group in range(angles_ref.shape[1] // GROUP):
        local = angles_ref[0, group * GROUP : (group + 1) * GROUP, :].astype(jnp.float32)
        stacked = jnp.concatenate(
            [local[:, p * SLOTS : (p + 1) * SLOTS] for p in range(SLOTS)], axis=0
        ).astype(jnp.bfloat16)
        block = jnp.where(own, dot(stacked, spread), 0.0).astype(jnp.bfloat16)
        for side in range(sides):
            to = pl.multiple_of(position_ref[side] * strip, strip)
            blocks_ref[0, group, pl.ds(to, strip), :] = block[side * strip : (side + 1) * strip]


def mix_kernel(owner_ref, place_ref, order_ref, recv_ref, rank_ref, blocks_ref, out_ref, ins, outs):
    step = pl.program_id(0)
    devices, sides = recv_ref.shape[:2]
    unit = ins.shape[3]
    rows = devices * unit
    groups = blocks_ref.shape[1]
    strip = blocks_ref.shape[2] // sides
    pairs = devices // 2

    @pl.when(step == 0)
    def _():
        @pl.loop(0, devices)
        def _(source):
            for index in range(devices):
                owner = owner_ref[source, index]
                place = place_ref[source, index]
                at = (index % pairs) * unit
                for side in range(sides):
                    block = recv_ref[source, side, at : at + unit, :]
                    if index >= pairs:
                        block = pltpu.roll(block.astype(jnp.float32), HALF, 1).astype(jnp.bfloat16)
                    ins[side, owner, place] = block

    rows_iota, lanes_iota = iotas(rows)
    gathered = []
    for side in range(sides):
        source = as_column(rank_ref[0, side], rows_iota, lanes_iota)
        operand = ins[side, step].reshape(rows, LANES)
        gathered.append(dot(one_hot(source == lanes_iota), operand).astype(jnp.bfloat16))
    mixed = []
    for group in range(groups):
        operand = jnp.concatenate(
            [part[group * strip : (group + 1) * strip] for part in gathered], axis=0
        )
        mixed.append(dot(blocks_ref[0, group], operand).astype(jnp.bfloat16))
    for side in range(sides):
        operand = jnp.concatenate(
            [part[side * strip : (side + 1) * strip] for part in mixed], axis=0
        )
        outs[side, step] = (
            dot(one_hot(rows_iota == rank_ref[0, side]), operand)
            .astype(jnp.bfloat16)
            .reshape(devices, unit, LANES)
        )

    @pl.when(step == pl.num_programs(0) - 1)
    def _():
        low = lax.broadcasted_iota(jnp.int32, (unit, LANES), 1) < HALF

        @pl.loop(0, devices)
        def _(source):
            for index in range(pairs):
                owner = owner_ref[source, index]
                place = place_ref[source, index]
                owner_far = owner_ref[source, index + pairs]
                place_far = place_ref[source, index + pairs]
                for side in range(sides):
                    near = outs[side, owner, place].astype(jnp.float32)
                    far = outs[side, owner_far, place_far].astype(jnp.float32)
                    joined = jnp.where(low, near, pltpu.roll(far, HALF, 1)).astype(jnp.bfloat16)
                    out_ref[order_ref[side], source, index * unit : (index + 1) * unit, :] = joined


VMEM_BYTES = 24 * 1024 * 1024
VMEM_MOST = 60 * 1024 * 1024


def params(limit=VMEM_BYTES):
    return pltpu.CompilerParams(vmem_limit_bytes=limit)


def cost(flops, moved, waves=0):
    return pl.CostEstimate(flops=flops, bytes_accessed=moved, transcendentals=waves)


def whole_spec(array):
    zeros = (0,) * array.ndim
    return pl.BlockSpec(array.shape, lambda i, *_: zeros)


def weight_spec(section, features):
    return pl.BlockSpec((1, features, features), lambda i, *_: (section, 0, 0))


def run_front(current, where, received, own, start, sides, back_rows, rank_rows, weights, section, targets):
    _, rows, features = current.shape
    count = where.shape[0]
    narrow = features // HALF
    row_spec = pl.BlockSpec((1, 1, rows), lambda i, where: (start + i, 0, 0))
    first_target = 9 + len(received)
    return pl.pallas_call(
        functools.partial(front_kernel, own, count),
        grid_spec=pltpu.PrefetchScalarGridSpec(
            num_scalar_prefetch=1,
            grid=(count,),
            in_specs=[
                pl.BlockSpec((1, rows, features), lambda i, where: (where[i], 0, 0)),
                row_spec,
                row_spec,
            ]
            + [weight_spec(section, features)] * 5
            + [whole_spec(array) for array in received]
            + [pl.BlockSpec(memory_space=pl.ANY)] * len(targets),
            out_specs=[
                pl.BlockSpec((1, rows, features), lambda i, where: (start + i, 0, 0)),
                pl.BlockSpec((narrow, 1, rows // 2, LANES), lambda i, where: (0, start + i, 0, 0)),
            ],
            scratch_shapes=[pltpu.VMEM((rows, features), jnp.bfloat16)],
        ),
        out_shape=[
            jax.ShapeDtypeStruct((sides, rows, features), jnp.bfloat16),
            jax.ShapeDtypeStruct((narrow, sides, rows // 2, LANES), jnp.bfloat16),
        ],
        input_output_aliases={first_target + index: index for index in range(len(targets))},
        compiler_params=params(VMEM_BYTES if section else VMEM_MOST),
        cost_estimate=cost(12 * count * rows * features**2, 8 * count * rows * features),
        name="front",
    )(where, current, back_rows, rank_rows, *weights[:5], *received, *targets)


def run_back(second, packed, where, to, start, rank_rows, weights, at, total):
    _, rows, features = second.shape
    count = where.shape[0]
    narrow = packed.shape[1]
    return pl.pallas_call(
        back_kernel,
        grid_spec=pltpu.PrefetchScalarGridSpec(
            num_scalar_prefetch=2,
            grid=(count,),
            in_specs=[
                pl.BlockSpec((1, rows, features), lambda i, *_: (start + i, 0, 0)),
                pl.BlockSpec((1, narrow, rows // 2, LANES), lambda i, where, to: (where[i], 0, 0, 0)),
                pl.BlockSpec((1, 1, rows), lambda i, *_: (start + i, 0, 0)),
            ]
            + [weight_spec(index, features) for index in at],
            out_specs=pl.BlockSpec((1, rows, features), lambda i, where, to: (to[i], 0, 0)),
        ),
        out_shape=jax.ShapeDtypeStruct((total, rows, features), jnp.bfloat16),
        compiler_params=params(),
        cost_estimate=cost(8 * count * rows * features**2, 6 * count * rows * features),
        name="back",
    )(where, to, second, packed, rank_rows, *weights)


def rank_spec(entries):
    return pl.BlockSpec((1,) + entries.shape[1:], lambda i, *_: (i, 0, 0, 0))


def run_tables(places, order, position, entries, angles):
    owners = entries.shape[0]
    atoms = angles.shape[1]
    groups = atoms // GROUP
    span = GROUP * SLOTS
    return pl.pallas_call(
        table_kernel,
        grid_spec=pltpu.PrefetchScalarGridSpec(
            num_scalar_prefetch=3,
            grid=(owners,),
            in_specs=[
                rank_spec(entries),
                pl.BlockSpec((1, atoms, angles.shape[2]), lambda i, places, *_: (places[i], 0, 0)),
            ],
            out_specs=[
                rank_spec(entries),
                pl.BlockSpec((1, groups, span, span), lambda i, *_: (i, 0, 0, 0)),
            ],
        ),
        out_shape=[
            jax.ShapeDtypeStruct(entries.shape, jnp.int32),
            jax.ShapeDtypeStruct((owners, groups, span, span), jnp.bfloat16),
        ],
        compiler_params=params(),
        cost_estimate=cost(0, 8 * owners * groups * span**2),
        name="tables",
    )(places, order, position, entries, angles)


def run_mix(owner_of, place_of, order, received, rank, blocks):
    devices, sides, half, _ = received.shape
    unit = 2 * half // devices
    smem = pl.BlockSpec(memory_space=pltpu.SMEM)
    shape = (sides, devices, half, LANES)
    scratch = pltpu.VMEM((sides, devices, devices, unit, LANES), jnp.bfloat16)
    return pl.pallas_call(
        mix_kernel,
        grid=(devices,),
        in_specs=[
            smem,
            smem,
            smem,
            whole_spec(received),
            rank_spec(rank),
            pl.BlockSpec((1,) + blocks.shape[1:], lambda i: (i, 0, 0, 0)),
        ],
        out_specs=pl.BlockSpec(shape, lambda i: (0, 0, 0, 0)),
        out_shape=jax.ShapeDtypeStruct(shape, jnp.bfloat16),
        scratch_shapes=[scratch, scratch],
        compiler_params=params(),
        cost_estimate=cost(10 * devices * sides * half**2 * LANES, 16 * devices * sides * half**2),
        name="mix",
    )(owner_of, place_of, order, received, rank, blocks)


def unit_tables(entries, capacity, unit):
    owners, sides, rows = entries.shape
    ids = jnp.arange(owners, dtype=jnp.int32)
    source = entries.reshape(owners, sides * rows) // capacity
    counts = jnp.sum((source[None] == ids[:, None, None]).astype(jnp.int32), axis=2) // (unit * sides)
    before = ids[:, None] < ids[None, :]
    starts = jnp.sum(jnp.where(before[None], counts[:, :, None], 0), axis=1)
    places = jnp.sum(jnp.where(before[:, :, None], counts[:, None, :], 0), axis=0)
    inside = (starts[:, :, None] <= ids) & (ids < (starts + counts)[:, :, None])
    owner_of = jnp.sum(jnp.where(inside, ids[None, :, None], 0), axis=1)
    place_of = jnp.sum(jnp.where(inside, (places - starts)[:, :, None] + ids, 0), axis=1)
    return owner_of, place_of


def ranks(values):
    return jnp.sum((values[:, :, None] < values[:, None, :]).astype(jnp.int32), axis=1)


CHUNKS = 2


def reorder(values, order):
    hits = order[:, None] == jnp.arange(values.shape[0], dtype=jnp.int32)
    return jnp.sum(jnp.where(hits[:, :, None], values[None], 0), axis=1)


def shift(values, offset, wide):
    if offset == 0:
        return values
    return lax.ppermute(values, "wide", [(i, i ^ offset) for i in range(wide)])


def swap(values):
    return lax.all_to_all(values, "narrow", 0, 0, tiled=True)


BASE = 64


def share_lists(listed, angles, after):
    narrow = lax.axis_size("narrow")
    atoms, width = angles.shape
    digits = jnp.stack([listed // BASE, listed % BASE]).reshape(atoms, -1).astype(jnp.bfloat16)
    shared = jnp.concatenate([angles, digits], axis=1)[None]
    held = [0]
    hop = narrow // 2
    while hop:
        if hop == 1:
            shared, after = lax.optimization_barrier((shared, after))
        other = lax.ppermute(shared, "narrow", [(i, i ^ hop) for i in range(narrow)])
        shared = jnp.concatenate([shared, other], axis=0)
        held += [offset ^ hop for offset in held]
        hop //= 2
    inverse = jnp.array([held.index(offset) for offset in range(narrow)], jnp.int32)
    mine = lax.axis_index("narrow").astype(jnp.int32)
    owners = jnp.arange(narrow, dtype=jnp.int32) ^ mine
    places = jnp.sum(jnp.where(owners[:, None] == jnp.arange(narrow), inverse, 0), axis=1)
    digits = shared[:, :, width:].reshape((narrow, 2) + listed.shape).astype(jnp.int32)
    entries = digits[:, 0] * BASE + digits[:, 1]
    entries = reorder(entries.reshape(narrow, -1), places).reshape(entries.shape)
    return entries, shared, places, after


def tiled_local(messages, reverse_position, route_slot, atom_slots, angles, weights):
    wide = lax.axis_size("wide")
    narrow = lax.axis_size("narrow")
    edge_rows, features = messages.shape
    rows = edge_rows // wide
    unit = rows // narrow
    capacity = 2 * edge_rows // narrow
    atoms = angles.shape[0]
    group_id = lax.axis_index("wide").astype(jnp.int32)
    offsets = [offset for index in range(wide // 2) for offset in (index, wide - 1 - index)]
    order = group_id ^ jnp.array(offsets, jnp.int32)
    inverse = jnp.array([offsets.index(offset) for offset in range(wide)], jnp.int32)
    owners_wide = (jnp.arange(wide, dtype=jnp.int32) ^ group_id)[:, None]
    position = jnp.sum(jnp.where(owners_wide == jnp.arange(wide), inverse, 0), axis=1)
    half = wide // 2
    pieces = [(0, 1), (1, wide - 1)]
    halves = [(0, half), (half, wide - half)]

    blocks_of = messages.reshape(wide, rows, features)
    sent = [
        lax.dynamic_index_in_dim(blocks_of, group_id ^ offset, 0, False) for offset in offsets[1:]
    ]
    *sent, atom_slots, route_slot, reverse_position = lax.optimization_barrier(
        (*sent, atom_slots, route_slot, reverse_position)
    )
    received = {offset: shift(part, offset, wide) for offset, part in zip(offsets[1:], sent)}
    listed = atom_slots.reshape(atoms // GROUP, GROUP, wide, SLOTS // wide)
    listed = reorder(jnp.transpose(listed, (2, 0, 3, 1)).reshape(wide, rows), order)
    rank = reorder(ranks(route_slot.reshape(wide, rows)), order)
    back_rows = reorder(reverse_position.reshape(wide, rows), order)

    current = {start: (blocks_of, order[start : start + count]) for start, count in pieces}
    tables = None
    for section in range(BLOCKS):
        last = section == BLOCKS - 1
        targets = []
        for start, count in halves if section else pieces:
            array, where = current[start]
            needed = [received[offset] for offset in offsets[start : start + count] if offset]
            targets = list(run_front(
                array, where, needed, start == 0, start, wide,
                back_rows[:, None, :], rank[:, None, :], weights, section, targets,
            ))
        second, packed = targets
        if tables is None:
            entries, all_angles, owner_places, packed = share_lists(listed, angles, packed)
            packed, late_rank = lax.optimization_barrier((packed, rank))
            owner_of, place_of = unit_tables(entries, capacity, unit)
            tables = run_tables(owner_places, order, position, entries[:, :, None, :], all_angles)
            partner_rank = jnp.stack(
                [shift(late_rank[place], offset, wide) for place, offset in enumerate(offsets)]
            )
            hits = back_rows[:, :, None] == jnp.arange(rows, dtype=jnp.int32)
            turned_rank = jnp.sum(jnp.where(hits, partner_rank[:, None, :], 0), axis=2)[:, None, :]
        mixed = run_mix(owner_of, place_of, order, swap(packed), *tables)
        late, at = weights[5:], [section] * 3
        if not last:
            mixed, *late = lax.optimization_barrier((mixed, *late))
            late, at = [jnp.stack([weight[section] for weight in late])] * 3, range(3)
        mixed = mixed.reshape(wide * narrow, rows // 2, LANES)
        returned = lax.all_to_all(mixed, ("wide", "narrow"), 0, 0, tiled=True)
        returned = returned.reshape(wide, narrow, rows // 2, LANES)
        if last:
            current = run_back(second, returned, order, order, 0, turned_rank, late, at, wide)
            return current.reshape(edge_rows, features)
        for start, count in halves:
            plain = jnp.arange(count, dtype=jnp.int32)
            where = order[start : start + count]
            result = run_back(second, returned, where, plain, start, turned_rank, late, at, count)
            current[start] = (result, plain)
            for index, offset in enumerate(offsets[start : start + count]):
                if offset:
                    received[offset] = shift(result[index], offset, wide)


def local(
    messages,
    reverse_position,
    route_slot,
    atom_slots,
    angles,
    weight_message,
    weight_reverse,
    weight_combine,
    weight_inner,
    weight_outer,
    weight_lift,
    weight_expand,
    weight_reduce,
):
    weights = (
        weight_message,
        weight_reverse,
        weight_combine,
        weight_inner,
        weight_outer,
        weight_lift,
        weight_expand,
        weight_reduce,
    )
    wide = lax.axis_size("wide")
    narrow = lax.axis_size("narrow")
    edge_rows, features = messages.shape
    unit = edge_rows // wide // narrow
    fits = (
        features == narrow * HALF
        and unit % 16 == 0
        and narrow % 2 == 0
        and wide >= 4
        and wide & (wide - 1) == 0
        and narrow & (narrow - 1) == 0
        and angles.shape[0] % GROUP == 0
        and (SLOTS // wide * GROUP) % 16 == 0
    )
    run = tiled_local if fits else general_local
    return run(messages, reverse_position, route_slot, atom_slots, angles, weights)


def solution(mesh):
    in_specs = (
        P(("wide", "narrow"), None),
        P(("wide", "narrow")),
        P(("wide", "narrow")),
        P(("wide", "narrow")),
        P(("wide", "narrow"), None),
        P(),
        P(),
        P(),
        P(),
        P(),
        P(),
        P(),
        P(),
    )
    out_specs = P(("wide", "narrow"), None)
    return jax.shard_map(local, mesh=mesh, in_specs=in_specs, out_specs=out_specs, check_vma=False)
```

```python
import functools

import jax
import jax.numpy as jnp
from jax import lax
from jax.experimental import pallas as pl
from jax.experimental.pallas import tpu as pltpu
from jax.sharding import PartitionSpec as P

SLOTS = 32
BLOCKS = 2
LANES = 128
HALF = LANES // 2
GROUP = 8
PAIR = 2


ROOT_HALF = 0.7071067811865476


def project(operand, weight):
    return jnp.dot(operand, weight, preferred_element_type=jnp.float32)


def residual(previous, branch):
    return ((previous.astype(jnp.float32) + branch) * ROOT_HALF).astype(jnp.bfloat16)


def reverse_edges(values, partner_rows):
    exchanged = lax.all_to_all(values, "wide", split_axis=0, concat_axis=0, tiled=True)
    return jnp.take(exchanged, partner_rows, axis=0)


def edge_front(current, reverse, weights, section_index):
    hidden = jax.nn.silu(
        project(current, weights[0][section_index]) + project(reverse, weights[1][section_index])
    ).astype(jnp.bfloat16)
    first_res = residual(current, project(hidden, weights[2][section_index]))
    inner_value = jax.nn.silu(project(first_res, weights[3][section_index])).astype(jnp.bfloat16)
    return residual(first_res, jax.nn.silu(project(inner_value, weights[4][section_index])))


def edge_back(second, turned, weights, section_index):
    third_res = residual(second, jax.nn.silu(project(turned, weights[5][section_index])))
    expand = jax.nn.silu(project(third_res, weights[6][section_index])).astype(jnp.bfloat16)
    return residual(third_res, jax.nn.silu(project(expand, weights[7][section_index])))


def owners_mix(second, route_slot, atom_slots, mixing):
    features = second.shape[1]
    buffer_rows = 2 * second.shape[0]
    outgoing = jnp.zeros((buffer_rows, features), jnp.bfloat16).at[route_slot].set(second)
    received = lax.all_to_all(outgoing, "narrow", split_axis=0, concat_axis=0, tiled=True)
    gathered = jnp.take(received, atom_slots, axis=0).reshape(mixing.shape[0], SLOTS, features)
    mixed_rows = jnp.einsum(
        "apq,aqd->apd", mixing, gathered, preferred_element_type=jnp.float32
    ).astype(jnp.bfloat16)
    return mixed_rows.reshape(-1, features)


def back_to_edges(mixed_flat, route_slot, atom_slots):
    features = mixed_flat.shape[1]
    buffer_rows = 2 * route_slot.shape[0]
    answer = jnp.zeros((buffer_rows, features), jnp.bfloat16).at[atom_slots].set(mixed_flat)
    incoming = lax.all_to_all(answer, "narrow", split_axis=0, concat_axis=0, tiled=True)
    return jnp.take(incoming, route_slot, axis=0)


def general_local(messages, reverse_position, route_slot, atom_slots, angles, weights):
    edge_rows = messages.shape[0]
    sub_rows = edge_rows // lax.axis_size("wide")
    partner_rows = jnp.arange(edge_rows, dtype=jnp.int32) // sub_rows * sub_rows + reverse_position
    mixing = angles.reshape(angles.shape[0], SLOTS, SLOTS)
    current = messages
    for section_index in range(BLOCKS):
        reverse = reverse_edges(current, partner_rows)
        second = edge_front(current, reverse, weights, section_index)
        mixed_flat = owners_mix(second, route_slot, atom_slots, mixing)
        returned = back_to_edges(mixed_flat, route_slot, atom_slots)
        turned = reverse_edges(returned, partner_rows)
        current = edge_back(second, turned, weights, section_index)
    return current


def silu(value):
    return 0.5 * value * (1.0 + jnp.tanh(0.5 * value))


def dot(left, right):
    return jnp.dot(left, right, preferred_element_type=jnp.float32)


def halve(previous, branch):
    return ((previous.astype(jnp.float32) + branch) * ROOT_HALF).astype(jnp.bfloat16)


def iotas(size):
    shape = (size, size)
    return lax.broadcasted_iota(jnp.int32, shape, 0), lax.broadcasted_iota(jnp.int32, shape, 1)


def as_column(row, rows_iota, lanes_iota):
    return jnp.sum(jnp.where(rows_iota == lanes_iota, row, 0), axis=1, keepdims=True)


def one_hot(mask):
    return jnp.where(mask, 1.0, 0.0).astype(jnp.bfloat16)


def row_parts(rows):
    half = rows // 2
    return [slice(0, half), slice(half, rows)]


def front_kernel(own, count, where_ref, cur_ref, back_ref, rank_ref, wm, wr, wc, wi, wo, *refs):
    recv_refs, (second_ref, packed_ref, reverse_ref) = refs[: count - own], refs[-3:]
    rows_iota, lanes_iota = iotas(cur_ref.shape[1])
    partner = as_column(back_ref[0], rows_iota, lanes_iota)
    hot = one_hot(partner == lanes_iota)
    sources = ([cur_ref.at[0]] if own else []) + list(recv_refs)
    for index in range(count):

        @pl.when(pl.program_id(0) == index)
        def _():
            reverse_ref[...] = dot(hot, sources[index][...]).astype(jnp.bfloat16)

    parts = row_parts(cur_ref.shape[1])
    current = [cur_ref[0, part, :] for part in parts]
    sums = [dot(rows, wm[0]) + dot(reverse_ref[part, :], wr[0]) for rows, part in zip(current, parts)]
    hidden = [silu(rows).astype(jnp.bfloat16) for rows in sums]
    first_res = [halve(rows, dot(left, wc[0])) for rows, left in zip(current, hidden)]
    inner = [silu(dot(rows, wi[0])).astype(jnp.bfloat16) for rows in first_res]
    for rows, left, part in zip(first_res, inner, parts):
        second_ref[0, part, :] = halve(rows, silu(dot(left, wo[0])))
    second = second_ref[0]
    ordered = dot(one_hot(rows_iota == rank_ref[0]), second)
    half = ordered.shape[0] // 2
    low = lax.broadcasted_iota(jnp.int32, (half, LANES), 1) < HALF
    for tile in range(ordered.shape[1] // LANES):
        top = ordered[:half, tile * LANES : (tile + 1) * LANES]
        bottom = ordered[half:, tile * LANES : (tile + 1) * LANES]
        packed_ref[2 * tile, 0] = jnp.where(low, top, pltpu.roll(bottom, HALF, 1)).astype(jnp.bfloat16)
        packed_ref[2 * tile + 1, 0] = jnp.where(low, pltpu.roll(top, HALF, 1), bottom).astype(jnp.bfloat16)


def back_kernel(from_ref, to_ref, second_ref, packed_ref, rank_ref, wl, we, wd, out_ref):
    rows_iota, lanes_iota = iotas(second_ref.shape[1])
    half = rows_iota.shape[0] // 2
    low = lax.broadcasted_iota(jnp.int32, (half, LANES), 1) < HALF
    tops, bottoms = [], []
    for tile in range(second_ref.shape[2] // LANES):
        even = packed_ref[0, 2 * tile].astype(jnp.float32)
        odd = packed_ref[0, 2 * tile + 1].astype(jnp.float32)
        tops.append(jnp.where(low, even, pltpu.roll(odd, HALF, 1)).astype(jnp.bfloat16))
        bottoms.append(jnp.where(low, pltpu.roll(even, HALF, 1), odd).astype(jnp.bfloat16))
    ordered = jnp.concatenate(
        [jnp.concatenate(tops, axis=1), jnp.concatenate(bottoms, axis=1)], axis=0
    )
    source = as_column(rank_ref[0], rows_iota, lanes_iota)
    hot = one_hot(source == lanes_iota)
    parts = row_parts(hot.shape[0])
    turned = [dot(hot[part, :], ordered).astype(jnp.bfloat16) for part in parts]
    third_res = [
        halve(second_ref[0, part, :], silu(dot(rows, wl[0]))) for rows, part in zip(turned, parts)
    ]
    expand = [silu(dot(rows, we[0])).astype(jnp.bfloat16) for rows in third_res]
    for rows, left, part in zip(third_res, expand, parts):
        out_ref[0, part, :] = halve(rows, silu(dot(left, wd[0])))


def table_kernel(places_ref, order_ref, position_ref, entry_ref, angles_ref, rank_ref, blocks_ref):
    sides, _, size = entry_ref.shape[1:]
    rows_iota, lanes_iota = iotas(size)
    for side in range(sides):
        row = entry_ref[0, side]
        column = as_column(row, rows_iota, lanes_iota)
        rank_ref[0, side] = jnp.sum(jnp.where(column < row, 1, 0), axis=0, keepdims=True)
    span = GROUP * SLOTS
    strip = span // sides
    rows_iota, lanes_iota = iotas(span)
    own = rows_iota % GROUP == lanes_iota % GROUP
    spread_rows = lax.broadcasted_iota(jnp.int32, (SLOTS, span), 0)
    spread_lanes = lax.broadcasted_iota(jnp.int32, (SLOTS, span), 1)
    side_at = jnp.zeros((SLOTS, span), jnp.int32)
    for place in range(sides):
        side_at = jnp.where(spread_lanes // strip == place, order_ref[place], side_at)
    spread = one_hot(side_at * (SLOTS // sides) + spread_lanes % strip // GROUP == spread_rows)
    for group in range(angles_ref.shape[1] // GROUP):
        local = angles_ref[0, group * GROUP : (group + 1) * GROUP, :].astype(jnp.float32)
        stacked = jnp.concatenate(
            [local[:, p * SLOTS : (p + 1) * SLOTS] for p in range(SLOTS)], axis=0
        ).astype(jnp.bfloat16)
        block = jnp.where(own, dot(stacked, spread), 0.0).astype(jnp.bfloat16)
        for side in range(sides):
            to = pl.multiple_of(position_ref[side] * strip, strip)
            blocks_ref[0, group, pl.ds(to, strip), :] = block[side * strip : (side + 1) * strip]


def mix_kernel(owner_ref, place_ref, order_ref, recv_ref, rank_ref, blocks_ref, out_ref, ins, outs):
    step = pl.program_id(0)
    devices, sides = recv_ref.shape[:2]
    unit = ins.shape[3]
    rows = devices * unit
    groups = blocks_ref.shape[1]
    strip = blocks_ref.shape[2] // sides
    pairs = devices // 2

    @pl.when(step == 0)
    def _():
        @pl.loop(0, devices)
        def _(source):
            for index in range(devices):
                owner = owner_ref[source, index]
                place = place_ref[source, index]
                at = (index % pairs) * unit
                for side in range(sides):
                    block = recv_ref[source, side, at : at + unit, :]
                    if index >= pairs:
                        block = pltpu.roll(block.astype(jnp.float32), HALF, 1).astype(jnp.bfloat16)
                    ins[side, owner, place] = block

    rows_iota, lanes_iota = iotas(rows)
    pair = range(PAIR)
    gathered = [[] for _ in pair]
    for side in range(sides):
        for index in pair:
            source = as_column(rank_ref[index, side], rows_iota, lanes_iota)
            operand = ins[side, PAIR * step + index].reshape(rows, LANES)
            gathered[index].append(dot(one_hot(source == lanes_iota), operand).astype(jnp.bfloat16))
    mixed = [[] for _ in pair]
    for group in range(groups):
        for index in pair:
            operand = jnp.concatenate(
                [part[group * strip : (group + 1) * strip] for part in gathered[index]], axis=0
            )
            mixed[index].append(dot(blocks_ref[index, group], operand).astype(jnp.bfloat16))
    for side in range(sides):
        for index in pair:
            operand = jnp.concatenate(
                [part[side * strip : (side + 1) * strip] for part in mixed[index]], axis=0
            )
            outs[side, PAIR * step + index] = (
                dot(one_hot(rows_iota == rank_ref[index, side]), operand)
                .astype(jnp.bfloat16)
                .reshape(devices, unit, LANES)
            )

    @pl.when(step == pl.num_programs(0) - 1)
    def _():
        low = lax.broadcasted_iota(jnp.int32, (unit, LANES), 1) < HALF

        @pl.loop(0, devices)
        def _(source):
            for index in range(pairs):
                owner = owner_ref[source, index]
                place = place_ref[source, index]
                owner_far = owner_ref[source, index + pairs]
                place_far = place_ref[source, index + pairs]
                for side in range(sides):
                    near = outs[side, owner, place].astype(jnp.float32)
                    far = outs[side, owner_far, place_far].astype(jnp.float32)
                    joined = jnp.where(low, near, pltpu.roll(far, HALF, 1)).astype(jnp.bfloat16)
                    out_ref[order_ref[side], source, index * unit : (index + 1) * unit, :] = joined


VMEM_BYTES = 24 * 1024 * 1024
VMEM_MOST = 60 * 1024 * 1024


def params(limit=VMEM_BYTES):
    return pltpu.CompilerParams(vmem_limit_bytes=limit)


def cost(flops, moved, waves=0):
    return pl.CostEstimate(flops=flops, bytes_accessed=moved, transcendentals=waves)


def whole_spec(array):
    zeros = (0,) * array.ndim
    return pl.BlockSpec(array.shape, lambda i, *_: zeros)


def weight_spec(section, features):
    return pl.BlockSpec((1, features, features), lambda i, *_: (section, 0, 0))


def run_front(current, where, received, own, start, sides, back_rows, rank_rows, weights, section, targets):
    _, rows, features = current.shape
    count = where.shape[0]
    narrow = features // HALF
    row_spec = pl.BlockSpec((1, 1, rows), lambda i, where: (start + i, 0, 0))
    first_target = 9 + len(received)
    return pl.pallas_call(
        functools.partial(front_kernel, own, count),
        grid_spec=pltpu.PrefetchScalarGridSpec(
            num_scalar_prefetch=1,
            grid=(count,),
            in_specs=[
                pl.BlockSpec((1, rows, features), lambda i, where: (where[i], 0, 0)),
                row_spec,
                row_spec,
            ]
            + [weight_spec(section, features)] * 5
            + [whole_spec(array) for array in received]
            + [pl.BlockSpec(memory_space=pl.ANY)] * len(targets),
            out_specs=[
                pl.BlockSpec((1, rows, features), lambda i, where: (start + i, 0, 0)),
                pl.BlockSpec((narrow, 1, rows // 2, LANES), lambda i, where: (0, start + i, 0, 0)),
            ],
            scratch_shapes=[pltpu.VMEM((rows, features), jnp.bfloat16)],
        ),
        out_shape=[
            jax.ShapeDtypeStruct((sides, rows, features), jnp.bfloat16),
            jax.ShapeDtypeStruct((narrow, sides, rows // 2, LANES), jnp.bfloat16),
        ],
        input_output_aliases={first_target + index: index for index in range(len(targets))},
        compiler_params=params(VMEM_BYTES if section else VMEM_MOST),
        cost_estimate=cost(12 * count * rows * features**2, 8 * count * rows * features),
        name="front",
    )(where, current, back_rows, rank_rows, *weights[:5], *received, *targets)


def run_back(second, packed, where, to, start, rank_rows, weights, at, total):
    _, rows, features = second.shape
    count = where.shape[0]
    narrow = packed.shape[1]
    return pl.pallas_call(
        back_kernel,
        grid_spec=pltpu.PrefetchScalarGridSpec(
            num_scalar_prefetch=2,
            grid=(count,),
            in_specs=[
                pl.BlockSpec((1, rows, features), lambda i, *_: (start + i, 0, 0)),
                pl.BlockSpec((1, narrow, rows // 2, LANES), lambda i, where, to: (where[i], 0, 0, 0)),
                pl.BlockSpec((1, 1, rows), lambda i, *_: (start + i, 0, 0)),
            ]
            + [weight_spec(index, features) for index in at],
            out_specs=pl.BlockSpec((1, rows, features), lambda i, where, to: (to[i], 0, 0)),
        ),
        out_shape=jax.ShapeDtypeStruct((total, rows, features), jnp.bfloat16),
        compiler_params=params(),
        cost_estimate=cost(8 * count * rows * features**2, 6 * count * rows * features),
        name="back",
    )(where, to, second, packed, rank_rows, *weights)


def rank_spec(entries):
    return pl.BlockSpec((1,) + entries.shape[1:], lambda i, *_: (i, 0, 0, 0))


def run_tables(places, order, position, entries, angles):
    owners = entries.shape[0]
    atoms = angles.shape[1]
    groups = atoms // GROUP
    span = GROUP * SLOTS
    return pl.pallas_call(
        table_kernel,
        grid_spec=pltpu.PrefetchScalarGridSpec(
            num_scalar_prefetch=3,
            grid=(owners,),
            in_specs=[
                rank_spec(entries),
                pl.BlockSpec((1, atoms, angles.shape[2]), lambda i, places, *_: (places[i], 0, 0)),
            ],
            out_specs=[
                rank_spec(entries),
                pl.BlockSpec((1, groups, span, span), lambda i, *_: (i, 0, 0, 0)),
            ],
        ),
        out_shape=[
            jax.ShapeDtypeStruct(entries.shape, jnp.int32),
            jax.ShapeDtypeStruct((owners, groups, span, span), jnp.bfloat16),
        ],
        compiler_params=params(),
        cost_estimate=cost(0, 8 * owners * groups * span**2),
        name="tables",
    )(places, order, position, entries, angles)


def run_mix(owner_of, place_of, order, received, rank, blocks):
    devices, sides, half, _ = received.shape
    unit = 2 * half // devices
    smem = pl.BlockSpec(memory_space=pltpu.SMEM)
    shape = (sides, devices, half, LANES)
    scratch = pltpu.VMEM((sides, devices, devices, unit, LANES), jnp.bfloat16)
    return pl.pallas_call(
        mix_kernel,
        grid=(devices // PAIR,),
        in_specs=[
            smem,
            smem,
            smem,
            whole_spec(received),
            pl.BlockSpec((PAIR,) + rank.shape[1:], lambda i: (i, 0, 0, 0)),
            pl.BlockSpec((PAIR,) + blocks.shape[1:], lambda i: (i, 0, 0, 0)),
        ],
        out_specs=pl.BlockSpec(shape, lambda i: (0, 0, 0, 0)),
        out_shape=jax.ShapeDtypeStruct(shape, jnp.bfloat16),
        scratch_shapes=[scratch, scratch],
        compiler_params=params(),
        cost_estimate=cost(10 * devices * sides * half**2 * LANES, 16 * devices * sides * half**2),
        name="mix",
    )(owner_of, place_of, order, received, rank, blocks)


def unit_tables(entries, capacity, unit):
    owners, sides, rows = entries.shape
    ids = jnp.arange(owners, dtype=jnp.int32)
    source = entries.reshape(owners, sides * rows) // capacity
    counts = jnp.sum((source[None] == ids[:, None, None]).astype(jnp.int32), axis=2) // (unit * sides)
    before = ids[:, None] < ids[None, :]
    starts = jnp.sum(jnp.where(before[None], counts[:, :, None], 0), axis=1)
    places = jnp.sum(jnp.where(before[:, :, None], counts[:, None, :], 0), axis=0)
    inside = (starts[:, :, None] <= ids) & (ids < (starts + counts)[:, :, None])
    owner_of = jnp.sum(jnp.where(inside, ids[None, :, None], 0), axis=1)
    place_of = jnp.sum(jnp.where(inside, (places - starts)[:, :, None] + ids, 0), axis=1)
    return owner_of, place_of


def ranks(values):
    return jnp.sum((values[:, :, None] < values[:, None, :]).astype(jnp.int32), axis=1)


CHUNKS = 2


def reorder(values, order):
    hits = order[:, None] == jnp.arange(values.shape[0], dtype=jnp.int32)
    return jnp.sum(jnp.where(hits[:, :, None], values[None], 0), axis=1)


def shift(values, offset, wide):
    if offset == 0:
        return values
    return lax.ppermute(values, "wide", [(i, i ^ offset) for i in range(wide)])


def swap(values):
    return lax.all_to_all(values, "narrow", 0, 0, tiled=True)


BASE = 64


def share_lists(listed, angles, after):
    narrow = lax.axis_size("narrow")
    atoms, width = angles.shape
    digits = jnp.stack([listed // BASE, listed % BASE]).reshape(atoms, -1).astype(jnp.bfloat16)
    shared = jnp.concatenate([angles, digits], axis=1)[None]
    held = [0]
    hop = narrow // 2
    while hop:
        if hop == 1:
            shared, after = lax.optimization_barrier((shared, after))
        other = lax.ppermute(shared, "narrow", [(i, i ^ hop) for i in range(narrow)])
        shared = jnp.concatenate([shared, other], axis=0)
        held += [offset ^ hop for offset in held]
        hop //= 2
    inverse = jnp.array([held.index(offset) for offset in range(narrow)], jnp.int32)
    mine = lax.axis_index("narrow").astype(jnp.int32)
    owners = jnp.arange(narrow, dtype=jnp.int32) ^ mine
    places = jnp.sum(jnp.where(owners[:, None] == jnp.arange(narrow), inverse, 0), axis=1)
    digits = shared[:, :, width:].reshape((narrow, 2) + listed.shape).astype(jnp.int32)
    entries = digits[:, 0] * BASE + digits[:, 1]
    entries = reorder(entries.reshape(narrow, -1), places).reshape(entries.shape)
    return entries, shared, places, after


def tiled_local(messages, reverse_position, route_slot, atom_slots, angles, weights):
    wide = lax.axis_size("wide")
    narrow = lax.axis_size("narrow")
    edge_rows, features = messages.shape
    rows = edge_rows // wide
    unit = rows // narrow
    capacity = 2 * edge_rows // narrow
    atoms = angles.shape[0]
    group_id = lax.axis_index("wide").astype(jnp.int32)
    offsets = [offset for index in range(wide // 2) for offset in (index, wide - 1 - index)]
    order = group_id ^ jnp.array(offsets, jnp.int32)
    inverse = jnp.array([offsets.index(offset) for offset in range(wide)], jnp.int32)
    owners_wide = (jnp.arange(wide, dtype=jnp.int32) ^ group_id)[:, None]
    position = jnp.sum(jnp.where(owners_wide == jnp.arange(wide), inverse, 0), axis=1)
    half = wide // 2
    pieces = [(0, 1), (1, wide - 1)]
    halves = [(0, half), (half, wide - half)]

    blocks_of = messages.reshape(wide, rows, features)
    sent = [
        lax.dynamic_index_in_dim(blocks_of, group_id ^ offset, 0, False) for offset in offsets[1:]
    ]
    *sent, atom_slots, route_slot, reverse_position = lax.optimization_barrier(
        (*sent, atom_slots, route_slot, reverse_position)
    )
    received = {offset: shift(part, offset, wide) for offset, part in zip(offsets[1:], sent)}
    listed = atom_slots.reshape(atoms // GROUP, GROUP, wide, SLOTS // wide)
    listed = reorder(jnp.transpose(listed, (2, 0, 3, 1)).reshape(wide, rows), order)
    rank = reorder(ranks(route_slot.reshape(wide, rows)), order)
    back_rows = reorder(reverse_position.reshape(wide, rows), order)

    current = {start: (blocks_of, order[start : start + count]) for start, count in pieces}
    tables = None
    for section in range(BLOCKS):
        last = section == BLOCKS - 1
        targets = []
        for start, count in halves if section else pieces:
            array, where = current[start]
            needed = [received[offset] for offset in offsets[start : start + count] if offset]
            targets = list(run_front(
                array, where, needed, start == 0, start, wide,
                back_rows[:, None, :], rank[:, None, :], weights, section, targets,
            ))
        second, packed = targets
        if tables is None:
            entries, all_angles, owner_places, packed = share_lists(listed, angles, packed)
            packed, late_rank = lax.optimization_barrier((packed, rank))
            owner_of, place_of = unit_tables(entries, capacity, unit)
            tables = run_tables(owner_places, order, position, entries[:, :, None, :], all_angles)
            partner_rank = jnp.stack(
                [shift(late_rank[place], offset, wide) for place, offset in enumerate(offsets)]
            )
            hits = back_rows[:, :, None] == jnp.arange(rows, dtype=jnp.int32)
            turned_rank = jnp.sum(jnp.where(hits, partner_rank[:, None, :], 0), axis=2)[:, None, :]
        mixed = run_mix(owner_of, place_of, order, swap(packed), *tables)
        late, at = weights[5:], [section] * 3
        if not last:
            mixed, *late = lax.optimization_barrier((mixed, *late))
            late, at = [jnp.stack([weight[section] for weight in late])] * 3, range(3)
        mixed = mixed.reshape(wide * narrow, rows // 2, LANES)
        returned = lax.all_to_all(mixed, ("wide", "narrow"), 0, 0, tiled=True)
        returned = returned.reshape(wide, narrow, rows // 2, LANES)
        if last:
            current = run_back(second, returned, order, order, 0, turned_rank, late, at, wide)
            return current.reshape(edge_rows, features)
        for start, count in halves:
            plain = jnp.arange(count, dtype=jnp.int32)
            where = order[start : start + count]
            result = run_back(second, returned, where, plain, start, turned_rank, late, at, count)
            current[start] = (result, plain)
            for index, offset in enumerate(offsets[start : start + count]):
                if offset:
                    received[offset] = shift(result[index], offset, wide)


def local(
    messages,
    reverse_position,
    route_slot,
    atom_slots,
    angles,
    weight_message,
    weight_reverse,
    weight_combine,
    weight_inner,
    weight_outer,
    weight_lift,
    weight_expand,
    weight_reduce,
):
    weights = (
        weight_message,
        weight_reverse,
        weight_combine,
        weight_inner,
        weight_outer,
        weight_lift,
        weight_expand,
        weight_reduce,
    )
    wide = lax.axis_size("wide")
    narrow = lax.axis_size("narrow")
    edge_rows, features = messages.shape
    unit = edge_rows // wide // narrow
    fits = (
        features == narrow * HALF
        and unit % 16 == 0
        and narrow % 2 == 0
        and wide >= 4
        and wide & (wide - 1) == 0
        and narrow & (narrow - 1) == 0
        and angles.shape[0] % GROUP == 0
        and (SLOTS // wide * GROUP) % 16 == 0
    )
    run = tiled_local if fits else general_local
    return run(messages, reverse_position, route_slot, atom_slots, angles, weights)


def solution(mesh):
    in_specs = (
        P(("wide", "narrow"), None),
        P(("wide", "narrow")),
        P(("wide", "narrow")),
        P(("wide", "narrow")),
        P(("wide", "narrow"), None),
        P(),
        P(),
        P(),
        P(),
        P(),
        P(),
        P(),
        P(),
    )
    out_specs = P(("wide", "narrow"), None)
    return jax.shard_map(local, mesh=mesh, in_specs=in_specs, out_specs=out_specs, check_vma=False)
```

```python
import functools

import jax
import jax.numpy as jnp
from jax import lax
from jax.experimental import pallas as pl
from jax.experimental.pallas import tpu as pltpu
from jax.sharding import PartitionSpec as P

SLOTS = 32
BLOCKS = 2
LANES = 128
HALF = LANES // 2
GROUP = 8
PAIR = 4


ROOT_HALF = 0.7071067811865476


def project(operand, weight):
    return jnp.dot(operand, weight, preferred_element_type=jnp.float32)


def residual(previous, branch):
    return ((previous.astype(jnp.float32) + branch) * ROOT_HALF).astype(jnp.bfloat16)


def reverse_edges(values, partner_rows):
    exchanged = lax.all_to_all(values, "wide", split_axis=0, concat_axis=0, tiled=True)
    return jnp.take(exchanged, partner_rows, axis=0)


def edge_front(current, reverse, weights, section_index):
    hidden = jax.nn.silu(
        project(current, weights[0][section_index]) + project(reverse, weights[1][section_index])
    ).astype(jnp.bfloat16)
    first_res = residual(current, project(hidden, weights[2][section_index]))
    inner_value = jax.nn.silu(project(first_res, weights[3][section_index])).astype(jnp.bfloat16)
    return residual(first_res, jax.nn.silu(project(inner_value, weights[4][section_index])))


def edge_back(second, turned, weights, section_index):
    third_res = residual(second, jax.nn.silu(project(turned, weights[5][section_index])))
    expand = jax.nn.silu(project(third_res, weights[6][section_index])).astype(jnp.bfloat16)
    return residual(third_res, jax.nn.silu(project(expand, weights[7][section_index])))


def owners_mix(second, route_slot, atom_slots, mixing):
    features = second.shape[1]
    buffer_rows = 2 * second.shape[0]
    outgoing = jnp.zeros((buffer_rows, features), jnp.bfloat16).at[route_slot].set(second)
    received = lax.all_to_all(outgoing, "narrow", split_axis=0, concat_axis=0, tiled=True)
    gathered = jnp.take(received, atom_slots, axis=0).reshape(mixing.shape[0], SLOTS, features)
    mixed_rows = jnp.einsum(
        "apq,aqd->apd", mixing, gathered, preferred_element_type=jnp.float32
    ).astype(jnp.bfloat16)
    return mixed_rows.reshape(-1, features)


def back_to_edges(mixed_flat, route_slot, atom_slots):
    features = mixed_flat.shape[1]
    buffer_rows = 2 * route_slot.shape[0]
    answer = jnp.zeros((buffer_rows, features), jnp.bfloat16).at[atom_slots].set(mixed_flat)
    incoming = lax.all_to_all(answer, "narrow", split_axis=0, concat_axis=0, tiled=True)
    return jnp.take(incoming, route_slot, axis=0)


def general_local(messages, reverse_position, route_slot, atom_slots, angles, weights):
    edge_rows = messages.shape[0]
    sub_rows = edge_rows // lax.axis_size("wide")
    partner_rows = jnp.arange(edge_rows, dtype=jnp.int32) // sub_rows * sub_rows + reverse_position
    mixing = angles.reshape(angles.shape[0], SLOTS, SLOTS)
    current = messages
    for section_index in range(BLOCKS):
        reverse = reverse_edges(current, partner_rows)
        second = edge_front(current, reverse, weights, section_index)
        mixed_flat = owners_mix(second, route_slot, atom_slots, mixing)
        returned = back_to_edges(mixed_flat, route_slot, atom_slots)
        turned = reverse_edges(returned, partner_rows)
        current = edge_back(second, turned, weights, section_index)
    return current


def silu(value):
    return 0.5 * value * (1.0 + jnp.tanh(0.5 * value))


def dot(left, right):
    return jnp.dot(left, right, preferred_element_type=jnp.float32)


def halve(previous, branch):
    return ((previous.astype(jnp.float32) + branch) * ROOT_HALF).astype(jnp.bfloat16)


def iotas(size):
    shape = (size, size)
    return lax.broadcasted_iota(jnp.int32, shape, 0), lax.broadcasted_iota(jnp.int32, shape, 1)


def as_column(row, rows_iota, lanes_iota):
    return jnp.sum(jnp.where(rows_iota == lanes_iota, row, 0), axis=1, keepdims=True)


def one_hot(mask):
    return jnp.where(mask, 1.0, 0.0).astype(jnp.bfloat16)


def row_parts(rows):
    half = rows // 2
    return [slice(0, half), slice(half, rows)]


def front_kernel(own, count, where_ref, cur_ref, back_ref, rank_ref, wm, wr, wc, wi, wo, *refs):
    recv_refs, (second_ref, packed_ref, reverse_ref) = refs[: count - own], refs[-3:]
    rows_iota, lanes_iota = iotas(cur_ref.shape[1])
    partner = as_column(back_ref[0], rows_iota, lanes_iota)
    hot = one_hot(partner == lanes_iota)
    sources = ([cur_ref.at[0]] if own else []) + list(recv_refs)
    for index in range(count):

        @pl.when(pl.program_id(0) == index)
        def _():
            reverse_ref[...] = dot(hot, sources[index][...]).astype(jnp.bfloat16)

    parts = row_parts(cur_ref.shape[1])
    current = [cur_ref[0, part, :] for part in parts]
    sums = [dot(rows, wm[0]) + dot(reverse_ref[part, :], wr[0]) for rows, part in zip(current, parts)]
    hidden = [silu(rows).astype(jnp.bfloat16) for rows in sums]
    first_res = [halve(rows, dot(left, wc[0])) for rows, left in zip(current, hidden)]
    inner = [silu(dot(rows, wi[0])).astype(jnp.bfloat16) for rows in first_res]
    for rows, left, part in zip(first_res, inner, parts):
        second_ref[0, part, :] = halve(rows, silu(dot(left, wo[0])))
    second = second_ref[0]
    ordered = dot(one_hot(rows_iota == rank_ref[0]), second)
    half = ordered.shape[0] // 2
    low = lax.broadcasted_iota(jnp.int32, (half, LANES), 1) < HALF
    for tile in range(ordered.shape[1] // LANES):
        top = ordered[:half, tile * LANES : (tile + 1) * LANES]
        bottom = ordered[half:, tile * LANES : (tile + 1) * LANES]
        packed_ref[2 * tile, 0] = jnp.where(low, top, pltpu.roll(bottom, HALF, 1)).astype(jnp.bfloat16)
        packed_ref[2 * tile + 1, 0] = jnp.where(low, pltpu.roll(top, HALF, 1), bottom).astype(jnp.bfloat16)


def back_kernel(from_ref, to_ref, second_ref, packed_ref, rank_ref, wl, we, wd, out_ref):
    rows_iota, lanes_iota = iotas(second_ref.shape[1])
    half = rows_iota.shape[0] // 2
    low = lax.broadcasted_iota(jnp.int32, (half, LANES), 1) < HALF
    tops, bottoms = [], []
    for tile in range(second_ref.shape[2] // LANES):
        even = packed_ref[0, 2 * tile].astype(jnp.float32)
        odd = packed_ref[0, 2 * tile + 1].astype(jnp.float32)
        tops.append(jnp.where(low, even, pltpu.roll(odd, HALF, 1)).astype(jnp.bfloat16))
        bottoms.append(jnp.where(low, pltpu.roll(even, HALF, 1), odd).astype(jnp.bfloat16))
    ordered = jnp.concatenate(
        [jnp.concatenate(tops, axis=1), jnp.concatenate(bottoms, axis=1)], axis=0
    )
    source = as_column(rank_ref[0], rows_iota, lanes_iota)
    hot = one_hot(source == lanes_iota)
    parts = row_parts(hot.shape[0])
    turned = [dot(hot[part, :], ordered).astype(jnp.bfloat16) for part in parts]
    third_res = [
        halve(second_ref[0, part, :], silu(dot(rows, wl[0]))) for rows, part in zip(turned, parts)
    ]
    expand = [silu(dot(rows, we[0])).astype(jnp.bfloat16) for rows in third_res]
    for rows, left, part in zip(third_res, expand, parts):
        out_ref[0, part, :] = halve(rows, silu(dot(left, wd[0])))


def table_kernel(places_ref, order_ref, position_ref, entry_ref, angles_ref, rank_ref, blocks_ref):
    sides, _, size = entry_ref.shape[1:]
    rows_iota, lanes_iota = iotas(size)
    for side in range(sides):
        row = entry_ref[0, side]
        column = as_column(row, rows_iota, lanes_iota)
        rank_ref[0, side] = jnp.sum(jnp.where(column < row, 1, 0), axis=0, keepdims=True)
    span = GROUP * SLOTS
    strip = span // sides
    rows_iota, lanes_iota = iotas(span)
    own = rows_iota % GROUP == lanes_iota % GROUP
    spread_rows = lax.broadcasted_iota(jnp.int32, (SLOTS, span), 0)
    spread_lanes = lax.broadcasted_iota(jnp.int32, (SLOTS, span), 1)
    side_at = jnp.zeros((SLOTS, span), jnp.int32)
    for place in range(sides):
        side_at = jnp.where(spread_lanes // strip == place, order_ref[place], side_at)
    spread = one_hot(side_at * (SLOTS // sides) + spread_lanes % strip // GROUP == spread_rows)
    for group in range(angles_ref.shape[1] // GROUP):
        local = angles_ref[0, group * GROUP : (group + 1) * GROUP, :].astype(jnp.float32)
        stacked = jnp.concatenate(
            [local[:, p * SLOTS : (p + 1) * SLOTS] for p in range(SLOTS)], axis=0
        ).astype(jnp.bfloat16)
        block = jnp.where(own, dot(stacked, spread), 0.0).astype(jnp.bfloat16)
        for side in range(sides):
            to = pl.multiple_of(position_ref[side] * strip, strip)
            blocks_ref[0, group, pl.ds(to, strip), :] = block[side * strip : (side + 1) * strip]


def mix_kernel(owner_ref, place_ref, order_ref, recv_ref, rank_ref, blocks_ref, out_ref, ins, outs):
    step = pl.program_id(0)
    devices, sides = recv_ref.shape[:2]
    unit = ins.shape[3]
    rows = devices * unit
    groups = blocks_ref.shape[1]
    strip = blocks_ref.shape[2] // sides
    pairs = devices // 2

    @pl.when(step == 0)
    def _():
        @pl.loop(0, devices)
        def _(source):
            for index in range(devices):
                owner = owner_ref[source, index]
                place = place_ref[source, index]
                at = (index % pairs) * unit
                for side in range(sides):
                    block = recv_ref[source, side, at : at + unit, :]
                    if index >= pairs:
                        block = pltpu.roll(block.astype(jnp.float32), HALF, 1).astype(jnp.bfloat16)
                    ins[side, owner, place] = block

    rows_iota, lanes_iota = iotas(rows)
    pair = range(PAIR)
    gathered = [[] for _ in pair]
    for side in range(sides):
        for index in pair:
            source = as_column(rank_ref[index, side], rows_iota, lanes_iota)
            operand = ins[side, PAIR * step + index].reshape(rows, LANES)
            gathered[index].append(dot(one_hot(source == lanes_iota), operand).astype(jnp.bfloat16))
    mixed = [[] for _ in pair]
    for group in range(groups):
        for index in pair:
            operand = jnp.concatenate(
                [part[group * strip : (group + 1) * strip] for part in gathered[index]], axis=0
            )
            mixed[index].append(dot(blocks_ref[index, group], operand).astype(jnp.bfloat16))
    for side in range(sides):
        for index in pair:
            operand = jnp.concatenate(
                [part[side * strip : (side + 1) * strip] for part in mixed[index]], axis=0
            )
            outs[side, PAIR * step + index] = (
                dot(one_hot(rows_iota == rank_ref[index, side]), operand)
                .astype(jnp.bfloat16)
                .reshape(devices, unit, LANES)
            )

    @pl.when(step == pl.num_programs(0) - 1)
    def _():
        low = lax.broadcasted_iota(jnp.int32, (unit, LANES), 1) < HALF

        @pl.loop(0, devices)
        def _(source):
            for index in range(pairs):
                owner = owner_ref[source, index]
                place = place_ref[source, index]
                owner_far = owner_ref[source, index + pairs]
                place_far = place_ref[source, index + pairs]
                for side in range(sides):
                    near = outs[side, owner, place].astype(jnp.float32)
                    far = outs[side, owner_far, place_far].astype(jnp.float32)
                    joined = jnp.where(low, near, pltpu.roll(far, HALF, 1)).astype(jnp.bfloat16)
                    out_ref[order_ref[side], source, index * unit : (index + 1) * unit, :] = joined


VMEM_BYTES = 24 * 1024 * 1024
VMEM_MOST = 60 * 1024 * 1024


def params(limit=VMEM_BYTES):
    return pltpu.CompilerParams(vmem_limit_bytes=limit)


def cost(flops, moved, waves=0):
    return pl.CostEstimate(flops=flops, bytes_accessed=moved, transcendentals=waves)


def whole_spec(array):
    zeros = (0,) * array.ndim
    return pl.BlockSpec(array.shape, lambda i, *_: zeros)


def weight_spec(section, features):
    return pl.BlockSpec((1, features, features), lambda i, *_: (section, 0, 0))


def run_front(current, where, received, own, start, sides, back_rows, rank_rows, weights, section, targets):
    _, rows, features = current.shape
    count = where.shape[0]
    narrow = features // HALF
    row_spec = pl.BlockSpec((1, 1, rows), lambda i, where: (start + i, 0, 0))
    first_target = 9 + len(received)
    return pl.pallas_call(
        functools.partial(front_kernel, own, count),
        grid_spec=pltpu.PrefetchScalarGridSpec(
            num_scalar_prefetch=1,
            grid=(count,),
            in_specs=[
                pl.BlockSpec((1, rows, features), lambda i, where: (where[i], 0, 0)),
                row_spec,
                row_spec,
            ]
            + [weight_spec(section, features)] * 5
            + [whole_spec(array) for array in received]
            + [pl.BlockSpec(memory_space=pl.ANY)] * len(targets),
            out_specs=[
                pl.BlockSpec((1, rows, features), lambda i, where: (start + i, 0, 0)),
                pl.BlockSpec((narrow, 1, rows // 2, LANES), lambda i, where: (0, start + i, 0, 0)),
            ],
            scratch_shapes=[pltpu.VMEM((rows, features), jnp.bfloat16)],
        ),
        out_shape=[
            jax.ShapeDtypeStruct((sides, rows, features), jnp.bfloat16),
            jax.ShapeDtypeStruct((narrow, sides, rows // 2, LANES), jnp.bfloat16),
        ],
        input_output_aliases={first_target + index: index for index in range(len(targets))},
        compiler_params=params(VMEM_BYTES if section else VMEM_MOST),
        cost_estimate=cost(12 * count * rows * features**2, 8 * count * rows * features),
        name="front",
    )(where, current, back_rows, rank_rows, *weights[:5], *received, *targets)


def run_back(second, packed, where, to, start, rank_rows, weights, at, total):
    _, rows, features = second.shape
    count = where.shape[0]
    narrow = packed.shape[1]
    return pl.pallas_call(
        back_kernel,
        grid_spec=pltpu.PrefetchScalarGridSpec(
            num_scalar_prefetch=2,
            grid=(count,),
            in_specs=[
                pl.BlockSpec((1, rows, features), lambda i, *_: (start + i, 0, 0)),
                pl.BlockSpec((1, narrow, rows // 2, LANES), lambda i, where, to: (where[i], 0, 0, 0)),
                pl.BlockSpec((1, 1, rows), lambda i, *_: (start + i, 0, 0)),
            ]
            + [weight_spec(index, features) for index in at],
            out_specs=pl.BlockSpec((1, rows, features), lambda i, where, to: (to[i], 0, 0)),
        ),
        out_shape=jax.ShapeDtypeStruct((total, rows, features), jnp.bfloat16),
        compiler_params=params(),
        cost_estimate=cost(8 * count * rows * features**2, 6 * count * rows * features),
        name="back",
    )(where, to, second, packed, rank_rows, *weights)


def rank_spec(entries):
    return pl.BlockSpec((1,) + entries.shape[1:], lambda i, *_: (i, 0, 0, 0))


def run_tables(places, order, position, entries, angles):
    owners = entries.shape[0]
    atoms = angles.shape[1]
    groups = atoms // GROUP
    span = GROUP * SLOTS
    return pl.pallas_call(
        table_kernel,
        grid_spec=pltpu.PrefetchScalarGridSpec(
            num_scalar_prefetch=3,
            grid=(owners,),
            in_specs=[
                rank_spec(entries),
                pl.BlockSpec((1, atoms, angles.shape[2]), lambda i, places, *_: (places[i], 0, 0)),
            ],
            out_specs=[
                rank_spec(entries),
                pl.BlockSpec((1, groups, span, span), lambda i, *_: (i, 0, 0, 0)),
            ],
        ),
        out_shape=[
            jax.ShapeDtypeStruct(entries.shape, jnp.int32),
            jax.ShapeDtypeStruct((owners, groups, span, span), jnp.bfloat16),
        ],
        compiler_params=params(),
        cost_estimate=cost(0, 8 * owners * groups * span**2),
        name="tables",
    )(places, order, position, entries, angles)


def run_mix(owner_of, place_of, order, received, rank, blocks):
    devices, sides, half, _ = received.shape
    unit = 2 * half // devices
    smem = pl.BlockSpec(memory_space=pltpu.SMEM)
    shape = (sides, devices, half, LANES)
    scratch = pltpu.VMEM((sides, devices, devices, unit, LANES), jnp.bfloat16)
    return pl.pallas_call(
        mix_kernel,
        grid=(devices // PAIR,),
        in_specs=[
            smem,
            smem,
            smem,
            whole_spec(received),
            pl.BlockSpec((PAIR,) + rank.shape[1:], lambda i: (i, 0, 0, 0)),
            pl.BlockSpec((PAIR,) + blocks.shape[1:], lambda i: (i, 0, 0, 0)),
        ],
        out_specs=pl.BlockSpec(shape, lambda i: (0, 0, 0, 0)),
        out_shape=jax.ShapeDtypeStruct(shape, jnp.bfloat16),
        scratch_shapes=[scratch, scratch],
        compiler_params=params(),
        cost_estimate=cost(10 * devices * sides * half**2 * LANES, 16 * devices * sides * half**2),
        name="mix",
    )(owner_of, place_of, order, received, rank, blocks)


def unit_tables(entries, capacity, unit):
    owners, sides, rows = entries.shape
    ids = jnp.arange(owners, dtype=jnp.int32)
    source = entries.reshape(owners, sides * rows) // capacity
    counts = jnp.sum((source[None] == ids[:, None, None]).astype(jnp.int32), axis=2) // (unit * sides)
    before = ids[:, None] < ids[None, :]
    starts = jnp.sum(jnp.where(before[None], counts[:, :, None], 0), axis=1)
    places = jnp.sum(jnp.where(before[:, :, None], counts[:, None, :], 0), axis=0)
    inside = (starts[:, :, None] <= ids) & (ids < (starts + counts)[:, :, None])
    owner_of = jnp.sum(jnp.where(inside, ids[None, :, None], 0), axis=1)
    place_of = jnp.sum(jnp.where(inside, (places - starts)[:, :, None] + ids, 0), axis=1)
    return owner_of, place_of


def ranks(values):
    return jnp.sum((values[:, :, None] < values[:, None, :]).astype(jnp.int32), axis=1)


CHUNKS = 2


def reorder(values, order):
    hits = order[:, None] == jnp.arange(values.shape[0], dtype=jnp.int32)
    return jnp.sum(jnp.where(hits[:, :, None], values[None], 0), axis=1)


def shift(values, offset, wide):
    if offset == 0:
        return values
    return lax.ppermute(values, "wide", [(i, i ^ offset) for i in range(wide)])


def swap(values):
    return lax.all_to_all(values, "narrow", 0, 0, tiled=True)


BASE = 64


def share_lists(listed, angles, after):
    narrow = lax.axis_size("narrow")
    atoms, width = angles.shape
    digits = jnp.stack([listed // BASE, listed % BASE]).reshape(atoms, -1).astype(jnp.bfloat16)
    shared = jnp.concatenate([angles, digits], axis=1)[None]
    held = [0]
    hop = narrow // 2
    while hop:
        if hop == 1:
            shared, after = lax.optimization_barrier((shared, after))
        other = lax.ppermute(shared, "narrow", [(i, i ^ hop) for i in range(narrow)])
        shared = jnp.concatenate([shared, other], axis=0)
        held += [offset ^ hop for offset in held]
        hop //= 2
    inverse = jnp.array([held.index(offset) for offset in range(narrow)], jnp.int32)
    mine = lax.axis_index("narrow").astype(jnp.int32)
    owners = jnp.arange(narrow, dtype=jnp.int32) ^ mine
    places = jnp.sum(jnp.where(owners[:, None] == jnp.arange(narrow), inverse, 0), axis=1)
    digits = shared[:, :, width:].reshape((narrow, 2) + listed.shape).astype(jnp.int32)
    entries = digits[:, 0] * BASE + digits[:, 1]
    entries = reorder(entries.reshape(narrow, -1), places).reshape(entries.shape)
    return entries, shared, places, after


def tiled_local(messages, reverse_position, route_slot, atom_slots, angles, weights):
    wide = lax.axis_size("wide")
    narrow = lax.axis_size("narrow")
    edge_rows, features = messages.shape
    rows = edge_rows // wide
    unit = rows // narrow
    capacity = 2 * edge_rows // narrow
    atoms = angles.shape[0]
    group_id = lax.axis_index("wide").astype(jnp.int32)
    offsets = [offset for index in range(wide // 2) for offset in (index, wide - 1 - index)]
    order = group_id ^ jnp.array(offsets, jnp.int32)
    inverse = jnp.array([offsets.index(offset) for offset in range(wide)], jnp.int32)
    owners_wide = (jnp.arange(wide, dtype=jnp.int32) ^ group_id)[:, None]
    position = jnp.sum(jnp.where(owners_wide == jnp.arange(wide), inverse, 0), axis=1)
    half = wide // 2
    pieces = [(0, 1), (1, wide - 1)]
    halves = [(half, wide - half), (0, half)]
    later = [(half, wide - half), (0, 1), (1, half - 1)]

    blocks_of = messages.reshape(wide, rows, features)
    sent = [
        lax.dynamic_index_in_dim(blocks_of, group_id ^ offset, 0, False) for offset in offsets[1:]
    ]
    *sent, atom_slots, route_slot, reverse_position = lax.optimization_barrier(
        (*sent, atom_slots, route_slot, reverse_position)
    )
    received = {offset: shift(part, offset, wide) for offset, part in zip(offsets[1:], sent)}
    listed = atom_slots.reshape(atoms // GROUP, GROUP, wide, SLOTS // wide)
    listed = reorder(jnp.transpose(listed, (2, 0, 3, 1)).reshape(wide, rows), order)
    rank = reorder(ranks(route_slot.reshape(wide, rows)), order)
    back_rows = reorder(reverse_position.reshape(wide, rows), order)

    current = {start: (blocks_of, order[start : start + count]) for start, count in pieces}
    tables = None
    for section in range(BLOCKS):
        last = section == BLOCKS - 1
        targets = []
        for start, count in later if section else pieces:
            array, where = current[start]
            needed = [received[offset] for offset in offsets[start : start + count] if offset]
            targets = list(run_front(
                array, where, needed, start == 0, start, wide,
                back_rows[:, None, :], rank[:, None, :], weights, section, targets,
            ))
        second, packed = targets
        if tables is None:
            entries, all_angles, owner_places, packed = share_lists(listed, angles, packed)
            packed, late_rank = lax.optimization_barrier((packed, rank))
            owner_of, place_of = unit_tables(entries, capacity, unit)
            tables = run_tables(owner_places, order, position, entries[:, :, None, :], all_angles)
            partner_rank = jnp.stack(
                [shift(late_rank[place], offset, wide) for place, offset in enumerate(offsets)]
            )
            hits = back_rows[:, :, None] == jnp.arange(rows, dtype=jnp.int32)
            turned_rank = jnp.sum(jnp.where(hits, partner_rank[:, None, :], 0), axis=2)[:, None, :]
        mixed = run_mix(owner_of, place_of, order, swap(packed), *tables)
        late, at = weights[5:], [section] * 3
        if not last:
            mixed, *late = lax.optimization_barrier((mixed, *late))
            late, at = [jnp.stack([weight[section] for weight in late])] * 3, range(3)
        mixed = mixed.reshape(wide * narrow, rows // 2, LANES)
        returned = lax.all_to_all(mixed, ("wide", "narrow"), 0, 0, tiled=True)
        returned = returned.reshape(wide, narrow, rows // 2, LANES)
        if last:
            current = run_back(second, returned, order, order, 0, turned_rank, late, at, wide)
            return current.reshape(edge_rows, features)
        for start, count in halves:
            plain = jnp.arange(count, dtype=jnp.int32)
            where = order[start : start + count]
            result = run_back(second, returned, where, plain, start, turned_rank, late, at, count)
            for first, number in later:
                if start <= first < start + count:
                    current[first] = (result, first - start + jnp.arange(number, dtype=jnp.int32))
            for index, offset in enumerate(offsets[start : start + count]):
                if offset:
                    received[offset] = shift(result[index], offset, wide)


def local(
    messages,
    reverse_position,
    route_slot,
    atom_slots,
    angles,
    weight_message,
    weight_reverse,
    weight_combine,
    weight_inner,
    weight_outer,
    weight_lift,
    weight_expand,
    weight_reduce,
):
    weights = (
        weight_message,
        weight_reverse,
        weight_combine,
        weight_inner,
        weight_outer,
        weight_lift,
        weight_expand,
        weight_reduce,
    )
    wide = lax.axis_size("wide")
    narrow = lax.axis_size("narrow")
    edge_rows, features = messages.shape
    unit = edge_rows // wide // narrow
    fits = (
        features == narrow * HALF
        and unit % 16 == 0
        and narrow % 2 == 0
        and wide >= 4
        and narrow % PAIR == 0
        and wide & (wide - 1) == 0
        and narrow & (narrow - 1) == 0
        and angles.shape[0] % GROUP == 0
        and (SLOTS // wide * GROUP) % 16 == 0
    )
    run = tiled_local if fits else general_local
    return run(messages, reverse_position, route_slot, atom_slots, angles, weights)


def solution(mesh):
    in_specs = (
        P(("wide", "narrow"), None),
        P(("wide", "narrow")),
        P(("wide", "narrow")),
        P(("wide", "narrow")),
        P(("wide", "narrow"), None),
        P(),
        P(),
        P(),
        P(),
        P(),
        P(),
        P(),
        P(),
    )
    out_specs = P(("wide", "narrow"), None)
    return jax.shard_map(local, mesh=mesh, in_specs=in_specs, out_specs=out_specs, check_vma=False)
```

```python
import functools

import jax
import jax.numpy as jnp
from jax import lax
from jax.experimental import pallas as pl
from jax.experimental.pallas import tpu as pltpu
from jax.sharding import PartitionSpec as P

SLOTS = 32
BLOCKS = 2
LANES = 128
HALF = LANES // 2
GROUP = 8
PAIR = 4


ROOT_HALF = 0.7071067811865476


def project(operand, weight):
    return jnp.dot(operand, weight, preferred_element_type=jnp.float32)


def residual(previous, branch):
    return ((previous.astype(jnp.float32) + branch) * ROOT_HALF).astype(jnp.bfloat16)


def reverse_edges(values, partner_rows):
    exchanged = lax.all_to_all(values, "wide", split_axis=0, concat_axis=0, tiled=True)
    return jnp.take(exchanged, partner_rows, axis=0)


def edge_front(current, reverse, weights, section_index):
    hidden = jax.nn.silu(
        project(current, weights[0][section_index]) + project(reverse, weights[1][section_index])
    ).astype(jnp.bfloat16)
    first_res = residual(current, project(hidden, weights[2][section_index]))
    inner_value = jax.nn.silu(project(first_res, weights[3][section_index])).astype(jnp.bfloat16)
    return residual(first_res, jax.nn.silu(project(inner_value, weights[4][section_index])))


def edge_back(second, turned, weights, section_index):
    third_res = residual(second, jax.nn.silu(project(turned, weights[5][section_index])))
    expand = jax.nn.silu(project(third_res, weights[6][section_index])).astype(jnp.bfloat16)
    return residual(third_res, jax.nn.silu(project(expand, weights[7][section_index])))


def owners_mix(second, route_slot, atom_slots, mixing):
    features = second.shape[1]
    buffer_rows = 2 * second.shape[0]
    outgoing = jnp.zeros((buffer_rows, features), jnp.bfloat16).at[route_slot].set(second)
    received = lax.all_to_all(outgoing, "narrow", split_axis=0, concat_axis=0, tiled=True)
    gathered = jnp.take(received, atom_slots, axis=0).reshape(mixing.shape[0], SLOTS, features)
    mixed_rows = jnp.einsum(
        "apq,aqd->apd", mixing, gathered, preferred_element_type=jnp.float32
    ).astype(jnp.bfloat16)
    return mixed_rows.reshape(-1, features)


def back_to_edges(mixed_flat, route_slot, atom_slots):
    features = mixed_flat.shape[1]
    buffer_rows = 2 * route_slot.shape[0]
    answer = jnp.zeros((buffer_rows, features), jnp.bfloat16).at[atom_slots].set(mixed_flat)
    incoming = lax.all_to_all(answer, "narrow", split_axis=0, concat_axis=0, tiled=True)
    return jnp.take(incoming, route_slot, axis=0)


def general_local(messages, reverse_position, route_slot, atom_slots, angles, weights):
    edge_rows = messages.shape[0]
    sub_rows = edge_rows // lax.axis_size("wide")
    partner_rows = jnp.arange(edge_rows, dtype=jnp.int32) // sub_rows * sub_rows + reverse_position
    mixing = angles.reshape(angles.shape[0], SLOTS, SLOTS)
    current = messages
    for section_index in range(BLOCKS):
        reverse = reverse_edges(current, partner_rows)
        second = edge_front(current, reverse, weights, section_index)
        mixed_flat = owners_mix(second, route_slot, atom_slots, mixing)
        returned = back_to_edges(mixed_flat, route_slot, atom_slots)
        turned = reverse_edges(returned, partner_rows)
        current = edge_back(second, turned, weights, section_index)
    return current


def silu(value):
    return 0.5 * value * (1.0 + jnp.tanh(0.5 * value))


def dot(left, right):
    return jnp.dot(left, right, preferred_element_type=jnp.float32)


def halve(previous, branch):
    return ((previous.astype(jnp.float32) + branch) * ROOT_HALF).astype(jnp.bfloat16)


def iotas(size):
    shape = (size, size)
    return lax.broadcasted_iota(jnp.int32, shape, 0), lax.broadcasted_iota(jnp.int32, shape, 1)


def as_column(row, rows_iota, lanes_iota):
    return jnp.sum(jnp.where(rows_iota == lanes_iota, row, 0), axis=1, keepdims=True)


def one_hot(mask):
    return jnp.where(mask, 1.0, 0.0).astype(jnp.bfloat16)


def row_parts(rows):
    size = rows // 3 if rows % 48 == 0 else rows // 2
    return [slice(start, start + size) for start in range(0, rows, size)]


def front_kernel(own, count, where_ref, cur_ref, back_ref, rank_ref, wm, wr, wc, wi, wo, *refs):
    recv_refs, (second_ref, packed_ref, reverse_ref) = refs[: count - own], refs[-3:]
    rows_iota, lanes_iota = iotas(cur_ref.shape[1])
    partner = as_column(back_ref[0], rows_iota, lanes_iota)
    hot = one_hot(partner == lanes_iota)
    sources = ([cur_ref.at[0]] if own else []) + list(recv_refs)
    for index in range(count):

        @pl.when(pl.program_id(0) == index)
        def _():
            reverse_ref[...] = dot(hot, sources[index][...]).astype(jnp.bfloat16)

    parts = row_parts(cur_ref.shape[1])
    current = [cur_ref[0, part, :] for part in parts]
    sums = [dot(rows, wm[0]) + dot(reverse_ref[part, :], wr[0]) for rows, part in zip(current, parts)]
    hidden = [silu(rows).astype(jnp.bfloat16) for rows in sums]
    first_res = [halve(rows, dot(left, wc[0])) for rows, left in zip(current, hidden)]
    inner = [silu(dot(rows, wi[0])).astype(jnp.bfloat16) for rows in first_res]
    for rows, left, part in zip(first_res, inner, parts):
        second_ref[0, part, :] = halve(rows, silu(dot(left, wo[0])))
    second = second_ref[0]
    ordered = dot(one_hot(rows_iota == rank_ref[0]), second)
    half = ordered.shape[0] // 2
    low = lax.broadcasted_iota(jnp.int32, (half, LANES), 1) < HALF
    for tile in range(ordered.shape[1] // LANES):
        top = ordered[:half, tile * LANES : (tile + 1) * LANES]
        bottom = ordered[half:, tile * LANES : (tile + 1) * LANES]
        packed_ref[2 * tile, 0] = jnp.where(low, top, pltpu.roll(bottom, HALF, 1)).astype(jnp.bfloat16)
        packed_ref[2 * tile + 1, 0] = jnp.where(low, pltpu.roll(top, HALF, 1), bottom).astype(jnp.bfloat16)


def back_kernel(from_ref, to_ref, second_ref, packed_ref, rank_ref, wl, we, wd, out_ref):
    rows_iota, lanes_iota = iotas(second_ref.shape[1])
    half = rows_iota.shape[0] // 2
    low = lax.broadcasted_iota(jnp.int32, (half, LANES), 1) < HALF
    tops, bottoms = [], []
    for tile in range(second_ref.shape[2] // LANES):
        even = packed_ref[0, 2 * tile].astype(jnp.float32)
        odd = packed_ref[0, 2 * tile + 1].astype(jnp.float32)
        tops.append(jnp.where(low, even, pltpu.roll(odd, HALF, 1)).astype(jnp.bfloat16))
        bottoms.append(jnp.where(low, pltpu.roll(even, HALF, 1), odd).astype(jnp.bfloat16))
    ordered = jnp.concatenate(
        [jnp.concatenate(tops, axis=1), jnp.concatenate(bottoms, axis=1)], axis=0
    )
    source = as_column(rank_ref[0], rows_iota, lanes_iota)
    hot = one_hot(source == lanes_iota)
    parts = row_parts(hot.shape[0])
    turned = [dot(hot[part, :], ordered).astype(jnp.bfloat16) for part in parts]
    third_res = [
        halve(second_ref[0, part, :], silu(dot(rows, wl[0]))) for rows, part in zip(turned, parts)
    ]
    expand = [silu(dot(rows, we[0])).astype(jnp.bfloat16) for rows in third_res]
    for rows, left, part in zip(third_res, expand, parts):
        out_ref[0, part, :] = halve(rows, silu(dot(left, wd[0])))


def table_kernel(places_ref, order_ref, position_ref, entry_ref, angles_ref, rank_ref, blocks_ref):
    sides, _, size = entry_ref.shape[1:]
    rows_iota, lanes_iota = iotas(size)
    for side in range(sides):
        row = entry_ref[0, side]
        column = as_column(row, rows_iota, lanes_iota)
        rank_ref[0, side] = jnp.sum(jnp.where(column < row, 1, 0), axis=0, keepdims=True)
    span = GROUP * SLOTS
    strip = span // sides
    rows_iota, lanes_iota = iotas(span)
    own = rows_iota % GROUP == lanes_iota % GROUP
    spread_rows = lax.broadcasted_iota(jnp.int32, (SLOTS, span), 0)
    spread_lanes = lax.broadcasted_iota(jnp.int32, (SLOTS, span), 1)
    side_at = jnp.zeros((SLOTS, span), jnp.int32)
    for place in range(sides):
        side_at = jnp.where(spread_lanes // strip == place, order_ref[place], side_at)
    spread = one_hot(side_at * (SLOTS // sides) + spread_lanes % strip // GROUP == spread_rows)
    for group in range(angles_ref.shape[1] // GROUP):
        local = angles_ref[0, group * GROUP : (group + 1) * GROUP, :].astype(jnp.float32)
        stacked = jnp.concatenate(
            [local[:, p * SLOTS : (p + 1) * SLOTS] for p in range(SLOTS)], axis=0
        ).astype(jnp.bfloat16)
        block = jnp.where(own, dot(stacked, spread), 0.0).astype(jnp.bfloat16)
        for side in range(sides):
            to = pl.multiple_of(position_ref[side] * strip, strip)
            blocks_ref[0, group, pl.ds(to, strip), :] = block[side * strip : (side + 1) * strip]


def mix_kernel(owner_ref, place_ref, order_ref, recv_ref, rank_ref, blocks_ref, out_ref, ins, outs):
    step = pl.program_id(0)
    devices, sides = recv_ref.shape[:2]
    unit = ins.shape[3]
    rows = devices * unit
    groups = blocks_ref.shape[1]
    strip = blocks_ref.shape[2] // sides
    pairs = devices // 2

    @pl.when(step == 0)
    def _():
        @pl.loop(0, devices)
        def _(source):
            for index in range(devices):
                owner = owner_ref[source, index]
                place = place_ref[source, index]
                at = (index % pairs) * unit
                for side in range(sides):
                    block = recv_ref[source, side, at : at + unit, :]
                    if index >= pairs:
                        block = pltpu.roll(block.astype(jnp.float32), HALF, 1).astype(jnp.bfloat16)
                    ins[side, owner, place] = block

    rows_iota, lanes_iota = iotas(rows)
    pair = range(PAIR)
    gathered = [[] for _ in pair]
    for side in range(sides):
        for index in pair:
            source = as_column(rank_ref[index, side], rows_iota, lanes_iota)
            operand = ins[side, PAIR * step + index].reshape(rows, LANES)
            gathered[index].append(dot(one_hot(source == lanes_iota), operand).astype(jnp.bfloat16))
    mixed = [[] for _ in pair]
    for group in range(groups):
        for index in pair:
            operand = jnp.concatenate(
                [part[group * strip : (group + 1) * strip] for part in gathered[index]], axis=0
            )
            mixed[index].append(dot(blocks_ref[index, group], operand).astype(jnp.bfloat16))
    for side in range(sides):
        for index in pair:
            operand = jnp.concatenate(
                [part[side * strip : (side + 1) * strip] for part in mixed[index]], axis=0
            )
            outs[side, PAIR * step + index] = (
                dot(one_hot(rows_iota == rank_ref[index, side]), operand)
                .astype(jnp.bfloat16)
                .reshape(devices, unit, LANES)
            )

    @pl.when(step == pl.num_programs(0) - 1)
    def _():
        low = lax.broadcasted_iota(jnp.int32, (unit, LANES), 1) < HALF

        @pl.loop(0, devices)
        def _(source):
            for index in range(pairs):
                owner = owner_ref[source, index]
                place = place_ref[source, index]
                owner_far = owner_ref[source, index + pairs]
                place_far = place_ref[source, index + pairs]
                for side in range(sides):
                    near = outs[side, owner, place].astype(jnp.float32)
                    far = outs[side, owner_far, place_far].astype(jnp.float32)
                    joined = jnp.where(low, near, pltpu.roll(far, HALF, 1)).astype(jnp.bfloat16)
                    out_ref[order_ref[side], source, index * unit : (index + 1) * unit, :] = joined


VMEM_BYTES = 24 * 1024 * 1024
VMEM_MOST = 60 * 1024 * 1024


def params(limit=VMEM_BYTES):
    return pltpu.CompilerParams(vmem_limit_bytes=limit)


def cost(flops, moved, waves=0):
    return pl.CostEstimate(flops=flops, bytes_accessed=moved, transcendentals=waves)


def whole_spec(array):
    zeros = (0,) * array.ndim
    return pl.BlockSpec(array.shape, lambda i, *_: zeros)


def weight_spec(section, features):
    return pl.BlockSpec((1, features, features), lambda i, *_: (section, 0, 0))


def run_front(current, where, received, own, start, sides, back_rows, rank_rows, weights, section, targets):
    _, rows, features = current.shape
    count = where.shape[0]
    narrow = features // HALF
    row_spec = pl.BlockSpec((1, 1, rows), lambda i, where: (start + i, 0, 0))
    first_target = 9 + len(received)
    return pl.pallas_call(
        functools.partial(front_kernel, own, count),
        grid_spec=pltpu.PrefetchScalarGridSpec(
            num_scalar_prefetch=1,
            grid=(count,),
            in_specs=[
                pl.BlockSpec((1, rows, features), lambda i, where: (where[i], 0, 0)),
                row_spec,
                row_spec,
            ]
            + [weight_spec(section, features)] * 5
            + [whole_spec(array) for array in received]
            + [pl.BlockSpec(memory_space=pl.ANY)] * len(targets),
            out_specs=[
                pl.BlockSpec((1, rows, features), lambda i, where: (start + i, 0, 0)),
                pl.BlockSpec((narrow, 1, rows // 2, LANES), lambda i, where: (0, start + i, 0, 0)),
            ],
            scratch_shapes=[pltpu.VMEM((rows, features), jnp.bfloat16)],
        ),
        out_shape=[
            jax.ShapeDtypeStruct((sides, rows, features), jnp.bfloat16),
            jax.ShapeDtypeStruct((narrow, sides, rows // 2, LANES), jnp.bfloat16),
        ],
        input_output_aliases={first_target + index: index for index in range(len(targets))},
        compiler_params=params(VMEM_BYTES if section else VMEM_MOST),
        cost_estimate=cost(12 * count * rows * features**2, 8 * count * rows * features),
        name="front",
    )(where, current, back_rows, rank_rows, *weights[:5], *received, *targets)


def run_back(second, packed, where, to, start, rank_rows, weights, at, total):
    _, rows, features = second.shape
    count = where.shape[0]
    narrow = packed.shape[1]
    return pl.pallas_call(
        back_kernel,
        grid_spec=pltpu.PrefetchScalarGridSpec(
            num_scalar_prefetch=2,
            grid=(count,),
            in_specs=[
                pl.BlockSpec((1, rows, features), lambda i, *_: (start + i, 0, 0)),
                pl.BlockSpec((1, narrow, rows // 2, LANES), lambda i, where, to: (where[i], 0, 0, 0)),
                pl.BlockSpec((1, 1, rows), lambda i, *_: (start + i, 0, 0)),
            ]
            + [weight_spec(index, features) for index in at],
            out_specs=pl.BlockSpec((1, rows, features), lambda i, where, to: (to[i], 0, 0)),
        ),
        out_shape=jax.ShapeDtypeStruct((total, rows, features), jnp.bfloat16),
        compiler_params=params(),
        cost_estimate=cost(8 * count * rows * features**2, 6 * count * rows * features),
        name="back",
    )(where, to, second, packed, rank_rows, *weights)


def rank_spec(entries):
    return pl.BlockSpec((1,) + entries.shape[1:], lambda i, *_: (i, 0, 0, 0))


def run_tables(places, order, position, entries, angles):
    owners = entries.shape[0]
    atoms = angles.shape[1]
    groups = atoms // GROUP
    span = GROUP * SLOTS
    return pl.pallas_call(
        table_kernel,
        grid_spec=pltpu.PrefetchScalarGridSpec(
            num_scalar_prefetch=3,
            grid=(owners,),
            in_specs=[
                rank_spec(entries),
                pl.BlockSpec((1, atoms, angles.shape[2]), lambda i, places, *_: (places[i], 0, 0)),
            ],
            out_specs=[
                rank_spec(entries),
                pl.BlockSpec((1, groups, span, span), lambda i, *_: (i, 0, 0, 0)),
            ],
        ),
        out_shape=[
            jax.ShapeDtypeStruct(entries.shape, jnp.int32),
            jax.ShapeDtypeStruct((owners, groups, span, span), jnp.bfloat16),
        ],
        compiler_params=params(),
        cost_estimate=cost(0, 8 * owners * groups * span**2),
        name="tables",
    )(places, order, position, entries, angles)


def run_mix(owner_of, place_of, order, received, rank, blocks):
    devices, sides, half, _ = received.shape
    unit = 2 * half // devices
    smem = pl.BlockSpec(memory_space=pltpu.SMEM)
    shape = (sides, devices, half, LANES)
    scratch = pltpu.VMEM((sides, devices, devices, unit, LANES), jnp.bfloat16)
    return pl.pallas_call(
        mix_kernel,
        grid=(devices // PAIR,),
        in_specs=[
            smem,
            smem,
            smem,
            whole_spec(received),
            pl.BlockSpec((PAIR,) + rank.shape[1:], lambda i: (i, 0, 0, 0)),
            pl.BlockSpec((PAIR,) + blocks.shape[1:], lambda i: (i, 0, 0, 0)),
        ],
        out_specs=pl.BlockSpec(shape, lambda i: (0, 0, 0, 0)),
        out_shape=jax.ShapeDtypeStruct(shape, jnp.bfloat16),
        scratch_shapes=[scratch, scratch],
        compiler_params=params(),
        cost_estimate=cost(10 * devices * sides * half**2 * LANES, 16 * devices * sides * half**2),
        name="mix",
    )(owner_of, place_of, order, received, rank, blocks)


def unit_tables(entries, capacity, unit):
    owners, sides, rows = entries.shape
    ids = jnp.arange(owners, dtype=jnp.int32)
    source = entries.reshape(owners, sides * rows) // capacity
    counts = jnp.sum((source[None] == ids[:, None, None]).astype(jnp.int32), axis=2) // (unit * sides)
    before = ids[:, None] < ids[None, :]
    starts = jnp.sum(jnp.where(before[None], counts[:, :, None], 0), axis=1)
    places = jnp.sum(jnp.where(before[:, :, None], counts[:, None, :], 0), axis=0)
    inside = (starts[:, :, None] <= ids) & (ids < (starts + counts)[:, :, None])
    owner_of = jnp.sum(jnp.where(inside, ids[None, :, None], 0), axis=1)
    place_of = jnp.sum(jnp.where(inside, (places - starts)[:, :, None] + ids, 0), axis=1)
    return owner_of, place_of


def ranks(values):
    return jnp.sum((values[:, :, None] < values[:, None, :]).astype(jnp.int32), axis=1)


CHUNKS = 2


def reorder(values, order):
    hits = order[:, None] == jnp.arange(values.shape[0], dtype=jnp.int32)
    return jnp.sum(jnp.where(hits[:, :, None], values[None], 0), axis=1)


def shift(values, offset, wide):
    if offset == 0:
        return values
    return lax.ppermute(values, "wide", [(i, i ^ offset) for i in range(wide)])


def swap(values):
    return lax.all_to_all(values, "narrow", 0, 0, tiled=True)


BASE = 64


def share_lists(listed, angles, after):
    narrow = lax.axis_size("narrow")
    atoms, width = angles.shape
    digits = jnp.stack([listed // BASE, listed % BASE]).reshape(atoms, -1).astype(jnp.bfloat16)
    shared = jnp.concatenate([angles, digits], axis=1)[None]
    held = [0]
    hop = narrow // 2
    while hop:
        if hop == 1:
            shared, after = lax.optimization_barrier((shared, after))
        other = lax.ppermute(shared, "narrow", [(i, i ^ hop) for i in range(narrow)])
        shared = jnp.concatenate([shared, other], axis=0)
        held += [offset ^ hop for offset in held]
        hop //= 2
    inverse = jnp.array([held.index(offset) for offset in range(narrow)], jnp.int32)
    mine = lax.axis_index("narrow").astype(jnp.int32)
    owners = jnp.arange(narrow, dtype=jnp.int32) ^ mine
    places = jnp.sum(jnp.where(owners[:, None] == jnp.arange(narrow), inverse, 0), axis=1)
    digits = shared[:, :, width:].reshape((narrow, 2) + listed.shape).astype(jnp.int32)
    entries = digits[:, 0] * BASE + digits[:, 1]
    entries = reorder(entries.reshape(narrow, -1), places).reshape(entries.shape)
    return entries, shared, places, after


def tiled_local(messages, reverse_position, route_slot, atom_slots, angles, weights):
    wide = lax.axis_size("wide")
    narrow = lax.axis_size("narrow")
    edge_rows, features = messages.shape
    rows = edge_rows // wide
    unit = rows // narrow
    capacity = 2 * edge_rows // narrow
    atoms = angles.shape[0]
    group_id = lax.axis_index("wide").astype(jnp.int32)
    offsets = [offset for index in range(wide // 2) for offset in (index, wide - 1 - index)]
    order = group_id ^ jnp.array(offsets, jnp.int32)
    inverse = jnp.array([offsets.index(offset) for offset in range(wide)], jnp.int32)
    owners_wide = (jnp.arange(wide, dtype=jnp.int32) ^ group_id)[:, None]
    position = jnp.sum(jnp.where(owners_wide == jnp.arange(wide), inverse, 0), axis=1)
    half = wide // 2
    pieces = [(0, 1), (1, wide - 1)]
    halves = [(half, wide - half), (0, half)]
    later = [(half, wide - half), (0, 1), (1, half - 1)]

    blocks_of = messages.reshape(wide, rows, features)
    sent = [
        lax.dynamic_index_in_dim(blocks_of, group_id ^ offset, 0, False) for offset in offsets[1:]
    ]
    *sent, atom_slots, route_slot, reverse_position = lax.optimization_barrier(
        (*sent, atom_slots, route_slot, reverse_position)
    )
    received = {offset: shift(part, offset, wide) for offset, part in zip(offsets[1:], sent)}
    listed = atom_slots.reshape(atoms // GROUP, GROUP, wide, SLOTS // wide)
    listed = reorder(jnp.transpose(listed, (2, 0, 3, 1)).reshape(wide, rows), order)
    rank = reorder(ranks(route_slot.reshape(wide, rows)), order)
    back_rows = reorder(reverse_position.reshape(wide, rows), order)

    current = {start: (blocks_of, order[start : start + count]) for start, count in pieces}
    tables = None
    for section in range(BLOCKS):
        last = section == BLOCKS - 1
        targets = []
        for start, count in later if section else pieces:
            array, where = current[start]
            needed = [received[offset] for offset in offsets[start : start + count] if offset]
            targets = list(run_front(
                array, where, needed, start == 0, start, wide,
                back_rows[:, None, :], rank[:, None, :], weights, section, targets,
            ))
        second, packed = targets
        if tables is None:
            entries, all_angles, owner_places, packed = share_lists(listed, angles, packed)
            packed, late_rank = lax.optimization_barrier((packed, rank))
            owner_of, place_of = unit_tables(entries, capacity, unit)
            tables = run_tables(owner_places, order, position, entries[:, :, None, :], all_angles)
            partner_rank = jnp.stack(
                [shift(late_rank[place], offset, wide) for place, offset in enumerate(offsets)]
            )
            hits = back_rows[:, :, None] == jnp.arange(rows, dtype=jnp.int32)
            turned_rank = jnp.sum(jnp.where(hits, partner_rank[:, None, :], 0), axis=2)[:, None, :]
        mixed = run_mix(owner_of, place_of, order, swap(packed), *tables)
        late, at = weights[5:], [section] * 3
        if not last:
            mixed, *late = lax.optimization_barrier((mixed, *late))
            late, at = [jnp.stack([weight[section] for weight in late])] * 3, range(3)
        mixed = mixed.reshape(wide * narrow, rows // 2, LANES)
        returned = lax.all_to_all(mixed, ("wide", "narrow"), 0, 0, tiled=True)
        returned = returned.reshape(wide, narrow, rows // 2, LANES)
        if last:
            current = run_back(second, returned, order, order, 0, turned_rank, late, at, wide)
            return current.reshape(edge_rows, features)
        for start, count in halves:
            plain = jnp.arange(count, dtype=jnp.int32)
            where = order[start : start + count]
            result = run_back(second, returned, where, plain, start, turned_rank, late, at, count)
            for first, number in later:
                if start <= first < start + count:
                    current[first] = (result, first - start + jnp.arange(number, dtype=jnp.int32))
            for index, offset in enumerate(offsets[start : start + count]):
                if offset:
                    received[offset] = shift(result[index], offset, wide)


def local(
    messages,
    reverse_position,
    route_slot,
    atom_slots,
    angles,
    weight_message,
    weight_reverse,
    weight_combine,
    weight_inner,
    weight_outer,
    weight_lift,
    weight_expand,
    weight_reduce,
):
    weights = (
        weight_message,
        weight_reverse,
        weight_combine,
        weight_inner,
        weight_outer,
        weight_lift,
        weight_expand,
        weight_reduce,
    )
    wide = lax.axis_size("wide")
    narrow = lax.axis_size("narrow")
    edge_rows, features = messages.shape
    unit = edge_rows // wide // narrow
    fits = (
        features == narrow * HALF
        and unit % 16 == 0
        and narrow % 2 == 0
        and wide >= 4
        and narrow % PAIR == 0
        and wide & (wide - 1) == 0
        and narrow & (narrow - 1) == 0
        and angles.shape[0] % GROUP == 0
        and (SLOTS // wide * GROUP) % 16 == 0
    )
    run = tiled_local if fits else general_local
    return run(messages, reverse_position, route_slot, atom_slots, angles, weights)


def solution(mesh):
    in_specs = (
        P(("wide", "narrow"), None),
        P(("wide", "narrow")),
        P(("wide", "narrow")),
        P(("wide", "narrow")),
        P(("wide", "narrow"), None),
        P(),
        P(),
        P(),
        P(),
        P(),
        P(),
        P(),
        P(),
    )
    out_specs = P(("wide", "narrow"), None)
    return jax.shard_map(local, mesh=mesh, in_specs=in_specs, out_specs=out_specs, check_vma=False)
```

```python
import functools

import jax
import jax.numpy as jnp
from jax import lax
from jax.experimental import pallas as pl
from jax.experimental.pallas import tpu as pltpu
from jax.sharding import PartitionSpec as P

SLOTS = 32
BLOCKS = 2
LANES = 128
HALF = LANES // 2
GROUP = 8
PAIR = 4


ROOT_HALF = 0.7071067811865476


def project(operand, weight):
    return jnp.dot(operand, weight, preferred_element_type=jnp.float32)


def residual(previous, branch):
    return ((previous.astype(jnp.float32) + branch) * ROOT_HALF).astype(jnp.bfloat16)


def reverse_edges(values, partner_rows):
    exchanged = lax.all_to_all(values, "wide", split_axis=0, concat_axis=0, tiled=True)
    return jnp.take(exchanged, partner_rows, axis=0)


def edge_front(current, reverse, weights, section_index):
    hidden = jax.nn.silu(
        project(current, weights[0][section_index]) + project(reverse, weights[1][section_index])
    ).astype(jnp.bfloat16)
    first_res = residual(current, project(hidden, weights[2][section_index]))
    inner_value = jax.nn.silu(project(first_res, weights[3][section_index])).astype(jnp.bfloat16)
    return residual(first_res, jax.nn.silu(project(inner_value, weights[4][section_index])))


def edge_back(second, turned, weights, section_index):
    third_res = residual(second, jax.nn.silu(project(turned, weights[5][section_index])))
    expand = jax.nn.silu(project(third_res, weights[6][section_index])).astype(jnp.bfloat16)
    return residual(third_res, jax.nn.silu(project(expand, weights[7][section_index])))


def owners_mix(second, route_slot, atom_slots, mixing):
    features = second.shape[1]
    buffer_rows = 2 * second.shape[0]
    outgoing = jnp.zeros((buffer_rows, features), jnp.bfloat16).at[route_slot].set(second)
    received = lax.all_to_all(outgoing, "narrow", split_axis=0, concat_axis=0, tiled=True)
    gathered = jnp.take(received, atom_slots, axis=0).reshape(mixing.shape[0], SLOTS, features)
    mixed_rows = jnp.einsum(
        "apq,aqd->apd", mixing, gathered, preferred_element_type=jnp.float32
    ).astype(jnp.bfloat16)
    return mixed_rows.reshape(-1, features)


def back_to_edges(mixed_flat, route_slot, atom_slots):
    features = mixed_flat.shape[1]
    buffer_rows = 2 * route_slot.shape[0]
    answer = jnp.zeros((buffer_rows, features), jnp.bfloat16).at[atom_slots].set(mixed_flat)
    incoming = lax.all_to_all(answer, "narrow", split_axis=0, concat_axis=0, tiled=True)
    return jnp.take(incoming, route_slot, axis=0)


def general_local(messages, reverse_position, route_slot, atom_slots, angles, weights):
    edge_rows = messages.shape[0]
    sub_rows = edge_rows // lax.axis_size("wide")
    partner_rows = jnp.arange(edge_rows, dtype=jnp.int32) // sub_rows * sub_rows + reverse_position
    mixing = angles.reshape(angles.shape[0], SLOTS, SLOTS)
    current = messages
    for section_index in range(BLOCKS):
        reverse = reverse_edges(current, partner_rows)
        second = edge_front(current, reverse, weights, section_index)
        mixed_flat = owners_mix(second, route_slot, atom_slots, mixing)
        returned = back_to_edges(mixed_flat, route_slot, atom_slots)
        turned = reverse_edges(returned, partner_rows)
        current = edge_back(second, turned, weights, section_index)
    return current


def silu(value):
    return 0.5 * value * (1.0 + jnp.tanh(0.5 * value))


def dot(left, right):
    return jnp.dot(left, right, preferred_element_type=jnp.float32)


def halve(previous, branch):
    return ((previous.astype(jnp.float32) + branch) * ROOT_HALF).astype(jnp.bfloat16)


def iotas(size):
    shape = (size, size)
    return lax.broadcasted_iota(jnp.int32, shape, 0), lax.broadcasted_iota(jnp.int32, shape, 1)


def as_column(row, rows_iota, lanes_iota):
    return jnp.sum(jnp.where(rows_iota == lanes_iota, row, 0), axis=1, keepdims=True)


def one_hot(mask):
    return jnp.where(mask, 1.0, 0.0).astype(jnp.bfloat16)


def row_parts(rows):
    size = rows // 4 if rows % 64 == 0 else rows // 2
    return [slice(start, start + size) for start in range(0, rows, size)]


def front_kernel(own, count, where_ref, cur_ref, back_ref, rank_ref, wm, wr, wc, wi, wo, *refs):
    recv_refs, (second_ref, packed_ref, reverse_ref) = refs[: count - own], refs[-3:]
    rows_iota, lanes_iota = iotas(cur_ref.shape[1])
    partner = as_column(back_ref[0], rows_iota, lanes_iota)
    hot = one_hot(partner == lanes_iota)
    sources = ([cur_ref.at[0]] if own else []) + list(recv_refs)
    for index in range(count):

        def permute():
            reverse_ref[...] = dot(hot, sources[index][...]).astype(jnp.bfloat16)

        if count == 1:
            permute()
        else:
            pl.when(pl.program_id(0) == index)(permute)

    parts = row_parts(cur_ref.shape[1])
    current = [cur_ref[0, part, :] for part in parts]
    sums = [dot(rows, wm[0]) + dot(reverse_ref[part, :], wr[0]) for rows, part in zip(current, parts)]
    hidden = [silu(rows).astype(jnp.bfloat16) for rows in sums]
    first_res = [halve(rows, dot(left, wc[0])) for rows, left in zip(current, hidden)]
    inner = [silu(dot(rows, wi[0])).astype(jnp.bfloat16) for rows in first_res]
    for rows, left, part in zip(first_res, inner, parts):
        second_ref[0, part, :] = halve(rows, silu(dot(left, wo[0])))
    second = second_ref[0]
    ordered = dot(one_hot(rows_iota == rank_ref[0]), second)
    half = ordered.shape[0] // 2
    low = lax.broadcasted_iota(jnp.int32, (half, LANES), 1) < HALF
    for tile in range(ordered.shape[1] // LANES):
        top = ordered[:half, tile * LANES : (tile + 1) * LANES]
        bottom = ordered[half:, tile * LANES : (tile + 1) * LANES]
        packed_ref[2 * tile, 0] = jnp.where(low, top, pltpu.roll(bottom, HALF, 1)).astype(jnp.bfloat16)
        packed_ref[2 * tile + 1, 0] = jnp.where(low, pltpu.roll(top, HALF, 1), bottom).astype(jnp.bfloat16)


def back_kernel(from_ref, to_ref, second_ref, packed_ref, rank_ref, wl, we, wd, out_ref):
    rows_iota, lanes_iota = iotas(second_ref.shape[1])
    half = rows_iota.shape[0] // 2
    low = lax.broadcasted_iota(jnp.int32, (half, LANES), 1) < HALF
    tops, bottoms = [], []
    for tile in range(second_ref.shape[2] // LANES):
        even = packed_ref[0, 2 * tile].astype(jnp.float32)
        odd = packed_ref[0, 2 * tile + 1].astype(jnp.float32)
        tops.append(jnp.where(low, even, pltpu.roll(odd, HALF, 1)).astype(jnp.bfloat16))
        bottoms.append(jnp.where(low, pltpu.roll(even, HALF, 1), odd).astype(jnp.bfloat16))
    ordered = jnp.concatenate(
        [jnp.concatenate(tops, axis=1), jnp.concatenate(bottoms, axis=1)], axis=0
    )
    source = as_column(rank_ref[0], rows_iota, lanes_iota)
    hot = one_hot(source == lanes_iota)
    parts = row_parts(hot.shape[0])
    turned = [dot(hot[part, :], ordered).astype(jnp.bfloat16) for part in parts]
    third_res = [
        halve(second_ref[0, part, :], silu(dot(rows, wl[0]))) for rows, part in zip(turned, parts)
    ]
    expand = [silu(dot(rows, we[0])).astype(jnp.bfloat16) for rows in third_res]
    for rows, left, part in zip(third_res, expand, parts):
        out_ref[0, part, :] = halve(rows, silu(dot(left, wd[0])))


def table_kernel(places_ref, order_ref, position_ref, entry_ref, angles_ref, rank_ref, blocks_ref):
    sides, _, size = entry_ref.shape[1:]
    rows_iota, lanes_iota = iotas(size)
    for side in range(sides):
        row = entry_ref[0, side]
        column = as_column(row, rows_iota, lanes_iota)
        rank_ref[0, side] = jnp.sum(jnp.where(column < row, 1, 0), axis=0, keepdims=True)
    span = GROUP * SLOTS
    strip = span // sides
    rows_iota, lanes_iota = iotas(span)
    own = rows_iota % GROUP == lanes_iota % GROUP
    spread_rows = lax.broadcasted_iota(jnp.int32, (SLOTS, span), 0)
    spread_lanes = lax.broadcasted_iota(jnp.int32, (SLOTS, span), 1)
    side_at = jnp.zeros((SLOTS, span), jnp.int32)
    for place in range(sides):
        side_at = jnp.where(spread_lanes // strip == place, order_ref[place], side_at)
    spread = one_hot(side_at * (SLOTS // sides) + spread_lanes % strip // GROUP == spread_rows)
    for group in range(angles_ref.shape[1] // GROUP):
        local = angles_ref[0, group * GROUP : (group + 1) * GROUP, :].astype(jnp.float32)
        stacked = jnp.concatenate(
            [local[:, p * SLOTS : (p + 1) * SLOTS] for p in range(SLOTS)], axis=0
        ).astype(jnp.bfloat16)
        block = jnp.where(own, dot(stacked, spread), 0.0).astype(jnp.bfloat16)
        for side in range(sides):
            to = pl.multiple_of(position_ref[side] * strip, strip)
            blocks_ref[0, group, pl.ds(to, strip), :] = block[side * strip : (side + 1) * strip]


def mix_kernel(owner_ref, place_ref, order_ref, recv_ref, rank_ref, blocks_ref, out_ref, ins, outs):
    step = pl.program_id(0)
    devices, sides = recv_ref.shape[:2]
    unit = ins.shape[3]
    rows = devices * unit
    groups = blocks_ref.shape[1]
    strip = blocks_ref.shape[2] // sides
    pairs = devices // 2

    @pl.when(step == 0)
    def _():
        @pl.loop(0, devices)
        def _(source):
            for index in range(devices):
                owner = owner_ref[source, index]
                place = place_ref[source, index]
                at = (index % pairs) * unit
                for side in range(sides):
                    block = recv_ref[source, side, at : at + unit, :]
                    if index >= pairs:
                        block = pltpu.roll(block.astype(jnp.float32), HALF, 1).astype(jnp.bfloat16)
                    ins[side, owner, place] = block

    rows_iota, lanes_iota = iotas(rows)
    pair = range(PAIR)
    gathered = [[] for _ in pair]
    for side in range(sides):
        for index in pair:
            source = as_column(rank_ref[index, side], rows_iota, lanes_iota)
            operand = ins[side, PAIR * step + index].reshape(rows, LANES)
            gathered[index].append(dot(one_hot(source == lanes_iota), operand).astype(jnp.bfloat16))
    mixed = [[] for _ in pair]
    for group in range(groups):
        for index in pair:
            operand = jnp.concatenate(
                [part[group * strip : (group + 1) * strip] for part in gathered[index]], axis=0
            )
            mixed[index].append(dot(blocks_ref[index, group], operand).astype(jnp.bfloat16))
    for side in range(sides):
        for index in pair:
            operand = jnp.concatenate(
                [part[side * strip : (side + 1) * strip] for part in mixed[index]], axis=0
            )
            outs[side, PAIR * step + index] = (
                dot(one_hot(rows_iota == rank_ref[index, side]), operand)
                .astype(jnp.bfloat16)
                .reshape(devices, unit, LANES)
            )

    @pl.when(step == pl.num_programs(0) - 1)
    def _():
        low = lax.broadcasted_iota(jnp.int32, (unit, LANES), 1) < HALF

        @pl.loop(0, devices)
        def _(source):
            for index in range(pairs):
                owner = owner_ref[source, index]
                place = place_ref[source, index]
                owner_far = owner_ref[source, index + pairs]
                place_far = place_ref[source, index + pairs]
                for side in range(sides):
                    near = outs[side, owner, place].astype(jnp.float32)
                    far = outs[side, owner_far, place_far].astype(jnp.float32)
                    joined = jnp.where(low, near, pltpu.roll(far, HALF, 1)).astype(jnp.bfloat16)
                    out_ref[order_ref[side], source, index * unit : (index + 1) * unit, :] = joined


VMEM_BYTES = 24 * 1024 * 1024
VMEM_MOST = 60 * 1024 * 1024


def params(limit=VMEM_BYTES):
    return pltpu.CompilerParams(vmem_limit_bytes=limit)


def cost(flops, moved, waves=0):
    return pl.CostEstimate(flops=flops, bytes_accessed=moved, transcendentals=waves)


def whole_spec(array):
    zeros = (0,) * array.ndim
    return pl.BlockSpec(array.shape, lambda i, *_: zeros)


def weight_spec(section, features):
    return pl.BlockSpec((1, features, features), lambda i, *_: (section, 0, 0))


def run_front(current, where, received, own, start, sides, back_rows, rank_rows, weights, section, targets):
    _, rows, features = current.shape
    count = where.shape[0]
    narrow = features // HALF
    row_spec = pl.BlockSpec((1, 1, rows), lambda i, where: (start + i, 0, 0))
    first_target = 9 + len(received)
    return pl.pallas_call(
        functools.partial(front_kernel, own, count),
        grid_spec=pltpu.PrefetchScalarGridSpec(
            num_scalar_prefetch=1,
            grid=(count,),
            in_specs=[
                pl.BlockSpec((1, rows, features), lambda i, where: (where[i], 0, 0)),
                row_spec,
                row_spec,
            ]
            + [weight_spec(section, features)] * 5
            + [whole_spec(array) for array in received]
            + [pl.BlockSpec(memory_space=pl.ANY)] * len(targets),
            out_specs=[
                pl.BlockSpec((1, rows, features), lambda i, where: (start + i, 0, 0)),
                pl.BlockSpec((narrow, 1, rows // 2, LANES), lambda i, where: (0, start + i, 0, 0)),
            ],
            scratch_shapes=[pltpu.VMEM((rows, features), jnp.bfloat16)],
        ),
        out_shape=[
            jax.ShapeDtypeStruct((sides, rows, features), jnp.bfloat16),
            jax.ShapeDtypeStruct((narrow, sides, rows // 2, LANES), jnp.bfloat16),
        ],
        input_output_aliases={first_target + index: index for index in range(len(targets))},
        compiler_params=params(VMEM_BYTES if section else VMEM_MOST),
        cost_estimate=cost(12 * count * rows * features**2, 8 * count * rows * features),
        name="front",
    )(where, current, back_rows, rank_rows, *weights[:5], *received, *targets)


def run_back(second, packed, where, to, start, rank_rows, weights, at, total):
    _, rows, features = second.shape
    count = where.shape[0]
    narrow = packed.shape[1]
    return pl.pallas_call(
        back_kernel,
        grid_spec=pltpu.PrefetchScalarGridSpec(
            num_scalar_prefetch=2,
            grid=(count,),
            in_specs=[
                pl.BlockSpec((1, rows, features), lambda i, *_: (start + i, 0, 0)),
                pl.BlockSpec((1, narrow, rows // 2, LANES), lambda i, where, to: (where[i], 0, 0, 0)),
                pl.BlockSpec((1, 1, rows), lambda i, *_: (start + i, 0, 0)),
            ]
            + [weight_spec(index, features) for index in at],
            out_specs=pl.BlockSpec((1, rows, features), lambda i, where, to: (to[i], 0, 0)),
        ),
        out_shape=jax.ShapeDtypeStruct((total, rows, features), jnp.bfloat16),
        compiler_params=params(),
        cost_estimate=cost(8 * count * rows * features**2, 6 * count * rows * features),
        name="back",
    )(where, to, second, packed, rank_rows, *weights)


def rank_spec(entries):
    return pl.BlockSpec((1,) + entries.shape[1:], lambda i, *_: (i, 0, 0, 0))


def run_tables(places, order, position, entries, angles):
    owners = entries.shape[0]
    atoms = angles.shape[1]
    groups = atoms // GROUP
    span = GROUP * SLOTS
    return pl.pallas_call(
        table_kernel,
        grid_spec=pltpu.PrefetchScalarGridSpec(
            num_scalar_prefetch=3,
            grid=(owners,),
            in_specs=[
                rank_spec(entries),
                pl.BlockSpec((1, atoms, angles.shape[2]), lambda i, places, *_: (places[i], 0, 0)),
            ],
            out_specs=[
                rank_spec(entries),
                pl.BlockSpec((1, groups, span, span), lambda i, *_: (i, 0, 0, 0)),
            ],
        ),
        out_shape=[
            jax.ShapeDtypeStruct(entries.shape, jnp.int32),
            jax.ShapeDtypeStruct((owners, groups, span, span), jnp.bfloat16),
        ],
        compiler_params=params(),
        cost_estimate=cost(0, 8 * owners * groups * span**2),
        name="tables",
    )(places, order, position, entries, angles)


def run_mix(owner_of, place_of, order, received, rank, blocks):
    devices, sides, half, _ = received.shape
    unit = 2 * half // devices
    smem = pl.BlockSpec(memory_space=pltpu.SMEM)
    shape = (sides, devices, half, LANES)
    scratch = pltpu.VMEM((sides, devices, devices, unit, LANES), jnp.bfloat16)
    return pl.pallas_call(
        mix_kernel,
        grid=(devices // PAIR,),
        in_specs=[
            smem,
            smem,
            smem,
            whole_spec(received),
            pl.BlockSpec((PAIR,) + rank.shape[1:], lambda i: (i, 0, 0, 0)),
            pl.BlockSpec((PAIR,) + blocks.shape[1:], lambda i: (i, 0, 0, 0)),
        ],
        out_specs=pl.BlockSpec(shape, lambda i: (0, 0, 0, 0)),
        out_shape=jax.ShapeDtypeStruct(shape, jnp.bfloat16),
        scratch_shapes=[scratch, scratch],
        compiler_params=params(),
        cost_estimate=cost(10 * devices * sides * half**2 * LANES, 16 * devices * sides * half**2),
        name="mix",
    )(owner_of, place_of, order, received, rank, blocks)


def unit_tables(entries, capacity, unit):
    owners, sides, rows = entries.shape
    ids = jnp.arange(owners, dtype=jnp.int32)
    source = entries.reshape(owners, sides * rows) // capacity
    counts = jnp.sum((source[None] == ids[:, None, None]).astype(jnp.int32), axis=2) // (unit * sides)
    before = ids[:, None] < ids[None, :]
    starts = jnp.sum(jnp.where(before[None], counts[:, :, None], 0), axis=1)
    places = jnp.sum(jnp.where(before[:, :, None], counts[:, None, :], 0), axis=0)
    inside = (starts[:, :, None] <= ids) & (ids < (starts + counts)[:, :, None])
    owner_of = jnp.sum(jnp.where(inside, ids[None, :, None], 0), axis=1)
    place_of = jnp.sum(jnp.where(inside, (places - starts)[:, :, None] + ids, 0), axis=1)
    return owner_of, place_of


def ranks(values):
    return jnp.sum((values[:, :, None] < values[:, None, :]).astype(jnp.int32), axis=1)


CHUNKS = 2


def reorder(values, order):
    hits = order[:, None] == jnp.arange(values.shape[0], dtype=jnp.int32)
    return jnp.sum(jnp.where(hits[:, :, None], values[None], 0), axis=1)


def shift(values, offset, wide):
    if offset == 0:
        return values
    return lax.ppermute(values, "wide", [(i, i ^ offset) for i in range(wide)])


def swap(values):
    return lax.all_to_all(values, "narrow", 0, 0, tiled=True)


BASE = 64


def share_lists(listed, angles, after):
    narrow = lax.axis_size("narrow")
    atoms, width = angles.shape
    digits = jnp.stack([listed // BASE, listed % BASE]).reshape(atoms, -1).astype(jnp.bfloat16)
    shared = jnp.concatenate([angles, digits], axis=1)[None]
    held = [0]
    hop = narrow // 2
    while hop:
        if hop == 1:
            shared, after = lax.optimization_barrier((shared, after))
        other = lax.ppermute(shared, "narrow", [(i, i ^ hop) for i in range(narrow)])
        shared = jnp.concatenate([shared, other], axis=0)
        held += [offset ^ hop for offset in held]
        hop //= 2
    inverse = jnp.array([held.index(offset) for offset in range(narrow)], jnp.int32)
    mine = lax.axis_index("narrow").astype(jnp.int32)
    owners = jnp.arange(narrow, dtype=jnp.int32) ^ mine
    places = jnp.sum(jnp.where(owners[:, None] == jnp.arange(narrow), inverse, 0), axis=1)
    digits = shared[:, :, width:].reshape((narrow, 2) + listed.shape).astype(jnp.int32)
    entries = digits[:, 0] * BASE + digits[:, 1]
    entries = reorder(entries.reshape(narrow, -1), places).reshape(entries.shape)
    return entries, shared, places, after


def tiled_local(messages, reverse_position, route_slot, atom_slots, angles, weights):
    wide = lax.axis_size("wide")
    narrow = lax.axis_size("narrow")
    edge_rows, features = messages.shape
    rows = edge_rows // wide
    unit = rows // narrow
    capacity = 2 * edge_rows // narrow
    atoms = angles.shape[0]
    group_id = lax.axis_index("wide").astype(jnp.int32)
    offsets = [offset for index in range(wide // 2) for offset in (index, wide - 1 - index)]
    order = group_id ^ jnp.array(offsets, jnp.int32)
    inverse = jnp.array([offsets.index(offset) for offset in range(wide)], jnp.int32)
    owners_wide = (jnp.arange(wide, dtype=jnp.int32) ^ group_id)[:, None]
    position = jnp.sum(jnp.where(owners_wide == jnp.arange(wide), inverse, 0), axis=1)
    half = wide // 2
    pieces = [(0, 1), (1, wide - 1)]
    halves = [(half, wide - half), (0, half)]
    later = [(half, wide - half), (0, 1), (1, half - 1)]

    blocks_of = messages.reshape(wide, rows, features)
    sent = [
        lax.dynamic_index_in_dim(blocks_of, group_id ^ offset, 0, False) for offset in offsets[1:]
    ]
    *sent, atom_slots, route_slot, reverse_position = lax.optimization_barrier(
        (*sent, atom_slots, route_slot, reverse_position)
    )
    received = {offset: shift(part, offset, wide) for offset, part in zip(offsets[1:], sent)}
    listed = atom_slots.reshape(atoms // GROUP, GROUP, wide, SLOTS // wide)
    listed = reorder(jnp.transpose(listed, (2, 0, 3, 1)).reshape(wide, rows), order)
    rank = reorder(ranks(route_slot.reshape(wide, rows)), order)
    back_rows = reorder(reverse_position.reshape(wide, rows), order)

    current = {start: (blocks_of, order[start : start + count]) for start, count in pieces}
    tables = None
    for section in range(BLOCKS):
        last = section == BLOCKS - 1
        targets = []
        for start, count in later if section else pieces:
            array, where = current[start]
            needed = [received[offset] for offset in offsets[start : start + count] if offset]
            targets = list(run_front(
                array, where, needed, start == 0, start, wide,
                back_rows[:, None, :], rank[:, None, :], weights, section, targets,
            ))
        second, packed = targets
        if tables is None:
            entries, all_angles, owner_places, packed = share_lists(listed, angles, packed)
            packed, late_rank = lax.optimization_barrier((packed, rank))
            owner_of, place_of = unit_tables(entries, capacity, unit)
            tables = run_tables(owner_places, order, position, entries[:, :, None, :], all_angles)
            partner_rank = jnp.stack(
                [shift(late_rank[place], offset, wide) for place, offset in enumerate(offsets)]
            )
            hits = back_rows[:, :, None] == jnp.arange(rows, dtype=jnp.int32)
            turned_rank = jnp.sum(jnp.where(hits, partner_rank[:, None, :], 0), axis=2)[:, None, :]
        mixed = run_mix(owner_of, place_of, order, swap(packed), *tables)
        late, at = weights[5:], [section] * 3
        if not last:
            mixed, *late = lax.optimization_barrier((mixed, *late))
            late, at = [jnp.stack([weight[section] for weight in late])] * 3, range(3)
        mixed = mixed.reshape(wide * narrow, rows // 2, LANES)
        returned = lax.all_to_all(mixed, ("wide", "narrow"), 0, 0, tiled=True)
        returned = returned.reshape(wide, narrow, rows // 2, LANES)
        if last:
            current = run_back(second, returned, order, order, 0, turned_rank, late, at, wide)
            return current.reshape(edge_rows, features)
        for start, count in halves:
            plain = jnp.arange(count, dtype=jnp.int32)
            where = order[start : start + count]
            result = run_back(second, returned, where, plain, start, turned_rank, late, at, count)
            for first, number in later:
                if start <= first < start + count:
                    current[first] = (result, first - start + jnp.arange(number, dtype=jnp.int32))
            for index, offset in enumerate(offsets[start : start + count]):
                if offset:
                    received[offset] = shift(result[index], offset, wide)


def local(
    messages,
    reverse_position,
    route_slot,
    atom_slots,
    angles,
    weight_message,
    weight_reverse,
    weight_combine,
    weight_inner,
    weight_outer,
    weight_lift,
    weight_expand,
    weight_reduce,
):
    weights = (
        weight_message,
        weight_reverse,
        weight_combine,
        weight_inner,
        weight_outer,
        weight_lift,
        weight_expand,
        weight_reduce,
    )
    wide = lax.axis_size("wide")
    narrow = lax.axis_size("narrow")
    edge_rows, features = messages.shape
    unit = edge_rows // wide // narrow
    fits = (
        features == narrow * HALF
        and unit % 16 == 0
        and narrow % 2 == 0
        and wide >= 4
        and narrow % PAIR == 0
        and wide & (wide - 1) == 0
        and narrow & (narrow - 1) == 0
        and angles.shape[0] % GROUP == 0
        and (SLOTS // wide * GROUP) % 16 == 0
    )
    run = tiled_local if fits else general_local
    return run(messages, reverse_position, route_slot, atom_slots, angles, weights)


def solution(mesh):
    in_specs = (
        P(("wide", "narrow"), None),
        P(("wide", "narrow")),
        P(("wide", "narrow")),
        P(("wide", "narrow")),
        P(("wide", "narrow"), None),
        P(),
        P(),
        P(),
        P(),
        P(),
        P(),
        P(),
        P(),
    )
    out_specs = P(("wide", "narrow"), None)
    return jax.shard_map(local, mesh=mesh, in_specs=in_specs, out_specs=out_specs, check_vma=False)
```
